256 devices in a mesh: seq: 64 (over x, z_hi, y), batch: 4 (over z_lo, core).
Axes of the slice: x: 4, y: 4, z: 8 (z_hi: 4, z_lo: 2; z = z_hi * 2 + z_lo), core: 2. Of those that a mesh axis runs over, the one named last changes fastest.
Arguments:
- sequence: bfloat16 [32768, 512], P(('batch', 'seq')), parts along dimension 0, may hold values from -6 to 6
- upstream: bfloat16 [32768, 512], P(('batch', 'seq')), parts along dimension 0, may hold values from -6 to 6
- norm_gain: float32 [512], replicated, may hold values from 0.1 to 1.9
- in_proj: bfloat16 [512, 2304], replicated, may hold values from -0.25 to 0.25
- step_proj: bfloat16 [512, 16], replicated, may hold values from -0.25 to 0.25
- conv_weight: float32 [4, 1280], replicated, may hold values from -3 to 3
- conv_bias: float32 [1280], replicated, may hold values from -3 to 3
- step_bias: float32 [16], replicated, may hold values from -5.5 to -3.5
- decay_log: float32 [16], replicated
- skip_gain: float32 [16], replicated, may hold values from 0.5 to 2
- out_proj: bfloat16 [1024, 512], replicated, may hold values from -0.1875 to 0.1875
Outputs:
- layer_out: bfloat16 [32768, 512], P(('batch', 'seq')), parts along dimension 0
- grad_input: bfloat16 [32768, 512], P(('batch', 'seq')), parts along dimension 0
- grad_in_proj: float32 [2048, 2304], P(('batch', 'seq')), parts along dimension 0
- grad_out_proj: float32 [4096, 512], P(('batch', 'seq')), parts along dimension 0
The draws below stay inside these ranges and needn't reach their ends.
There are 4 independent parts, one for each index of `batch`. The reference program is written for one: setup_inputs(seed, part) draws one part's arguments, and reference() takes and returns one part's arrays. A program takes and returns all parts, laid end to end along the dimension named above; an argument that names none is the same for every part. Nothing has to cross between parts.
All inputs are finite; a program needn't handle non-finite values.
Results may differ from the reference program's by a relative error of at most 0.015.
Values may be sent and summed in bfloat16 or wider, within the bound.
No kernel may reach another device: no remote copies, remote signals or barrier semaphores. Data moves between devices by JAX's collectives and lax.ppermute only.
A program may use at most 192 MiB of HBM per device.

```python
import math
import jax
import jax.numpy as jnp
from jax import lax

D = 512
E = 1024
N = 128
H = 16
CONV = 4
TOK_DEV = 128
TOKENS = 8192
N_SEQ = 64


def draw_decay_log(key, part):
    key = jax.random.fold_in(key, 11)
    key_pick, key_slow, key_fast = jax.random.split(key, 3)
    share = 0.5
    picked = jax.random.uniform(key_pick, (H,), jnp.float32) < share
    slow_rate = jnp.exp(jax.random.uniform(key_slow, (H,), jnp.float32, math.log(0.5), math.log(2.0))) / (0.018 * TOKENS)
    fast_rate = jax.random.uniform(key_fast, (H,), jnp.float32, 1.0, 2.0)
    return jnp.log(jnp.where(picked, fast_rate, slow_rate)).astype(jnp.float32)


def level_of(rng, extent, pieces, low, high):
    loudness, own = 1.0, jax.random.fold_in(rng, 6)
    for axis_at, parts in pieces:
        draws = jnp.exp(jax.random.uniform(jax.random.fold_in(own, axis_at), (parts,), jnp.float32, low / len(pieces), high / len(pieces)))
        loudness = loudness * jnp.repeat(draws, extent[axis_at] // parts).reshape([-1 if axis == axis_at else 1 for axis in range(len(extent))])
    return loudness


def bell_draw(stream_key, extent, deviation, reach, cuts=(), kind=jnp.bfloat16):
    array = deviation * jax.random.normal(stream_key, extent, jnp.float32)
    if cuts:
        array = array * level_of(stream_key, extent, cuts, -0.22, 0.18)
    return jnp.clip(array, -reach, reach).astype(kind)


def setup_inputs(seed: int = 0, part: int = 0) -> dict:
    arg_keys = jax.random.split(jax.random.key(seed), 12)
    part_keys = jax.random.split(jax.random.fold_in(arg_keys[11], part), 12)
    return {
        "sequence": bell_draw(part_keys[0], (TOKENS, D), 1.0, 6.0, ((0, 64),)),
        "upstream": bell_draw(part_keys[1], (TOKENS, D), 1.0, 6.0, ((0, 64),)),
        "norm_gain": jnp.clip(1.0 + 0.18 * jax.random.normal(arg_keys[2], (D,), jnp.float32), 0.1, 1.9),
        "in_proj": bell_draw(arg_keys[3], (D, 2 * E + 2 * N), D ** -0.5, 0.25),
        "step_proj": bell_draw(arg_keys[4], (D, H), D ** -0.5, 0.25),
        "conv_weight": bell_draw(arg_keys[5], (CONV, E + 2 * N), 0.5, 3.0, (), jnp.float32),
        "conv_bias": bell_draw(arg_keys[6], (E + 2 * N,), 0.5, 3.0, (), jnp.float32),
        "step_bias": jnp.clip(jax.random.uniform(arg_keys[7], (H,), jnp.float32, -5.5, -3.5), -5.5, -3.5),
        "decay_log": draw_decay_log(jax.random.fold_in(arg_keys[11], 71), part),
        "skip_gain": jnp.clip(jax.random.uniform(arg_keys[9], (H,), jnp.float32, 0.5, 2.0), 0.5, 2.0),
        "out_proj": bell_draw(arg_keys[10], (E, D), E ** -0.5, 0.1875),
    }


epsilon = 1e-06

def normed(vector, norm_gain):
    scale = lax.rsqrt(lax.optimization_barrier(jnp.mean(vector * vector, axis=-1, keepdims=True)) + epsilon)
    return vector * scale * norm_gain

def contract_rows(left, right):
    return lax.dot_general(left, right, (((0,), (0,)), ((), ())), preferred_element_type=jnp.float32)

def contract_cols(left, right):
    return lax.dot_general(left, right, (((1,), (1,)), ((), ())), preferred_element_type=jnp.float32)

def prepare(extended, step_raw, conv_weight, conv_bias, step_bias, decay_log, inner_width):
    count_rows = step_raw.shape[0]
    convolved = conv_bias
    for tap in range(conv_weight.shape[0]):
        convolved = convolved + extended[tap:tap + count_rows] * conv_weight[tap]
    activated = jax.nn.silu(convolved)
    heads = step_raw.shape[1]
    state_dim = (activated.shape[1] - inner_width) // 2
    inputs_ssd = activated[:, :inner_width].reshape(count_rows, heads, inner_width // heads)
    b_matrix = activated[:, inner_width:inner_width + state_dim]
    c_matrix = activated[:, inner_width + state_dim:]
    step_size = jax.nn.softplus(step_raw + step_bias)
    log_decay = -jnp.exp(decay_log) * step_size
    cumul = jnp.cumsum(log_decay, axis=0)
    driven = inputs_ssd * step_size[:, :, None]
    totals = cumul[-1]
    weight_end = jnp.exp(totals[None, :] - cumul)
    local_state = jnp.einsum('th,thp,tn->hpn', weight_end, driven, b_matrix, precision=lax.Precision.HIGHEST)
    return ((inputs_ssd, b_matrix, c_matrix, cumul, driven), local_state, totals)

def finish(inner_vals, gate_rows, carried, skip_gain):
    inputs_ssd, b_matrix, c_matrix, cumul, driven = inner_vals
    count_rows = inputs_ssd.shape[0]
    scores = jnp.dot(c_matrix, b_matrix.T, precision=lax.Precision.HIGHEST)
    places = jnp.arange(count_rows)
    lower_mask = (places[:, None] >= places[None, :])[None, :, :]
    differ = cumul.T[:, :, None] - cumul.T[:, None, :]
    decays = jnp.where(lower_mask, jnp.exp(jnp.where(lower_mask, differ, 0.0)), 0.0)
    intra = jnp.einsum('hts,ts,shp->thp', decays, scores, driven, precision=lax.Precision.HIGHEST)
    carry_in = jnp.einsum('th,tn,hpn->thp', jnp.exp(cumul), c_matrix, carried, precision=lax.Precision.HIGHEST)
    mixed_heads = intra + carry_in + skip_gain[None, :, None] * inputs_ssd
    return (mixed_heads.reshape(count_rows, -1) * jax.nn.silu(gate_rows)).astype(jnp.bfloat16)

def ssd_core(gate_rows, xbc_rows, step_raw, conv_weight, conv_bias, step_bias, decay_log, skip_gain):
    channels = xbc_rows.shape[1]
    padded = jnp.concatenate([jnp.zeros((CONV - 1, channels), jnp.float32), xbc_rows], axis=0)
    start_state = jnp.zeros((H, E // H, N), jnp.float32)

    def block_step(carried, index):
        start = (index * TOK_DEV).astype(jnp.int32)
        extended = lax.dynamic_slice_in_dim(padded, start, TOK_DEV + CONV - 1, 0)
        raw_block = lax.dynamic_slice_in_dim(step_raw, start, TOK_DEV, 0)
        gate_block = lax.dynamic_slice_in_dim(gate_rows, start, TOK_DEV, 0)
        inner_vals, local_state, totals = prepare(extended, raw_block, conv_weight, conv_bias, step_bias, decay_log, E)
        gated = finish(inner_vals, gate_block, carried, skip_gain)
        carried = jnp.exp(totals)[:, None, None] * carried + local_state
        return (carried, gated)
    final_state, gated = lax.scan(block_step, start_state, jnp.arange(N_SEQ, dtype=jnp.int32))
    return gated.reshape(N_SEQ * TOK_DEV, E)

def run_frame(frame_in, cotangent, norm_gain, in_proj, step_proj, conv_weight, conv_bias, step_bias, decay_log, skip_gain, out_proj):
    normal_rows, pullback = jax.vjp(lambda vector: normed(vector, norm_gain), frame_in)
    normal_bf = normal_rows.astype(jnp.bfloat16)
    projected = jnp.dot(normal_bf, in_proj, preferred_element_type=jnp.float32)
    step_raw = jnp.dot(normal_bf, step_proj, preferred_element_type=jnp.float32)
    gate_rows = projected[:, :E]
    xbc_rows = lax.optimization_barrier(projected[:, E:].astype(jnp.bfloat16)).astype(jnp.float32)

    def core_fn(gate_in, xbc_in, raw_in):
        return ssd_core(gate_in, xbc_in, raw_in, conv_weight, conv_bias, step_bias, decay_log, skip_gain)
    gated, core_back = jax.vjp(core_fn, gate_rows, xbc_rows, step_raw)
    branch = jnp.dot(gated, out_proj, preferred_element_type=jnp.float32)
    out_term = contract_rows(gated, cotangent)
    d_gated = contract_cols(cotangent, out_proj).astype(jnp.bfloat16)
    d_gate, d_xbc, d_step = core_back(d_gated)
    d_proj = jnp.concatenate([d_gate, d_xbc], axis=1).astype(jnp.bfloat16)
    d_step_bf = d_step.astype(jnp.bfloat16)
    d_normed = contract_cols(d_proj, in_proj) + contract_cols(d_step_bf, step_proj)
    d_frame, = pullback(d_normed)
    in_term = contract_rows(normal_bf, d_proj)
    return (branch, d_frame, in_term, out_term)

def reference(sequence, upstream, norm_gain, in_proj, step_proj, conv_weight, conv_bias, step_bias, decay_log, skip_gain, out_proj):
    forward_in = sequence.astype(jnp.float32)
    params = (norm_gain, in_proj, step_proj, conv_weight, conv_bias, step_bias, decay_log, skip_gain, out_proj)
    branch_f, d_in_f, in_f, out_f = run_frame(forward_in, upstream, *params)
    branch_r, d_in_r, in_r, out_r = run_frame(forward_in[::-1, ::-1], upstream[::-1, ::-1], *params)
    layer_out = (branch_f + branch_r[::-1, ::-1]).astype(jnp.bfloat16)
    grad_input = (d_in_f + d_in_r[::-1, ::-1]).astype(jnp.bfloat16)
    return (layer_out, grad_input, in_f + in_r, out_f + out_r)
```

```python
import jax
import jax.numpy as jnp
from jax import lax
from jax.sharding import PartitionSpec as P

epsilon = 1e-06
SIDE = 4


def shift_pairs(stride, step):
    pairs = []
    for source in range(SIDE**3):
        digit = source // stride % SIDE
        pairs.append((source, source + ((digit + step) % SIDE - digit) * stride))
    return pairs


def reduce_axis(parts, stride):
    place = lax.axis_index("seq") // stride % SIDE
    total = lax.dynamic_index_in_dim(parts, place, 0, False)
    for step in range(1, SIDE):
        outgoing = lax.dynamic_index_in_dim(parts, (place + step) % SIDE, 0, False)
        total = total + lax.ppermute(
            outgoing.astype(jnp.bfloat16), "seq", shift_pairs(stride, step)
        ).astype(jnp.float32)
    return total


def reduce_by_axes(term):
    for stride in (SIDE * SIDE, SIDE, 1):
        term = reduce_axis(term.reshape(SIDE, term.shape[0] // SIDE, term.shape[1]), stride)
    return term


def reduce_at_once(term):
    count = lax.axis_size("seq")
    pieces = term.astype(jnp.bfloat16).reshape(count, term.shape[0] // count, term.shape[1])
    got = lax.all_to_all(pieces, "seq", 0, 0)
    return jnp.sum(got.astype(jnp.float32), axis=0)


def split3(value):
    high = value.astype(jnp.bfloat16)
    rest = value - high.astype(jnp.float32)
    mid = rest.astype(jnp.bfloat16)
    low = (rest - mid.astype(jnp.float32)).astype(jnp.bfloat16)
    return jnp.stack([high, mid, low], axis=-1)


def span_weights(totals):
    count = totals.shape[0]
    totals = jnp.maximum(totals, -200.0)
    upto = jnp.cumsum(totals)
    before = upto - totals
    places = jnp.arange(count)
    mask = places[:, None] > places[None, :]
    return jnp.where(mask, jnp.exp(jnp.where(mask, before[:, None] - upto[None, :], 0.0)), 0.0)


def scans(local_f, local_r, back_f, back_r, totals_f, totals_r):
    count = lax.axis_size("seq")
    heads, width, state = local_f.shape
    rows = heads * width // count
    stacked = jnp.stack([local_f, local_r, back_f, back_r]).astype(jnp.bfloat16)
    stacked = stacked.reshape(4, count, rows, state).transpose(1, 0, 2, 3).reshape(count, 4 * rows, state)
    extra = jnp.stack([split3(totals_f), split3(totals_r)], axis=1).reshape(heads, 1, 6)
    extra = jnp.repeat(jnp.pad(extra, ((0, 0), (0, 7), (0, state - 6))), count // heads, axis=0)
    got = lax.all_to_all(jnp.concatenate([stacked, extra], axis=1), "seq", 0, 0)
    tail = got[:, 4 * rows, :6].astype(jnp.float32).reshape(count, 2, 3)
    total = (tail[:, :, 2] + tail[:, :, 1]) + tail[:, :, 0]
    weights_f, weights_r = span_weights(total[:, 0]), span_weights(total[:, 1])
    weights = jnp.stack([weights_f, weights_r.T, weights_f.T, weights_r])
    blocks = got[:, : 4 * rows].reshape(count, 4, rows, state).astype(jnp.float32)
    mixed = jnp.einsum("sij,jsrn->isrn", weights, blocks, precision=lax.Precision.HIGHEST)
    mixed = mixed.astype(jnp.bfloat16).reshape(count, 4 * rows, state)
    back = lax.all_to_all(mixed, "seq", 0, 0)
    back = back.reshape(count, 4, rows, state).transpose(1, 0, 2, 3)
    back = back.reshape(4, heads, width, state).astype(jnp.float32)
    return back[0], back[1], back[2], back[3]


def padded(block, sides, width):
    for axis, dim in sides:
        count = lax.axis_size(axis)
        forward = [(i, i + 1) for i in range(count - 1)]
        backward = [(target, source) for source, target in forward]
        low = lax.ppermute(
            lax.slice_in_dim(block, block.shape[dim] - width, None, axis=dim), axis, forward
        )
        high = lax.ppermute(lax.slice_in_dim(block, 0, width, axis=dim), axis, backward)
        block = jnp.concatenate([low, block, high], axis=dim)
    return block


def normed(vector, norm_gain):
    scale = lax.rsqrt(jnp.mean(vector * vector, axis=-1, keepdims=True) + epsilon)
    return vector * scale * norm_gain


def contract_rows(left, right):
    return lax.dot_general(
        left, right, (((0,), (0,)), ((), ())), preferred_element_type=jnp.float32
    )


def contract_cols(left, right):
    return lax.dot_general(
        left, right, (((1,), (1,)), ((), ())), preferred_element_type=jnp.float32
    )


def prepare(extended, step_raw, conv_weight, conv_bias, step_bias, decay_log, inner_width):
    count_rows = step_raw.shape[0]
    convolved = conv_bias
    for tap in range(conv_weight.shape[0]):
        convolved = convolved + extended[tap : tap + count_rows] * conv_weight[tap]
    activated = jax.nn.silu(convolved)
    heads = step_raw.shape[1]
    state_dim = (activated.shape[1] - inner_width) // 2
    inputs_ssd = activated[:, :inner_width].reshape(count_rows, heads, inner_width // heads)
    b_matrix = activated[:, inner_width : inner_width + state_dim]
    c_matrix = activated[:, inner_width + state_dim :]
    step_size = jax.nn.softplus(step_raw + step_bias)
    log_decay = -jnp.exp(decay_log) * step_size
    cumul = jnp.cumsum(log_decay, axis=0)
    driven = inputs_ssd * step_size[:, :, None]
    totals = cumul[-1]
    weight_end = jnp.exp(totals[None, :] - cumul)
    local_state = jnp.einsum(
        "th,thp,tn->hpn", weight_end, driven, b_matrix, precision=lax.Precision.HIGHEST
    )
    return ((inputs_ssd, b_matrix, c_matrix, cumul, driven), local_state, totals)


def finish(inner_vals, gate_rows, carried, skip_gain):
    inputs_ssd, b_matrix, c_matrix, cumul, driven = inner_vals
    count_rows = inputs_ssd.shape[0]
    scores = jnp.dot(c_matrix, b_matrix.T, precision=lax.Precision.HIGHEST)
    places = jnp.arange(count_rows)
    lower_mask = (places[:, None] >= places[None, :])[None, :, :]
    differ = cumul.T[:, :, None] - cumul.T[:, None, :]
    decays = jnp.where(lower_mask, jnp.exp(jnp.where(lower_mask, differ, 0.0)), 0.0)
    intra = jnp.einsum("hts,ts,shp->thp", decays, scores, driven, precision=lax.Precision.HIGHEST)
    carry_in = jnp.einsum(
        "th,tn,hpn->thp", jnp.exp(cumul), c_matrix, carried, precision=lax.Precision.HIGHEST
    )
    mixed_heads = intra + carry_in + skip_gain[None, :, None] * inputs_ssd
    return (mixed_heads.reshape(count_rows, -1) * jax.nn.silu(gate_rows)).astype(jnp.bfloat16)


def frontend(frame_in, norm_gain, in_proj, step_proj, inner_width):
    normal_rows, pullback = jax.vjp(lambda vector: normed(vector, norm_gain), frame_in)
    normal_bf = normal_rows.astype(jnp.bfloat16)
    projected = jnp.dot(normal_bf, in_proj, preferred_element_type=jnp.float32)
    step_raw = jnp.dot(normal_bf, step_proj, preferred_element_type=jnp.float32)
    xbc_rows = lax.optimization_barrier(projected[:, inner_width:].astype(jnp.bfloat16))
    return (normal_bf, pullback, projected[:, :inner_width], xbc_rows, step_raw)


def backend(pullback, d_gate, d_xbc, d_step, in_proj, step_proj):
    d_proj = jnp.concatenate([d_gate, d_xbc], axis=1).astype(jnp.bfloat16)
    d_normed = contract_cols(d_proj, in_proj) + contract_cols(
        d_step.astype(jnp.bfloat16), step_proj
    )
    (d_frame,) = pullback(d_normed)
    return (d_frame, d_proj)


def shards(
    sequence,
    upstream,
    norm_gain,
    in_proj,
    step_proj,
    conv_weight,
    conv_bias,
    step_bias,
    decay_log,
    skip_gain,
    out_proj,
):
    inner_width = out_proj.shape[0]
    count_rows = sequence.shape[0]
    margin = conv_weight.shape[0] - 1
    forward_in = sequence.astype(jnp.float32)
    mirror_in = forward_in[::-1, ::-1]
    upstream_rev = upstream[::-1, ::-1]
    normal_f, pullback_f, gate_f, xbc_f, raw_f = frontend(
        forward_in, norm_gain, in_proj, step_proj, inner_width
    )
    normal_r, pullback_r, gate_r, xbc_r, raw_r = frontend(
        mirror_in, norm_gain, in_proj, step_proj, inner_width
    )
    packed = jnp.concatenate([xbc_r[count_rows - margin :], xbc_f[count_rows - margin :]], axis=0)
    widened = padded(packed, (("seq", 0),), margin)
    lead_f = widened[:margin]
    lead_r = widened[3 * margin :]
    extended_f = jnp.concatenate([lead_f, xbc_f], axis=0).astype(jnp.float32)
    extended_r = jnp.concatenate([lead_r, xbc_r], axis=0).astype(jnp.float32)

    def local_core(extended, raw_rows):
        return prepare(
            extended, raw_rows, conv_weight, conv_bias, step_bias, decay_log, inner_width
        )

    def local_post(inner_vals, gate_rows, carried):
        return finish(inner_vals, gate_rows, carried, skip_gain)

    pre_f, pre_back_f = jax.vjp(local_core, extended_f, raw_f)
    inner_f, local_f, totals_f = pre_f
    pre_r, pre_back_r = jax.vjp(local_core, extended_r, raw_r)
    inner_r, local_r, totals_r = pre_r
    d_gated_f = contract_cols(upstream, out_proj).astype(jnp.bfloat16)
    d_gated_r = contract_cols(upstream_rev, out_proj).astype(jnp.bfloat16)

    def back_state(inner_vals, gate_rows, d_gated):
        c_matrix, cumul = inner_vals[2], inner_vals[3]
        d_mixed = d_gated.astype(jnp.float32) * jax.nn.silu(gate_rows)
        d_mixed = d_mixed.reshape(count_rows, cumul.shape[1], -1)
        return jnp.einsum(
            "th,tn,thp->hpn", jnp.exp(cumul), c_matrix, d_mixed, precision=lax.Precision.HIGHEST
        )

    carried_f, carried_r, reach_f, reach_r = scans(
        local_f,
        local_r,
        back_state(inner_f, gate_f, d_gated_f),
        back_state(inner_r, gate_r, d_gated_r),
        totals_f,
        totals_r,
    )
    gated_f, post_back_f = jax.vjp(local_post, inner_f, gate_f, carried_f)
    d_inner_f, d_gate_f, _ = post_back_f(d_gated_f)
    gated_r, post_back_r = jax.vjp(local_post, inner_r, gate_r, carried_r)
    d_inner_r, d_gate_r, _ = post_back_r(d_gated_r)
    d_totals_f = jnp.exp(totals_f) * jnp.sum(carried_f * reach_f, axis=(1, 2))
    d_totals_r = jnp.exp(totals_r) * jnp.sum(carried_r * reach_r, axis=(1, 2))
    d_ext_f, d_raw_f = pre_back_f((d_inner_f, reach_f, d_totals_f))
    d_ext_r, d_raw_r = pre_back_r((d_inner_r, reach_r, d_totals_r))
    packed_grad = jnp.concatenate([d_ext_f[:margin], d_ext_r[:margin]], axis=0)
    returned = padded(packed_grad, (("seq", 0),), margin)
    d_xbc_f = jnp.concatenate(
        [d_ext_f[margin:count_rows], d_ext_f[count_rows:] + returned[3 * margin :]], axis=0
    )
    d_xbc_r = jnp.concatenate(
        [d_ext_r[margin:count_rows], d_ext_r[count_rows:] + returned[:margin]], axis=0
    )
    d_frame_f, d_proj_f = backend(pullback_f, d_gate_f, d_xbc_f, d_raw_f, in_proj, step_proj)
    d_frame_r, d_proj_r = backend(pullback_r, d_gate_r, d_xbc_r, d_raw_r, in_proj, step_proj)
    branch_f = jnp.dot(gated_f, out_proj, preferred_element_type=jnp.float32)
    branch_r = jnp.dot(gated_r, out_proj, preferred_element_type=jnp.float32)
    layer_out = (branch_f + branch_r[::-1, ::-1]).astype(jnp.bfloat16)
    grad_input = (d_frame_f + d_frame_r[::-1, ::-1]).astype(jnp.bfloat16)
    stacked_normal = jnp.concatenate([normal_f, normal_r], axis=0)
    stacked_proj = jnp.concatenate([d_proj_f, d_proj_r], axis=0)
    stacked_gated = jnp.concatenate([gated_f, gated_r], axis=0)
    stacked_up = jnp.concatenate([upstream, upstream_rev], axis=0)
    grad_out_proj = reduce_at_once(contract_rows(stacked_gated, stacked_up))
    grad_in_proj = reduce_by_axes(contract_rows(stacked_normal, stacked_proj))
    return (layer_out, grad_input, grad_in_proj, grad_out_proj)


def solution(mesh):
    return jax.shard_map(
        shards,
        mesh=mesh,
        in_specs=(
            P(("batch", "seq"), None),
            P(("batch", "seq"), None),
            P(),
            P(),
            P(),
            P(),
            P(),
            P(),
            P(),
            P(),
            P(),
        ),
        out_specs=(
            P(("batch", "seq"), None),
            P(("batch", "seq"), None),
            P(("batch", "seq"), None),
            P(("batch", "seq"), None),
        ),
        check_vma=False,
    )
```

```python
import functools

import jax
import jax.numpy as jnp
from jax import lax
from jax.experimental import pallas as pl
from jax.experimental.pallas import tpu as pltpu
from jax.sharding import PartitionSpec as P

epsilon = 1e-06
SIDE = 4
COUNT = SIDE**3
f32 = jnp.float32
bf16 = jnp.bfloat16
INTERPRET = False


def call(body, outs, args, scratch=(), scalars=0, flops=10**9, vmem=40 * 2**20):
    specs = [pl.BlockSpec(memory_space=pltpu.SMEM)] * scalars
    specs += [pl.BlockSpec(memory_space=pltpu.VMEM)] * (len(args) - scalars)
    moved = sum(a.size * a.dtype.itemsize for a in args)
    return pl.pallas_call(
        body,
        out_shape=[jax.ShapeDtypeStruct(shape, kind) for shape, kind in outs],
        in_specs=specs,
        out_specs=[pl.BlockSpec(memory_space=pltpu.VMEM)] * len(outs),
        scratch_shapes=list(scratch),
        compiler_params=pltpu.CompilerParams(vmem_limit_bytes=vmem),
        cost_estimate=pl.CostEstimate(flops=flops, bytes_accessed=moved, transcendentals=0),
        interpret=INTERPRET,
    )(*args)


def mm(left, right):
    return lax.dot_general(left, right, (((1,), (0,)), ((), ())), preferred_element_type=f32)


def mm_cols(left, right):
    return lax.dot_general(left, right, (((1,), (1,)), ((), ())), preferred_element_type=f32)


def mm_rows(left, right):
    return lax.dot_general(left, right, (((0,), (0,)), ((), ())), preferred_element_type=f32)


def iota(shape, dim):
    return lax.broadcasted_iota(jnp.int32, shape, dim)


def ones_where(mask):
    return jnp.where(mask, 1.0, 0.0).astype(bf16)


def anti(size):
    return ones_where(iota((size, size), 0) + iota((size, size), 1) == size - 1)


def pieces_of(value, count):
    found = []
    for _ in range(count):
        piece = value.astype(bf16)
        found.append(piece)
        value = value - piece.astype(f32)
    return found


def mirror_exact(block):
    turned = mm(block, anti(block.shape[1])).astype(bf16)
    return mm(anti(block.shape[0]), turned).astype(bf16)


def mirror_wide(block):
    high, low = pieces_of(block, 2)
    return mirror_exact(high).astype(f32) + mirror_exact(low).astype(f32)


def head_mask(heads, width):
    lanes = heads * width
    return ones_where(iota((heads, lanes), 0) == iota((heads, lanes), 1) // width)


def expand(value, mask):
    found = pieces_of(value, 3)
    return mm(jnp.concatenate(found, axis=1), jnp.concatenate([mask] * 3, axis=0))


def fold(value, mask):
    total = None
    for piece in pieces_of(value, 3):
        part = mm_cols(piece, mask)
        total = part if total is None else total + part
    return total


def triangle(size, low):
    rows, cols = iota((size, size), 0), iota((size, size), 1)
    return rows >= cols if low else rows <= cols


def tri_sum(mask, value):
    total = None
    for piece in pieces_of(value, 3):
        part = mm(ones_where(mask), piece)
        total = part if total is None else total + part
    return total


def tri_sum_turned(mask, value):
    total = None
    for piece in pieces_of(value, 3):
        part = mm_rows(piece, ones_where(mask))
        total = part if total is None else total + part
    return total


def softplus(value):
    return jnp.maximum(value, 0.0) + jnp.log1p(jnp.exp(-jnp.abs(value)))


def sigmoid(value):
    return 1.0 / (1.0 + jnp.exp(-value))


def norm_rows(block, gain):
    wide = block.astype(f32)
    scale = lax.rsqrt(jnp.mean(wide * wide, axis=-1, keepdims=True) + epsilon)
    return (wide * scale * gain).astype(bf16)


def pre_kernel(
    seq, up, low, high, gain, in_proj, step_proj, conv_w, conv_b, step_bias, decay_log, out_proj,
    payload, both, normal, cot, gate, conv, d_gated, raw, step, cumul, cumul_t,
    ext,
):
    rows = seq.shape[0]
    inner = out_proj.shape[0]
    heads = step_bias.shape[1]
    state = (conv_w.shape[1] - inner) // 2
    taps = conv_w.shape[0]
    both[:rows, :] = seq[...]
    both[rows:, :] = mirror_exact(seq[...])
    cot[:rows, :] = up[...]
    cot[rows:, :] = mirror_exact(up[...])
    halo = jnp.concatenate([low[...], mirror_exact(high[...])], axis=0)
    normal[...] = norm_rows(both[...], gain[...])
    normal_halo = norm_rows(halo, gain[...])
    gate[...] = mm(normal[...], in_proj[:, :inner])
    xbc = mm(normal[...], in_proj[:, inner:]).astype(bf16).astype(f32)
    xbc_halo = mm(normal_halo, in_proj[:, inner:]).astype(bf16).astype(f32)
    raw[...] = mm(normal[...], step_proj[...])
    d_gated[...] = mm_cols(cot[...], out_proj[...]).astype(bf16)
    margin = low.shape[0]
    mask = head_mask(heads, inner // heads)
    ends = []
    for frame in range(2):
        at = slice(frame * rows, (frame + 1) * rows)
        ext[:8, :] = xbc_halo[(frame + 1) * margin - 8 : (frame + 1) * margin, :]
        ext[8:, :] = xbc[at, :]
        found = conv_b[...]
        for tap in range(taps):
            start = 9 - taps + tap
            found = found + ext[start : start + rows, :] * conv_w[tap : tap + 1, :]
        conv[at, :] = found
        act = found * sigmoid(found)
        size = softplus(raw[at, :] + step_bias[...])
        decay = -jnp.exp(decay_log[...]) * size
        upto = tri_sum(triangle(rows, True), decay)
        step[at, :] = size
        cumul[at, :] = upto
        cumul_t[frame * heads : (frame + 1) * heads, :] = tri_sum_turned(triangle(rows, False), decay)
        end = upto[rows - 1 : rows, :]
        ends.append(end)
        spread = expand(jnp.concatenate([size * jnp.exp(end - upto), jnp.exp(upto)], axis=0), mask)
        driven = (act[:, :inner] * spread[:rows]).astype(bf16)
        local = mm_rows(driven, act[:, inner : inner + state].astype(bf16))
        wide = gate[at, :]
        d_mixed = d_gated[at, :].astype(f32) * (wide * sigmoid(wide))
        back = mm_rows((d_mixed * spread[rows:]).astype(bf16), act[:, inner + state :].astype(bf16))
        for place, block in ((frame, local), (2 + frame, back)):
            payload[:, 16 * place : 16 * place + 16, :] = block.reshape(COUNT, 16, state).astype(bf16)
    chunk_head = iota((COUNT, heads), 0) // (COUNT // heads)
    chosen = chunk_head == iota((COUNT, heads), 1)
    lanes = iota((COUNT, state), 1)
    packed = jnp.zeros((COUNT, state), f32)
    for frame in range(2):
        column = jnp.sum(jnp.where(chosen, ends[frame], 0.0), axis=1, keepdims=True)
        for nth, piece in enumerate(pieces_of(column, 3)):
            packed = jnp.where(lanes == 3 * frame + nth, piece.astype(f32), packed)
    tail = jnp.broadcast_to(packed.reshape(COUNT, 1, state), (COUNT, 8, state))
    payload[:, 64:, :] = tail.astype(bf16)


def scan_kernel(got, out, wide, done):
    count, rows, state = got.shape
    wide[...] = got[...].astype(f32).reshape(count * rows, state)
    tails = wide[pl.ds(64, count, stride=rows), :]
    above = iota((count, count), 0)
    beside = iota((count, count), 1)
    after = ones_where(above > beside)
    weights = []
    for frame in range(2):
        at = 3 * frame
        column = (tails[:, at + 2 : at + 3] + tails[:, at + 1 : at + 2]) + tails[:, at : at + 1]
        column = jnp.maximum(column, -110.0)
        line = jnp.sum(jnp.where(above == beside, column, 0.0), axis=0, keepdims=True)
        between = None
        for piece in pieces_of(jnp.where(beside < above, line, 0.0), 3):
            part = mm(piece, after)
            between = part if between is None else between + part
        found = jnp.where(above > beside, jnp.exp(between), 0.0)
        weights.append(pieces_of(found, 2))
    for place, (frame, turned) in enumerate(((0, False), (1, True), (0, True), (1, False))):
        pair = weights[frame]
        block = jnp.concatenate(
            [wide[pl.ds(16 * place + row, count, stride=rows), :] for row in range(16)], axis=1
        ).astype(bf16)
        if turned:
            mixed = mm_rows(jnp.concatenate(pair, axis=1), block)
        else:
            mixed = mm(jnp.concatenate(pair, axis=0), block)
        mixed = mixed[:count] + mixed[count:]
        for row in range(16):
            done[pl.ds(16 * place + row, count, stride=64), :] = mixed[:, state * row : state * (row + 1)]
    out[...] = done[...].reshape(count, 64, state).astype(bf16)


def intra_kernel(conv, gate, d_gated, step, cumul, cumul_t, mixed, d_driven, d_bc, d_cumul):
    rows = conv.shape[0] // 2
    inner = gate.shape[1]
    heads = step.shape[1]
    state = (conv.shape[1] - inner) // 2
    mask = head_mask(heads, inner // heads)
    lower = triangle(rows, True)
    first = iota((rows, 2 * inner // heads), 1) < inner // heads
    wide_pair = 2 * inner // heads
    for frame in range(2):
        at = slice(frame * rows, (frame + 1) * rows)
        found = conv[at, :]
        act = found * sigmoid(found)
        bmat = act[:, inner : inner + state].astype(bf16)
        cmat = act[:, inner + state :].astype(bf16)
        driven = act[:, :inner] * expand(step[at, :], mask)
        wide = gate[at, :]
        d_mixed = d_gated[at, :].astype(f32) * (wide * sigmoid(wide))
        scores = mm_cols(cmat, bmat)
        upto, line = cumul[at, :], cumul_t[frame * heads : (frame + 1) * heads, :]
        d_scores = jnp.zeros((rows, rows), f32)
        sums = []
        for pair in range(heads // 2):
            lanes = slice(pair * wide_pair, (pair + 1) * wide_pair)
            decays = []
            for head in (2 * pair, 2 * pair + 1):
                differ = upto[:, head : head + 1] - line[head : head + 1, :]
                decays.append(jnp.exp(jnp.where(lower, differ, -1e30)))
            weights = [(decay * scores).astype(bf16) for decay in decays]
            drive, d_mix = driven[:, lanes], d_mixed[:, lanes]
            drive_bf, d_mix_bf = drive.astype(bf16), d_mix.astype(bf16)
            drive_two = jnp.concatenate(
                [jnp.where(first, drive, 0.0), jnp.where(first, 0.0, drive)], axis=0
            ).astype(bf16)
            d_mix_two = jnp.concatenate(
                [jnp.where(first, d_mix, 0.0), jnp.where(first, 0.0, d_mix)], axis=0
            ).astype(bf16)
            mix = mm(jnp.concatenate(weights, axis=1), drive_two)
            d_weights = mm_cols(d_mix_two, drive_bf)
            d_drive = mm_rows(jnp.concatenate(weights, axis=0), d_mix_two)
            d_scores = d_scores + decays[0] * d_weights[:rows] + decays[1] * d_weights[rows:]
            mixed[at, lanes] = mix
            d_driven[at, lanes] = d_drive
            sums.append(d_mix_bf.astype(f32) * mix - drive_bf.astype(f32) * d_drive)
        d_scores = d_scores.astype(bf16)
        d_bc[at, :state] = mm_rows(d_scores, cmat)
        d_bc[at, state:] = mm(d_scores, bmat)
        d_cumul[at, :] = fold(jnp.concatenate(sums, axis=1), mask)


def post_kernel(
    got, conv, gate, d_gated, raw, step, cumul, mixed, d_driven, d_bc, d_cumul, step_bias, decay_log, skip_gain,
    gated, d_gate, d_conv, d_step,
):
    rows = conv.shape[0] // 2
    inner = gate.shape[1]
    heads = step.shape[1]
    state = (conv.shape[1] - inner) // 2
    mask = head_mask(heads, inner // heads)
    skip = expand(jnp.broadcast_to(skip_gain[...], (8, heads)), mask)[:1]
    for frame in range(2):
        at = slice(frame * rows, (frame + 1) * rows)
        found = conv[at, :]
        share = sigmoid(found)
        act = found * share
        inputs = act[:, :inner]
        bmat = act[:, inner : inner + state].astype(bf16)
        cmat = act[:, inner + state :].astype(bf16)
        upto = cumul[at, :]
        end = upto[rows - 1 : rows, :]
        spread = expand(jnp.concatenate([step[at, :], jnp.exp(upto), jnp.exp(end - upto)], axis=0), mask)
        sizes, grown, left = spread[:rows], spread[rows : 2 * rows], spread[2 * rows :]
        carried = got[:, 16 * frame : 16 * frame + 16, :].reshape(inner, state)
        reach = got[:, 32 + 16 * frame : 48 + 16 * frame, :].reshape(inner, state)
        inter = grown * mm_cols(cmat, carried)
        whole = mixed[at, :] + inter + skip * inputs
        wide = gate[at, :]
        opened = sigmoid(wide)
        silu = wide * opened
        gated[at, :] = (whole * silu).astype(bf16)
        d_out = d_gated[at, :].astype(f32)
        d_gate[at, :] = (d_out * whole * (opened * (1.0 + wide * (1.0 - opened)))).astype(bf16)
        d_mixed = d_out * silu
        d_cmat = d_bc[at, state:] + mm((d_mixed * grown).astype(bf16), carried)
        answer = left * mm_cols(bmat, reach)
        driven = inputs * sizes
        d_drive = d_driven[at, :] + answer
        d_bmat = d_bc[at, :state] + mm((left * driven).astype(bf16), reach)
        products = carried.astype(f32) * reach.astype(f32)
        met = None
        for piece in pieces_of(products, 3):
            part = mm_cols(jnp.ones((8, state), bf16), piece)
            met = part if met is None else met + part
        folded = fold(jnp.concatenate([driven * answer, d_mixed * inter, d_drive * inputs, met], axis=0), mask)
        held, entered, by_size = folded[:rows], folded[rows : 2 * rows], folded[2 * rows : 3 * rows]
        d_end = jnp.exp(end) * folded[3 * rows : 3 * rows + 1] + jnp.sum(held, axis=0, keepdims=True)
        d_decay = tri_sum(triangle(rows, False), d_cumul[at, :] + entered - held) + d_end
        d_size = by_size - jnp.exp(decay_log[...]) * d_decay
        d_step[at, :] = (d_size * sigmoid(raw[at, :] + step_bias[...])).astype(bf16)
        d_act = jnp.concatenate([skip * d_mixed + d_drive * sizes, d_bmat, d_cmat], axis=1)
        d_conv[at, :] = d_act * (share * (1.0 + found * (1.0 - share)))


def out_term_kernel(place, gated, cot, normal, d_gate, *refs):
    by_x, by_y, whole, parted = refs[:4], refs[4:8], refs[8], refs[9]
    columns = cot.shape[1]
    whole[...] = mm_rows(gated[...], cot[...])
    parted[...] = mm_rows(normal[...], d_gate[...]).reshape(parted.shape)
    chunk = whole.shape[0] // SIDE
    for step in range(SIDE):
        to_x = lax.rem(place[0] + step, SIDE)
        to_y = lax.rem(place[2] + step, SIDE)
        block = whole[pl.ds(pl.multiple_of(to_x * chunk, chunk), chunk), :].reshape(-1, 2, 8, columns)
        block = jnp.concatenate(
            [block[:, 0].reshape(-1, columns), block[:, 1].reshape(-1, columns)], axis=1
        )
        by_x[step][...] = block.astype(by_x[step].dtype)
        by_y[step][...] = parted[:, to_y].reshape(by_y[step].shape).astype(by_y[step].dtype)


def in_term_kernel(place, d_conv, ahead, behind, conv_w, normal, *refs):
    d_xbc, by_x, by_y, ext, whole, parted = refs[0], refs[1:5], refs[5:9], refs[9], refs[10], refs[11]
    rows = d_conv.shape[0] // 2
    taps = conv_w.shape[0]
    for frame, halo in enumerate((ahead, behind)):
        at = slice(frame * rows, (frame + 1) * rows)
        ext[:rows, :] = d_conv[at, :]
        ext[rows:, :] = halo[...]
        total = None
        for tap in range(taps):
            start = taps - 1 - tap
            part = ext[start : start + rows, :] * conv_w[tap : tap + 1, :]
            total = part if total is None else total + part
        d_xbc[at, :] = total.astype(bf16)
    half = whole.shape[1]
    whole[...] = mm_rows(normal[...], d_xbc[:, :half])
    parted[...] = mm_rows(normal[...], d_xbc[:, half:]).reshape(parted.shape)
    chunk = whole.shape[0] // SIDE
    for step in range(SIDE):
        to_x = lax.rem(place[0] + step, SIDE)
        to_y = lax.rem(place[2] + step, SIDE)
        block = whole[pl.ds(pl.multiple_of(to_x * chunk, chunk), chunk), :]
        by_x[step][...] = block.astype(by_x[step].dtype)
        by_y[step][...] = parted[:, to_y].reshape(by_y[step].shape).astype(by_y[step].dtype)


def result_kernel(both, gain, gated, out_proj, d_gate, d_xbc, d_step, in_proj, step_proj, layer, grad):
    rows = both.shape[0] // 2
    inner = out_proj.shape[0]
    branch = mm(gated[...], out_proj[...])
    layer[...] = (branch[:rows] + mirror_wide(branch[rows:])).astype(bf16)
    d_normal = mm_cols(d_gate[...], in_proj[:, :inner]) + mm_cols(d_xbc[...], in_proj[:, inner:])
    d_normal = d_normal + mm_cols(d_step[...], step_proj[...])
    wide = both[...].astype(f32)
    scale = lax.rsqrt(jnp.mean(wide * wide, axis=-1, keepdims=True) + epsilon)
    d_scaled = d_normal * gain[...]
    along = jnp.mean(d_scaled * wide, axis=-1, keepdims=True)
    d_wide = scale * d_scaled - wide * (scale * scale * scale * along)
    grad[...] = (d_wide[:rows] + mirror_wide(d_wide[rows:])).astype(bf16)


def total_of(refs):
    total = refs[0][...]
    for ref in refs[1:]:
        total = total + ref[...].astype(f32)
    return total


def first_sum_kernel(place, *refs):
    out_x, in_x, gate_y, in_y = refs[:4], refs[4:8], refs[8:12], refs[12:16]
    by_y, by_x, parted, whole = refs[16:20], refs[20:24], refs[24], refs[25]
    parted[...] = jnp.concatenate([total_of(out_x), total_of(in_x)], axis=1).reshape(parted.shape)
    whole[...] = jnp.concatenate([total_of(gate_y), total_of(in_y)], axis=1)
    chunk = whole.shape[0] // SIDE
    for step in range(SIDE):
        to_x = lax.rem(place[0] + step, SIDE)
        to_y = lax.rem(place[2] + step, SIDE)
        by_y[step][...] = parted[:, to_y].reshape(by_y[step].shape).astype(by_y[step].dtype)
        block = whole[pl.ds(pl.multiple_of(to_x * chunk, chunk), chunk), :]
        by_x[step][...] = block.astype(by_x[step].dtype)


def second_sum_kernel(place, *refs):
    first, second, by_z, keep = refs[:4], refs[4:8], refs[8:12], refs[12]
    keep[:, 0] = total_of(first).reshape(SIDE, 8, -1)
    keep[:, 1] = total_of(second).reshape(SIDE, 8, -1)
    for step in range(SIDE):
        to_z = lax.rem(place[1] + step, SIDE)
        by_z[step][...] = keep[to_z].reshape(by_z[step].shape).astype(by_z[step].dtype)


def last_sum_kernel(*refs):
    parts, grad_in, grad_out = refs[:4], refs[4], refs[5]
    total = total_of(parts)
    columns = grad_out.shape[1]
    grad_out[:8, :] = total[:8, :columns]
    grad_out[8:, :] = total[:8, columns : 2 * columns]
    grad_in[...] = jnp.concatenate([total[8:, : 2 * columns], total[:8, 2 * columns :], total[8:, 2 * columns :]], axis=1)


def axis_pairs(stride, step):
    pairs = []
    for source in range(COUNT):
        digit = source // stride % SIDE
        pairs.append((source, source + ((digit + step) % SIDE - digit) * stride))
    return pairs


def exchange(parts, stride):
    return [parts[0]] + [
        lax.ppermute(parts[step], "seq", axis_pairs(stride, step)) for step in range(1, SIDE)
    ]


def slots(rows, columns):
    return [((rows, columns), f32)] + [((rows, columns), bf16)] * (SIDE - 1)


def shards(
    sequence,
    upstream,
    norm_gain,
    in_proj,
    step_proj,
    conv_weight,
    conv_bias,
    step_bias,
    decay_log,
    skip_gain,
    out_proj,
):
    rows, width = sequence.shape
    inner = out_proj.shape[0]
    heads = step_bias.shape[0]
    state = inner // heads * 2
    channels = conv_weight.shape[1]
    both_rows = 2 * rows
    stride_x, stride_z, stride_y = SIDE * SIDE, SIDE, 1
    index = lax.axis_index("seq")
    place = jnp.stack([index // stride_x, index // stride_z % SIDE, index % SIDE]).astype(jnp.int32)
    upward = [(i, i + 1) for i in range(COUNT - 1)]
    downward = [(i + 1, i) for i in range(COUNT - 1)]
    low = lax.ppermute(sequence[rows - 16 :], "seq", upward)
    high = lax.ppermute(sequence[:16], "seq", downward)
    gain, bias, decay = norm_gain[None], step_bias[None], decay_log[None]
    payload, both, normal, cot, gate, conv, d_gated, raw, step, cumul, cumul_t = call(
        pre_kernel,
        [
            ((COUNT, 72, state), bf16),
            ((both_rows, width), bf16),
            ((both_rows, width), bf16),
            ((both_rows, width), bf16),
            ((both_rows, inner), f32),
            ((both_rows, channels), f32),
            ((both_rows, inner), bf16),
            ((both_rows, heads), f32),
            ((both_rows, heads), f32),
            ((both_rows, heads), f32),
            ((2 * heads, rows), f32),
        ],
        (
            sequence, upstream, low, high, gain, in_proj, step_proj,
            conv_weight, conv_bias[None], bias, decay, out_proj,
        ),
        [pltpu.VMEM((rows + 8, channels), f32)],
    )
    got = lax.all_to_all(payload, "seq", 0, 0)
    mixed, d_driven, d_bc, d_cumul = call(
        intra_kernel,
        [
            ((both_rows, inner), f32),
            ((both_rows, inner), f32),
            ((both_rows, 2 * state), f32),
            ((both_rows, heads), f32),
        ],
        (conv, gate, d_gated, step, cumul, cumul_t),
        flops=8 * 10**9,
    )
    (scanned,) = call(
        scan_kernel,
        [((COUNT, 64, state), bf16)],
        (got,),
        [pltpu.VMEM((COUNT * 72, state), f32), pltpu.VMEM((COUNT * 64, state), f32)],
    )
    states = lax.all_to_all(scanned, "seq", 0, 0)
    gated, d_gate, d_conv, d_step = call(
        post_kernel,
        [
            ((both_rows, inner), bf16),
            ((both_rows, inner), bf16),
            ((both_rows, channels), f32),
            ((both_rows, heads), bf16),
        ],
        (
            states, conv, gate, d_gated, raw, step, cumul, mixed, d_driven, d_bc, d_cumul,
            bias, decay, skip_gain[None],
        ),
    )
    ahead = lax.ppermute(d_conv[:8], "seq", downward)
    behind = lax.ppermute(d_conv[rows : rows + 8], "seq", upward)
    eighth = 8 * COUNT // SIDE
    half = (channels) // 2
    terms = call(
        out_term_kernel,
        slots(eighth, inner) + slots(eighth, inner),
        (place, gated, cot, normal, d_gate),
        [pltpu.VMEM((inner, width), f32), pltpu.VMEM((COUNT // SIDE, SIDE, 8, inner), f32)],
        scalars=1,
        flops=4 * 10**9,
    )
    out_x = exchange(terms[:4], stride_x)
    gate_y = exchange(terms[4:], stride_y)
    d_xbc, *terms = call(
        in_term_kernel,
        [((both_rows, channels), bf16)] + slots(eighth, half) + slots(eighth, half),
        (place, d_conv, ahead, behind, conv_weight, normal),
        [
            pltpu.VMEM((rows + 8, channels), f32),
            pltpu.VMEM((width, half), f32),
            pltpu.VMEM((COUNT // SIDE, SIDE, 8, half), f32),
        ],
        scalars=1,
    )
    in_x = exchange(terms[:4], stride_x)
    in_y = exchange(terms[4:], stride_y)
    layer_out, grad_input = call(
        result_kernel,
        [((rows, width), bf16), ((rows, width), bf16)],
        (both, gain, gated, out_proj, d_gate, d_xbc, d_step, in_proj, step_proj),
        flops=8 * 10**9,
    )
    joined = inner + half
    parts = call(
        first_sum_kernel,
        slots(eighth // SIDE, joined) + slots(eighth // SIDE, joined),
        (place, *out_x, *in_x, *gate_y, *in_y),
        [pltpu.VMEM((SIDE, SIDE, 8, joined), f32), pltpu.VMEM((eighth, joined), f32)],
        scalars=1,
    )
    first = exchange(parts[:4], stride_y)
    second = exchange(parts[4:], stride_x)
    parts = call(
        second_sum_kernel,
        slots(16, joined),
        (place, *first, *second),
        [pltpu.VMEM((SIDE, 2, 8, joined), f32)],
        scalars=1,
    )
    last = exchange(parts, stride_z)
    grad_in_proj, grad_out_proj = call(
        last_sum_kernel,
        [((8, inner + channels), f32), ((16, width), f32)],
        tuple(last),
    )
    return (layer_out, grad_input, grad_in_proj, grad_out_proj)


def solution(mesh):
    rows = P(("batch", "seq"), None)
    return jax.shard_map(
        shards,
        mesh=mesh,
        in_specs=(rows, rows) + (P(),) * 9,
        out_specs=(rows,) * 4,
        check_vma=False,
    )
```

```python
import functools

import jax
import jax.numpy as jnp
from jax import lax
from jax.experimental import pallas as pl
from jax.experimental.pallas import tpu as pltpu
from jax.sharding import PartitionSpec as P

epsilon = 1e-06
SIDE = 4
COUNT = SIDE**3
f32 = jnp.float32
bf16 = jnp.bfloat16
INTERPRET = False


def call(body, outs, args, scratch=(), scalars=0, flops=10**9, vmem=58 * 2**20):
    specs = [pl.BlockSpec(memory_space=pltpu.SMEM)] * scalars
    specs += [pl.BlockSpec(memory_space=pltpu.VMEM)] * (len(args) - scalars)
    moved = sum(a.size * a.dtype.itemsize for a in args)
    return pl.pallas_call(
        body,
        out_shape=[jax.ShapeDtypeStruct(shape, kind) for shape, kind in outs],
        in_specs=specs,
        out_specs=[pl.BlockSpec(memory_space=pltpu.VMEM)] * len(outs),
        scratch_shapes=list(scratch),
        compiler_params=pltpu.CompilerParams(vmem_limit_bytes=vmem),
        cost_estimate=pl.CostEstimate(flops=flops, bytes_accessed=moved, transcendentals=0),
        interpret=INTERPRET,
    )(*args)


def mm(left, right):
    return lax.dot_general(left, right, (((1,), (0,)), ((), ())), preferred_element_type=f32)


def mm_cols(left, right):
    return lax.dot_general(left, right, (((1,), (1,)), ((), ())), preferred_element_type=f32)


def mm_rows(left, right):
    return lax.dot_general(left, right, (((0,), (0,)), ((), ())), preferred_element_type=f32)


def iota(shape, dim):
    return lax.broadcasted_iota(jnp.int32, shape, dim)


def ones_where(mask):
    return jnp.where(mask, 1.0, 0.0).astype(bf16)


def anti(size):
    return ones_where(iota((size, size), 0) + iota((size, size), 1) == size - 1)


def pieces_of(value, count):
    found = []
    for _ in range(count):
        piece = value.astype(bf16)
        found.append(piece)
        value = value - piece.astype(f32)
    return found


def mirror_exact(block):
    turned = mm(block, anti(block.shape[1])).astype(bf16)
    return mm(anti(block.shape[0]), turned).astype(bf16)


def mirror_wide(block):
    high, low = pieces_of(block, 2)
    return mirror_exact(high).astype(f32) + mirror_exact(low).astype(f32)


def head_mask(heads, width):
    lanes = heads * width
    return ones_where(iota((heads, lanes), 0) == iota((heads, lanes), 1) // width)


def expand(value, mask):
    found = pieces_of(value, 3)
    return mm(jnp.concatenate(found, axis=1), jnp.concatenate([mask] * 3, axis=0))


def fold(value, mask):
    total = None
    for piece in pieces_of(value, 2):
        part = mm_cols(piece, mask)
        total = part if total is None else total + part
    return total


def triangle(size, low):
    rows, cols = iota((size, size), 0), iota((size, size), 1)
    return rows >= cols if low else rows <= cols


def tri_sum(mask, value):
    total = None
    for piece in pieces_of(value, 3):
        part = mm(ones_where(mask), piece)
        total = part if total is None else total + part
    return total


def tri_sum_turned(mask, value):
    total = None
    for piece in pieces_of(value, 3):
        part = mm_rows(piece, ones_where(mask))
        total = part if total is None else total + part
    return total


def softplus(value):
    return jnp.maximum(value, 0.0) + jnp.log1p(jnp.exp(-jnp.abs(value)))


def sigmoid(value):
    return 1.0 / (1.0 + jnp.exp(-value))


def norm_rows(block, gain):
    wide = block.astype(f32)
    scale = lax.rsqrt(jnp.mean(wide * wide, axis=-1, keepdims=True) + epsilon)
    return (wide * scale * gain.reshape(1, -1)).astype(bf16)


def pre_kernel(
    seq, up, low, high, gain, in_proj, step_proj, conv_w, conv_b, step_bias, decay_log, out_proj,
    payload, both, normal, normal_halo, cot, gate, conv, d_gated, raw, step, cumul, cumul_t,
    ext,
):
    rows = seq.shape[0]
    inner = out_proj.shape[0]
    heads = step_bias.shape[0]
    state = (conv_w.shape[1] - inner) // 2
    taps = conv_w.shape[0]
    both[:rows, :] = seq[...]
    both[rows:, :] = mirror_exact(seq[...])
    cot[:rows, :] = up[...]
    cot[rows:, :] = mirror_exact(up[...])
    halo = jnp.concatenate([low[...], mirror_exact(high[...])], axis=0)
    normal[...] = norm_rows(both[...], gain[...])
    normal_halo[...] = norm_rows(halo, gain[...])
    gate[...] = mm(normal[...], in_proj[:, :inner])
    xbc = mm(normal[...], in_proj[:, inner:]).astype(bf16).astype(f32)
    xbc_halo = mm(normal_halo[...], in_proj[:, inner:]).astype(bf16).astype(f32)
    raw[...] = mm_cols(normal[...], step_proj[...])
    d_gated[...] = mm_cols(cot[...], out_proj[...]).astype(bf16)
    margin = low.shape[0]
    mask = head_mask(heads, inner // heads)
    ends = []
    for frame in range(2):
        at = slice(frame * rows, (frame + 1) * rows)
        ext[:8, :] = xbc_halo[(frame + 1) * margin - 8 : (frame + 1) * margin, :]
        ext[8:, :] = xbc[at, :]
        found = conv_b[...].reshape(1, -1)
        for tap in range(taps):
            start = 9 - taps + tap
            found = found + ext[start : start + rows, :] * conv_w[tap : tap + 1, :]
        conv[at, :] = found
        act = found * sigmoid(found)
        size = softplus(raw[at, :] + step_bias[...].reshape(1, -1))
        decay = -jnp.exp(decay_log[...].reshape(1, -1)) * size
        upto = tri_sum(triangle(rows, True), decay)
        step[at, :] = size
        cumul[at, :] = upto
        cumul_t[frame * heads : (frame + 1) * heads, :] = tri_sum_turned(triangle(rows, False), decay)
        end = upto[rows - 1 : rows, :]
        ends.append(end)
        spread = expand(jnp.concatenate([size * jnp.exp(end - upto), jnp.exp(upto)], axis=0), mask)
        driven = (act[:, :inner] * spread[:rows]).astype(bf16)
        local = mm_rows(driven, act[:, inner : inner + state].astype(bf16))
        wide = gate[at, :]
        d_mixed = d_gated[at, :].astype(f32) * (wide * sigmoid(wide))
        back = mm_rows((d_mixed * spread[rows:]).astype(bf16), act[:, inner + state :].astype(bf16))
        part = inner // SIDE
        for place, block in ((frame, local), (2 + frame, back)):
            block = block.astype(bf16).reshape(SIDE, part, state)
            payload[:, place * part : (place + 1) * part, :] = block
    packed = pack_totals(ends, heads, state)
    for to in range(SIDE):
        shifted = ones_where(iota((16, heads), 1) == iota((16, heads), 0) + to * (heads // SIDE))
        payload[to, inner:, :] = mm(shifted, packed).astype(bf16)


def pack_totals(ends, heads, state):
    chosen = iota((heads, heads), 0) == iota((heads, heads), 1)
    lanes = iota((heads, state), 1)
    packed = jnp.zeros((heads, state), f32)
    for frame in range(2):
        column = jnp.sum(jnp.where(chosen, ends[frame], 0.0), axis=1, keepdims=True)
        packed = pack_column(packed, column, lanes, frame)
    return packed.astype(bf16)


def pack_column(packed, column, lanes, frame):
    for nth, piece in enumerate(pieces_of(column, 3)):
        packed = jnp.where(lanes == 3 * frame + nth, piece.astype(f32), packed)
    return packed


def unpack_column(packed, frame):
    at = 3 * frame
    return (packed[:, at + 2 : at + 3] + packed[:, at + 1 : at + 2]) + packed[:, at : at + 1]


SCANS = ((0, False), (1, True), (0, True), (1, False))


def chain(got, totals, place, state, visit):
    frame, turned = SCANS[place]
    part = state.shape[0]
    size = part // SIDE
    order = range(SIDE - 1, -1, -1) if turned else range(SIDE)
    for at in order:
        visit(at, state)
        grown = jnp.exp(totals[at][frame])
        factors = [
            jnp.broadcast_to(grown[head : head + 1, :], (size, 1)) for head in range(part // size)
        ]
        state = jnp.concatenate(factors, axis=0) * state
        state = state + got[at, place * part : (place + 1) * part, :].astype(f32)
    return state


def tails_of(got, inner):
    found = []
    for at in range(SIDE):
        tail = got[at, inner:, :].astype(f32)
        found.append([unpack_column(tail, frame) for frame in range(2)])
    return found


def group_kernel(got, out):
    state = got.shape[2]
    inner = got.shape[1] - 16
    part = inner // SIDE
    totals = tails_of(got, inner)
    for place in range(4):
        block = chain(got, totals, place, jnp.zeros((part, state), f32), lambda at, value: None)
        out[:, 16 * place : 16 * place + 16, :] = block.reshape(16, 16, state).astype(bf16)
    lanes = iota((16, state), 1)
    packed = jnp.zeros((16, state), f32)
    for frame in range(2):
        column = jnp.maximum(totals[0][frame], -110.0)
        for at in range(1, SIDE):
            column = column + jnp.maximum(totals[at][frame], -110.0)
        packed = pack_column(packed, column, lanes, frame)
    chosen = ones_where(iota((16, 16), 1) == iota((16, 16), 0) // SIDE)
    packed = mm(chosen, packed.astype(bf16))
    out[:, 64:, :] = jnp.broadcast_to(packed.reshape(16, 1, state), (16, 8, state)).astype(bf16)


def spread_kernel(got, entering, out):
    state = got.shape[2]
    inner = got.shape[1] - 16
    part = inner // SIDE
    totals = tails_of(got, inner)
    for place in range(4):

        def visit(at, value, place=place):
            out[at, place * part : (place + 1) * part, :] = value.astype(bf16)

        block = entering[:, 16 * place : 16 * place + 16, :].astype(f32).reshape(part, state)
        chain(got, totals, place, block, visit)


def scan_kernel(got, out, wide, done):
    count, rows, state = got.shape
    wide[...] = got[...].astype(f32).reshape(count * rows, state)
    tails = wide[pl.ds(64, count, stride=rows), :]
    above = iota((count, count), 0)
    beside = iota((count, count), 1)
    after = ones_where(above > beside)
    weights = []
    for frame in range(2):
        column = jnp.maximum(unpack_column(tails, frame), -110.0)
        line = jnp.sum(jnp.where(above == beside, column, 0.0), axis=0, keepdims=True)
        between = None
        for piece in pieces_of(jnp.where(beside < above, line, 0.0), 3):
            part = mm(piece, after)
            between = part if between is None else between + part
        found = jnp.where(above > beside, jnp.exp(between), 0.0)
        weights.append(pieces_of(found, 2))
    for place, (frame, turned) in enumerate(SCANS):
        pair = weights[frame]
        block = jnp.concatenate(
            [wide[pl.ds(16 * place + row, count, stride=rows), :] for row in range(16)], axis=1
        ).astype(bf16)
        if turned:
            mixed = mm_rows(jnp.concatenate(pair, axis=1), block)
        else:
            mixed = mm(jnp.concatenate(pair, axis=0), block)
        mixed = mixed[:count] + mixed[count:]
        for row in range(16):
            done[pl.ds(16 * place + row, count, stride=64), :] = mixed[:, state * row : state * (row + 1)]
    out[...] = done[...].reshape(count, 64, state).astype(bf16)


def intra_kernel(conv, gate, d_gated, step, cumul, cumul_t, mixed, d_driven, d_bc, d_cumul):
    rows = conv.shape[0] // 2
    inner = gate.shape[1]
    heads = step.shape[1]
    state = (conv.shape[1] - inner) // 2
    mask = head_mask(heads, inner // heads)
    lower = triangle(rows, True)
    first = iota((rows, 2 * inner // heads), 1) < inner // heads
    wide_pair = 2 * inner // heads
    for frame in range(2):
        at = slice(frame * rows, (frame + 1) * rows)
        found = conv[at, :]
        act = found * sigmoid(found)
        bmat = act[:, inner : inner + state].astype(bf16)
        cmat = act[:, inner + state :].astype(bf16)
        driven = act[:, :inner] * expand(step[at, :], mask)
        wide = gate[at, :]
        d_mixed = d_gated[at, :].astype(f32) * (wide * sigmoid(wide))
        scores = mm_cols(cmat, bmat)
        upto, line = cumul[at, :], cumul_t[frame * heads : (frame + 1) * heads, :]
        d_scores = jnp.zeros((rows, rows), f32)
        sums = []
        for pair in range(heads // 2):
            lanes = slice(pair * wide_pair, (pair + 1) * wide_pair)
            decays = []
            for head in (2 * pair, 2 * pair + 1):
                differ = upto[:, head : head + 1] - line[head : head + 1, :]
                decays.append(jnp.exp(jnp.where(lower, differ, -1e30)))
            weights = [(decay * scores).astype(bf16) for decay in decays]
            drive, d_mix = driven[:, lanes], d_mixed[:, lanes]
            drive_bf, d_mix_bf = drive.astype(bf16), d_mix.astype(bf16)
            drive_two = jnp.concatenate(
                [jnp.where(first, drive, 0.0), jnp.where(first, 0.0, drive)], axis=0
            ).astype(bf16)
            d_mix_two = jnp.concatenate(
                [jnp.where(first, d_mix, 0.0), jnp.where(first, 0.0, d_mix)], axis=0
            ).astype(bf16)
            mix = mm(jnp.concatenate(weights, axis=1), drive_two)
            d_weights = mm_cols(d_mix_two, drive_bf)
            d_drive = mm_rows(jnp.concatenate(weights, axis=0), d_mix_two)
            d_scores = d_scores + decays[0] * d_weights[:rows] + decays[1] * d_weights[rows:]
            mixed[at, lanes] = mix
            d_driven[at, lanes] = d_drive
            sums.append(d_mix_bf.astype(f32) * mix - drive_bf.astype(f32) * d_drive)
        d_scores = d_scores.astype(bf16)
        d_bc[at, :state] = mm_rows(d_scores, cmat)
        d_bc[at, state:] = mm(d_scores, bmat)
        d_cumul[at, :] = fold(jnp.concatenate(sums, axis=1), mask)


def post_kernel(
    place, got, conv, gate, d_gated, raw, step, cumul, mixed, d_driven, d_bc, d_cumul, step_bias, decay_log, skip_gain,
    conv_w, cot, normal, normal_halo,
    gated, d_gate, d_xbc, d_edge, d_ahead, d_step, *refs,
):
    by_x, by_y, ext, d_conv_out, whole, parted = refs[:4], refs[4:8], refs[8], refs[9], refs[10], refs[11]
    rows = conv.shape[0] // 2
    inner = gate.shape[1]
    heads = step.shape[1]
    state = (conv.shape[1] - inner) // 2
    mask = head_mask(heads, inner // heads)
    skip = expand(jnp.broadcast_to(skip_gain[...].reshape(1, -1), (8, heads)), mask)[:1]
    for frame in range(2):
        at = slice(frame * rows, (frame + 1) * rows)
        found = conv[at, :]
        share = sigmoid(found)
        act = found * share
        inputs = act[:, :inner]
        bmat = act[:, inner : inner + state].astype(bf16)
        cmat = act[:, inner + state :].astype(bf16)
        upto = cumul[at, :]
        end = upto[rows - 1 : rows, :]
        spread = expand(jnp.concatenate([step[at, :], jnp.exp(upto), jnp.exp(end - upto)], axis=0), mask)
        sizes, grown, left = spread[:rows], spread[rows : 2 * rows], spread[2 * rows :]
        part = inner // SIDE
        carried = got[:, frame * part : (frame + 1) * part, :].reshape(inner, state)
        reach = got[:, (2 + frame) * part : (3 + frame) * part, :].reshape(inner, state)
        inter = grown * mm_cols(cmat, carried)
        full = mixed[at, :] + inter + skip * inputs
        wide = gate[at, :]
        opened = sigmoid(wide)
        silu = wide * opened
        gated[at, :] = (full * silu).astype(bf16)
        d_out = d_gated[at, :].astype(f32)
        d_gate[at, :] = (d_out * full * (opened * (1.0 + wide * (1.0 - opened)))).astype(bf16)
        d_mixed = d_out * silu
        d_cmat = d_bc[at, state:] + mm((d_mixed * grown).astype(bf16), carried)
        answer = left * mm_cols(bmat, reach)
        driven = inputs * sizes
        d_drive = d_driven[at, :] + answer
        d_bmat = d_bc[at, :state] + mm((left * driven).astype(bf16), reach)
        products = carried.astype(f32) * reach.astype(f32)
        met = jnp.sum(products.reshape(heads, inner // heads, state), axis=1)
        met = jnp.sum(met, axis=1, keepdims=True)
        met = jnp.sum(jnp.where(iota((heads, heads), 0) == iota((heads, heads), 1), met, 0.0), axis=0, keepdims=True)
        folded = fold(jnp.concatenate([driven * answer, d_mixed * inter, d_drive * inputs], axis=0), mask)
        held, entered, by_size = folded[:rows], folded[rows : 2 * rows], folded[2 * rows :]
        d_end = jnp.exp(end) * met + jnp.sum(held, axis=0, keepdims=True)
        d_decay = tri_sum(triangle(rows, False), d_cumul[at, :] + entered - held) + d_end
        d_size = by_size - jnp.exp(decay_log[...].reshape(1, -1)) * d_decay
        d_step[at, :] = (d_size * sigmoid(raw[at, :] + step_bias[...].reshape(1, -1))).astype(bf16)
        d_act = jnp.concatenate([skip * d_mixed + d_drive * sizes, d_bmat, d_cmat], axis=1)
        margin = normal_halo.shape[0] // 2
        ext[:margin, :] = jnp.zeros((margin, ext.shape[1]), f32)
        ext[margin : margin + rows, :] = d_act * (share * (1.0 + found * (1.0 - share)))
        ext[margin + rows :, :] = jnp.zeros((8, ext.shape[1]), f32)
        taps = conv_w.shape[0]
        total = None
        for tap in range(taps):
            start = taps - 1 - tap
            part = ext[start : start + margin + rows, :] * conv_w[tap : tap + 1, :]
            total = part if total is None else total + part
        d_xbc[at, :] = total[margin:].astype(bf16)
        d_conv_out[frame * margin : (frame + 1) * margin, :] = total[:margin].astype(bf16)
        d_ahead[8 * frame : 8 * frame + 8, :] = total[margin - 8 : margin]
        d_edge[8 * frame : 8 * frame + 8, :] = total[margin + rows - 8 :]
    columns = cot.shape[1]
    half = d_xbc.shape[1] // 2
    out_term = mm_rows(gated[...], cot[...]).reshape(COUNT, 2, 8, columns)
    gate_term = mm_rows(normal[...], d_gate[...]).reshape(COUNT // SIDE, SIDE, 8, inner)
    in_term = mm_rows(normal[...], d_xbc[...]) + mm_rows(normal_halo[...], d_conv_out[...])
    whole[:, :columns] = out_term[:, 0].reshape(-1, columns)
    whole[:, columns : 2 * columns] = out_term[:, 1].reshape(-1, columns)
    whole[:, 2 * columns :] = in_term[:, :half]
    parted[:, :, :, :inner] = gate_term
    parted[:, :, :, inner:] = in_term[:, half:].reshape(COUNT // SIDE, SIDE, 8, half)
    send_x(place, whole, by_x)
    send_y(place, parted, by_y)


def send_x(place, whole, slots):
    chunk = whole.shape[0] // SIDE
    for step in range(SIDE):
        to = lax.rem(place[0] + step, SIDE)
        block = whole[pl.ds(pl.multiple_of(to * chunk, chunk), chunk), :]
        slots[step][...] = block.astype(slots[step].dtype)


def send_y(place, parted, slots):
    for step in range(SIDE):
        block = parted[:, lax.rem(place[2] + step, SIDE)]
        slots[step][...] = block.reshape(slots[step].shape).astype(slots[step].dtype)


def result_kernel(
    both, gain, gated, out_proj, d_gate, d_xbc, d_edge, ahead, behind, d_step, in_proj, step_proj,
    layer, grad, d_whole,
):
    rows = both.shape[0] // 2
    inner = out_proj.shape[0]
    branch = mm(gated[...], out_proj[...])
    layer[...] = (branch[:rows] + mirror_wide(branch[rows:])).astype(bf16)
    d_whole[...] = d_xbc[...]
    for frame, halo in enumerate((ahead, behind)):
        edge = d_edge[8 * frame : 8 * frame + 8, :] + halo[...]
        keep = d_xbc[(frame + 1) * rows - 16 : (frame + 1) * rows, :].astype(f32)
        edge = jnp.concatenate([keep[:8], edge], axis=0)
        d_whole[(frame + 1) * rows - 16 : (frame + 1) * rows, :] = edge.astype(bf16)
    d_normal = mm_cols(d_gate[...], in_proj[:, :inner]) + mm_cols(d_whole[...], in_proj[:, inner:])
    d_normal = d_normal + mm(d_step[...], step_proj[...])
    wide = both[...].astype(f32)
    scale = lax.rsqrt(jnp.mean(wide * wide, axis=-1, keepdims=True) + epsilon)
    d_scaled = d_normal * gain[...].reshape(1, -1)
    along = jnp.mean(d_scaled * wide, axis=-1, keepdims=True)
    d_wide = scale * d_scaled - wide * (scale * scale * scale * along)
    grad[...] = (d_wide[:rows] + mirror_wide(d_wide[rows:])).astype(bf16)


def total_of(refs):
    total = refs[0][...].astype(f32)
    for ref in refs[1:]:
        total = total + ref[...].astype(f32)
    return total


def first_sum_kernel(place, *refs):
    from_x, from_y, by_y, by_x, parted, whole = refs[:4], refs[4:8], refs[9:13], refs[13:17], refs[17], refs[18]
    parted[...] = total_of(from_x).reshape(parted.shape)
    whole[...] = total_of(from_y)
    send_y(place, parted, by_y)
    send_x(place, whole, by_x)


def second_sum_kernel(place, *refs):
    first, second, by_z, keep = refs[:4], refs[4:8], refs[8:12], refs[12]
    keep[:, 0] = total_of(first).reshape(SIDE, 8, -1)
    keep[:, 1] = total_of(second).reshape(SIDE, 8, -1)
    for step in range(SIDE):
        to = lax.rem(place[1] + step, SIDE)
        by_z[step][...] = keep[to].reshape(by_z[step].shape).astype(by_z[step].dtype)


def last_sum_kernel(*refs):
    grad_in, grad_out = refs[4:]
    total = total_of(refs[:4])
    columns = grad_out.shape[1]
    grad_out[:8, :] = total[:8, :columns]
    grad_out[8:, :] = total[:8, columns : 2 * columns]
    grad_in[...] = jnp.concatenate([total[8:, : 2 * columns], total[:8, 2 * columns :], total[8:, 2 * columns :]], axis=1)


def axis_pairs(stride, step):
    pairs = []
    for source in range(COUNT):
        digit = source // stride % SIDE
        pairs.append((source, source + ((digit + step) % SIDE - digit) * stride))
    return pairs


def exchange(parts, stride):
    return [parts[0]] + [lax.ppermute(parts[step], "seq", axis_pairs(stride, step)) for step in range(1, SIDE)]


def transpose_over(parts, groups):
    return lax.all_to_all(parts, "seq", 0, 0, axis_index_groups=groups)


def slots(rows, columns, kind):
    return [((rows, columns), kind)] + [((rows, columns), bf16)] * (SIDE - 1)


def shards(
    sequence,
    upstream,
    norm_gain,
    in_proj,
    step_proj,
    conv_weight,
    conv_bias,
    step_bias,
    decay_log,
    skip_gain,
    out_proj,
):
    rows, width = sequence.shape
    inner = out_proj.shape[0]
    heads = step_bias.shape[0]
    state = inner // heads * 2
    channels = conv_weight.shape[1]
    both_rows = 2 * rows
    stride_x, stride_z, stride_y = SIDE * SIDE, SIDE, 1
    index = lax.axis_index("seq")
    place = jnp.stack([index // stride_x, index // stride_z % SIDE, index % SIDE]).astype(jnp.int32)
    beside = [[SIDE * base + digit for digit in range(SIDE)] for base in range(COUNT // SIDE)]
    across = [[base + SIDE * digit for digit in range(COUNT // SIDE)] for base in range(SIDE)]
    upward = [(i, i + 1) for i in range(COUNT - 1)]
    downward = [(i + 1, i) for i in range(COUNT - 1)]
    low = lax.ppermute(sequence[rows - 16 :], "seq", upward)
    high = lax.ppermute(sequence[:16], "seq", downward)
    step_turned = step_proj.T
    payload, both, normal, normal_halo, cot, gate, conv, d_gated, raw, step, cumul, cumul_t = call(
        pre_kernel,
        [
            ((SIDE, inner + 16, state), bf16),
            ((both_rows, width), bf16),
            ((both_rows, width), bf16),
            ((32, width), bf16),
            ((both_rows, width), bf16),
            ((both_rows, inner), f32),
            ((both_rows, channels), f32),
            ((both_rows, inner), bf16),
            ((both_rows, heads), f32),
            ((both_rows, heads), f32),
            ((both_rows, heads), f32),
            ((2 * heads, rows), f32),
        ],
        (
            sequence, upstream, low, high, norm_gain, in_proj, step_turned,
            conv_weight, conv_bias, step_bias, decay_log, out_proj,
        ),
        [pltpu.VMEM((rows + 8, channels), f32)],
    )
    got = transpose_over(payload, beside)
    (summary,) = call(group_kernel, [((COUNT // SIDE, 72, state), bf16)], (got,), vmem=16 * 2**20)
    summaries = transpose_over(summary, across)
    mixed, d_driven, d_bc, d_cumul = call(
        intra_kernel,
        [
            ((both_rows, inner), f32),
            ((both_rows, inner), f32),
            ((both_rows, 2 * state), f32),
            ((both_rows, heads), f32),
        ],
        (conv, gate, d_gated, step, cumul, cumul_t),
        flops=8 * 10**9,
    )
    groups = COUNT // SIDE
    (scanned,) = call(
        scan_kernel,
        [((groups, 64, state), bf16)],
        (summaries,),
        [pltpu.VMEM((groups * 72, state), f32), pltpu.VMEM((groups * 64, state), f32)],
        vmem=16 * 2**20,
    )
    entering = transpose_over(scanned, across)
    (spread,) = call(spread_kernel, [((SIDE, inner, state), bf16)], (got, entering), vmem=16 * 2**20)
    states = transpose_over(spread, beside)
    eighth = 8 * COUNT // SIDE
    joined = inner + channels // 2
    gated, d_gate, d_xbc, d_edge, d_ahead, d_step, *parts = call(
        post_kernel,
        [
            ((both_rows, inner), bf16),
            ((both_rows, inner), bf16),
            ((both_rows, channels), bf16),
            ((16, channels), f32),
            ((16, channels), f32),
            ((both_rows, heads), bf16),
        ]
        + slots(eighth, joined, bf16) * 2,
        (
            place, states, conv, gate, d_gated, raw, step, cumul, mixed, d_driven, d_bc, d_cumul,
            step_bias, decay_log, skip_gain, conv_weight, cot, normal, normal_halo,
        ),
        [
            pltpu.VMEM((rows + 24, channels), f32),
            pltpu.VMEM((32, channels), bf16),
            pltpu.VMEM((8 * COUNT, joined), f32),
            pltpu.VMEM((COUNT // SIDE, SIDE, 8, joined), f32),
        ],
        scalars=1,
    )
    from_x = exchange(parts[:4], stride_x)
    from_y = exchange(parts[4:], stride_y)
    ahead = lax.ppermute(d_ahead[:8], "seq", downward)
    behind = lax.ppermute(d_ahead[8:], "seq", upward)
    layer_out, grad_input = call(
        result_kernel,
        [((rows, width), bf16), ((rows, width), bf16)],
        (
            both, norm_gain, gated, out_proj, d_gate, d_xbc, d_edge, ahead, behind, d_step,
            in_proj, step_turned,
        ),
        [pltpu.VMEM((both_rows, channels), bf16)],
        flops=8 * 10**9,
    )
    parts = call(
        first_sum_kernel,
        slots(eighth // SIDE, joined, f32) * 2,
        (place, *from_x, *from_y, layer_out),
        [pltpu.VMEM((SIDE, SIDE, 8, joined), f32), pltpu.VMEM((eighth, joined), f32)],
        scalars=1,
        vmem=16 * 2**20,
    )
    first = exchange(parts[:4], stride_y)
    second = exchange(parts[4:], stride_x)
    parts = call(
        second_sum_kernel,
        slots(16, joined, f32),
        (place, *first, *second),
        [pltpu.VMEM((SIDE, 2, 8, joined), f32)],
        scalars=1,
        vmem=16 * 2**20,
    )
    last = exchange(parts, stride_z)
    grad_in_proj, grad_out_proj = call(
        last_sum_kernel,
        [((8, inner + channels), f32), ((16, width), f32)],
        tuple(last),
        vmem=16 * 2**20,
    )
    return (layer_out, grad_input, grad_in_proj, grad_out_proj)


def solution(mesh):
    rows = P(("batch", "seq"), None)
    return jax.shard_map(
        shards,
        mesh=mesh,
        in_specs=(rows, rows) + (P(),) * 9,
        out_specs=(rows,) * 4,
        check_vma=False,
    )
```

```python
import functools

import jax
import jax.numpy as jnp
from jax import lax
from jax.experimental import pallas as pl
from jax.experimental.pallas import tpu as pltpu
from jax.sharding import PartitionSpec as P

epsilon = 1e-06
SIDE = 4
COUNT = SIDE**3
f32 = jnp.float32
bf16 = jnp.bfloat16
INTERPRET = False


def call(body, outs, args, scratch=(), scalars=0, unused=0, flops=10**9, vmem=58 * 2**20):
    after = len(args) - unused
    specs = [pl.BlockSpec(memory_space=pltpu.SMEM)] * scalars
    specs += [pl.BlockSpec(memory_space=pltpu.VMEM)] * (after - scalars)
    specs += [pl.BlockSpec(memory_space=pl.ANY)] * unused
    moved = sum(a.size * a.dtype.itemsize for a in args[:after])

    def used(*refs):
        body(*refs[:after], *refs[len(args) :])

    return pl.pallas_call(
        used,
        out_shape=[jax.ShapeDtypeStruct(shape, kind) for shape, kind in outs],
        in_specs=specs,
        out_specs=[pl.BlockSpec(memory_space=pltpu.VMEM)] * len(outs),
        scratch_shapes=list(scratch),
        compiler_params=pltpu.CompilerParams(vmem_limit_bytes=vmem),
        cost_estimate=pl.CostEstimate(flops=flops, bytes_accessed=moved, transcendentals=0),
        interpret=INTERPRET,
    )(*args)


def mm(left, right):
    return lax.dot_general(left, right, (((1,), (0,)), ((), ())), preferred_element_type=f32)


def mm_cols(left, right):
    return lax.dot_general(left, right, (((1,), (1,)), ((), ())), preferred_element_type=f32)


def mm_rows(left, right):
    return lax.dot_general(left, right, (((0,), (0,)), ((), ())), preferred_element_type=f32)


def iota(shape, dim):
    return lax.broadcasted_iota(jnp.int32, shape, dim)


def ones_where(mask):
    return jnp.where(mask, 1.0, 0.0).astype(bf16)


def anti(size):
    return ones_where(iota((size, size), 0) + iota((size, size), 1) == size - 1)


def pieces_of(value, count):
    found = []
    for _ in range(count):
        piece = value.astype(bf16)
        found.append(piece)
        value = value - piece.astype(f32)
    return found


def mirror_exact(block):
    turned = mm(block, anti(block.shape[1])).astype(bf16)
    return mm(anti(block.shape[0]), turned).astype(bf16)


def mirror_wide(block):
    high, low = pieces_of(block, 2)
    return mirror_exact(high).astype(f32) + mirror_exact(low).astype(f32)


def head_mask(heads, width):
    lanes = heads * width
    return ones_where(iota((heads, lanes), 0) == iota((heads, lanes), 1) // width)


def expand(value, mask):
    found = pieces_of(value, 3)
    return mm(jnp.concatenate(found, axis=1), jnp.concatenate([mask] * 3, axis=0))


def fold(value, mask):
    total = None
    for piece in pieces_of(value, 2):
        part = mm_cols(piece, mask)
        total = part if total is None else total + part
    return total


def triangle(size, low):
    rows, cols = iota((size, size), 0), iota((size, size), 1)
    return rows >= cols if low else rows <= cols


def tri_sum(mask, value):
    total = None
    for piece in pieces_of(value, 3):
        part = mm(ones_where(mask), piece)
        total = part if total is None else total + part
    return total


def tri_sum_turned(mask, value):
    total = None
    for piece in pieces_of(value, 3):
        part = mm_rows(piece, ones_where(mask))
        total = part if total is None else total + part
    return total


def softplus(value):
    return jnp.maximum(value, 0.0) + jnp.log1p(jnp.exp(-jnp.abs(value)))


def sigmoid(value):
    return 1.0 / (1.0 + jnp.exp(-value))


def norm_rows(block, gain):
    wide = block.astype(f32)
    scale = lax.rsqrt(jnp.mean(wide * wide, axis=-1, keepdims=True) + epsilon)
    return (wide * scale * gain.reshape(1, -1)).astype(bf16)


def pre_kernel(
    seq, up, low, high, gain, in_proj, step_proj, conv_w, conv_b, step_bias, decay_log, out_proj,
    payload, both, normal, normal_halo, cot, gate, conv, d_gated, raw, step, cumul, cumul_t,
    ext,
):
    rows = seq.shape[0]
    inner = out_proj.shape[0]
    heads = step_bias.shape[0]
    state = (conv_w.shape[1] - inner) // 2
    taps = conv_w.shape[0]
    both[:rows, :] = seq[...]
    both[rows:, :] = mirror_exact(seq[...])
    cot[:rows, :] = up[...]
    cot[rows:, :] = mirror_exact(up[...])
    halo = jnp.concatenate([low[...], mirror_exact(high[...])], axis=0)
    normal[...] = norm_rows(both[...], gain[...])
    normal_halo[...] = norm_rows(halo, gain[...])
    gate[...] = mm(normal[...], in_proj[:, :inner])
    xbc = mm(normal[...], in_proj[:, inner:]).astype(bf16).astype(f32)
    xbc_halo = mm(normal_halo[...], in_proj[:, inner:]).astype(bf16).astype(f32)
    raw[...] = mm_cols(normal[...], step_proj[...])
    d_gated[...] = mm_cols(cot[...], out_proj[...]).astype(bf16)
    margin = low.shape[0]
    mask = head_mask(heads, inner // heads)
    ends = []
    for frame in range(2):
        at = slice(frame * rows, (frame + 1) * rows)
        ext[:8, :] = xbc_halo[(frame + 1) * margin - 8 : (frame + 1) * margin, :]
        ext[8:, :] = xbc[at, :]
        found = conv_b[...].reshape(1, -1)
        for tap in range(taps):
            start = 9 - taps + tap
            found = found + ext[start : start + rows, :] * conv_w[tap : tap + 1, :]
        conv[at, :] = found
        act = found * sigmoid(found)
        size = softplus(raw[at, :] + step_bias[...].reshape(1, -1))
        decay = -jnp.exp(decay_log[...].reshape(1, -1)) * size
        upto = tri_sum(triangle(rows, True), decay)
        step[at, :] = size
        cumul[at, :] = upto
        cumul_t[frame * heads : (frame + 1) * heads, :] = tri_sum_turned(triangle(rows, False), decay)
        end = upto[rows - 1 : rows, :]
        ends.append(end)
        spread = expand(jnp.concatenate([size * jnp.exp(end - upto), jnp.exp(upto)], axis=0), mask)
        driven = (act[:, :inner] * spread[:rows]).astype(bf16)
        local = mm_rows(driven, act[:, inner : inner + state].astype(bf16))
        wide = gate[at, :]
        d_mixed = d_gated[at, :].astype(f32) * (wide * sigmoid(wide))
        back = mm_rows((d_mixed * spread[rows:]).astype(bf16), act[:, inner + state :].astype(bf16))
        part = inner // SIDE
        for place, block in ((frame, local), (2 + frame, back)):
            block = block.astype(bf16).reshape(SIDE, part, state)
            payload[:, place * part : (place + 1) * part, :] = block
    packed = pack_totals(ends, heads, state)
    for to in range(SIDE):
        shifted = ones_where(iota((16, heads), 1) == iota((16, heads), 0) + to * (heads // SIDE))
        payload[to, inner:, :] = mm(shifted, packed).astype(bf16)


def pack_totals(ends, heads, state):
    chosen = iota((heads, heads), 0) == iota((heads, heads), 1)
    lanes = iota((heads, state), 1)
    packed = jnp.zeros((heads, state), f32)
    for frame in range(2):
        column = jnp.sum(jnp.where(chosen, ends[frame], 0.0), axis=1, keepdims=True)
        packed = pack_column(packed, column, lanes, frame)
    return packed.astype(bf16)


def pack_column(packed, column, lanes, frame):
    for nth, piece in enumerate(pieces_of(column, 3)):
        packed = jnp.where(lanes == 3 * frame + nth, piece.astype(f32), packed)
    return packed


def unpack_column(packed, frame):
    at = 3 * frame
    return (packed[:, at + 2 : at + 3] + packed[:, at + 1 : at + 2]) + packed[:, at : at + 1]


SCANS = ((0, False), (1, True), (0, True), (1, False))


def chain(got, totals, place, state, visit):
    frame, turned = SCANS[place]
    part = state.shape[0]
    size = part // SIDE
    order = range(SIDE - 1, -1, -1) if turned else range(SIDE)
    for at in order:
        visit(at, state)
        grown = jnp.exp(totals[at][frame])
        factors = [
            jnp.broadcast_to(grown[head : head + 1, :], (size, 1)) for head in range(part // size)
        ]
        state = jnp.concatenate(factors, axis=0) * state
        state = state + got[at, place * part : (place + 1) * part, :].astype(f32)
    return state


def tails_of(got, inner):
    found = []
    for at in range(SIDE):
        tail = got[at, inner:, :].astype(f32)
        found.append([unpack_column(tail, frame) for frame in range(2)])
    return found


def group_kernel(got, out):
    state = got.shape[2]
    inner = got.shape[1] - 16
    part = inner // SIDE
    totals = tails_of(got, inner)
    for place in range(4):
        block = chain(got, totals, place, jnp.zeros((part, state), f32), lambda at, value: None)
        out[:, 16 * place : 16 * place + 16, :] = block.reshape(16, 16, state).astype(bf16)
    lanes = iota((16, state), 1)
    packed = jnp.zeros((16, state), f32)
    for frame in range(2):
        column = jnp.maximum(totals[0][frame], -110.0)
        for at in range(1, SIDE):
            column = column + jnp.maximum(totals[at][frame], -110.0)
        packed = pack_column(packed, column, lanes, frame)
    chosen = ones_where(iota((16, 16), 1) == iota((16, 16), 0) // SIDE)
    packed = mm(chosen, packed.astype(bf16))
    out[:, 64:, :] = jnp.broadcast_to(packed.reshape(16, 1, state), (16, 8, state)).astype(bf16)


def spread_kernel(got, entering, out):
    state = got.shape[2]
    inner = got.shape[1] - 16
    part = inner // SIDE
    totals = tails_of(got, inner)
    for place in range(4):

        def visit(at, value, place=place):
            out[at, place * part : (place + 1) * part, :] = value.astype(bf16)

        block = entering[:, 16 * place : 16 * place + 16, :].astype(f32).reshape(part, state)
        chain(got, totals, place, block, visit)


def scan_kernel(got, out, wide, done):
    count, rows, state = got.shape
    wide[...] = got[...].astype(f32).reshape(count * rows, state)
    tails = wide[pl.ds(64, count, stride=rows), :]
    above = iota((count, count), 0)
    beside = iota((count, count), 1)
    after = ones_where(above > beside)
    weights = []
    for frame in range(2):
        column = jnp.maximum(unpack_column(tails, frame), -110.0)
        line = jnp.sum(jnp.where(above == beside, column, 0.0), axis=0, keepdims=True)
        between = None
        for piece in pieces_of(jnp.where(beside < above, line, 0.0), 3):
            part = mm(piece, after)
            between = part if between is None else between + part
        found = jnp.where(above > beside, jnp.exp(between), 0.0)
        weights.append(pieces_of(found, 2))
    for place, (frame, turned) in enumerate(SCANS):
        pair = weights[frame]
        block = jnp.concatenate(
            [wide[pl.ds(16 * place + row, count, stride=rows), :] for row in range(16)], axis=1
        ).astype(bf16)
        if turned:
            mixed = mm_rows(jnp.concatenate(pair, axis=1), block)
        else:
            mixed = mm(jnp.concatenate(pair, axis=0), block)
        mixed = mixed[:count] + mixed[count:]
        for row in range(16):
            done[pl.ds(16 * place + row, count, stride=64), :] = mixed[:, state * row : state * (row + 1)]
    out[...] = done[...].reshape(count, 64, state).astype(bf16)


def intra_kernel(conv, gate, d_gated, step, cumul, cumul_t, mixed, d_driven, d_bc, d_cumul):
    rows = conv.shape[0] // 2
    inner = gate.shape[1]
    heads = step.shape[1]
    state = (conv.shape[1] - inner) // 2
    mask = head_mask(heads, inner // heads)
    lower = triangle(rows, True)
    first = iota((rows, 2 * inner // heads), 1) < inner // heads
    wide_pair = 2 * inner // heads
    for frame in range(2):
        at = slice(frame * rows, (frame + 1) * rows)
        found = conv[at, :]
        act = found * sigmoid(found)
        bmat = act[:, inner : inner + state].astype(bf16)
        cmat = act[:, inner + state :].astype(bf16)
        driven = act[:, :inner] * expand(step[at, :], mask)
        wide = gate[at, :]
        d_mixed = d_gated[at, :].astype(f32) * (wide * sigmoid(wide))
        scores = mm_cols(cmat, bmat)
        upto, line = cumul[at, :], cumul_t[frame * heads : (frame + 1) * heads, :]
        d_scores = jnp.zeros((rows, rows), f32)
        sums = []
        for pair in range(heads // 2):
            lanes = slice(pair * wide_pair, (pair + 1) * wide_pair)
            decays = []
            for head in (2 * pair, 2 * pair + 1):
                differ = upto[:, head : head + 1] - line[head : head + 1, :]
                decays.append(jnp.exp(jnp.where(lower, differ, -1e30)))
            weights = [(decay * scores).astype(bf16) for decay in decays]
            drive, d_mix = driven[:, lanes], d_mixed[:, lanes]
            drive_bf, d_mix_bf = drive.astype(bf16), d_mix.astype(bf16)
            drive_two = jnp.concatenate(
                [jnp.where(first, drive, 0.0), jnp.where(first, 0.0, drive)], axis=0
            ).astype(bf16)
            d_mix_two = jnp.concatenate(
                [jnp.where(first, d_mix, 0.0), jnp.where(first, 0.0, d_mix)], axis=0
            ).astype(bf16)
            mix = mm(jnp.concatenate(weights, axis=1), drive_two)
            d_weights = mm_cols(d_mix_two, drive_bf)
            d_drive = mm_rows(jnp.concatenate(weights, axis=0), d_mix_two)
            d_scores = d_scores + decays[0] * d_weights[:rows] + decays[1] * d_weights[rows:]
            mixed[at, lanes] = mix
            d_driven[at, lanes] = d_drive
            sums.append(d_mix_bf.astype(f32) * mix - drive_bf.astype(f32) * d_drive)
        d_scores = d_scores.astype(bf16)
        d_bc[at, :state] = mm_rows(d_scores, cmat)
        d_bc[at, state:] = mm(d_scores, bmat)
        d_cumul[at, :] = fold(jnp.concatenate(sums, axis=1), mask)


def post_kernel(
    place, got, conv, gate, d_gated, raw, step, cumul, mixed, d_driven, d_bc, d_cumul, step_bias, decay_log, skip_gain,
    conv_w, cot, normal, normal_halo,
    gated, d_gate, d_xbc, d_edge, d_ahead, d_step, *refs,
):
    by_x, by_y, ext, d_conv_out, whole, parted = refs[:4], refs[4:8], refs[8], refs[9], refs[10], refs[11]
    rows = conv.shape[0] // 2
    inner = gate.shape[1]
    heads = step.shape[1]
    state = (conv.shape[1] - inner) // 2
    mask = head_mask(heads, inner // heads)
    skip = expand(jnp.broadcast_to(skip_gain[...].reshape(1, -1), (8, heads)), mask)[:1]
    for frame in range(2):
        at = slice(frame * rows, (frame + 1) * rows)
        found = conv[at, :]
        share = sigmoid(found)
        act = found * share
        inputs = act[:, :inner]
        bmat = act[:, inner : inner + state].astype(bf16)
        cmat = act[:, inner + state :].astype(bf16)
        upto = cumul[at, :]
        end = upto[rows - 1 : rows, :]
        spread = expand(jnp.concatenate([step[at, :], jnp.exp(upto), jnp.exp(end - upto)], axis=0), mask)
        sizes, grown, left = spread[:rows], spread[rows : 2 * rows], spread[2 * rows :]
        part = inner // SIDE
        carried = got[:, frame * part : (frame + 1) * part, :].reshape(inner, state)
        reach = got[:, (2 + frame) * part : (3 + frame) * part, :].reshape(inner, state)
        inter = grown * mm_cols(cmat, carried)
        full = mixed[at, :] + inter + skip * inputs
        wide = gate[at, :]
        opened = sigmoid(wide)
        silu = wide * opened
        gated[at, :] = (full * silu).astype(bf16)
        d_out = d_gated[at, :].astype(f32)
        d_gate[at, :] = (d_out * full * (opened * (1.0 + wide * (1.0 - opened)))).astype(bf16)
        d_mixed = d_out * silu
        d_cmat = d_bc[at, state:] + mm((d_mixed * grown).astype(bf16), carried)
        answer = left * mm_cols(bmat, reach)
        driven = inputs * sizes
        d_drive = d_driven[at, :] + answer
        d_bmat = d_bc[at, :state] + mm((left * driven).astype(bf16), reach)
        products = carried.astype(f32) * reach.astype(f32)
        met = jnp.sum(products.reshape(heads, inner // heads, state), axis=1)
        met = jnp.sum(met, axis=1, keepdims=True)
        met = jnp.sum(jnp.where(iota((heads, heads), 0) == iota((heads, heads), 1), met, 0.0), axis=0, keepdims=True)
        folded = fold(jnp.concatenate([driven * answer, d_mixed * inter, d_drive * inputs], axis=0), mask)
        held, entered, by_size = folded[:rows], folded[rows : 2 * rows], folded[2 * rows :]
        d_end = jnp.exp(end) * met + jnp.sum(held, axis=0, keepdims=True)
        d_decay = tri_sum(triangle(rows, False), d_cumul[at, :] + entered - held) + d_end
        d_size = by_size - jnp.exp(decay_log[...].reshape(1, -1)) * d_decay
        d_step[at, :] = (d_size * sigmoid(raw[at, :] + step_bias[...].reshape(1, -1))).astype(bf16)
        d_act = jnp.concatenate([skip * d_mixed + d_drive * sizes, d_bmat, d_cmat], axis=1)
        margin = normal_halo.shape[0] // 2
        ext[:margin, :] = jnp.zeros((margin, ext.shape[1]), f32)
        ext[margin : margin + rows, :] = d_act * (share * (1.0 + found * (1.0 - share)))
        ext[margin + rows :, :] = jnp.zeros((8, ext.shape[1]), f32)
        taps = conv_w.shape[0]
        total = None
        for tap in range(taps):
            start = taps - 1 - tap
            part = ext[start : start + margin + rows, :] * conv_w[tap : tap + 1, :]
            total = part if total is None else total + part
        d_xbc[at, :] = total[margin:].astype(bf16)
        d_conv_out[frame * margin : (frame + 1) * margin, :] = total[:margin].astype(bf16)
        d_ahead[8 * frame : 8 * frame + 8, :] = total[margin - 8 : margin]
        d_edge[8 * frame : 8 * frame + 8, :] = total[margin + rows - 8 :]
    columns = cot.shape[1]
    half = d_xbc.shape[1] // 2
    out_term = mm_rows(gated[...], cot[...]).reshape(COUNT, 2, 8, columns)
    gate_term = mm_rows(normal[...], d_gate[...]).reshape(COUNT // SIDE, SIDE, 8, inner)
    in_term = mm_rows(normal[...], d_xbc[...]) + mm_rows(normal_halo[...], d_conv_out[...])
    whole[:, :columns] = out_term[:, 0].reshape(-1, columns)
    whole[:, columns : 2 * columns] = out_term[:, 1].reshape(-1, columns)
    whole[:, 2 * columns :] = in_term[:, :half]
    parted[:, :, :, :inner] = gate_term
    parted[:, :, :, inner:] = in_term[:, half:].reshape(COUNT // SIDE, SIDE, 8, half)
    send_x(place, whole, by_x)
    send_y(place, parted, by_y)


def send_x(place, whole, slots):
    chunk = whole.shape[0] // SIDE
    for step in range(SIDE):
        to = lax.rem(place[0] + step, SIDE)
        block = whole[pl.ds(pl.multiple_of(to * chunk, chunk), chunk), :]
        slots[step][...] = block.astype(slots[step].dtype)


def send_y(place, parted, slots):
    for step in range(SIDE):
        block = parted[:, lax.rem(place[2] + step, SIDE)]
        slots[step][...] = block.reshape(slots[step].shape).astype(slots[step].dtype)


def result_kernel(both, gated, out_proj, d_gate, d_xbc, d_step, in_proj, step_proj, layer, d_normal):
    rows = both.shape[0] // 2
    inner = out_proj.shape[0]
    branch = mm(gated[...], out_proj[...])
    layer[...] = (branch[:rows] + mirror_wide(branch[rows:])).astype(bf16)
    found = mm_cols(d_gate[...], in_proj[:, :inner]) + mm(d_step[...], step_proj[...])
    keep = iota((d_xbc.shape[0], 1), 0) % rows < rows - 8
    edgeless = jnp.where(keep, d_xbc[...].astype(f32), 0.0).astype(bf16)
    d_normal[...] = found + mm_cols(edgeless, in_proj[:, inner:])


def input_kernel(both, gain, d_normal, d_edge, ahead, behind, in_proj, grad, d_whole):
    rows = both.shape[0] // 2
    inner = in_proj.shape[1] - d_edge.shape[1]
    edge = (d_edge[...] + jnp.concatenate([ahead[...], behind[...]], axis=0)).astype(bf16)
    added = mm_cols(edge, in_proj[:, inner:])
    d_whole[...] = d_normal[...]
    for frame in range(2):
        last = slice((frame + 1) * rows - 8, (frame + 1) * rows)
        d_whole[last, :] = d_whole[last, :] + added[8 * frame : 8 * frame + 8]
    wide = both[...].astype(f32)
    scale = lax.rsqrt(jnp.mean(wide * wide, axis=-1, keepdims=True) + epsilon)
    d_scaled = d_whole[...] * gain[...].reshape(1, -1)
    along = jnp.mean(d_scaled * wide, axis=-1, keepdims=True)
    d_wide = scale * d_scaled - wide * (scale * scale * scale * along)
    grad[...] = (d_wide[:rows] + mirror_wide(d_wide[rows:])).astype(bf16)


def edge_kernel(d_ahead, ahead, behind):
    ahead[...] = d_ahead[:8, :]
    behind[...] = d_ahead[8:, :]


def total_of(refs):
    total = refs[0][...].astype(f32)
    for ref in refs[1:]:
        total = total + ref[...].astype(f32)
    return total


def first_sum_kernel(place, *refs):
    from_x, from_y, by_y, by_x, parted, whole = refs[:4], refs[4:8], refs[8:12], refs[12:16], refs[16], refs[17]
    parted[...] = total_of(from_x).reshape(parted.shape)
    whole[...] = total_of(from_y)
    send_y(place, parted, by_y)
    send_x(place, whole, by_x)


def second_sum_kernel(*refs):
    first, second, by_z = refs[:4], refs[4:8], refs[8]
    first = total_of(first).reshape(SIDE, 8, -1)
    second = total_of(second).reshape(SIDE, 8, -1)
    for to in range(SIDE):
        by_z[to] = jnp.concatenate([first[to], second[to]], axis=0).astype(bf16)


def last_sum_kernel(parts, grad_in, grad_out):
    total = parts[0].astype(f32)
    for step in range(1, SIDE):
        total = total + parts[step].astype(f32)
    columns = grad_out.shape[1]
    grad_out[:8, :] = total[:8, :columns]
    grad_out[8:, :] = total[:8, columns : 2 * columns]
    grad_in[...] = jnp.concatenate([total[8:, : 2 * columns], total[:8, 2 * columns :], total[8:, 2 * columns :]], axis=1)


def axis_pairs(stride, step):
    pairs = []
    for source in range(COUNT):
        digit = source // stride % SIDE
        pairs.append((source, source + ((digit + step) % SIDE - digit) * stride))
    return pairs


def exchange(parts, stride):
    return [parts[0]] + [lax.ppermute(parts[step], "seq", axis_pairs(stride, step)) for step in range(1, SIDE)]


def transpose_over(parts, groups):
    return lax.all_to_all(parts, "seq", 0, 0, axis_index_groups=groups)


def slots(rows, columns, kind):
    return [((rows, columns), kind)] + [((rows, columns), bf16)] * (SIDE - 1)


def shards(
    sequence,
    upstream,
    norm_gain,
    in_proj,
    step_proj,
    conv_weight,
    conv_bias,
    step_bias,
    decay_log,
    skip_gain,
    out_proj,
):
    rows, width = sequence.shape
    inner = out_proj.shape[0]
    heads = step_bias.shape[0]
    state = inner // heads * 2
    channels = conv_weight.shape[1]
    both_rows = 2 * rows
    stride_x, stride_z, stride_y = SIDE * SIDE, SIDE, 1
    index = lax.axis_index("seq")
    place = jnp.stack([index // stride_x, index // stride_z % SIDE, index % SIDE]).astype(jnp.int32)
    aligned = [[base + SIDE * digit for digit in range(SIDE)] for base in range(COUNT) if base // SIDE % SIDE == 0]
    beside = [[SIDE * base + digit for digit in range(SIDE)] for base in range(COUNT // SIDE)]
    across = [[base + SIDE * digit for digit in range(COUNT // SIDE)] for base in range(SIDE)]
    upward = [(i, i + 1) for i in range(COUNT - 1)]
    downward = [(i + 1, i) for i in range(COUNT - 1)]
    low = lax.ppermute(sequence[rows - 16 :], "seq", upward)
    high = lax.ppermute(sequence[:16], "seq", downward)
    step_turned = step_proj.T
    payload, both, normal, normal_halo, cot, gate, conv, d_gated, raw, step, cumul, cumul_t = call(
        pre_kernel,
        [
            ((SIDE, inner + 16, state), bf16),
            ((both_rows, width), bf16),
            ((both_rows, width), bf16),
            ((32, width), bf16),
            ((both_rows, width), bf16),
            ((both_rows, inner), f32),
            ((both_rows, channels), f32),
            ((both_rows, inner), bf16),
            ((both_rows, heads), f32),
            ((both_rows, heads), f32),
            ((both_rows, heads), f32),
            ((2 * heads, rows), f32),
        ],
        (
            sequence, upstream, low, high, norm_gain, in_proj, step_turned,
            conv_weight, conv_bias, step_bias, decay_log, out_proj,
        ),
        [pltpu.VMEM((rows + 8, channels), f32)],
    )
    got = transpose_over(payload, beside)
    (summary,) = call(group_kernel, [((COUNT // SIDE, 72, state), bf16)], (got,), vmem=16 * 2**20)
    summaries = transpose_over(summary, across)
    mixed, d_driven, d_bc, d_cumul = call(
        intra_kernel,
        [
            ((both_rows, inner), f32),
            ((both_rows, inner), f32),
            ((both_rows, 2 * state), f32),
            ((both_rows, heads), f32),
        ],
        (conv, gate, d_gated, step, cumul, cumul_t),
        flops=8 * 10**9,
    )
    groups = COUNT // SIDE
    (scanned,) = call(
        scan_kernel,
        [((groups, 64, state), bf16)],
        (summaries,),
        [pltpu.VMEM((groups * 72, state), f32), pltpu.VMEM((groups * 64, state), f32)],
        vmem=16 * 2**20,
    )
    entering = transpose_over(scanned, across)
    (spread,) = call(spread_kernel, [((SIDE, inner, state), bf16)], (got, entering), vmem=16 * 2**20)
    states = transpose_over(spread, beside)
    eighth = 8 * COUNT // SIDE
    joined = inner + channels // 2
    gated, d_gate, d_xbc, d_edge, d_ahead, d_step, *parts = call(
        post_kernel,
        [
            ((both_rows, inner), bf16),
            ((both_rows, inner), bf16),
            ((both_rows, channels), bf16),
            ((16, channels), f32),
            ((16, channels), f32),
            ((both_rows, heads), bf16),
        ]
        + slots(eighth, joined, bf16) * 2,
        (
            place, states, conv, gate, d_gated, raw, step, cumul, mixed, d_driven, d_bc, d_cumul,
            step_bias, decay_log, skip_gain, conv_weight, cot, normal, normal_halo,
        ),
        [
            pltpu.VMEM((rows + 24, channels), f32),
            pltpu.VMEM((32, channels), bf16),
            pltpu.VMEM((8 * COUNT, joined), f32),
            pltpu.VMEM((COUNT // SIDE, SIDE, 8, joined), f32),
        ],
        scalars=1,
    )
    from_x = exchange(parts[:4], stride_x)
    from_y = exchange(parts[4:], stride_y)
    ahead, behind = call(
        edge_kernel,
        [((8, channels), f32)] * 2,
        (d_ahead, from_y[1]),
        unused=1,
        flops=10**6,
        vmem=16 * 2**20,
    )
    ahead = lax.ppermute(ahead, "seq", downward)
    behind = lax.ppermute(behind, "seq", upward)
    layer_out, d_normal = call(
        result_kernel,
        [((rows, width), bf16), ((both_rows, width), f32)],
        (both, gated, out_proj, d_gate, d_xbc, d_step, in_proj, step_turned),
        flops=8 * 10**9,
    )
    from_x, from_y, layer_out, ahead, behind = lax.optimization_barrier((from_x, from_y, layer_out, ahead, behind))
    parts = call(
        first_sum_kernel,
        slots(eighth // SIDE, joined, f32) * 2,
        (place, *from_x, *from_y),
        [pltpu.VMEM((SIDE, SIDE, 8, joined), f32), pltpu.VMEM((eighth, joined), f32)],
        scalars=1,
        vmem=16 * 2**20,
    )
    first = exchange(parts[:4], stride_y)
    second = exchange(parts[4:], stride_x)
    (grad_input,) = call(
        input_kernel,
        [((rows, width), bf16)],
        (both, norm_gain, d_normal, d_edge, ahead, behind, in_proj),
        [pltpu.VMEM((both_rows, width), f32)],
        flops=4 * 10**9,
    )
    (by_z,) = call(
        second_sum_kernel,
        [((SIDE, 16, joined), bf16)],
        (*first, *second),
        vmem=16 * 2**20,
    )
    last = transpose_over(by_z, aligned)
    grad_in_proj, grad_out_proj = call(
        last_sum_kernel,
        [((8, inner + channels), f32), ((16, width), f32)],
        (last,),
        vmem=16 * 2**20,
    )
    return (layer_out, grad_input, grad_in_proj, grad_out_proj)


def solution(mesh):
    rows = P(("batch", "seq"), None)
    return jax.shard_map(
        shards,
        mesh=mesh,
        in_specs=(rows, rows) + (P(),) * 9,
        out_specs=(rows,) * 4,
        check_vma=False,
    )
```

```python
import functools

import jax
import jax.numpy as jnp
from jax import lax
from jax.experimental import pallas as pl
from jax.experimental.pallas import tpu as pltpu
from jax.sharding import PartitionSpec as P

epsilon = 1e-06
SIDE = 4
COUNT = SIDE**3
f32 = jnp.float32
bf16 = jnp.bfloat16
INTERPRET = False


def call(body, outs, args, scratch=(), scalars=0, unused=0, flops=10**9, vmem=58 * 2**20):
    after = len(args) - unused
    specs = [pl.BlockSpec(memory_space=pltpu.SMEM)] * scalars
    specs += [pl.BlockSpec(memory_space=pltpu.VMEM)] * (after - scalars)
    specs += [pl.BlockSpec(memory_space=pl.ANY)] * unused
    moved = sum(a.size * a.dtype.itemsize for a in args[:after])

    def used(*refs):
        body(*refs[:after], *refs[len(args) :])

    return pl.pallas_call(
        used,
        out_shape=[jax.ShapeDtypeStruct(shape, kind) for shape, kind in outs],
        in_specs=specs,
        out_specs=[pl.BlockSpec(memory_space=pltpu.VMEM)] * len(outs),
        scratch_shapes=list(scratch),
        compiler_params=pltpu.CompilerParams(vmem_limit_bytes=vmem),
        cost_estimate=pl.CostEstimate(flops=flops, bytes_accessed=moved, transcendentals=0),
        interpret=INTERPRET,
    )(*args)


def mm(left, right):
    return lax.dot_general(left, right, (((1,), (0,)), ((), ())), preferred_element_type=f32)


def mm_cols(left, right):
    return lax.dot_general(left, right, (((1,), (1,)), ((), ())), preferred_element_type=f32)


def mm_rows(left, right):
    return lax.dot_general(left, right, (((0,), (0,)), ((), ())), preferred_element_type=f32)


def iota(shape, dim):
    return lax.broadcasted_iota(jnp.int32, shape, dim)


def ones_where(mask):
    return jnp.where(mask, 1.0, 0.0).astype(bf16)


def anti(size):
    return ones_where(iota((size, size), 0) + iota((size, size), 1) == size - 1)


def pieces_of(value, count):
    found = []
    for _ in range(count):
        piece = value.astype(bf16)
        found.append(piece)
        value = value - piece.astype(f32)
    return found


def mirror_exact(block):
    turned = mm(block, anti(block.shape[1])).astype(bf16)
    return mm(anti(block.shape[0]), turned).astype(bf16)


def mirror_wide(block):
    high, low = pieces_of(block, 2)
    return mirror_exact(high).astype(f32) + mirror_exact(low).astype(f32)


def head_mask(heads, width):
    lanes = heads * width
    return ones_where(iota((heads, lanes), 0) == iota((heads, lanes), 1) // width)


def expand(value, mask):
    found = pieces_of(value, 3)
    return mm(jnp.concatenate(found, axis=1), jnp.concatenate([mask] * 3, axis=0))


def fold(value, mask):
    total = None
    for piece in pieces_of(value, 2):
        part = mm_cols(piece, mask)
        total = part if total is None else total + part
    return total


def triangle(size, low):
    rows, cols = iota((size, size), 0), iota((size, size), 1)
    return rows >= cols if low else rows <= cols


def tri_sum(mask, value):
    total = None
    for piece in pieces_of(value, 3):
        part = mm(ones_where(mask), piece)
        total = part if total is None else total + part
    return total


def tri_sum_turned(mask, value):
    total = None
    for piece in pieces_of(value, 3):
        part = mm_rows(piece, ones_where(mask))
        total = part if total is None else total + part
    return total


def softplus(value):
    return jnp.maximum(value, 0.0) + jnp.log1p(jnp.exp(-jnp.abs(value)))


def sigmoid(value):
    return 1.0 / (1.0 + jnp.exp(-value))


def norm_rows(block, gain):
    wide = block.astype(f32)
    scale = lax.rsqrt(jnp.mean(wide * wide, axis=-1, keepdims=True) + epsilon)
    return (wide * scale * gain.reshape(1, -1)).astype(bf16)


def pre_kernel(
    seq, up, low, high, gain, in_proj, step_proj, conv_w, conv_b, step_bias, decay_log, out_proj,
    payload, both, normal, normal_halo, cot, gate, conv, d_gated, raw, step, cumul, cumul_t,
    ext,
):
    rows = seq.shape[0]
    inner = out_proj.shape[0]
    heads = step_bias.shape[0]
    state = (conv_w.shape[1] - inner) // 2
    taps = conv_w.shape[0]
    both[:rows, :] = seq[...]
    both[rows:, :] = mirror_exact(seq[...])
    cot[:rows, :] = up[...]
    cot[rows:, :] = mirror_exact(up[...])
    halo = jnp.concatenate([low[...], mirror_exact(high[...])], axis=0)
    normal[...] = norm_rows(both[...], gain[...])
    normal_halo[...] = norm_rows(halo, gain[...])
    gate[...] = mm(normal[...], in_proj[:, :inner])
    xbc = mm(normal[...], in_proj[:, inner:]).astype(bf16).astype(f32)
    xbc_halo = mm(normal_halo[...], in_proj[:, inner:]).astype(bf16).astype(f32)
    raw[...] = mm_cols(normal[...], step_proj[...])
    d_gated[...] = mm_cols(cot[...], out_proj[...]).astype(bf16)
    margin = low.shape[0]
    mask = head_mask(heads, inner // heads)
    ends = []
    for frame in range(2):
        at = slice(frame * rows, (frame + 1) * rows)
        ext[:8, :] = xbc_halo[(frame + 1) * margin - 8 : (frame + 1) * margin, :]
        ext[8:, :] = xbc[at, :]
        found = conv_b[...].reshape(1, -1)
        for tap in range(taps):
            start = 9 - taps + tap
            found = found + ext[start : start + rows, :] * conv_w[tap : tap + 1, :]
        conv[at, :] = found
        act = found * sigmoid(found)
        size = softplus(raw[at, :] + step_bias[...].reshape(1, -1))
        decay = -jnp.exp(decay_log[...].reshape(1, -1)) * size
        upto = tri_sum(triangle(rows, True), decay)
        step[at, :] = size
        cumul[at, :] = upto
        cumul_t[frame * heads : (frame + 1) * heads, :] = tri_sum_turned(triangle(rows, False), decay)
        end = upto[rows - 1 : rows, :]
        ends.append(end)
        spread = expand(jnp.concatenate([size * jnp.exp(end - upto), jnp.exp(upto)], axis=0), mask)
        driven = (act[:, :inner] * spread[:rows]).astype(bf16)
        local = mm_rows(driven, act[:, inner : inner + state].astype(bf16))
        wide = gate[at, :]
        d_mixed = d_gated[at, :].astype(f32) * (wide * sigmoid(wide))
        back = mm_rows((d_mixed * spread[rows:]).astype(bf16), act[:, inner + state :].astype(bf16))
        part = inner // SIDE
        for place, block in ((frame, local), (2 + frame, back)):
            block = block.astype(bf16).reshape(SIDE, part, state)
            payload[:, place * part : (place + 1) * part, :] = block
    packed = pack_totals(ends, heads, state)
    for to in range(SIDE):
        shifted = ones_where(iota((16, heads), 1) == iota((16, heads), 0) + to * (heads // SIDE))
        payload[to, inner:, :] = mm(shifted, packed).astype(bf16)


def pack_totals(ends, heads, state):
    chosen = iota((heads, heads), 0) == iota((heads, heads), 1)
    lanes = iota((heads, state), 1)
    packed = jnp.zeros((heads, state), f32)
    for frame in range(2):
        column = jnp.sum(jnp.where(chosen, ends[frame], 0.0), axis=1, keepdims=True)
        packed = pack_column(packed, column, lanes, frame)
    return packed.astype(bf16)


def pack_column(packed, column, lanes, frame):
    for nth, piece in enumerate(pieces_of(column, 3)):
        packed = jnp.where(lanes == 3 * frame + nth, piece.astype(f32), packed)
    return packed


def unpack_column(packed, frame):
    at = 3 * frame
    return (packed[:, at + 2 : at + 3] + packed[:, at + 1 : at + 2]) + packed[:, at : at + 1]


SCANS = ((0, False), (1, True), (0, True), (1, False))


def chain(got, totals, place, state, visit):
    frame, turned = SCANS[place]
    part = state.shape[0]
    size = part // SIDE
    order = range(SIDE - 1, -1, -1) if turned else range(SIDE)
    for at in order:
        visit(at, state)
        grown = jnp.exp(totals[at][frame])
        factors = [
            jnp.broadcast_to(grown[head : head + 1, :], (size, 1)) for head in range(part // size)
        ]
        state = jnp.concatenate(factors, axis=0) * state
        state = state + got[at, place * part : (place + 1) * part, :].astype(f32)
    return state


def tails_of(got, inner):
    found = []
    for at in range(SIDE):
        tail = got[at, inner:, :].astype(f32)
        found.append([unpack_column(tail, frame) for frame in range(2)])
    return found


def group_kernel(got, out):
    state = got.shape[2]
    inner = got.shape[1] - 16
    part = inner // SIDE
    totals = tails_of(got, inner)
    for place in range(4):
        block = chain(got, totals, place, jnp.zeros((part, state), f32), lambda at, value: None)
        out[:, 16 * place : 16 * place + 16, :] = block.reshape(16, 16, state).astype(bf16)
    lanes = iota((16, state), 1)
    packed = jnp.zeros((16, state), f32)
    for frame in range(2):
        column = jnp.maximum(totals[0][frame], -110.0)
        for at in range(1, SIDE):
            column = column + jnp.maximum(totals[at][frame], -110.0)
        packed = pack_column(packed, column, lanes, frame)
    chosen = ones_where(iota((16, 16), 1) == iota((16, 16), 0) // SIDE)
    packed = mm(chosen, packed.astype(bf16))
    out[:, 64:, :] = jnp.broadcast_to(packed.reshape(16, 1, state), (16, 8, state)).astype(bf16)


def spread_kernel(got, entering, out):
    state = got.shape[2]
    inner = got.shape[1] - 16
    part = inner // SIDE
    totals = tails_of(got, inner)
    for place in range(4):

        def visit(at, value, place=place):
            out[at, place * part : (place + 1) * part, :] = value.astype(bf16)

        block = entering[:, 16 * place : 16 * place + 16, :].astype(f32).reshape(part, state)
        chain(got, totals, place, block, visit)


def scan_kernel(got, out, wide, done):
    count, rows, state = got.shape
    wide[...] = got[...].astype(f32).reshape(count * rows, state)
    tails = wide[pl.ds(64, count, stride=rows), :]
    above = iota((count, count), 0)
    beside = iota((count, count), 1)
    after = ones_where(above > beside)
    weights = []
    for frame in range(2):
        column = jnp.maximum(unpack_column(tails, frame), -110.0)
        line = jnp.sum(jnp.where(above == beside, column, 0.0), axis=0, keepdims=True)
        between = None
        for piece in pieces_of(jnp.where(beside < above, line, 0.0), 3):
            part = mm(piece, after)
            between = part if between is None else between + part
        found = jnp.where(above > beside, jnp.exp(between), 0.0)
        weights.append(pieces_of(found, 2))
    for place, (frame, turned) in enumerate(SCANS):
        pair = weights[frame]
        block = jnp.concatenate(
            [wide[pl.ds(16 * place + row, count, stride=rows), :] for row in range(16)], axis=1
        ).astype(bf16)
        if turned:
            mixed = mm_rows(jnp.concatenate(pair, axis=1), block)
        else:
            mixed = mm(jnp.concatenate(pair, axis=0), block)
        mixed = mixed[:count] + mixed[count:]
        for row in range(16):
            done[pl.ds(16 * place + row, count, stride=64), :] = mixed[:, state * row : state * (row + 1)]
    out[...] = done[...].reshape(count, 64, state).astype(bf16)


def intra_kernel(conv, gate, d_gated, step, cumul, cumul_t, mixed, d_driven, d_bc, d_cumul):
    rows = conv.shape[0] // 2
    inner = gate.shape[1]
    heads = step.shape[1]
    state = (conv.shape[1] - inner) // 2
    mask = head_mask(heads, inner // heads)
    lower = triangle(rows, True)
    first = iota((rows, 2 * inner // heads), 1) < inner // heads
    wide_pair = 2 * inner // heads
    for frame in range(2):
        at = slice(frame * rows, (frame + 1) * rows)
        found = conv[at, :]
        act = found * sigmoid(found)
        bmat = act[:, inner : inner + state].astype(bf16)
        cmat = act[:, inner + state :].astype(bf16)
        driven = act[:, :inner] * expand(step[at, :], mask)
        wide = gate[at, :]
        d_mixed = d_gated[at, :].astype(f32) * (wide * sigmoid(wide))
        scores = mm_cols(cmat, bmat)
        upto, line = cumul[at, :], cumul_t[frame * heads : (frame + 1) * heads, :]
        d_scores = jnp.zeros((rows, rows), f32)
        sums = []
        for pair in range(heads // 2):
            lanes = slice(pair * wide_pair, (pair + 1) * wide_pair)
            decays = []
            for head in (2 * pair, 2 * pair + 1):
                differ = upto[:, head : head + 1] - line[head : head + 1, :]
                decays.append(jnp.exp(jnp.where(lower, differ, -1e30)))
            weights = [(decay * scores).astype(bf16) for decay in decays]
            drive, d_mix = driven[:, lanes], d_mixed[:, lanes]
            drive_bf, d_mix_bf = drive.astype(bf16), d_mix.astype(bf16)
            drive_two = jnp.concatenate(
                [jnp.where(first, drive, 0.0), jnp.where(first, 0.0, drive)], axis=0
            ).astype(bf16)
            d_mix_two = jnp.concatenate(
                [jnp.where(first, d_mix, 0.0), jnp.where(first, 0.0, d_mix)], axis=0
            ).astype(bf16)
            mix = mm(jnp.concatenate(weights, axis=1), drive_two)
            d_weights = mm_cols(d_mix_two, drive_bf)
            d_drive = mm_rows(jnp.concatenate(weights, axis=0), d_mix_two)
            d_scores = d_scores + decays[0] * d_weights[:rows] + decays[1] * d_weights[rows:]
            mixed[at, lanes] = mix
            d_driven[at, lanes] = d_drive
            sums.append(d_mix_bf.astype(f32) * mix - drive_bf.astype(f32) * d_drive)
        d_scores = d_scores.astype(bf16)
        d_bc[at, :state] = mm_rows(d_scores, cmat)
        d_bc[at, state:] = mm(d_scores, bmat)
        d_cumul[at, :] = fold(jnp.concatenate(sums, axis=1), mask)


def post_kernel(
    place, got, conv, gate, d_gated, raw, step, cumul, mixed, d_driven, d_bc, d_cumul, step_bias, decay_log, skip_gain,
    conv_w, cot, normal, normal_halo,
    gated, d_gate, d_xbc, d_first, d_second, d_step, *refs,
):
    by_x, by_y, ext, d_conv_out, whole, parted = refs[:4], refs[4:8], refs[8], refs[9], refs[10], refs[11]
    rows = conv.shape[0] // 2
    inner = gate.shape[1]
    heads = step.shape[1]
    state = (conv.shape[1] - inner) // 2
    mask = head_mask(heads, inner // heads)
    skip = expand(jnp.broadcast_to(skip_gain[...].reshape(1, -1), (8, heads)), mask)[:1]
    for frame in range(2):
        at = slice(frame * rows, (frame + 1) * rows)
        found = conv[at, :]
        share = sigmoid(found)
        act = found * share
        inputs = act[:, :inner]
        bmat = act[:, inner : inner + state].astype(bf16)
        cmat = act[:, inner + state :].astype(bf16)
        upto = cumul[at, :]
        end = upto[rows - 1 : rows, :]
        spread = expand(jnp.concatenate([step[at, :], jnp.exp(upto), jnp.exp(end - upto)], axis=0), mask)
        sizes, grown, left = spread[:rows], spread[rows : 2 * rows], spread[2 * rows :]
        part = inner // SIDE
        carried = got[:, frame * part : (frame + 1) * part, :].reshape(inner, state)
        reach = got[:, (2 + frame) * part : (3 + frame) * part, :].reshape(inner, state)
        inter = grown * mm_cols(cmat, carried)
        full = mixed[at, :] + inter + skip * inputs
        wide = gate[at, :]
        opened = sigmoid(wide)
        silu = wide * opened
        gated[at, :] = (full * silu).astype(bf16)
        d_out = d_gated[at, :].astype(f32)
        d_gate[at, :] = (d_out * full * (opened * (1.0 + wide * (1.0 - opened)))).astype(bf16)
        d_mixed = d_out * silu
        d_cmat = d_bc[at, state:] + mm((d_mixed * grown).astype(bf16), carried)
        answer = left * mm_cols(bmat, reach)
        driven = inputs * sizes
        d_drive = d_driven[at, :] + answer
        d_bmat = d_bc[at, :state] + mm((left * driven).astype(bf16), reach)
        products = carried.astype(f32) * reach.astype(f32)
        met = jnp.sum(products.reshape(heads, inner // heads, state), axis=1)
        met = jnp.sum(met, axis=1, keepdims=True)
        met = jnp.sum(jnp.where(iota((heads, heads), 0) == iota((heads, heads), 1), met, 0.0), axis=0, keepdims=True)
        folded = fold(jnp.concatenate([driven * answer, d_mixed * inter, d_drive * inputs], axis=0), mask)
        held, entered, by_size = folded[:rows], folded[rows : 2 * rows], folded[2 * rows :]
        d_end = jnp.exp(end) * met + jnp.sum(held, axis=0, keepdims=True)
        d_decay = tri_sum(triangle(rows, False), d_cumul[at, :] + entered - held) + d_end
        d_size = by_size - jnp.exp(decay_log[...].reshape(1, -1)) * d_decay
        d_step[at, :] = (d_size * sigmoid(raw[at, :] + step_bias[...].reshape(1, -1))).astype(bf16)
        d_act = jnp.concatenate([skip * d_mixed + d_drive * sizes, d_bmat, d_cmat], axis=1)
        margin = normal_halo.shape[0] // 2
        ext[:margin, :] = jnp.zeros((margin, ext.shape[1]), f32)
        ext[margin : margin + rows, :] = d_act * (share * (1.0 + found * (1.0 - share)))
        ext[margin + rows :, :] = jnp.zeros((8, ext.shape[1]), f32)
        taps = conv_w.shape[0]
        total = None
        for tap in range(taps):
            start = taps - 1 - tap
            part = ext[start : start + margin + rows, :] * conv_w[tap : tap + 1, :]
            total = part if total is None else total + part
        d_xbc[at, :] = total[margin:].astype(bf16)
        d_conv_out[frame * margin : (frame + 1) * margin, :] = total[:margin].astype(bf16)
        (d_first, d_second)[frame][...] = total[margin - 8 : margin]
    columns = cot.shape[1]
    half = d_xbc.shape[1] // 2
    out_term = mm_rows(gated[...], cot[...]).reshape(COUNT, 2, 8, columns)
    gate_term = mm_rows(normal[...], d_gate[...]).reshape(COUNT // SIDE, SIDE, 8, inner)
    in_term = mm_rows(normal[...], d_xbc[...]) + mm_rows(normal_halo[...], d_conv_out[...])
    whole[:, :columns] = out_term[:, 0].reshape(-1, columns)
    whole[:, columns : 2 * columns] = out_term[:, 1].reshape(-1, columns)
    whole[:, 2 * columns :] = in_term[:, :half]
    parted[:, :, :, :inner] = gate_term
    parted[:, :, :, inner:] = in_term[:, half:].reshape(COUNT // SIDE, SIDE, 8, half)
    ring_out(lambda step: chunk_x(place, whole, step), by_x)
    ring_out(lambda step: chunk_y(place, parted, step), by_y)


def chunk_x(place, whole, step):
    chunk = whole.shape[0] // SIDE
    to = lax.rem(place[0] + step, SIDE)
    return whole[pl.ds(pl.multiple_of(to * chunk, chunk), chunk), :].astype(bf16)


def chunk_y(place, parted, step):
    block = parted[:, lax.rem(place[2] + step, SIDE)]
    return block.reshape(-1, block.shape[-1]).astype(bf16)


def ring_out(chunk_of, slots):
    keep, base, right, left = slots
    half = keep.shape[0] // 2
    keep[...] = chunk_of(0)
    ahead, opposite, behind = chunk_of(1), chunk_of(2), chunk_of(3)
    base[:half, :], base[half:, :] = ahead[:half], behind[half:]
    right[:half, :], right[half:, :] = opposite[:half], ahead[half:]
    left[:half, :], left[half:, :] = behind[:half], opposite[half:]


def relay_kernel(base_x, right_x, left_x, base_y, right_y, left_y, to_low, to_high, *outs):
    for base, right, left, on_right, on_left in (
        (base_x, right_x, left_x, outs[0], outs[1]),
        (base_y, right_y, left_y, outs[2], outs[3]),
    ):
        half = base.shape[0] // 2
        columns = base.shape[1]
        on_right[:, :columns] = (base[:half, :].astype(f32) + right[:half, :].astype(f32)).astype(bf16)
        on_left[:, :columns] = (base[half:, :].astype(f32) + left[half:, :].astype(f32)).astype(bf16)
    for target, edge in ((outs[2], to_high), (outs[3], to_low)):
        target[:, columns:] = jnp.concatenate([edge[...], jnp.zeros(edge.shape, bf16)], axis=0)


def ring_total(keep, right, left, on_right, on_left):
    half = keep.shape[0] // 2
    columns = keep.shape[1]
    first = keep[:half, :].astype(f32) + left[:half, :].astype(f32) + on_right[:, :columns].astype(f32)
    second = keep[half:, :].astype(f32) + right[half:, :].astype(f32) + on_left[:, :columns].astype(f32)
    return jnp.concatenate([first, second], axis=0)


def send_x(place, whole, slots):
    chunk = whole.shape[0] // SIDE
    for step in range(SIDE):
        to = lax.rem(place[0] + step, SIDE)
        block = whole[pl.ds(pl.multiple_of(to * chunk, chunk), chunk), :]
        slots[step][...] = block.astype(slots[step].dtype)


def send_y(place, parted, slots):
    for step in range(SIDE):
        block = parted[:, lax.rem(place[2] + step, SIDE)]
        slots[step][...] = block.reshape(slots[step].shape).astype(slots[step].dtype)


def norm_back(block, d_normal, gain):
    wide = block.astype(f32)
    scale = lax.rsqrt(jnp.mean(wide * wide, axis=-1, keepdims=True) + epsilon)
    d_scaled = d_normal * gain.reshape(1, -1)
    along = jnp.mean(d_scaled * wide, axis=-1, keepdims=True)
    return scale * d_scaled - wide * (scale * scale * scale * along)


def fold_rows(block):
    return jnp.concatenate([block[:, 128 * nth : 128 * (nth + 1)] for nth in range(4)], axis=0)


def unfold_rows(block):
    return jnp.concatenate([block[8 * nth : 8 * (nth + 1)] for nth in range(4)], axis=1)


def scalar_flag(condition):
    return jnp.where(condition, 1.0, 0.0)


def result_kernel(
    place, both, gain, gated, out_proj, d_gate, d_xbc, d_first, d_second, low, high, d_step, in_proj, step_proj,
    layer, base, to_low, to_high, d_whole,
):
    rows = both.shape[0] // 2
    inner = out_proj.shape[0]
    branch = mm(gated[...], out_proj[...])
    layer[...] = (branch[:rows] + mirror_wide(branch[rows:])).astype(bf16)
    d_whole[: 2 * rows, :] = d_xbc[...]
    edges = jnp.concatenate([d_first[...], d_second[...]], axis=0)
    d_whole[2 * rows :, :] = edges.astype(bf16)
    through = mm_cols(d_whole[...], in_proj[:, inner:])
    d_normal = mm_cols(d_gate[...], in_proj[:, :inner]) + through[: 2 * rows]
    d_normal = d_normal + mm(d_step[...], step_proj[...])
    d_wide = norm_back(both[...], d_normal, gain[...])
    base[...] = d_wide[:rows] + mirror_wide(d_wide[rows:])
    first = norm_back(low[8:, :], through[2 * rows : 2 * rows + 8], gain[...])
    second = norm_back(mirror_exact(high[...])[8:, :], through[2 * rows + 8 :], gain[...])
    at_start = (place[0] + place[1] + place[2]) == 0
    at_end = (place[0] + place[1] + place[2]) == 3 * (SIDE - 1)
    to_low[...] = fold_rows(first * (1.0 - scalar_flag(at_start))).astype(bf16)
    to_high[...] = fold_rows(mirror_wide(second) * (1.0 - scalar_flag(at_end))).astype(bf16)


def total_of(refs):
    total = refs[0][...].astype(f32)
    for ref in refs[1:]:
        total = total + ref[...].astype(f32)
    return total


def first_sum_kernel(place, *refs):
    from_x, from_y, by_y, by_x, kept = refs[:5], refs[5:10], refs[10:14], refs[14:18], refs[18]
    parted, whole = refs[19], refs[20]
    parted[...] = ring_total(*from_x).reshape(parted.shape)
    whole[...] = ring_total(*from_y)
    send_y(place, parted, by_y)
    columns = whole.shape[1]
    chunk = whole.shape[0] // SIDE
    for step in range(SIDE):
        to = lax.rem(place[0] + step, SIDE)
        block = whole[pl.ds(pl.multiple_of(to * chunk, chunk), chunk), :]
        by_x[step][:, :columns] = block.astype(by_x[step].dtype)
    high = from_y[3][:32, columns:].astype(f32)
    low = from_y[4][:32, columns:].astype(f32)
    on_high = scalar_flag((place[2] == 0) & (place[1] == SIDE - 1))
    on_low = scalar_flag((place[2] == SIDE - 1) & (place[1] == 0))
    by_x[1][:, columns:] = (high * on_high).astype(bf16)
    by_x[3][:, columns:] = (low * on_low).astype(bf16)
    kept[:32, :] = high * (1.0 - on_high)
    kept[32:, :] = low * (1.0 - on_low)


def second_sum_kernel(place, *refs):
    first, second, kept, by_z = refs[:4], refs[4:8], refs[8], refs[9]
    columns = first[0].shape[1]
    high = kept[:32, :] + second[1][:, columns:].astype(f32)
    low = kept[32:, :] + second[3][:, columns:].astype(f32)
    first = total_of(first).reshape(SIDE, 8, -1)
    total = second[0][...]
    for step in range(1, SIDE):
        total = total + second[step][:, :columns].astype(f32)
    second = total.reshape(SIDE, 8, -1)
    above = scalar_flag(place[2] == 0)
    below = scalar_flag(place[2] == SIDE - 1)
    for to in range(SIDE):
        own = scalar_flag(place[1] == to)
        share_high = own * (1.0 - above) + scalar_flag(lax.rem(place[1] + 1, SIDE) == to) * above
        share_low = own * (1.0 - below) + scalar_flag(lax.rem(place[1] + SIDE - 1, SIDE) == to) * below
        edges = [high[:16] * share_high, high[16:] * share_high, low[:16] * share_low, low[16:] * share_low]
        by_z[to, :, :columns] = jnp.concatenate([first[to], second[to]], axis=0).astype(bf16)
        by_z[to, :, columns:] = jnp.concatenate(edges, axis=1).astype(bf16)


def last_sum_kernel(parts, base, grad_in, grad_out, grad):
    total = parts[0].astype(f32)
    for step in range(1, SIDE):
        total = total + parts[step].astype(f32)
    columns = grad_out.shape[1]
    joined = total.shape[1] - 512
    grad_out[:8, :] = total[:8, :columns]
    grad_out[8:, :] = total[:8, columns : 2 * columns]
    grad_in[...] = jnp.concatenate(
        [total[8:, : 2 * columns], total[:8, 2 * columns : joined], total[8:, 2 * columns : joined]], axis=1
    )
    edges = total[:, joined:]
    high = unfold_rows(jnp.concatenate([edges[:, :128], edges[:, 128:256]], axis=0))
    low = unfold_rows(jnp.concatenate([edges[:, 256:384], edges[:, 384:]], axis=0))
    rows = base.shape[0]
    whole = jnp.concatenate([base[:8, :] + high, base[8 : rows - 8, :], base[rows - 8 :, :] + low], axis=0)
    grad[...] = whole.astype(bf16)


def axis_pairs(stride, step):
    pairs = []
    for source in range(COUNT):
        digit = source // stride % SIDE
        pairs.append((source, source + ((digit + step) % SIDE - digit) * stride))
    return pairs


def exchange(parts, stride):
    return [parts[0]] + [lax.ppermute(parts[step], "seq", axis_pairs(stride, step)) for step in range(1, SIDE)]


def around(to_right, to_left, stride):
    return (
        lax.ppermute(to_right, "seq", axis_pairs(stride, 1)),
        lax.ppermute(to_left, "seq", axis_pairs(stride, SIDE - 1)),
    )


def transpose_over(parts, groups):
    return lax.all_to_all(parts, "seq", 0, 0, axis_index_groups=groups)


def slots(rows, columns, kind):
    return [((rows, columns), kind)] + [((rows, columns), bf16)] * (SIDE - 1)


def shards(
    sequence,
    upstream,
    norm_gain,
    in_proj,
    step_proj,
    conv_weight,
    conv_bias,
    step_bias,
    decay_log,
    skip_gain,
    out_proj,
):
    rows, width = sequence.shape
    inner = out_proj.shape[0]
    heads = step_bias.shape[0]
    state = inner // heads * 2
    channels = conv_weight.shape[1]
    both_rows = 2 * rows
    stride_x, stride_z, stride_y = SIDE * SIDE, SIDE, 1
    index = lax.axis_index("seq")
    place = jnp.stack([index // stride_x, index // stride_z % SIDE, index % SIDE]).astype(jnp.int32)
    aligned = [[base + SIDE * digit for digit in range(SIDE)] for base in range(COUNT) if base // SIDE % SIDE == 0]
    beside = [[SIDE * base + digit for digit in range(SIDE)] for base in range(COUNT // SIDE)]
    across = [[base + SIDE * digit for digit in range(COUNT // SIDE)] for base in range(SIDE)]
    upward = [(i, i + 1) for i in range(COUNT - 1)]
    downward = [(i + 1, i) for i in range(COUNT - 1)]
    low = lax.ppermute(sequence[rows - 16 :], "seq", upward)
    high = lax.ppermute(sequence[:16], "seq", downward)
    step_turned = step_proj.T
    payload, both, normal, normal_halo, cot, gate, conv, d_gated, raw, step, cumul, cumul_t = call(
        pre_kernel,
        [
            ((SIDE, inner + 16, state), bf16),
            ((both_rows, width), bf16),
            ((both_rows, width), bf16),
            ((32, width), bf16),
            ((both_rows, width), bf16),
            ((both_rows, inner), f32),
            ((both_rows, channels), f32),
            ((both_rows, inner), bf16),
            ((both_rows, heads), f32),
            ((both_rows, heads), f32),
            ((both_rows, heads), f32),
            ((2 * heads, rows), f32),
        ],
        (
            sequence, upstream, low, high, norm_gain, in_proj, step_turned,
            conv_weight, conv_bias, step_bias, decay_log, out_proj,
        ),
        [pltpu.VMEM((rows + 8, channels), f32)],
    )
    got = transpose_over(payload, beside)
    (summary,) = call(group_kernel, [((COUNT // SIDE, 72, state), bf16)], (got,), vmem=16 * 2**20)
    summaries = transpose_over(summary, across)
    mixed, d_driven, d_bc, d_cumul = call(
        intra_kernel,
        [
            ((both_rows, inner), f32),
            ((both_rows, inner), f32),
            ((both_rows, 2 * state), f32),
            ((both_rows, heads), f32),
        ],
        (conv, gate, d_gated, step, cumul, cumul_t),
        flops=8 * 10**9,
    )
    groups = COUNT // SIDE
    (scanned,) = call(
        scan_kernel,
        [((groups, 64, state), bf16)],
        (summaries,),
        [pltpu.VMEM((groups * 72, state), f32), pltpu.VMEM((groups * 64, state), f32)],
        vmem=16 * 2**20,
    )
    entering = transpose_over(scanned, across)
    (spread,) = call(spread_kernel, [((SIDE, inner, state), bf16)], (got, entering), vmem=16 * 2**20)
    states = transpose_over(spread, beside)
    eighth = 8 * COUNT // SIDE
    joined = inner + channels // 2
    gated, d_gate, d_xbc, d_first, d_second, d_step, *parts = call(
        post_kernel,
        [
            ((both_rows, inner), bf16),
            ((both_rows, inner), bf16),
            ((both_rows, channels), bf16),
            ((8, channels), f32),
            ((8, channels), f32),
            ((both_rows, heads), bf16),
        ]
        + slots(eighth, joined, bf16) * 2,
        (
            place, states, conv, gate, d_gated, raw, step, cumul, mixed, d_driven, d_bc, d_cumul,
            step_bias, decay_log, skip_gain, conv_weight, cot, normal, normal_halo,
        ),
        [
            pltpu.VMEM((rows + 24, channels), f32),
            pltpu.VMEM((32, channels), bf16),
            pltpu.VMEM((8 * COUNT, joined), f32),
            pltpu.VMEM((COUNT // SIDE, SIDE, 8, joined), f32),
        ],
        scalars=1,
    )
    layer_out, base, to_low, to_high = call(
        result_kernel,
        [((rows, width), bf16), ((rows, width), f32), ((32, 128), bf16), ((32, 128), bf16)],
        (
            place, both, norm_gain, gated, out_proj, d_gate, d_xbc, d_first, d_second, low, high, d_step,
            in_proj, step_turned,
        ),
        [pltpu.VMEM((both_rows + 16, channels), bf16)],
        scalars=1,
        flops=8 * 10**9,
    )
    keep_x, base_x, right_x, left_x, keep_y, base_y, right_y, left_y = parts
    right_x, left_x = around(right_x, left_x, stride_x)
    right_y, left_y = around(right_y, left_y, stride_y)
    relayed = call(
        relay_kernel,
        [((eighth // 2, joined), bf16)] * 2 + [((eighth // 2, joined + 128), bf16)] * 2,
        (base_x, right_x, left_x, base_y, right_y, left_y, to_low, to_high),
        vmem=16 * 2**20,
    )
    from_x = [keep_x, right_x, left_x, *around(relayed[0], relayed[1], stride_x)]
    from_y = [keep_y, right_y, left_y, *around(relayed[2], relayed[3], stride_y)]
    small = eighth // SIDE
    *parts, kept = call(
        first_sum_kernel,
        slots(small, joined, f32)
        + [((small, joined), f32), ((small, joined + 128), bf16), ((small, joined), bf16), ((small, joined + 128), bf16)]
        + [((64, 128), f32)],
        (place, *from_x, *from_y),
        [pltpu.VMEM((SIDE, SIDE, 8, joined), f32), pltpu.VMEM((eighth, joined), f32)],
        scalars=1,
        vmem=16 * 2**20,
    )
    first = exchange(parts[:4], stride_y)
    second = exchange(parts[4:], stride_x)
    (by_z,) = call(
        second_sum_kernel,
        [((SIDE, 16, joined + 512), bf16)],
        (place, *first, *second, kept),
        scalars=1,
        vmem=16 * 2**20,
    )
    last = transpose_over(by_z, aligned)
    grad_in_proj, grad_out_proj, grad_input = call(
        last_sum_kernel,
        [((8, inner + channels), f32), ((16, width), f32), ((rows, width), bf16)],
        (last, base),
        vmem=16 * 2**20,
    )
    return (layer_out, grad_input, grad_in_proj, grad_out_proj)


def solution(mesh):
    rows = P(("batch", "seq"), None)
    return jax.shard_map(
        shards,
        mesh=mesh,
        in_specs=(rows, rows) + (P(),) * 9,
        out_specs=(rows,) * 4,
        check_vma=False,
    )
```

```python
import functools

import jax
import jax.numpy as jnp
from jax import lax
from jax.experimental import pallas as pl
from jax.experimental.pallas import tpu as pltpu
from jax.sharding import PartitionSpec as P

epsilon = 1e-06
SIDE = 4
COUNT = SIDE**3
f32 = jnp.float32
bf16 = jnp.bfloat16
INTERPRET = False


def call(body, outs, args, scratch=(), scalars=0, unused=0, flops=10**9, vmem=58 * 2**20):
    after = len(args) - unused
    specs = [pl.BlockSpec(memory_space=pltpu.SMEM)] * scalars
    specs += [pl.BlockSpec(memory_space=pltpu.VMEM)] * (after - scalars)
    specs += [pl.BlockSpec(memory_space=pl.ANY)] * unused
    moved = sum(a.size * a.dtype.itemsize for a in args[:after])

    def used(*refs):
        body(*refs[:after], *refs[len(args) :])

    return pl.pallas_call(
        used,
        out_shape=[jax.ShapeDtypeStruct(shape, kind) for shape, kind in outs],
        in_specs=specs,
        out_specs=[pl.BlockSpec(memory_space=pltpu.VMEM)] * len(outs),
        scratch_shapes=list(scratch),
        compiler_params=pltpu.CompilerParams(vmem_limit_bytes=vmem),
        cost_estimate=pl.CostEstimate(flops=flops, bytes_accessed=moved, transcendentals=0),
        interpret=INTERPRET,
    )(*args)


def mm(left, right):
    return lax.dot_general(left, right, (((1,), (0,)), ((), ())), preferred_element_type=f32)


def mm_cols(left, right):
    return lax.dot_general(left, right, (((1,), (1,)), ((), ())), preferred_element_type=f32)


def mm_rows(left, right):
    return lax.dot_general(left, right, (((0,), (0,)), ((), ())), preferred_element_type=f32)


def iota(shape, dim):
    return lax.broadcasted_iota(jnp.int32, shape, dim)


def ones_where(mask):
    return jnp.where(mask, 1.0, 0.0).astype(bf16)


def anti(size):
    return ones_where(iota((size, size), 0) + iota((size, size), 1) == size - 1)


def pieces_of(value, count):
    found = []
    for _ in range(count):
        piece = value.astype(bf16)
        found.append(piece)
        value = value - piece.astype(f32)
    return found


def mirror_exact(block):
    turned = mm(block, anti(block.shape[1])).astype(bf16)
    return mm(anti(block.shape[0]), turned).astype(bf16)


def mirror_wide(block):
    high, low = pieces_of(block, 2)
    return mirror_exact(high).astype(f32) + mirror_exact(low).astype(f32)


def head_mask(heads, width):
    lanes = heads * width
    return ones_where(iota((heads, lanes), 0) == iota((heads, lanes), 1) // width)


def expand(value, mask):
    found = pieces_of(value, 3)
    return mm(jnp.concatenate(found, axis=1), jnp.concatenate([mask] * 3, axis=0))


def fold(value, mask):
    total = None
    for piece in pieces_of(value, 2):
        part = mm_cols(piece, mask)
        total = part if total is None else total + part
    return total


def triangle(size, low):
    rows, cols = iota((size, size), 0), iota((size, size), 1)
    return rows >= cols if low else rows <= cols


def tri_sum(mask, value):
    total = None
    for piece in pieces_of(value, 3):
        part = mm(ones_where(mask), piece)
        total = part if total is None else total + part
    return total


def tri_sum_turned(mask, value):
    total = None
    for piece in pieces_of(value, 3):
        part = mm_rows(piece, ones_where(mask))
        total = part if total is None else total + part
    return total


def softplus(value):
    return jnp.maximum(value, 0.0) + jnp.log1p(jnp.exp(-jnp.abs(value)))


def sigmoid(value):
    return 1.0 / (1.0 + jnp.exp(-value))


def norm_rows(block, gain):
    wide = block.astype(f32)
    scale = lax.rsqrt(jnp.mean(wide * wide, axis=-1, keepdims=True) + epsilon)
    return (wide * scale * gain.reshape(1, -1)).astype(bf16)


def project_kernel(
    seq, up, gain, in_proj, step_proj, step_bias, decay_log, out_proj,
    both, normal, xbc, gate, cot, d_gated, raw, step, cumul, cumul_t, weighted,
):
    rows = seq.shape[0]
    inner = out_proj.shape[0]
    heads = step_bias.shape[0]
    both[:rows, :] = seq[...]
    both[rows:, :] = mirror_exact(seq[...])
    normal[...] = norm_rows(both[...], gain[...])
    raw[...] = mm_cols(normal[...], step_proj[...])
    xbc[...] = mm(normal[...], in_proj[:, inner:]).astype(bf16)
    gate[...] = mm(normal[...], in_proj[:, :inner])
    cot[:rows, :] = up[...]
    cot[rows:, :] = mirror_exact(up[...])
    d_gated[...] = mm_cols(cot[...], out_proj[...]).astype(bf16)
    mask = head_mask(heads, inner // heads)
    for frame in range(2):
        at = slice(frame * rows, (frame + 1) * rows)
        size = softplus(raw[at, :] + step_bias[...].reshape(1, -1))
        decay = -jnp.exp(decay_log[...].reshape(1, -1)) * size
        upto = tri_sum(triangle(rows, True), decay)
        step[at, :] = size
        cumul[at, :] = upto
        cumul_t[frame * heads : (frame + 1) * heads, :] = tri_sum_turned(triangle(rows, False), decay)
        wide = gate[at, :]
        d_mixed = d_gated[at, :].astype(f32) * (wide * sigmoid(wide))
        weighted[at, :] = (d_mixed * expand(jnp.exp(upto), mask)).astype(bf16)


def local_kernel(
    low, high, xbc, in_proj, step, cumul, weighted, gain, conv_w, conv_b,
    payload, conv, normal_halo,
    ext,
):
    rows = xbc.shape[0] // 2
    inner = weighted.shape[1]
    heads = step.shape[1]
    state = (conv_w.shape[1] - inner) // 2
    taps = conv_w.shape[0]
    margin = low.shape[0]
    halo = jnp.concatenate([low[...], mirror_exact(high[...])], axis=0)
    normal_halo[...] = norm_rows(halo, gain[...])
    xbc_halo = mm(normal_halo[...], in_proj[:, inner:]).astype(bf16).astype(f32)
    mask = head_mask(heads, inner // heads)
    ends = []
    for frame in range(2):
        at = slice(frame * rows, (frame + 1) * rows)
        ext[:8, :] = xbc_halo[(frame + 1) * margin - 8 : (frame + 1) * margin, :]
        ext[8:, :] = xbc[at, :].astype(f32)
        found = conv_b[...].reshape(1, -1)
        for tap in range(taps):
            start = 9 - taps + tap
            found = found + ext[start : start + rows, :] * conv_w[tap : tap + 1, :]
        conv[at, :] = found
        act = found * sigmoid(found)
        upto = cumul[at, :]
        end = upto[rows - 1 : rows, :]
        ends.append(end)
        spread = expand(step[at, :] * jnp.exp(end - upto), mask)
        driven = (act[:, :inner] * spread).astype(bf16)
        local = mm_rows(driven, act[:, inner : inner + state].astype(bf16))
        back = mm_rows(weighted[at, :], act[:, inner + state :].astype(bf16))
        part = inner // SIDE
        for place, block in ((frame, local), (2 + frame, back)):
            block = block.astype(bf16).reshape(SIDE, part, state)
            payload[:, place * part : (place + 1) * part, :] = block
    packed = pack_totals(ends, heads, state)
    for to in range(SIDE):
        shifted = ones_where(iota((16, heads), 1) == iota((16, heads), 0) + to * (heads // SIDE))
        payload[to, inner:, :] = mm(shifted, packed).astype(bf16)


def pack_totals(ends, heads, state):
    chosen = iota((heads, heads), 0) == iota((heads, heads), 1)
    lanes = iota((heads, state), 1)
    packed = jnp.zeros((heads, state), f32)
    for frame in range(2):
        column = jnp.sum(jnp.where(chosen, ends[frame], 0.0), axis=1, keepdims=True)
        packed = pack_column(packed, column, lanes, frame)
    return packed.astype(bf16)


def pack_column(packed, column, lanes, frame):
    for nth, piece in enumerate(pieces_of(column, 3)):
        packed = jnp.where(lanes == 3 * frame + nth, piece.astype(f32), packed)
    return packed


def unpack_column(packed, frame):
    at = 3 * frame
    return (packed[:, at + 2 : at + 3] + packed[:, at + 1 : at + 2]) + packed[:, at : at + 1]


SCANS = ((0, False), (1, True), (0, True), (1, False))


def chain(got, totals, place, state, visit):
    frame, turned = SCANS[place]
    part = state.shape[0]
    size = part // SIDE
    order = range(SIDE - 1, -1, -1) if turned else range(SIDE)
    for at in order:
        visit(at, state)
        grown = jnp.exp(totals[at][frame])
        factors = [
            jnp.broadcast_to(grown[head : head + 1, :], (size, 1)) for head in range(part // size)
        ]
        state = jnp.concatenate(factors, axis=0) * state
        state = state + got[at, place * part : (place + 1) * part, :].astype(f32)
    return state


def tails_of(got, inner):
    found = []
    for at in range(SIDE):
        tail = got[at, inner:, :].astype(f32)
        found.append([unpack_column(tail, frame) for frame in range(2)])
    return found


def group_kernel(got, out):
    state = got.shape[2]
    inner = got.shape[1] - 16
    part = inner // SIDE
    totals = tails_of(got, inner)
    for place in range(4):
        block = chain(got, totals, place, jnp.zeros((part, state), f32), lambda at, value: None)
        out[:, 16 * place : 16 * place + 16, :] = block.reshape(16, 16, state).astype(bf16)
    lanes = iota((16, state), 1)
    packed = jnp.zeros((16, state), f32)
    for frame in range(2):
        column = jnp.maximum(totals[0][frame], -110.0)
        for at in range(1, SIDE):
            column = column + jnp.maximum(totals[at][frame], -110.0)
        packed = pack_column(packed, column, lanes, frame)
    chosen = ones_where(iota((16, 16), 1) == iota((16, 16), 0) // SIDE)
    packed = mm(chosen, packed.astype(bf16))
    out[:, 64:, :] = jnp.broadcast_to(packed.reshape(16, 1, state), (16, 8, state)).astype(bf16)


def spread_kernel(got, entering, out):
    state = got.shape[2]
    inner = got.shape[1] - 16
    part = inner // SIDE
    totals = tails_of(got, inner)
    for place in range(4):

        def visit(at, value, place=place):
            out[at, place * part : (place + 1) * part, :] = value.astype(bf16)

        block = entering[:, 16 * place : 16 * place + 16, :].astype(f32).reshape(part, state)
        chain(got, totals, place, block, visit)


def scan_kernel(got, out, wide, done):
    count, rows, state = got.shape
    wide[...] = got[...].astype(f32).reshape(count * rows, state)
    tails = wide[pl.ds(64, count, stride=rows), :]
    above = iota((count, count), 0)
    beside = iota((count, count), 1)
    after = ones_where(above > beside)
    weights = []
    for frame in range(2):
        column = jnp.maximum(unpack_column(tails, frame), -110.0)
        line = jnp.sum(jnp.where(above == beside, column, 0.0), axis=0, keepdims=True)
        between = None
        for piece in pieces_of(jnp.where(beside < above, line, 0.0), 3):
            part = mm(piece, after)
            between = part if between is None else between + part
        found = jnp.where(above > beside, jnp.exp(between), 0.0)
        weights.append(pieces_of(found, 2))
    for place, (frame, turned) in enumerate(SCANS):
        pair = weights[frame]
        block = jnp.concatenate(
            [wide[pl.ds(16 * place + row, count, stride=rows), :] for row in range(16)], axis=1
        ).astype(bf16)
        if turned:
            mixed = mm_rows(jnp.concatenate(pair, axis=1), block)
        else:
            mixed = mm(jnp.concatenate(pair, axis=0), block)
        mixed = mixed[:count] + mixed[count:]
        for row in range(16):
            done[pl.ds(16 * place + row, count, stride=64), :] = mixed[:, state * row : state * (row + 1)]
    out[...] = done[...].reshape(count, 64, state).astype(bf16)


def intra_kernel(conv, gate, d_gated, step, cumul, cumul_t, mixed, d_driven, d_bc, d_cumul):
    rows = conv.shape[0] // 2
    inner = gate.shape[1]
    heads = step.shape[1]
    state = (conv.shape[1] - inner) // 2
    mask = head_mask(heads, inner // heads)
    lower = triangle(rows, True)
    first = iota((rows, 2 * inner // heads), 1) < inner // heads
    wide_pair = 2 * inner // heads
    for frame in range(2):
        at = slice(frame * rows, (frame + 1) * rows)
        found = conv[at, :]
        act = found * sigmoid(found)
        bmat = act[:, inner : inner + state].astype(bf16)
        cmat = act[:, inner + state :].astype(bf16)
        driven = act[:, :inner] * expand(step[at, :], mask)
        wide = gate[at, :]
        d_mixed = d_gated[at, :].astype(f32) * (wide * sigmoid(wide))
        scores = mm_cols(cmat, bmat)
        upto, line = cumul[at, :], cumul_t[frame * heads : (frame + 1) * heads, :]
        d_scores = jnp.zeros((rows, rows), f32)
        sums = []
        for pair in range(heads // 2):
            lanes = slice(pair * wide_pair, (pair + 1) * wide_pair)
            decays = []
            for head in (2 * pair, 2 * pair + 1):
                differ = upto[:, head : head + 1] - line[head : head + 1, :]
                decays.append(jnp.exp(jnp.where(lower, differ, -1e30)))
            weights = [(decay * scores).astype(bf16) for decay in decays]
            drive, d_mix = driven[:, lanes], d_mixed[:, lanes]
            drive_bf, d_mix_bf = drive.astype(bf16), d_mix.astype(bf16)
            drive_two = jnp.concatenate(
                [jnp.where(first, drive, 0.0), jnp.where(first, 0.0, drive)], axis=0
            ).astype(bf16)
            d_mix_two = jnp.concatenate(
                [jnp.where(first, d_mix, 0.0), jnp.where(first, 0.0, d_mix)], axis=0
            ).astype(bf16)
            mix = mm(jnp.concatenate(weights, axis=1), drive_two)
            d_weights = mm_cols(d_mix_two, drive_bf)
            d_drive = mm_rows(jnp.concatenate(weights, axis=0), d_mix_two)
            d_scores = d_scores + decays[0] * d_weights[:rows] + decays[1] * d_weights[rows:]
            mixed[at, lanes] = mix
            d_driven[at, lanes] = d_drive
            sums.append(d_mix_bf.astype(f32) * mix - drive_bf.astype(f32) * d_drive)
        d_scores = d_scores.astype(bf16)
        d_bc[at, :state] = mm_rows(d_scores, cmat)
        d_bc[at, state:] = mm(d_scores, bmat)
        d_cumul[at, :] = fold(jnp.concatenate(sums, axis=1), mask)


def post_kernel(
    place, got, conv, gate, d_gated, raw, step, cumul, mixed, d_driven, d_bc, d_cumul, step_bias, decay_log, skip_gain,
    conv_w, cot, normal, normal_halo,
    gated, d_gate, d_xbc, d_first, d_second, d_step, *refs,
):
    by_x, by_y, ext, d_conv_out, whole, parted = refs[:4], refs[4:8], refs[8], refs[9], refs[10], refs[11]
    rows = conv.shape[0] // 2
    inner = gate.shape[1]
    heads = step.shape[1]
    state = (conv.shape[1] - inner) // 2
    mask = head_mask(heads, inner // heads)
    skip = expand(jnp.broadcast_to(skip_gain[...].reshape(1, -1), (8, heads)), mask)[:1]
    for frame in range(2):
        at = slice(frame * rows, (frame + 1) * rows)
        found = conv[at, :]
        share = sigmoid(found)
        act = found * share
        inputs = act[:, :inner]
        bmat = act[:, inner : inner + state].astype(bf16)
        cmat = act[:, inner + state :].astype(bf16)
        upto = cumul[at, :]
        end = upto[rows - 1 : rows, :]
        spread = expand(jnp.concatenate([step[at, :], jnp.exp(upto), jnp.exp(end - upto)], axis=0), mask)
        sizes, grown, left = spread[:rows], spread[rows : 2 * rows], spread[2 * rows :]
        part = inner // SIDE
        carried = got[:, frame * part : (frame + 1) * part, :].reshape(inner, state)
        reach = got[:, (2 + frame) * part : (3 + frame) * part, :].reshape(inner, state)
        inter = grown * mm_cols(cmat, carried)
        full = mixed[at, :] + inter + skip * inputs
        wide = gate[at, :]
        opened = sigmoid(wide)
        silu = wide * opened
        gated[at, :] = (full * silu).astype(bf16)
        d_out = d_gated[at, :].astype(f32)
        d_gate[at, :] = (d_out * full * (opened * (1.0 + wide * (1.0 - opened)))).astype(bf16)
        d_mixed = d_out * silu
        d_cmat = d_bc[at, state:] + mm((d_mixed * grown).astype(bf16), carried)
        answer = left * mm_cols(bmat, reach)
        driven = inputs * sizes
        d_drive = d_driven[at, :] + answer
        d_bmat = d_bc[at, :state] + mm((left * driven).astype(bf16), reach)
        products = carried.astype(f32) * reach.astype(f32)
        met = jnp.sum(products.reshape(heads, inner // heads, state), axis=1)
        met = jnp.sum(met, axis=1, keepdims=True)
        met = jnp.sum(jnp.where(iota((heads, heads), 0) == iota((heads, heads), 1), met, 0.0), axis=0, keepdims=True)
        folded = fold(jnp.concatenate([driven * answer, d_mixed * inter, d_drive * inputs], axis=0), mask)
        held, entered, by_size = folded[:rows], folded[rows : 2 * rows], folded[2 * rows :]
        d_end = jnp.exp(end) * met + jnp.sum(held, axis=0, keepdims=True)
        d_decay = tri_sum(triangle(rows, False), d_cumul[at, :] + entered - held) + d_end
        d_size = by_size - jnp.exp(decay_log[...].reshape(1, -1)) * d_decay
        d_step[at, :] = (d_size * sigmoid(raw[at, :] + step_bias[...].reshape(1, -1))).astype(bf16)
        d_act = jnp.concatenate([skip * d_mixed + d_drive * sizes, d_bmat, d_cmat], axis=1)
        margin = normal_halo.shape[0] // 2
        ext[:margin, :] = jnp.zeros((margin, ext.shape[1]), f32)
        ext[margin : margin + rows, :] = d_act * (share * (1.0 + found * (1.0 - share)))
        ext[margin + rows :, :] = jnp.zeros((8, ext.shape[1]), f32)
        taps = conv_w.shape[0]
        total = None
        for tap in range(taps):
            start = taps - 1 - tap
            part = ext[start : start + margin + rows, :] * conv_w[tap : tap + 1, :]
            total = part if total is None else total + part
        d_xbc[at, :] = total[margin:].astype(bf16)
        d_conv_out[frame * margin : (frame + 1) * margin, :] = total[:margin].astype(bf16)
        (d_first, d_second)[frame][...] = total[margin - 8 : margin]
    columns = cot.shape[1]
    half = d_xbc.shape[1] // 2
    out_term = mm_rows(gated[...], cot[...]).reshape(COUNT, 2, 8, columns)
    gate_term = mm_rows(normal[...], d_gate[...]).reshape(COUNT // SIDE, SIDE, 8, inner)
    in_term = mm_rows(normal[...], d_xbc[...]) + mm_rows(normal_halo[...], d_conv_out[...])
    whole[:, :columns] = out_term[:, 0].reshape(-1, columns)
    whole[:, columns : 2 * columns] = out_term[:, 1].reshape(-1, columns)
    whole[:, 2 * columns :] = in_term[:, :half]
    parted[:, :, :, :inner] = gate_term
    parted[:, :, :, inner:] = in_term[:, half:].reshape(COUNT // SIDE, SIDE, 8, half)
    ring_out(lambda step: chunk_x(place, whole, step), by_x)
    ring_out(lambda step: chunk_y(place, parted, step), by_y)


def chunk_x(place, whole, step):
    chunk = whole.shape[0] // SIDE
    to = lax.rem(place[0] + step, SIDE)
    return whole[pl.ds(pl.multiple_of(to * chunk, chunk), chunk), :].astype(bf16)


def chunk_y(place, parted, step):
    block = parted[:, lax.rem(place[2] + step, SIDE)]
    return block.reshape(-1, block.shape[-1]).astype(bf16)


def ring_out(chunk_of, slots):
    keep, base, right, left = slots
    half = keep.shape[0] // 2
    keep[...] = chunk_of(0)
    ahead, opposite, behind = chunk_of(1), chunk_of(2), chunk_of(3)
    base[:half, :], base[half:, :] = ahead[:half], behind[half:]
    right[:half, :], right[half:, :] = opposite[:half], ahead[half:]
    left[:half, :], left[half:, :] = behind[:half], opposite[half:]


def relay_kernel(base_x, right_x, left_x, base_y, right_y, left_y, to_both, *outs):
    for base, right, left, on_right, on_left in (
        (base_x, right_x, left_x, outs[0], outs[1]),
        (base_y, right_y, left_y, outs[2], outs[3]),
    ):
        half = base.shape[0] // 2
        columns = base.shape[1]
        on_right[:, :columns] = (base[:half, :].astype(f32) + right[:half, :].astype(f32)).astype(bf16)
        on_left[:, :columns] = (base[half:, :].astype(f32) + left[half:, :].astype(f32)).astype(bf16)
    outs[2][:32, columns:] = to_both[:32, :]
    outs[3][:32, columns:] = to_both[32:, :]
    for target in outs[2:]:
        target[32:, columns:] = jnp.zeros((32, 128), bf16)


def ring_total(keep, right, left, on_right, on_left):
    half = keep.shape[0] // 2
    columns = keep.shape[1]
    first = keep[:half, :].astype(f32) + left[:half, :].astype(f32) + on_right[:, :columns].astype(f32)
    second = keep[half:, :].astype(f32) + right[half:, :].astype(f32) + on_left[:, :columns].astype(f32)
    return jnp.concatenate([first, second], axis=0)


def send_x(place, whole, slots):
    chunk = whole.shape[0] // SIDE
    for step in range(SIDE):
        to = lax.rem(place[0] + step, SIDE)
        block = whole[pl.ds(pl.multiple_of(to * chunk, chunk), chunk), :]
        slots[step][...] = block.astype(slots[step].dtype)


def send_y(place, parted, slots):
    for step in range(SIDE):
        block = parted[:, lax.rem(place[2] + step, SIDE)]
        slots[step][...] = block.reshape(slots[step].shape).astype(slots[step].dtype)


def norm_back(block, d_normal, gain):
    wide = block.astype(f32)
    scale = lax.rsqrt(jnp.mean(wide * wide, axis=-1, keepdims=True) + epsilon)
    d_scaled = d_normal * gain.reshape(1, -1)
    along = jnp.mean(d_scaled * wide, axis=-1, keepdims=True)
    return scale * d_scaled - wide * (scale * scale * scale * along)


def fold_rows(block):
    return jnp.concatenate([block[:, 128 * nth : 128 * (nth + 1)] for nth in range(4)], axis=0)


def unfold_rows(block):
    return jnp.concatenate([block[8 * nth : 8 * (nth + 1)] for nth in range(4)], axis=1)


def scalar_flag(condition):
    return jnp.where(condition, 1.0, 0.0)


def result_kernel(
    place, both, gain, gated, out_proj, d_gate, d_xbc, d_first, d_second, low, high, d_step, in_proj, step_proj,
    layer, base, to_both, d_whole,
):
    rows = both.shape[0] // 2
    inner = out_proj.shape[0]
    branch = mm(gated[...], out_proj[...])
    layer[...] = (branch[:rows] + mirror_wide(branch[rows:])).astype(bf16)
    d_whole[: 2 * rows, :] = d_xbc[...]
    edges = jnp.concatenate([d_first[...], d_second[...]], axis=0)
    d_whole[2 * rows :, :] = edges.astype(bf16)
    through = mm_cols(d_whole[...], in_proj[:, inner:])
    d_normal = mm_cols(d_gate[...], in_proj[:, :inner]) + through[: 2 * rows]
    d_normal = d_normal + mm(d_step[...], step_proj[...])
    d_wide = norm_back(both[...], d_normal, gain[...])
    base[...] = d_wide[:rows] + mirror_wide(d_wide[rows:])
    first = norm_back(low[8:, :], through[2 * rows : 2 * rows + 8], gain[...])
    second = norm_back(mirror_exact(high[...])[8:, :], through[2 * rows + 8 :], gain[...])
    at_start = (place[0] + place[1] + place[2]) == 0
    at_end = (place[0] + place[1] + place[2]) == 3 * (SIDE - 1)
    to_both[32:, :] = fold_rows(first * (1.0 - scalar_flag(at_start))).astype(bf16)
    to_both[:32, :] = fold_rows(mirror_wide(second) * (1.0 - scalar_flag(at_end))).astype(bf16)


def total_of(refs):
    total = refs[0][...].astype(f32)
    for ref in refs[1:]:
        total = total + ref[...].astype(f32)
    return total


def first_sum_kernel(place, *refs):
    from_x, from_y, by_y, by_x, kept = refs[:5], refs[5:10], refs[10:14], refs[14:18], refs[18]
    parted, whole = refs[19], refs[20]
    parted[...] = ring_total(*from_x).reshape(parted.shape)
    whole[...] = ring_total(*from_y)
    send_y(place, parted, by_y)
    columns = whole.shape[1]
    chunk = whole.shape[0] // SIDE
    for step in range(SIDE):
        to = lax.rem(place[0] + step, SIDE)
        block = whole[pl.ds(pl.multiple_of(to * chunk, chunk), chunk), :]
        by_x[step][:, :columns] = block.astype(by_x[step].dtype)
    high = from_y[3][:32, columns:].astype(f32)
    low = from_y[4][:32, columns:].astype(f32)
    on_high = scalar_flag((place[2] == 0) & (place[1] == SIDE - 1))
    on_low = scalar_flag((place[2] == SIDE - 1) & (place[1] == 0))
    by_x[1][:, columns:] = (high * on_high).astype(bf16)
    by_x[3][:, columns:] = (low * on_low).astype(bf16)
    kept[:32, :] = high * (1.0 - on_high)
    kept[32:, :] = low * (1.0 - on_low)


def second_sum_kernel(place, *refs):
    first, second, kept, by_z = refs[:4], refs[4:8], refs[8], refs[9]
    columns = first[0].shape[1]
    high = kept[:32, :] + second[1][:, columns:].astype(f32)
    low = kept[32:, :] + second[3][:, columns:].astype(f32)
    first = total_of(first).reshape(SIDE, 8, -1)
    total = second[0][...]
    for step in range(1, SIDE):
        total = total + second[step][:, :columns].astype(f32)
    second = total.reshape(SIDE, 8, -1)
    above = scalar_flag(place[2] == 0)
    below = scalar_flag(place[2] == SIDE - 1)
    for to in range(SIDE):
        own = scalar_flag(place[1] == to)
        share_high = own * (1.0 - above) + scalar_flag(lax.rem(place[1] + 1, SIDE) == to) * above
        share_low = own * (1.0 - below) + scalar_flag(lax.rem(place[1] + SIDE - 1, SIDE) == to) * below
        edges = [high[:16] * share_high, high[16:] * share_high, low[:16] * share_low, low[16:] * share_low]
        by_z[to, :, :columns] = jnp.concatenate([first[to], second[to]], axis=0).astype(bf16)
        by_z[to, :, columns:] = jnp.concatenate(edges, axis=1).astype(bf16)


def last_sum_kernel(parts, base, grad_in, grad_out, grad):
    total = parts[0].astype(f32)
    for step in range(1, SIDE):
        total = total + parts[step].astype(f32)
    columns = grad_out.shape[1]
    joined = total.shape[1] - 512
    grad_out[:8, :] = total[:8, :columns]
    grad_out[8:, :] = total[:8, columns : 2 * columns]
    grad_in[...] = jnp.concatenate(
        [total[8:, : 2 * columns], total[:8, 2 * columns : joined], total[8:, 2 * columns : joined]], axis=1
    )
    edges = total[:, joined:]
    high = unfold_rows(jnp.concatenate([edges[:, :128], edges[:, 128:256]], axis=0))
    low = unfold_rows(jnp.concatenate([edges[:, 256:384], edges[:, 384:]], axis=0))
    rows = base.shape[0]
    whole = jnp.concatenate([base[:8, :] + high, base[8 : rows - 8, :], base[rows - 8 :, :] + low], axis=0)
    grad[...] = whole.astype(bf16)


def axis_pairs(stride, step):
    pairs = []
    for source in range(COUNT):
        digit = source // stride % SIDE
        pairs.append((source, source + ((digit + step) % SIDE - digit) * stride))
    return pairs


def exchange(parts, stride):
    return [parts[0]] + [lax.ppermute(parts[step], "seq", axis_pairs(stride, step)) for step in range(1, SIDE)]


def around(to_right, to_left, stride):
    return (
        lax.ppermute(to_right, "seq", axis_pairs(stride, 1)),
        lax.ppermute(to_left, "seq", axis_pairs(stride, SIDE - 1)),
    )


def transpose_over(parts, groups):
    return lax.all_to_all(parts, "seq", 0, 0, axis_index_groups=groups)


def slots(rows, columns, kind):
    return [((rows, columns), kind)] + [((rows, columns), bf16)] * (SIDE - 1)


def shards(
    sequence,
    upstream,
    norm_gain,
    in_proj,
    step_proj,
    conv_weight,
    conv_bias,
    step_bias,
    decay_log,
    skip_gain,
    out_proj,
):
    rows, width = sequence.shape
    inner = out_proj.shape[0]
    heads = step_bias.shape[0]
    state = inner // heads * 2
    channels = conv_weight.shape[1]
    both_rows = 2 * rows
    stride_x, stride_z, stride_y = SIDE * SIDE, SIDE, 1
    index = lax.axis_index("seq")
    place = jnp.stack([index // stride_x, index // stride_z % SIDE, index % SIDE]).astype(jnp.int32)
    aligned = [[base + SIDE * digit for digit in range(SIDE)] for base in range(COUNT) if base // SIDE % SIDE == 0]
    beside = [[SIDE * base + digit for digit in range(SIDE)] for base in range(COUNT // SIDE)]
    across = [[base + SIDE * digit for digit in range(COUNT // SIDE)] for base in range(SIDE)]
    upward = [(i, i + 1) for i in range(COUNT - 1)]
    downward = [(i + 1, i) for i in range(COUNT - 1)]
    low = lax.ppermute(sequence[rows - 16 :], "seq", upward)
    high = lax.ppermute(sequence[:16], "seq", downward)
    step_turned = step_proj.T
    both, normal, xbc, gate, cot, d_gated, raw, step, cumul, cumul_t, weighted = call(
        project_kernel,
        [
            ((both_rows, width), bf16),
            ((both_rows, width), bf16),
            ((both_rows, channels), bf16),
            ((both_rows, inner), f32),
            ((both_rows, width), bf16),
            ((both_rows, inner), bf16),
            ((both_rows, heads), f32),
            ((both_rows, heads), f32),
            ((both_rows, heads), f32),
            ((2 * heads, rows), f32),
            ((both_rows, inner), bf16),
        ],
        (sequence, upstream, norm_gain, in_proj, step_turned, step_bias, decay_log, out_proj),
        flops=4 * 10**9,
    )
    payload, conv, normal_halo = call(
        local_kernel,
        [
            ((SIDE, inner + 16, state), bf16),
            ((both_rows, channels), f32),
            ((32, width), bf16),
        ],
        (low, high, xbc, in_proj, step, cumul, weighted, norm_gain, conv_weight, conv_bias),
        [pltpu.VMEM((rows + 8, channels), f32)],
    )
    got = transpose_over(payload, beside)
    (summary,) = call(group_kernel, [((COUNT // SIDE, 72, state), bf16)], (got,), vmem=16 * 2**20)
    summaries = transpose_over(summary, across)
    mixed, d_driven, d_bc, d_cumul = call(
        intra_kernel,
        [
            ((both_rows, inner), f32),
            ((both_rows, inner), f32),
            ((both_rows, 2 * state), f32),
            ((both_rows, heads), f32),
        ],
        (conv, gate, d_gated, step, cumul, cumul_t),
        flops=8 * 10**9,
    )
    groups = COUNT // SIDE
    (scanned,) = call(
        scan_kernel,
        [((groups, 64, state), bf16)],
        (summaries,),
        [pltpu.VMEM((groups * 72, state), f32), pltpu.VMEM((groups * 64, state), f32)],
        vmem=16 * 2**20,
    )
    entering = transpose_over(scanned, across)
    (spread,) = call(spread_kernel, [((SIDE, inner, state), bf16)], (got, entering), vmem=16 * 2**20)
    states = transpose_over(spread, beside)
    eighth = 8 * COUNT // SIDE
    joined = inner + channels // 2
    gated, d_gate, d_xbc, d_first, d_second, d_step, *parts = call(
        post_kernel,
        [
            ((both_rows, inner), bf16),
            ((both_rows, inner), bf16),
            ((both_rows, channels), bf16),
            ((8, channels), f32),
            ((8, channels), f32),
            ((both_rows, heads), bf16),
        ]
        + slots(eighth, joined, bf16) * 2,
        (
            place, states, conv, gate, d_gated, raw, step, cumul, mixed, d_driven, d_bc, d_cumul,
            step_bias, decay_log, skip_gain, conv_weight, cot, normal, normal_halo,
        ),
        [
            pltpu.VMEM((rows + 24, channels), f32),
            pltpu.VMEM((32, channels), bf16),
            pltpu.VMEM((8 * COUNT, joined), f32),
            pltpu.VMEM((COUNT // SIDE, SIDE, 8, joined), f32),
        ],
        vmem=54 * 2**20,
        scalars=1,
    )
    layer_out, base, to_both = call(
        result_kernel,
        [((rows, width), bf16), ((rows, width), f32), ((64, 128), bf16)],
        (
            place, both, norm_gain, gated, out_proj, d_gate, d_xbc, d_first, d_second, low, high, d_step,
            in_proj, step_turned,
        ),
        [pltpu.VMEM((both_rows + 16, channels), bf16)],
        scalars=1,
        flops=8 * 10**9,
    )
    keep_x, base_x, right_x, left_x, keep_y, base_y, right_y, left_y = parts
    right_x, left_x = around(right_x, left_x, stride_x)
    right_y, left_y = around(right_y, left_y, stride_y)
    relayed = call(
        relay_kernel,
        [((eighth // 2, joined), bf16)] * 2 + [((eighth // 2, joined + 128), bf16)] * 2,
        (base_x, right_x, left_x, base_y, right_y, left_y, to_both),
        vmem=16 * 2**20,
    )
    from_x = [keep_x, right_x, left_x, *around(relayed[0], relayed[1], stride_x)]
    from_y = [keep_y, right_y, left_y, *around(relayed[2], relayed[3], stride_y)]
    small = eighth // SIDE
    *parts, kept = call(
        first_sum_kernel,
        slots(small, joined, f32)
        + [((small, joined), f32), ((small, joined + 128), bf16), ((small, joined), bf16), ((small, joined + 128), bf16)]
        + [((64, 128), f32)],
        (place, *from_x, *from_y),
        [pltpu.VMEM((SIDE, SIDE, 8, joined), f32), pltpu.VMEM((eighth, joined), f32)],
        scalars=1,
        vmem=16 * 2**20,
    )
    first = exchange(parts[:4], stride_y)
    second = exchange(parts[4:], stride_x)
    (by_z,) = call(
        second_sum_kernel,
        [((SIDE, 16, joined + 512), bf16)],
        (place, *first, *second, kept),
        scalars=1,
        vmem=16 * 2**20,
    )
    last = transpose_over(by_z, aligned)
    grad_in_proj, grad_out_proj, grad_input = call(
        last_sum_kernel,
        [((8, inner + channels), f32), ((16, width), f32), ((rows, width), bf16)],
        (last, base),
        vmem=16 * 2**20,
    )
    return (layer_out, grad_input, grad_in_proj, grad_out_proj)


def solution(mesh):
    rows = P(("batch", "seq"), None)
    return jax.shard_map(
        shards,
        mesh=mesh,
        in_specs=(rows, rows) + (P(),) * 9,
        out_specs=(rows,) * 4,
        check_vma=False,
    )
```

```python
import functools

import jax
import jax.numpy as jnp
from jax import lax
from jax.experimental import pallas as pl
from jax.experimental.pallas import tpu as pltpu
from jax.sharding import PartitionSpec as P

epsilon = 1e-06
SIDE = 4
COUNT = SIDE**3
f32 = jnp.float32
bf16 = jnp.bfloat16
INTERPRET = False


def call(body, outs, args, scratch=(), scalars=0, unused=0, flops=10**9, vmem=58 * 2**20):
    after = len(args) - unused
    specs = [pl.BlockSpec(memory_space=pltpu.SMEM)] * scalars
    specs += [pl.BlockSpec(memory_space=pltpu.VMEM)] * (after - scalars)
    specs += [pl.BlockSpec(memory_space=pl.ANY)] * unused
    moved = sum(a.size * a.dtype.itemsize for a in args[:after])

    def used(*refs):
        body(*refs[:after], *refs[len(args) :])

    return pl.pallas_call(
        used,
        out_shape=[jax.ShapeDtypeStruct(shape, kind) for shape, kind in outs],
        in_specs=specs,
        out_specs=[pl.BlockSpec(memory_space=pltpu.VMEM)] * len(outs),
        scratch_shapes=list(scratch),
        compiler_params=pltpu.CompilerParams(vmem_limit_bytes=vmem),
        cost_estimate=pl.CostEstimate(flops=flops, bytes_accessed=moved, transcendentals=0),
        interpret=INTERPRET,
    )(*args)


def mm(left, right):
    return lax.dot_general(left, right, (((1,), (0,)), ((), ())), preferred_element_type=f32)


def mm_cols(left, right):
    return lax.dot_general(left, right, (((1,), (1,)), ((), ())), preferred_element_type=f32)


def mm_rows(left, right):
    return lax.dot_general(left, right, (((0,), (0,)), ((), ())), preferred_element_type=f32)


def iota(shape, dim):
    return lax.broadcasted_iota(jnp.int32, shape, dim)


def ones_where(mask):
    return jnp.where(mask, 1.0, 0.0).astype(bf16)


def anti(size):
    return ones_where(iota((size, size), 0) + iota((size, size), 1) == size - 1)


def pieces_of(value, count):
    found = []
    for _ in range(count):
        piece = value.astype(bf16)
        found.append(piece)
        value = value - piece.astype(f32)
    return found


def mirror_exact(block):
    turned = mm(block, anti(block.shape[1])).astype(bf16)
    return mm(anti(block.shape[0]), turned).astype(bf16)


def mirror_wide(block):
    high, low = pieces_of(block, 2)
    return mirror_exact(high).astype(f32) + mirror_exact(low).astype(f32)


def head_mask(heads, width):
    lanes = heads * width
    return ones_where(iota((heads, lanes), 0) == iota((heads, lanes), 1) // width)


def expand(value, mask):
    found = pieces_of(value, 3)
    return mm(jnp.concatenate(found, axis=1), jnp.concatenate([mask] * 3, axis=0))


def fold(value, mask):
    total = None
    for piece in pieces_of(value, 2):
        part = mm_cols(piece, mask)
        total = part if total is None else total + part
    return total


def triangle(size, low):
    rows, cols = iota((size, size), 0), iota((size, size), 1)
    return rows >= cols if low else rows <= cols


def tri_sum(mask, value):
    total = None
    for piece in pieces_of(value, 3):
        part = mm(ones_where(mask), piece)
        total = part if total is None else total + part
    return total


def tri_sum_turned(mask, value):
    total = None
    for piece in pieces_of(value, 3):
        part = mm_rows(piece, ones_where(mask))
        total = part if total is None else total + part
    return total


def softplus(value):
    return jnp.maximum(value, 0.0) + jnp.log1p(jnp.exp(-jnp.abs(value)))


def sigmoid(value):
    return 1.0 / (1.0 + jnp.exp(-value))


def norm_rows(block, gain):
    wide = block.astype(f32)
    scale = lax.rsqrt(jnp.mean(wide * wide, axis=-1, keepdims=True) + epsilon)
    return (wide * scale * gain.reshape(1, -1)).astype(bf16)


def pre_kernel(
    seq, up, low, high, gain, in_proj, step_proj, conv_w, conv_b, step_bias, decay_log, out_proj,
    payload, both, normal, normal_halo, cot, gate, conv, d_gated, raw, step, cumul, cumul_t,
    ext,
):
    rows = seq.shape[0]
    inner = out_proj.shape[0]
    heads = step_bias.shape[0]
    state = (conv_w.shape[1] - inner) // 2
    taps = conv_w.shape[0]
    both[:rows, :] = seq[...]
    both[rows:, :] = mirror_exact(seq[...])
    cot[:rows, :] = up[...]
    cot[rows:, :] = mirror_exact(up[...])
    halo = jnp.concatenate([low[...], mirror_exact(high[...])], axis=0)
    normal[...] = norm_rows(both[...], gain[...])
    normal_halo[...] = norm_rows(halo, gain[...])
    gate[...] = mm(normal[...], in_proj[:, :inner]).astype(bf16)
    xbc = mm(normal[...], in_proj[:, inner:]).astype(bf16).astype(f32)
    xbc_halo = mm(normal_halo[...], in_proj[:, inner:]).astype(bf16).astype(f32)
    raw[...] = mm_cols(normal[...], step_proj[...])
    d_gated[...] = mm_cols(cot[...], out_proj[...]).astype(bf16)
    margin = low.shape[0]
    mask = head_mask(heads, inner // heads)
    ends = []
    for frame in range(2):
        at = slice(frame * rows, (frame + 1) * rows)
        ext[:8, :] = xbc_halo[(frame + 1) * margin - 8 : (frame + 1) * margin, :]
        ext[8:, :] = xbc[at, :]
        found = conv_b[...].reshape(1, -1)
        for tap in range(taps):
            start = 9 - taps + tap
            found = found + ext[start : start + rows, :] * conv_w[tap : tap + 1, :]
        conv[at, :] = found.astype(bf16)
        act = found * sigmoid(found)
        size = softplus(raw[at, :] + step_bias[...].reshape(1, -1))
        decay = -jnp.exp(decay_log[...].reshape(1, -1)) * size
        upto = tri_sum(triangle(rows, True), decay)
        step[at, :] = size
        cumul[at, :] = upto
        cumul_t[frame * heads : (frame + 1) * heads, :] = tri_sum_turned(triangle(rows, False), decay)
        end = upto[rows - 1 : rows, :]
        ends.append(end)
        spread = expand(jnp.concatenate([size * jnp.exp(end - upto), jnp.exp(upto)], axis=0), mask)
        driven = (act[:, :inner] * spread[:rows]).astype(bf16)
        local = mm_rows(driven, act[:, inner : inner + state].astype(bf16))
        wide = gate[at, :].astype(f32)
        d_mixed = d_gated[at, :].astype(f32) * (wide * sigmoid(wide))
        back = mm_rows((d_mixed * spread[rows:]).astype(bf16), act[:, inner + state :].astype(bf16))
        part = inner // SIDE
        for place, block in ((frame, local), (2 + frame, back)):
            block = block.astype(bf16).reshape(SIDE, part, state)
            payload[:, place * part : (place + 1) * part, :] = block
    packed = pack_totals(ends, heads, state)
    for to in range(SIDE):
        shifted = ones_where(iota((16, heads), 1) == iota((16, heads), 0) + to * (heads // SIDE))
        payload[to, inner:, :] = mm(shifted, packed).astype(bf16)


def pack_totals(ends, heads, state):
    chosen = iota((heads, heads), 0) == iota((heads, heads), 1)
    lanes = iota((heads, state), 1)
    packed = jnp.zeros((heads, state), f32)
    for frame in range(2):
        column = jnp.sum(jnp.where(chosen, ends[frame], 0.0), axis=1, keepdims=True)
        packed = pack_column(packed, column, lanes, frame)
    return packed.astype(bf16)


def pack_column(packed, column, lanes, frame):
    for nth, piece in enumerate(pieces_of(column, 3)):
        packed = jnp.where(lanes == 3 * frame + nth, piece.astype(f32), packed)
    return packed


def unpack_column(packed, frame):
    at = 3 * frame
    return (packed[:, at + 2 : at + 3] + packed[:, at + 1 : at + 2]) + packed[:, at : at + 1]


SCANS = ((0, False), (1, True), (0, True), (1, False))


def chain(got, totals, place, state, visit):
    frame, turned = SCANS[place]
    part = state.shape[0]
    size = part // SIDE
    order = range(SIDE - 1, -1, -1) if turned else range(SIDE)
    for at in order:
        visit(at, state)
        grown = jnp.exp(totals[at][frame])
        factors = [
            jnp.broadcast_to(grown[head : head + 1, :], (size, 1)) for head in range(part // size)
        ]
        state = jnp.concatenate(factors, axis=0) * state
        state = state + got[at, place * part : (place + 1) * part, :].astype(f32)
    return state


def tails_of(got, inner):
    found = []
    for at in range(SIDE):
        tail = got[at, inner:, :].astype(f32)
        found.append([unpack_column(tail, frame) for frame in range(2)])
    return found


def group_kernel(got, out):
    state = got.shape[2]
    inner = got.shape[1] - 16
    part = inner // SIDE
    totals = tails_of(got, inner)
    for place in range(4):
        block = chain(got, totals, place, jnp.zeros((part, state), f32), lambda at, value: None)
        out[:, 16 * place : 16 * place + 16, :] = block.reshape(16, 16, state).astype(bf16)
    lanes = iota((16, state), 1)
    packed = jnp.zeros((16, state), f32)
    for frame in range(2):
        column = jnp.maximum(totals[0][frame], -110.0)
        for at in range(1, SIDE):
            column = column + jnp.maximum(totals[at][frame], -110.0)
        packed = pack_column(packed, column, lanes, frame)
    chosen = ones_where(iota((16, 16), 1) == iota((16, 16), 0) // SIDE)
    packed = mm(chosen, packed.astype(bf16))
    out[:, 64:, :] = jnp.broadcast_to(packed.reshape(16, 1, state), (16, 8, state)).astype(bf16)


def spread_kernel(got, entering, out):
    state = got.shape[2]
    inner = got.shape[1] - 16
    part = inner // SIDE
    totals = tails_of(got, inner)
    for place in range(4):

        def visit(at, value, place=place):
            out[at, place * part : (place + 1) * part, :] = value.astype(bf16)

        block = entering[:, 16 * place : 16 * place + 16, :].astype(f32).reshape(part, state)
        chain(got, totals, place, block, visit)


def scan_kernel(got, out, wide, done):
    count, rows, state = got.shape
    wide[...] = got[...].astype(f32).reshape(count * rows, state)
    tails = wide[pl.ds(64, count, stride=rows), :]
    above = iota((count, count), 0)
    beside = iota((count, count), 1)
    after = ones_where(above > beside)
    weights = []
    for frame in range(2):
        column = jnp.maximum(unpack_column(tails, frame), -110.0)
        line = jnp.sum(jnp.where(above == beside, column, 0.0), axis=0, keepdims=True)
        between = None
        for piece in pieces_of(jnp.where(beside < above, line, 0.0), 3):
            part = mm(piece, after)
            between = part if between is None else between + part
        found = jnp.where(above > beside, jnp.exp(between), 0.0)
        weights.append(pieces_of(found, 2))
    for place, (frame, turned) in enumerate(SCANS):
        pair = weights[frame]
        block = jnp.concatenate(
            [wide[pl.ds(16 * place + row, count, stride=rows), :] for row in range(16)], axis=1
        ).astype(bf16)
        if turned:
            mixed = mm_rows(jnp.concatenate(pair, axis=1), block)
        else:
            mixed = mm(jnp.concatenate(pair, axis=0), block)
        mixed = mixed[:count] + mixed[count:]
        for row in range(16):
            done[pl.ds(16 * place + row, count, stride=64), :] = mixed[:, state * row : state * (row + 1)]
    out[...] = done[...].reshape(count, 64, state).astype(bf16)


def intra_kernel(conv, gate, d_gated, step, cumul, cumul_t, mixed, d_driven, d_bc, d_cumul):
    rows = conv.shape[0] // 2
    inner = gate.shape[1]
    heads = step.shape[1]
    state = (conv.shape[1] - inner) // 2
    mask = head_mask(heads, inner // heads)
    lower = triangle(rows, True)
    first = iota((rows, 2 * inner // heads), 1) < inner // heads
    wide_pair = 2 * inner // heads
    for frame in range(2):
        at = slice(frame * rows, (frame + 1) * rows)
        found = conv[at, :].astype(f32)
        act = found * sigmoid(found)
        bmat = act[:, inner : inner + state].astype(bf16)
        cmat = act[:, inner + state :].astype(bf16)
        driven = act[:, :inner] * expand(step[at, :], mask)
        wide = gate[at, :].astype(f32)
        d_mixed = d_gated[at, :].astype(f32) * (wide * sigmoid(wide))
        scores = mm_cols(cmat, bmat)
        upto, line = cumul[at, :], cumul_t[frame * heads : (frame + 1) * heads, :]
        d_scores = jnp.zeros((rows, rows), f32)
        sums = []
        for pair in range(heads // 2):
            lanes = slice(pair * wide_pair, (pair + 1) * wide_pair)
            decays = []
            for head in (2 * pair, 2 * pair + 1):
                differ = upto[:, head : head + 1] - line[head : head + 1, :]
                decays.append(jnp.exp(jnp.where(lower, differ, -1e30)))
            weights = [(decay * scores).astype(bf16) for decay in decays]
            drive, d_mix = driven[:, lanes], d_mixed[:, lanes]
            drive_bf, d_mix_bf = drive.astype(bf16), d_mix.astype(bf16)
            drive_two = jnp.concatenate(
                [jnp.where(first, drive, 0.0), jnp.where(first, 0.0, drive)], axis=0
            ).astype(bf16)
            d_mix_two = jnp.concatenate(
                [jnp.where(first, d_mix, 0.0), jnp.where(first, 0.0, d_mix)], axis=0
            ).astype(bf16)
            mix = mm(jnp.concatenate(weights, axis=1), drive_two)
            d_weights = mm_cols(d_mix_two, drive_bf)
            d_drive = mm_rows(jnp.concatenate(weights, axis=0), d_mix_two)
            d_scores = d_scores + decays[0] * d_weights[:rows] + decays[1] * d_weights[rows:]
            mixed[at, lanes] = mix.astype(bf16)
            d_driven[at, lanes] = d_drive.astype(bf16)
            sums.append(d_mix_bf.astype(f32) * mix - drive_bf.astype(f32) * d_drive)
        d_scores = d_scores.astype(bf16)
        d_bc[at, :state] = mm_rows(d_scores, cmat)
        d_bc[at, state:] = mm(d_scores, bmat)
        d_cumul[at, :] = fold(jnp.concatenate(sums, axis=1), mask)


def post_kernel(
    place, got, conv, gate, d_gated, raw, step, cumul, mixed, d_driven, d_bc, d_cumul, step_bias, decay_log, skip_gain,
    conv_w, cot, normal, normal_halo,
    gated, d_gate, d_xbc, d_first, d_second, d_step, *refs,
):
    by_x, by_y, ext, d_conv_out, whole, parted = refs[:4], refs[4:8], refs[8], refs[9], refs[10], refs[11]
    rows = conv.shape[0] // 2
    inner = gate.shape[1]
    heads = step.shape[1]
    state = (conv.shape[1] - inner) // 2
    mask = head_mask(heads, inner // heads)
    skip = expand(jnp.broadcast_to(skip_gain[...].reshape(1, -1), (8, heads)), mask)[:1]
    for frame in range(2):
        at = slice(frame * rows, (frame + 1) * rows)
        found = conv[at, :].astype(f32)
        share = sigmoid(found)
        act = found * share
        inputs = act[:, :inner]
        bmat = act[:, inner : inner + state].astype(bf16)
        cmat = act[:, inner + state :].astype(bf16)
        upto = cumul[at, :]
        end = upto[rows - 1 : rows, :]
        spread = expand(jnp.concatenate([step[at, :], jnp.exp(upto), jnp.exp(end - upto)], axis=0), mask)
        sizes, grown, left = spread[:rows], spread[rows : 2 * rows], spread[2 * rows :]
        part = inner // SIDE
        carried = got[:, frame * part : (frame + 1) * part, :].reshape(inner, state)
        reach = got[:, (2 + frame) * part : (3 + frame) * part, :].reshape(inner, state)
        inter = grown * mm_cols(cmat, carried)
        full = mixed[at, :].astype(f32) + inter + skip * inputs
        wide = gate[at, :].astype(f32)
        opened = sigmoid(wide)
        silu = wide * opened
        gated[at, :] = (full * silu).astype(bf16)
        d_out = d_gated[at, :].astype(f32)
        d_gate[at, :] = (d_out * full * (opened * (1.0 + wide * (1.0 - opened)))).astype(bf16)
        d_mixed = d_out * silu
        d_cmat = d_bc[at, state:] + mm((d_mixed * grown).astype(bf16), carried)
        answer = left * mm_cols(bmat, reach)
        driven = inputs * sizes
        d_drive = d_driven[at, :].astype(f32) + answer
        d_bmat = d_bc[at, :state] + mm((left * driven).astype(bf16), reach)
        products = carried.astype(f32) * reach.astype(f32)
        met = jnp.sum(products.reshape(heads, inner // heads, state), axis=1)
        met = jnp.sum(met, axis=1, keepdims=True)
        met = jnp.sum(jnp.where(iota((heads, heads), 0) == iota((heads, heads), 1), met, 0.0), axis=0, keepdims=True)
        folded = fold(jnp.concatenate([driven * answer, d_mixed * inter, d_drive * inputs], axis=0), mask)
        held, entered, by_size = folded[:rows], folded[rows : 2 * rows], folded[2 * rows :]
        d_end = jnp.exp(end) * met + jnp.sum(held, axis=0, keepdims=True)
        d_decay = tri_sum(triangle(rows, False), d_cumul[at, :] + entered - held) + d_end
        d_size = by_size - jnp.exp(decay_log[...].reshape(1, -1)) * d_decay
        d_step[at, :] = (d_size * sigmoid(raw[at, :] + step_bias[...].reshape(1, -1))).astype(bf16)
        d_act = jnp.concatenate([skip * d_mixed + d_drive * sizes, d_bmat, d_cmat], axis=1)
        margin = normal_halo.shape[0] // 2
        ext[:margin, :] = jnp.zeros((margin, ext.shape[1]), f32)
        ext[margin : margin + rows, :] = d_act * (share * (1.0 + found * (1.0 - share)))
        ext[margin + rows :, :] = jnp.zeros((8, ext.shape[1]), f32)
        taps = conv_w.shape[0]
        total = None
        for tap in range(taps):
            start = taps - 1 - tap
            part = ext[start : start + margin + rows, :] * conv_w[tap : tap + 1, :]
            total = part if total is None else total + part
        d_xbc[at, :] = total[margin:].astype(bf16)
        d_conv_out[frame * margin : (frame + 1) * margin, :] = total[:margin].astype(bf16)
        (d_first, d_second)[frame][...] = total[margin - 8 : margin]
    columns = cot.shape[1]
    half = d_xbc.shape[1] // 2
    out_term = mm_rows(gated[...], cot[...]).reshape(COUNT, 2, 8, columns)
    gate_term = mm_rows(normal[...], d_gate[...]).reshape(COUNT // SIDE, SIDE, 8, inner)
    in_term = mm_rows(normal[...], d_xbc[...]) + mm_rows(normal_halo[...], d_conv_out[...])
    whole[:, :columns] = out_term[:, 0].reshape(-1, columns)
    whole[:, columns : 2 * columns] = out_term[:, 1].reshape(-1, columns)
    whole[:, 2 * columns :] = in_term[:, :half]
    parted[:, :, :, :inner] = gate_term
    parted[:, :, :, inner:] = in_term[:, half:].reshape(COUNT // SIDE, SIDE, 8, half)
    ring_out(lambda step: chunk_x(place, whole, step), by_x)
    ring_out(lambda step: chunk_y(place, parted, step), by_y)


def chunk_x(place, whole, step):
    chunk = whole.shape[0] // SIDE
    to = lax.rem(place[0] + step, SIDE)
    return whole[pl.ds(pl.multiple_of(to * chunk, chunk), chunk), :].astype(bf16)


def chunk_y(place, parted, step):
    block = parted[:, lax.rem(place[2] + step, SIDE)]
    return block.reshape(-1, block.shape[-1]).astype(bf16)


def ring_out(chunk_of, slots):
    keep, base, right, left = slots
    half = keep.shape[0] // 2
    keep[...] = chunk_of(0)
    ahead, opposite, behind = chunk_of(1), chunk_of(2), chunk_of(3)
    base[:half, :], base[half:, :] = ahead[:half], behind[half:]
    right[:half, :], right[half:, :] = opposite[:half], ahead[half:]
    left[:half, :], left[half:, :] = behind[:half], opposite[half:]


def relay_kernel(base_x, right_x, left_x, base_y, right_y, left_y, to_both, *outs):
    for base, right, left, on_right, on_left in (
        (base_x, right_x, left_x, outs[0], outs[1]),
        (base_y, right_y, left_y, outs[2], outs[3]),
    ):
        half = base.shape[0] // 2
        columns = base.shape[1]
        on_right[:, :columns] = (base[:half, :].astype(f32) + right[:half, :].astype(f32)).astype(bf16)
        on_left[:, :columns] = (base[half:, :].astype(f32) + left[half:, :].astype(f32)).astype(bf16)
    outs[2][:32, columns:] = to_both[:32, :]
    outs[3][:32, columns:] = to_both[32:, :]
    for target in outs[2:]:
        target[32:, columns:] = jnp.zeros((32, 128), bf16)


def ring_total(keep, right, left, on_right, on_left):
    half = keep.shape[0] // 2
    columns = keep.shape[1]
    first = keep[:half, :].astype(f32) + left[:half, :].astype(f32) + on_right[:, :columns].astype(f32)
    second = keep[half:, :].astype(f32) + right[half:, :].astype(f32) + on_left[:, :columns].astype(f32)
    return jnp.concatenate([first, second], axis=0)


def send_x(place, whole, slots):
    chunk = whole.shape[0] // SIDE
    for step in range(SIDE):
        to = lax.rem(place[0] + step, SIDE)
        block = whole[pl.ds(pl.multiple_of(to * chunk, chunk), chunk), :]
        slots[step][...] = block.astype(slots[step].dtype)


def send_y(place, parted, slots):
    for step in range(SIDE):
        block = parted[:, lax.rem(place[2] + step, SIDE)]
        slots[step][...] = block.reshape(slots[step].shape).astype(slots[step].dtype)


def norm_back(block, d_normal, gain):
    wide = block.astype(f32)
    scale = lax.rsqrt(jnp.mean(wide * wide, axis=-1, keepdims=True) + epsilon)
    d_scaled = d_normal * gain.reshape(1, -1)
    along = jnp.mean(d_scaled * wide, axis=-1, keepdims=True)
    return scale * d_scaled - wide * (scale * scale * scale * along)


def fold_rows(block):
    return jnp.concatenate([block[:, 128 * nth : 128 * (nth + 1)] for nth in range(4)], axis=0)


def unfold_rows(block):
    return jnp.concatenate([block[8 * nth : 8 * (nth + 1)] for nth in range(4)], axis=1)


def scalar_flag(condition):
    return jnp.where(condition, 1.0, 0.0)


def result_kernel(
    place, both, gain, gated, out_proj, d_gate, d_xbc, d_first, d_second, low, high, d_step, in_proj, step_proj,
    layer, base, to_both, d_whole,
):
    rows = both.shape[0] // 2
    inner = out_proj.shape[0]
    branch = mm(gated[...], out_proj[...])
    layer[...] = (branch[:rows] + mirror_wide(branch[rows:])).astype(bf16)
    d_whole[: 2 * rows, :] = d_xbc[...]
    edges = jnp.concatenate([d_first[...], d_second[...]], axis=0)
    d_whole[2 * rows :, :] = edges.astype(bf16)
    through = mm_cols(d_whole[...], in_proj[:, inner:])
    d_normal = mm_cols(d_gate[...], in_proj[:, :inner]) + through[: 2 * rows]
    d_normal = d_normal + mm(d_step[...], step_proj[...])
    d_wide = norm_back(both[...], d_normal, gain[...])
    base[...] = d_wide[:rows] + mirror_wide(d_wide[rows:])
    first = norm_back(low[8:, :], through[2 * rows : 2 * rows + 8], gain[...])
    second = norm_back(mirror_exact(high[...])[8:, :], through[2 * rows + 8 :], gain[...])
    at_start = (place[0] + place[1] + place[2]) == 0
    at_end = (place[0] + place[1] + place[2]) == 3 * (SIDE - 1)
    to_both[32:, :] = fold_rows(first * (1.0 - scalar_flag(at_start))).astype(bf16)
    to_both[:32, :] = fold_rows(mirror_wide(second) * (1.0 - scalar_flag(at_end))).astype(bf16)


def total_of(refs):
    total = refs[0][...].astype(f32)
    for ref in refs[1:]:
        total = total + ref[...].astype(f32)
    return total


def first_sum_kernel(place, *refs):
    from_x, from_y, by_y, by_x, kept = refs[:5], refs[5:10], refs[10:14], refs[14:18], refs[18]
    parted, whole = refs[19], refs[20]
    parted[...] = ring_total(*from_x).reshape(parted.shape)
    whole[...] = ring_total(*from_y)
    send_y(place, parted, by_y)
    columns = whole.shape[1]
    chunk = whole.shape[0] // SIDE
    for step in range(SIDE):
        to = lax.rem(place[0] + step, SIDE)
        block = whole[pl.ds(pl.multiple_of(to * chunk, chunk), chunk), :]
        by_x[step][:, :columns] = block.astype(by_x[step].dtype)
    high = from_y[3][:32, columns:].astype(f32)
    low = from_y[4][:32, columns:].astype(f32)
    on_high = scalar_flag((place[2] == 0) & (place[1] == SIDE - 1))
    on_low = scalar_flag((place[2] == SIDE - 1) & (place[1] == 0))
    by_x[1][:, columns:] = (high * on_high).astype(bf16)
    by_x[3][:, columns:] = (low * on_low).astype(bf16)
    kept[:32, :] = high * (1.0 - on_high)
    kept[32:, :] = low * (1.0 - on_low)


def second_sum_kernel(place, *refs):
    first, second, kept, by_z, kept_on, keep = refs[:4], refs[4:8], refs[8], refs[9:13], refs[13], refs[14]
    columns = first[0].shape[1]
    high = kept[:32, :] + second[1][:, columns:].astype(f32)
    low = kept[32:, :] + second[3][:, columns:].astype(f32)
    first = total_of(first).reshape(SIDE, 8, -1)
    total = second[0][...]
    for step in range(1, SIDE):
        total = total + second[step][:, :columns].astype(f32)
    second = total.reshape(SIDE, 8, -1)
    above = scalar_flag(place[2] == 0)
    below = scalar_flag(place[2] == SIDE - 1)
    keep[:, 0] = first
    keep[:, 1] = second
    for step in range(SIDE):
        block = keep[lax.rem(place[1] + step, SIDE)].reshape(16, columns)
        by_z[step][:, :columns] = block.astype(by_z[step].dtype)
    for step, edge, share in ((1, high, above), (3, low, below)):
        edge = edge * share
        by_z[step][:, columns:] = jnp.concatenate([edge[:16], edge[16:]], axis=1).astype(bf16)
    kept_on[:32, :] = high * (1.0 - above)
    kept_on[32:, :] = low * (1.0 - below)


def last_sum_kernel(own, up, across, down, kept, base, grad_in, grad_out, grad):
    joined = own.shape[1]
    total = own[...] + up[:, :joined].astype(f32) + across[...].astype(f32) + down[:, :joined].astype(f32)
    columns = grad_out.shape[1]
    grad_out[:8, :] = total[:8, :columns]
    grad_out[8:, :] = total[:8, columns : 2 * columns]
    grad_in[...] = jnp.concatenate([total[8:, : 2 * columns], total[:8, 2 * columns :], total[8:, 2 * columns :]], axis=1)
    edges = []
    for nth, recv in enumerate((up, down)):
        recv = recv[:, joined:].astype(f32)
        recv = jnp.concatenate([recv[:, :128], recv[:, 128:]], axis=0)
        edges.append(unfold_rows(kept[32 * nth : 32 * nth + 32, :] + recv))
    rows = base.shape[0]
    whole = jnp.concatenate([base[:8, :] + edges[0], base[8 : rows - 8, :], base[rows - 8 :, :] + edges[1]], axis=0)
    grad[...] = whole.astype(bf16)


def axis_pairs(stride, step):
    pairs = []
    for source in range(COUNT):
        digit = source // stride % SIDE
        pairs.append((source, source + ((digit + step) % SIDE - digit) * stride))
    return pairs


def exchange(parts, stride):
    return [parts[0]] + [lax.ppermute(parts[step], "seq", axis_pairs(stride, step)) for step in range(1, SIDE)]


def around(to_right, to_left, stride):
    return (
        lax.ppermute(to_right, "seq", axis_pairs(stride, 1)),
        lax.ppermute(to_left, "seq", axis_pairs(stride, SIDE - 1)),
    )


def transpose_over(parts, groups):
    return lax.all_to_all(parts, "seq", 0, 0, axis_index_groups=groups)


def slots(rows, columns, kind):
    return [((rows, columns), kind)] + [((rows, columns), bf16)] * (SIDE - 1)


def shards(
    sequence,
    upstream,
    norm_gain,
    in_proj,
    step_proj,
    conv_weight,
    conv_bias,
    step_bias,
    decay_log,
    skip_gain,
    out_proj,
):
    rows, width = sequence.shape
    inner = out_proj.shape[0]
    heads = step_bias.shape[0]
    state = inner // heads * 2
    channels = conv_weight.shape[1]
    both_rows = 2 * rows
    stride_x, stride_z, stride_y = SIDE * SIDE, SIDE, 1
    index = lax.axis_index("seq")
    place = jnp.stack([index // stride_x, index // stride_z % SIDE, index % SIDE]).astype(jnp.int32)
    beside = [[SIDE * base + digit for digit in range(SIDE)] for base in range(COUNT // SIDE)]
    across = [[base + SIDE * digit for digit in range(COUNT // SIDE)] for base in range(SIDE)]
    upward = [(i, i + 1) for i in range(COUNT - 1)]
    downward = [(i + 1, i) for i in range(COUNT - 1)]
    low = lax.ppermute(sequence[rows - 16 :], "seq", upward)
    high = lax.ppermute(sequence[:16], "seq", downward)
    step_turned = step_proj.T
    payload, both, normal, normal_halo, cot, gate, conv, d_gated, raw, step, cumul, cumul_t = call(
        pre_kernel,
        [
            ((SIDE, inner + 16, state), bf16),
            ((both_rows, width), bf16),
            ((both_rows, width), bf16),
            ((32, width), bf16),
            ((both_rows, width), bf16),
            ((both_rows, inner), bf16),
            ((both_rows, channels), bf16),
            ((both_rows, inner), bf16),
            ((both_rows, heads), f32),
            ((both_rows, heads), f32),
            ((both_rows, heads), f32),
            ((2 * heads, rows), f32),
        ],
        (
            sequence, upstream, low, high, norm_gain, in_proj, step_turned,
            conv_weight, conv_bias, step_bias, decay_log, out_proj,
        ),
        [pltpu.VMEM((rows + 8, channels), f32)],
    )
    got = transpose_over(payload, beside)
    (summary,) = call(group_kernel, [((COUNT // SIDE, 72, state), bf16)], (got,), vmem=16 * 2**20)
    summaries = transpose_over(summary, across)
    mixed, d_driven, d_bc, d_cumul = call(
        intra_kernel,
        [
            ((both_rows, inner), bf16),
            ((both_rows, inner), bf16),
            ((both_rows, 2 * state), f32),
            ((both_rows, heads), f32),
        ],
        (conv, gate, d_gated, step, cumul, cumul_t),
        flops=8 * 10**9,
    )
    groups = COUNT // SIDE
    (scanned,) = call(
        scan_kernel,
        [((groups, 64, state), bf16)],
        (summaries,),
        [pltpu.VMEM((groups * 72, state), f32), pltpu.VMEM((groups * 64, state), f32)],
        vmem=16 * 2**20,
    )
    entering = transpose_over(scanned, across)
    (spread,) = call(spread_kernel, [((SIDE, inner, state), bf16)], (got, entering), vmem=16 * 2**20)
    states = transpose_over(spread, beside)
    eighth = 8 * COUNT // SIDE
    joined = inner + channels // 2
    gated, d_gate, d_xbc, d_first, d_second, d_step, *parts = call(
        post_kernel,
        [
            ((both_rows, inner), bf16),
            ((both_rows, inner), bf16),
            ((both_rows, channels), bf16),
            ((8, channels), f32),
            ((8, channels), f32),
            ((both_rows, heads), bf16),
        ]
        + slots(eighth, joined, bf16) * 2,
        (
            place, states, conv, gate, d_gated, raw, step, cumul, mixed, d_driven, d_bc, d_cumul,
            step_bias, decay_log, skip_gain, conv_weight, cot, normal, normal_halo,
        ),
        [
            pltpu.VMEM((rows + 24, channels), f32),
            pltpu.VMEM((32, channels), bf16),
            pltpu.VMEM((8 * COUNT, joined), f32),
            pltpu.VMEM((COUNT // SIDE, SIDE, 8, joined), f32),
        ],
        scalars=1,
    )
    layer_out, base, to_both = call(
        result_kernel,
        [((rows, width), bf16), ((rows, width), f32), ((64, 128), bf16)],
        (
            place, both, norm_gain, gated, out_proj, d_gate, d_xbc, d_first, d_second, low, high, d_step,
            in_proj, step_turned,
        ),
        [pltpu.VMEM((both_rows + 16, channels), bf16)],
        scalars=1,
        flops=8 * 10**9,
    )
    keep_x, base_x, right_x, left_x, keep_y, base_y, right_y, left_y = parts
    right_x, left_x = around(right_x, left_x, stride_x)
    right_y, left_y = around(right_y, left_y, stride_y)
    relayed = call(
        relay_kernel,
        [((eighth // 2, joined), bf16)] * 2 + [((eighth // 2, joined + 128), bf16)] * 2,
        (base_x, right_x, left_x, base_y, right_y, left_y, to_both),
        vmem=16 * 2**20,
    )
    from_x = [keep_x, right_x, left_x, *around(relayed[0], relayed[1], stride_x)]
    from_y = [keep_y, right_y, left_y, *around(relayed[2], relayed[3], stride_y)]
    small = eighth // SIDE
    *parts, kept = call(
        first_sum_kernel,
        slots(small, joined, f32)
        + [((small, joined), f32), ((small, joined + 128), bf16), ((small, joined), bf16), ((small, joined + 128), bf16)]
        + [((64, 128), f32)],
        (place, *from_x, *from_y),
        [pltpu.VMEM((SIDE, SIDE, 8, joined), f32), pltpu.VMEM((eighth, joined), f32)],
        scalars=1,
        vmem=16 * 2**20,
    )
    first = exchange(parts[:4], stride_y)
    second = exchange(parts[4:], stride_x)
    *parts, kept = call(
        second_sum_kernel,
        [((16, joined), f32), ((16, joined + 256), bf16), ((16, joined), bf16), ((16, joined + 256), bf16)]
        + [((64, 128), f32)],
        (place, *first, *second, kept),
        [pltpu.VMEM((SIDE, 2, 8, joined), f32)],
        scalars=1,
        vmem=16 * 2**20,
    )
    last = exchange(parts, stride_z)
    grad_in_proj, grad_out_proj, grad_input = call(
        last_sum_kernel,
        [((8, inner + channels), f32), ((16, width), f32), ((rows, width), bf16)],
        (*last, kept, base),
        vmem=16 * 2**20,
    )
    return (layer_out, grad_input, grad_in_proj, grad_out_proj)


def solution(mesh):
    rows = P(("batch", "seq"), None)
    return jax.shard_map(
        shards,
        mesh=mesh,
        in_specs=(rows, rows) + (P(),) * 9,
        out_specs=(rows,) * 4,
        check_vma=False,
    )
```

```python
import functools

import jax
import jax.numpy as jnp
from jax import lax
from jax.experimental import pallas as pl
from jax.experimental.pallas import tpu as pltpu
from jax.sharding import PartitionSpec as P

epsilon = 1e-06
SIDE = 4
COUNT = SIDE**3
f32 = jnp.float32
bf16 = jnp.bfloat16
INTERPRET = False


def call(body, outs, args, scratch=(), scalars=0, unused=0, flops=10**9, vmem=58 * 2**20):
    after = len(args) - unused
    specs = [pl.BlockSpec(memory_space=pltpu.SMEM)] * scalars
    specs += [pl.BlockSpec(memory_space=pltpu.VMEM)] * (after - scalars)
    specs += [pl.BlockSpec(memory_space=pl.ANY)] * unused
    moved = sum(a.size * a.dtype.itemsize for a in args[:after])

    def used(*refs):
        body(*refs[:after], *refs[len(args) :])

    return pl.pallas_call(
        used,
        out_shape=[jax.ShapeDtypeStruct(shape, kind) for shape, kind in outs],
        in_specs=specs,
        out_specs=[pl.BlockSpec(memory_space=pltpu.VMEM)] * len(outs),
        scratch_shapes=list(scratch),
        compiler_params=pltpu.CompilerParams(vmem_limit_bytes=vmem),
        cost_estimate=pl.CostEstimate(flops=flops, bytes_accessed=moved, transcendentals=0),
        interpret=INTERPRET,
    )(*args)


def mm(left, right):
    return lax.dot_general(left, right, (((1,), (0,)), ((), ())), preferred_element_type=f32)


def mm_cols(left, right):
    return lax.dot_general(left, right, (((1,), (1,)), ((), ())), preferred_element_type=f32)


def mm_rows(left, right):
    return lax.dot_general(left, right, (((0,), (0,)), ((), ())), preferred_element_type=f32)


def iota(shape, dim):
    return lax.broadcasted_iota(jnp.int32, shape, dim)


def ones_where(mask):
    return jnp.where(mask, 1.0, 0.0).astype(bf16)


def anti(size):
    return ones_where(iota((size, size), 0) + iota((size, size), 1) == size - 1)


def pieces_of(value, count):
    found = []
    for _ in range(count):
        piece = value.astype(bf16)
        found.append(piece)
        value = value - piece.astype(f32)
    return found


def mirror_exact(block):
    turned = mm(block, anti(block.shape[1])).astype(bf16)
    return mm(anti(block.shape[0]), turned).astype(bf16)


def mirror_wide(block):
    high, low = pieces_of(block, 2)
    return mirror_exact(high).astype(f32) + mirror_exact(low).astype(f32)


def head_mask(heads, width):
    lanes = heads * width
    return ones_where(iota((heads, lanes), 0) == iota((heads, lanes), 1) // width)


def expand(value, mask):
    found = pieces_of(value, 3)
    return mm(jnp.concatenate(found, axis=1), jnp.concatenate([mask] * 3, axis=0))


def fold(value, mask, count=2):
    total = None
    for piece in pieces_of(value, count):
        part = mm_cols(piece, mask)
        total = part if total is None else total + part
    return total


def triangle(size, low):
    rows, cols = iota((size, size), 0), iota((size, size), 1)
    return rows >= cols if low else rows <= cols


def tri_sum(mask, value):
    total = None
    for piece in pieces_of(value, 3):
        part = mm(ones_where(mask), piece)
        total = part if total is None else total + part
    return total


def tri_sum_turned(mask, value):
    total = None
    for piece in pieces_of(value, 3):
        part = mm_rows(piece, ones_where(mask))
        total = part if total is None else total + part
    return total


def softplus(value):
    return jnp.maximum(value, 0.0) + jnp.log1p(jnp.exp(-jnp.abs(value)))


def sigmoid(value):
    return 1.0 / (1.0 + jnp.exp(-value))


def norm_rows(block, gain):
    wide = block.astype(f32)
    scale = lax.rsqrt(jnp.mean(wide * wide, axis=-1, keepdims=True) + epsilon)
    return (wide * scale * gain.reshape(1, -1)).astype(bf16)


def pre_kernel(
    seq, up, low, high, gain, in_proj, step_proj, conv_w, conv_b, step_bias, decay_log, out_proj,
    payload, both, normal, normal_halo, cot, gate, conv, d_gated, raw, step, cumul, cumul_t,
    ext,
):
    rows = seq.shape[0]
    inner = out_proj.shape[0]
    heads = step_bias.shape[0]
    state = (conv_w.shape[1] - inner) // 2
    taps = conv_w.shape[0]
    both[:rows, :] = seq[...]
    both[rows:, :] = mirror_exact(seq[...])
    cot[:rows, :] = up[...]
    cot[rows:, :] = mirror_exact(up[...])
    halo = jnp.concatenate([low[...], mirror_exact(high[...])], axis=0)
    normal[...] = norm_rows(both[...], gain[...])
    normal_halo[...] = norm_rows(halo, gain[...])
    gate[...] = mm(normal[...], in_proj[:, :inner]).astype(bf16)
    xbc = mm(normal[...], in_proj[:, inner:]).astype(bf16).astype(f32)
    xbc_halo = mm(normal_halo[...], in_proj[:, inner:]).astype(bf16).astype(f32)
    raw[...] = mm_cols(normal[...], step_proj[...])
    d_gated[...] = mm_cols(cot[...], out_proj[...]).astype(bf16)
    margin = low.shape[0]
    mask = head_mask(heads, inner // heads)
    ends = []
    for frame in range(2):
        at = slice(frame * rows, (frame + 1) * rows)
        ext[:8, :] = xbc_halo[(frame + 1) * margin - 8 : (frame + 1) * margin, :]
        ext[8:, :] = xbc[at, :]
        found = conv_b[...].reshape(1, -1)
        for tap in range(taps):
            start = 9 - taps + tap
            found = found + ext[start : start + rows, :] * conv_w[tap : tap + 1, :]
        conv[at, :] = found.astype(bf16)
        act = found * sigmoid(found)
        size = softplus(raw[at, :] + step_bias[...].reshape(1, -1))
        decay = -jnp.exp(decay_log[...].reshape(1, -1)) * size
        upto = tri_sum(triangle(rows, True), decay)
        step[at, :] = size
        cumul[at, :] = upto
        cumul_t[frame * heads : (frame + 1) * heads, :] = tri_sum_turned(triangle(rows, False), decay)
        end = upto[rows - 1 : rows, :]
        ends.append(end)
        spread = expand(jnp.concatenate([size * jnp.exp(end - upto), jnp.exp(upto)], axis=0), mask)
        driven = (act[:, :inner] * spread[:rows]).astype(bf16)
        local = mm_rows(driven, act[:, inner : inner + state].astype(bf16))
        wide = gate[at, :].astype(f32)
        d_mixed = d_gated[at, :].astype(f32) * (wide * sigmoid(wide))
        back = mm_rows((d_mixed * spread[rows:]).astype(bf16), act[:, inner + state :].astype(bf16))
        part = inner // SIDE
        for place, block in ((frame, local), (2 + frame, back)):
            block = block.astype(bf16).reshape(SIDE, part, state)
            payload[:, place * part : (place + 1) * part, :] = block
    packed = pack_totals(ends, heads, state)
    for to in range(SIDE):
        shifted = ones_where(iota((16, heads), 1) == iota((16, heads), 0) + to * (heads // SIDE))
        payload[to, inner:, :] = mm(shifted, packed).astype(bf16)


def pack_totals(ends, heads, state):
    chosen = iota((heads, heads), 0) == iota((heads, heads), 1)
    lanes = iota((heads, state), 1)
    packed = jnp.zeros((heads, state), f32)
    for frame in range(2):
        column = jnp.sum(jnp.where(chosen, ends[frame], 0.0), axis=1, keepdims=True)
        packed = pack_column(packed, column, lanes, frame)
    return packed.astype(bf16)


def pack_column(packed, column, lanes, frame):
    for nth, piece in enumerate(pieces_of(column, 3)):
        packed = jnp.where(lanes == 3 * frame + nth, piece.astype(f32), packed)
    return packed


def unpack_column(packed, frame):
    at = 3 * frame
    return (packed[:, at + 2 : at + 3] + packed[:, at + 1 : at + 2]) + packed[:, at : at + 1]


SCANS = ((0, False), (1, True), (0, True), (1, False))


def chain(got, totals, place, state, visit):
    frame, turned = SCANS[place]
    part = state.shape[0]
    size = part // SIDE
    order = range(SIDE - 1, -1, -1) if turned else range(SIDE)
    for at in order:
        visit(at, state)
        grown = jnp.exp(totals[at][frame])
        factors = [
            jnp.broadcast_to(grown[head : head + 1, :], (size, 1)) for head in range(part // size)
        ]
        state = jnp.concatenate(factors, axis=0) * state
        state = state + got[at, place * part : (place + 1) * part, :].astype(f32)
    return state


def tails_of(got, inner):
    found = []
    for at in range(SIDE):
        tail = got[at, inner:, :].astype(f32)
        found.append([unpack_column(tail, frame) for frame in range(2)])
    return found


def group_kernel(got, out):
    state = got.shape[2]
    inner = got.shape[1] - 16
    part = inner // SIDE
    totals = tails_of(got, inner)
    for place in range(4):
        block = chain(got, totals, place, jnp.zeros((part, state), f32), lambda at, value: None)
        out[:, 16 * place : 16 * place + 16, :] = block.reshape(16, 16, state).astype(bf16)
    lanes = iota((16, state), 1)
    packed = jnp.zeros((16, state), f32)
    for frame in range(2):
        column = jnp.maximum(totals[0][frame], -110.0)
        for at in range(1, SIDE):
            column = column + jnp.maximum(totals[at][frame], -110.0)
        packed = pack_column(packed, column, lanes, frame)
    chosen = ones_where(iota((16, 16), 1) == iota((16, 16), 0) // SIDE)
    packed = mm(chosen, packed.astype(bf16))
    out[:, 64:, :] = jnp.broadcast_to(packed.reshape(16, 1, state), (16, 8, state)).astype(bf16)


def spread_kernel(got, entering, out):
    state = got.shape[2]
    inner = got.shape[1] - 16
    part = inner // SIDE
    totals = tails_of(got, inner)
    for place in range(4):

        def visit(at, value, place=place):
            out[at, place * part : (place + 1) * part, :] = value.astype(bf16)

        block = entering[:, 16 * place : 16 * place + 16, :].astype(f32).reshape(part, state)
        chain(got, totals, place, block, visit)


def scan_kernel(got, out, wide, done):
    count, rows, state = got.shape
    wide[...] = got[...].astype(f32).reshape(count * rows, state)
    tails = wide[pl.ds(64, count, stride=rows), :]
    above = iota((count, count), 0)
    beside = iota((count, count), 1)
    after = ones_where(above > beside)
    weights = []
    for frame in range(2):
        column = jnp.maximum(unpack_column(tails, frame), -110.0)
        line = jnp.sum(jnp.where(above == beside, column, 0.0), axis=0, keepdims=True)
        between = None
        for piece in pieces_of(jnp.where(beside < above, line, 0.0), 3):
            part = mm(piece, after)
            between = part if between is None else between + part
        found = jnp.where(above > beside, jnp.exp(between), 0.0)
        weights.append(pieces_of(found, 2))
    for place, (frame, turned) in enumerate(SCANS):
        pair = weights[frame]
        block = jnp.concatenate(
            [wide[pl.ds(16 * place + row, count, stride=rows), :] for row in range(16)], axis=1
        ).astype(bf16)
        if turned:
            mixed = mm_rows(jnp.concatenate(pair, axis=1), block)
        else:
            mixed = mm(jnp.concatenate(pair, axis=0), block)
        mixed = mixed[:count] + mixed[count:]
        for row in range(16):
            done[pl.ds(16 * place + row, count, stride=64), :] = mixed[:, state * row : state * (row + 1)]
    out[...] = done[...].reshape(count, 64, state).astype(bf16)


def intra_kernel(
    conv, gate, d_gated, step, cumul, cumul_t, normal, normal_halo,
    mixed, d_driven, d_bc, d_cumul, normal_t, halo_t,
):
    for source, target in ((normal, normal_t), (normal_halo, halo_t)):
        count = source.shape[0]
        same = iota((count, count), 0) == iota((count, count), 1)
        target[...] = mm_rows(source[...], ones_where(same)).astype(bf16)
    rows = conv.shape[0] // 2
    inner = gate.shape[1]
    heads = step.shape[1]
    state = (conv.shape[1] - inner) // 2
    mask = head_mask(heads, inner // heads)
    lower = triangle(rows, True)
    first = iota((rows, 2 * inner // heads), 1) < inner // heads
    wide_pair = 2 * inner // heads
    for frame in range(2):
        at = slice(frame * rows, (frame + 1) * rows)
        found = conv[at, :].astype(f32)
        act = found * sigmoid(found)
        bmat = act[:, inner : inner + state].astype(bf16)
        cmat = act[:, inner + state :].astype(bf16)
        driven = act[:, :inner] * expand(step[at, :], mask)
        wide = gate[at, :].astype(f32)
        d_mixed = d_gated[at, :].astype(f32) * (wide * sigmoid(wide))
        scores = mm_cols(cmat, bmat)
        upto, line = cumul[at, :], cumul_t[frame * heads : (frame + 1) * heads, :]
        d_scores = jnp.zeros((rows, rows), f32)
        sums = []
        for pair in range(heads // 2):
            lanes = slice(pair * wide_pair, (pair + 1) * wide_pair)
            decays = []
            for head in (2 * pair, 2 * pair + 1):
                differ = upto[:, head : head + 1] - line[head : head + 1, :]
                decays.append(jnp.exp(jnp.where(lower, differ, -1e30)))
            weights = [(decay * scores).astype(bf16) for decay in decays]
            drive, d_mix = driven[:, lanes], d_mixed[:, lanes]
            drive_bf, d_mix_bf = drive.astype(bf16), d_mix.astype(bf16)
            drive_two = jnp.concatenate(
                [jnp.where(first, drive, 0.0), jnp.where(first, 0.0, drive)], axis=0
            ).astype(bf16)
            d_mix_two = jnp.concatenate(
                [jnp.where(first, d_mix, 0.0), jnp.where(first, 0.0, d_mix)], axis=0
            ).astype(bf16)
            mix = mm(jnp.concatenate(weights, axis=1), drive_two)
            d_weights = mm_cols(d_mix_two, drive_bf)
            d_drive = mm_rows(jnp.concatenate(weights, axis=0), d_mix_two)
            d_scores = d_scores + decays[0] * d_weights[:rows] + decays[1] * d_weights[rows:]
            mixed[at, lanes] = mix.astype(bf16)
            d_driven[at, lanes] = d_drive.astype(bf16)
            sums.append(d_mix_bf.astype(f32) * mix - drive_bf.astype(f32) * d_drive)
        d_scores = d_scores.astype(bf16)
        d_bc[at, :state] = mm_rows(d_scores, cmat)
        d_bc[at, state:] = mm(d_scores, bmat)
        d_cumul[at, :] = fold(jnp.concatenate(sums, axis=1), mask)


def post_kernel(
    place, got, conv, gate, d_gated, raw, step, cumul, mixed, d_driven, d_bc, d_cumul, step_bias, decay_log, skip_gain,
    conv_w, cot, normal_t, halo_t,
    gated, d_gate, d_xbc, d_first, d_second, d_step, *refs,
):
    by_x, by_y, ext, d_conv_out, whole, parted = refs[:4], refs[4:8], refs[8], refs[9], refs[10], refs[11]
    rows = conv.shape[0] // 2
    inner = gate.shape[1]
    heads = step.shape[1]
    state = (conv.shape[1] - inner) // 2
    mask = head_mask(heads, inner // heads)
    skip = expand(jnp.broadcast_to(skip_gain[...].reshape(1, -1), (8, heads)), mask)[:1]
    for frame in range(2):
        at = slice(frame * rows, (frame + 1) * rows)
        found = conv[at, :].astype(f32)
        share = sigmoid(found)
        act = found * share
        inputs = act[:, :inner]
        bmat = act[:, inner : inner + state].astype(bf16)
        cmat = act[:, inner + state :].astype(bf16)
        upto = cumul[at, :]
        end = upto[rows - 1 : rows, :]
        spread = expand(jnp.concatenate([step[at, :], jnp.exp(upto), jnp.exp(end - upto)], axis=0), mask)
        sizes, grown, left = spread[:rows], spread[rows : 2 * rows], spread[2 * rows :]
        part = inner // SIDE
        carried = got[:, frame * part : (frame + 1) * part, :].reshape(inner, state)
        reach = got[:, (2 + frame) * part : (3 + frame) * part, :].reshape(inner, state)
        inter = grown * mm_cols(cmat, carried)
        full = mixed[at, :].astype(f32) + inter + skip * inputs
        wide = gate[at, :].astype(f32)
        opened = sigmoid(wide)
        silu = wide * opened
        gated[at, :] = (full * silu).astype(bf16)
        d_out = d_gated[at, :].astype(f32)
        d_gate[at, :] = (d_out * full * (opened * (1.0 + wide * (1.0 - opened)))).astype(bf16)
        d_mixed = d_out * silu
        d_cmat = d_bc[at, state:] + mm((d_mixed * grown).astype(bf16), carried)
        answer = left * mm_cols(bmat, reach)
        driven = inputs * sizes
        d_drive = d_driven[at, :].astype(f32) + answer
        d_bmat = d_bc[at, :state] + mm((left * driven).astype(bf16), reach)
        products = carried.astype(f32) * reach.astype(f32)
        met = jnp.sum(products.reshape(heads, inner // heads, state), axis=1)
        met = jnp.sum(met, axis=1, keepdims=True)
        met = jnp.sum(jnp.where(iota((heads, heads), 0) == iota((heads, heads), 1), met, 0.0), axis=0, keepdims=True)
        folded = fold(jnp.concatenate([driven * answer, d_mixed * inter, d_drive * inputs], axis=0), mask, 1)
        held, entered, by_size = folded[:rows], folded[rows : 2 * rows], folded[2 * rows :]
        d_end = jnp.exp(end) * met + jnp.sum(held, axis=0, keepdims=True)
        d_decay = tri_sum(triangle(rows, False), d_cumul[at, :] + entered - held) + d_end
        d_size = by_size - jnp.exp(decay_log[...].reshape(1, -1)) * d_decay
        d_step[at, :] = (d_size * sigmoid(raw[at, :] + step_bias[...].reshape(1, -1))).astype(bf16)
        d_act = jnp.concatenate([skip * d_mixed + d_drive * sizes, d_bmat, d_cmat], axis=1)
        margin = halo_t.shape[1] // 2
        ext[:margin, :] = jnp.zeros((margin, ext.shape[1]), f32)
        ext[margin : margin + rows, :] = d_act * (share * (1.0 + found * (1.0 - share)))
        ext[margin + rows :, :] = jnp.zeros((8, ext.shape[1]), f32)
        taps = conv_w.shape[0]
        total = None
        for tap in range(taps):
            start = taps - 1 - tap
            part = ext[start : start + margin + rows, :] * conv_w[tap : tap + 1, :]
            total = part if total is None else total + part
        d_xbc[at, :] = total[margin:].astype(bf16)
        d_conv_out[frame * margin : (frame + 1) * margin, :] = total[:margin].astype(bf16)
        (d_first, d_second)[frame][...] = total[margin - 8 : margin]
    columns = cot.shape[1]
    half = d_xbc.shape[1] // 2
    out_term = mm_rows(gated[...], cot[...]).reshape(COUNT, 2, 8, columns)
    gate_term = mm(normal_t[...], d_gate[...]).reshape(COUNT // SIDE, SIDE, 8, inner)
    in_term = mm(normal_t[...], d_xbc[...]) + mm(halo_t[...], d_conv_out[...])
    whole[:, :columns] = out_term[:, 0].reshape(-1, columns).astype(bf16)
    whole[:, columns : 2 * columns] = out_term[:, 1].reshape(-1, columns).astype(bf16)
    whole[:, 2 * columns :] = in_term[:, :half].astype(bf16)
    parted[:, :, :, :inner] = gate_term
    parted[:, :, :, inner:] = in_term[:, half:].reshape(COUNT // SIDE, SIDE, 8, half)
    ring_out(lambda step: chunk_x(place, whole, step), by_x)
    ring_out(lambda step: chunk_y(place, parted, step), by_y)


def chunk_x(place, whole, step):
    chunk = whole.shape[0] // SIDE
    to = lax.rem(place[0] + step, SIDE)
    return whole[pl.ds(pl.multiple_of(to * chunk, chunk), chunk), :].astype(bf16)


def chunk_y(place, parted, step):
    block = parted[:, lax.rem(place[2] + step, SIDE)]
    return block.reshape(-1, block.shape[-1]).astype(bf16)


def ring_out(chunk_of, slots):
    keep, base, right, left = slots
    half = keep.shape[0] // 2
    keep[...] = chunk_of(0)
    ahead, opposite, behind = chunk_of(1), chunk_of(2), chunk_of(3)
    base[:half, :], base[half:, :] = ahead[:half], behind[half:]
    right[:half, :], right[half:, :] = opposite[:half], ahead[half:]
    left[:half, :], left[half:, :] = behind[:half], opposite[half:]


def relay_kernel(base_x, right_x, left_x, base_y, right_y, left_y, to_both, *outs):
    for base, right, left, on_right, on_left in (
        (base_x, right_x, left_x, outs[0], outs[1]),
        (base_y, right_y, left_y, outs[2], outs[3]),
    ):
        half = base.shape[0] // 2
        columns = base.shape[1]
        on_right[:, :columns] = (base[:half, :].astype(f32) + right[:half, :].astype(f32)).astype(bf16)
        on_left[:, :columns] = (base[half:, :].astype(f32) + left[half:, :].astype(f32)).astype(bf16)
    outs[2][:32, columns:] = to_both[:32, :]
    outs[3][:32, columns:] = to_both[32:, :]
    for target in outs[2:]:
        target[32:, columns:] = jnp.zeros((32, 128), bf16)


def ring_total(keep, right, left, on_right, on_left):
    half = keep.shape[0] // 2
    columns = keep.shape[1]
    first = keep[:half, :].astype(f32) + left[:half, :].astype(f32) + on_right[:, :columns].astype(f32)
    second = keep[half:, :].astype(f32) + right[half:, :].astype(f32) + on_left[:, :columns].astype(f32)
    return jnp.concatenate([first, second], axis=0)


def send_x(place, whole, slots):
    chunk = whole.shape[0] // SIDE
    for step in range(SIDE):
        to = lax.rem(place[0] + step, SIDE)
        block = whole[pl.ds(pl.multiple_of(to * chunk, chunk), chunk), :]
        slots[step][...] = block.astype(slots[step].dtype)


def send_y(place, parted, slots):
    for step in range(SIDE):
        block = parted[:, lax.rem(place[2] + step, SIDE)]
        slots[step][...] = block.reshape(slots[step].shape).astype(slots[step].dtype)


def norm_back(block, d_normal, gain):
    wide = block.astype(f32)
    scale = lax.rsqrt(jnp.mean(wide * wide, axis=-1, keepdims=True) + epsilon)
    d_scaled = d_normal * gain.reshape(1, -1)
    along = jnp.mean(d_scaled * wide, axis=-1, keepdims=True)
    return scale * d_scaled - wide * (scale * scale * scale * along)


def fold_rows(block):
    return jnp.concatenate([block[:, 128 * nth : 128 * (nth + 1)] for nth in range(4)], axis=0)


def unfold_rows(block):
    return jnp.concatenate([block[8 * nth : 8 * (nth + 1)] for nth in range(4)], axis=1)


def scalar_flag(condition):
    return jnp.where(condition, 1.0, 0.0)


def result_kernel(
    place, both, gain, gated, out_proj, d_gate, d_xbc, d_first, d_second, low, high, d_step, in_proj, step_proj,
    layer, base, to_both, d_whole,
):
    rows = both.shape[0] // 2
    inner = out_proj.shape[0]
    branch = mm(gated[...], out_proj[...])
    layer[...] = (branch[:rows] + mirror_wide(branch[rows:])).astype(bf16)
    d_whole[: 2 * rows, :] = d_xbc[...]
    edges = jnp.concatenate([d_first[...], d_second[...]], axis=0)
    d_whole[2 * rows :, :] = edges.astype(bf16)
    through = mm_cols(d_whole[...], in_proj[:, inner:])
    d_normal = mm_cols(d_gate[...], in_proj[:, :inner]) + through[: 2 * rows]
    d_normal = d_normal + mm(d_step[...], step_proj[...])
    d_wide = norm_back(both[...], d_normal, gain[...])
    base[...] = d_wide[:rows] + mirror_wide(d_wide[rows:])
    first = norm_back(low[8:, :], through[2 * rows : 2 * rows + 8], gain[...])
    second = norm_back(mirror_exact(high[...])[8:, :], through[2 * rows + 8 :], gain[...])
    at_start = (place[0] + place[1] + place[2]) == 0
    at_end = (place[0] + place[1] + place[2]) == 3 * (SIDE - 1)
    to_both[32:, :] = fold_rows(first * (1.0 - scalar_flag(at_start))).astype(bf16)
    to_both[:32, :] = fold_rows(mirror_wide(second) * (1.0 - scalar_flag(at_end))).astype(bf16)


def total_of(refs):
    total = refs[0][...].astype(f32)
    for ref in refs[1:]:
        total = total + ref[...].astype(f32)
    return total


def first_sum_kernel(place, *refs):
    from_x, from_y, by_y, by_x, kept = refs[:5], refs[5:10], refs[10:14], refs[14:18], refs[18]
    parted, whole = refs[19], refs[20]
    parted[...] = ring_total(*from_x).reshape(parted.shape)
    whole[...] = ring_total(*from_y)
    send_y(place, parted, by_y)
    columns = whole.shape[1]
    chunk = whole.shape[0] // SIDE
    for step in range(SIDE):
        to = lax.rem(place[0] + step, SIDE)
        block = whole[pl.ds(pl.multiple_of(to * chunk, chunk), chunk), :]
        by_x[step][:, :columns] = block.astype(by_x[step].dtype)
    high = from_y[3][:32, columns:].astype(f32)
    low = from_y[4][:32, columns:].astype(f32)
    on_high = scalar_flag((place[2] == 0) & (place[1] == SIDE - 1))
    on_low = scalar_flag((place[2] == SIDE - 1) & (place[1] == 0))
    by_x[1][:, columns:] = (high * on_high).astype(bf16)
    by_x[3][:, columns:] = (low * on_low).astype(bf16)
    kept[:32, :] = high * (1.0 - on_high)
    kept[32:, :] = low * (1.0 - on_low)


def second_sum_kernel(place, *refs):
    first, second, kept, by_z, kept_on, keep = refs[:4], refs[4:8], refs[8], refs[9:13], refs[13], refs[14]
    columns = first[0].shape[1]
    high = kept[:32, :] + second[1][:, columns:].astype(f32)
    low = kept[32:, :] + second[3][:, columns:].astype(f32)
    first = total_of(first).reshape(SIDE, 8, -1)
    total = second[0][...]
    for step in range(1, SIDE):
        total = total + second[step][:, :columns].astype(f32)
    second = total.reshape(SIDE, 8, -1)
    above = scalar_flag(place[2] == 0)
    below = scalar_flag(place[2] == SIDE - 1)
    keep[:, 0] = first
    keep[:, 1] = second
    for step in range(SIDE):
        block = keep[lax.rem(place[1] + step, SIDE)].reshape(16, columns)
        by_z[step][:, :columns] = block.astype(by_z[step].dtype)
    for step, edge, share in ((1, high, above), (3, low, below)):
        edge = edge * share
        by_z[step][:, columns:] = jnp.concatenate([edge[:16], edge[16:]], axis=1).astype(bf16)
    kept_on[:32, :] = high * (1.0 - above)
    kept_on[32:, :] = low * (1.0 - below)


def last_sum_kernel(own, up, across, down, kept, base, grad_in, grad_out, grad):
    joined = own.shape[1]
    total = own[...] + up[:, :joined].astype(f32) + across[...].astype(f32) + down[:, :joined].astype(f32)
    columns = grad_out.shape[1]
    grad_out[:8, :] = total[:8, :columns]
    grad_out[8:, :] = total[:8, columns : 2 * columns]
    grad_in[...] = jnp.concatenate([total[8:, : 2 * columns], total[:8, 2 * columns :], total[8:, 2 * columns :]], axis=1)
    edges = []
    for nth, recv in enumerate((up, down)):
        recv = recv[:, joined:].astype(f32)
        recv = jnp.concatenate([recv[:, :128], recv[:, 128:]], axis=0)
        edges.append(unfold_rows(kept[32 * nth : 32 * nth + 32, :] + recv))
    rows = base.shape[0]
    whole = jnp.concatenate([base[:8, :] + edges[0], base[8 : rows - 8, :], base[rows - 8 :, :] + edges[1]], axis=0)
    grad[...] = whole.astype(bf16)


def axis_pairs(stride, step):
    pairs = []
    for source in range(COUNT):
        digit = source // stride % SIDE
        pairs.append((source, source + ((digit + step) % SIDE - digit) * stride))
    return pairs


def exchange(parts, stride):
    return [parts[0]] + [lax.ppermute(parts[step], "seq", axis_pairs(stride, step)) for step in range(1, SIDE)]


def around(to_right, to_left, stride):
    return (
        lax.ppermute(to_right, "seq", axis_pairs(stride, 1)),
        lax.ppermute(to_left, "seq", axis_pairs(stride, SIDE - 1)),
    )


def transpose_over(parts, groups):
    return lax.all_to_all(parts, "seq", 0, 0, axis_index_groups=groups)


def slots(rows, columns, kind):
    return [((rows, columns), kind)] + [((rows, columns), bf16)] * (SIDE - 1)


def shards(
    sequence,
    upstream,
    norm_gain,
    in_proj,
    step_proj,
    conv_weight,
    conv_bias,
    step_bias,
    decay_log,
    skip_gain,
    out_proj,
):
    rows, width = sequence.shape
    inner = out_proj.shape[0]
    heads = step_bias.shape[0]
    state = inner // heads * 2
    channels = conv_weight.shape[1]
    both_rows = 2 * rows
    stride_x, stride_z, stride_y = SIDE * SIDE, SIDE, 1
    index = lax.axis_index("seq")
    place = jnp.stack([index // stride_x, index // stride_z % SIDE, index % SIDE]).astype(jnp.int32)
    beside = [[SIDE * base + digit for digit in range(SIDE)] for base in range(COUNT // SIDE)]
    across = [[base + SIDE * digit for digit in range(COUNT // SIDE)] for base in range(SIDE)]
    upward = [(i, i + 1) for i in range(COUNT - 1)]
    downward = [(i + 1, i) for i in range(COUNT - 1)]
    low = lax.ppermute(sequence[rows - 16 :], "seq", upward)
    high = lax.ppermute(sequence[:16], "seq", downward)
    step_turned = step_proj.T
    payload, both, normal, normal_halo, cot, gate, conv, d_gated, raw, step, cumul, cumul_t = call(
        pre_kernel,
        [
            ((SIDE, inner + 16, state), bf16),
            ((both_rows, width), bf16),
            ((both_rows, width), bf16),
            ((32, width), bf16),
            ((both_rows, width), bf16),
            ((both_rows, inner), bf16),
            ((both_rows, channels), bf16),
            ((both_rows, inner), bf16),
            ((both_rows, heads), f32),
            ((both_rows, heads), f32),
            ((both_rows, heads), f32),
            ((2 * heads, rows), f32),
        ],
        (
            sequence, upstream, low, high, norm_gain, in_proj, step_turned,
            conv_weight, conv_bias, step_bias, decay_log, out_proj,
        ),
        [pltpu.VMEM((rows + 8, channels), f32)],
    )
    got = transpose_over(payload, beside)
    (summary,) = call(group_kernel, [((COUNT // SIDE, 72, state), bf16)], (got,), vmem=16 * 2**20)
    summaries = transpose_over(summary, across)
    mixed, d_driven, d_bc, d_cumul, normal_t, halo_t = call(
        intra_kernel,
        [
            ((both_rows, inner), bf16),
            ((both_rows, inner), bf16),
            ((both_rows, 2 * state), f32),
            ((both_rows, heads), f32),
            ((width, both_rows), bf16),
            ((width, 32), bf16),
        ],
        (conv, gate, d_gated, step, cumul, cumul_t, normal, normal_halo),
        flops=8 * 10**9,
    )
    groups = COUNT // SIDE
    (scanned,) = call(
        scan_kernel,
        [((groups, 64, state), bf16)],
        (summaries,),
        [pltpu.VMEM((groups * 72, state), f32), pltpu.VMEM((groups * 64, state), f32)],
        vmem=16 * 2**20,
    )
    entering = transpose_over(scanned, across)
    (spread,) = call(spread_kernel, [((SIDE, inner, state), bf16)], (got, entering), vmem=16 * 2**20)
    states = transpose_over(spread, beside)
    eighth = 8 * COUNT // SIDE
    joined = inner + channels // 2
    gated, d_gate, d_xbc, d_first, d_second, d_step, *parts = call(
        post_kernel,
        [
            ((both_rows, inner), bf16),
            ((both_rows, inner), bf16),
            ((both_rows, channels), bf16),
            ((8, channels), f32),
            ((8, channels), f32),
            ((both_rows, heads), bf16),
        ]
        + slots(eighth, joined, bf16) * 2,
        (
            place, states, conv, gate, d_gated, raw, step, cumul, mixed, d_driven, d_bc, d_cumul,
            step_bias, decay_log, skip_gain, conv_weight, cot, normal_t, halo_t,
        ),
        [
            pltpu.VMEM((rows + 24, channels), f32),
            pltpu.VMEM((32, channels), bf16),
            pltpu.VMEM((8 * COUNT, joined), bf16),
            pltpu.VMEM((COUNT // SIDE, SIDE, 8, joined), f32),
        ],
        scalars=1,
    )
    layer_out, base, to_both = call(
        result_kernel,
        [((rows, width), bf16), ((rows, width), f32), ((64, 128), bf16)],
        (
            place, both, norm_gain, gated, out_proj, d_gate, d_xbc, d_first, d_second, low, high, d_step,
            in_proj, step_turned,
        ),
        [pltpu.VMEM((both_rows + 16, channels), bf16)],
        scalars=1,
        flops=8 * 10**9,
    )
    keep_x, base_x, right_x, left_x, keep_y, base_y, right_y, left_y = parts
    right_x, left_x = around(right_x, left_x, stride_x)
    right_y, left_y = around(right_y, left_y, stride_y)
    relayed = call(
        relay_kernel,
        [((eighth // 2, joined), bf16)] * 2 + [((eighth // 2, joined + 128), bf16)] * 2,
        (base_x, right_x, left_x, base_y, right_y, left_y, to_both),
        vmem=16 * 2**20,
    )
    from_x = [keep_x, right_x, left_x, *around(relayed[0], relayed[1], stride_x)]
    from_y = [keep_y, right_y, left_y, *around(relayed[2], relayed[3], stride_y)]
    small = eighth // SIDE
    *parts, kept = call(
        first_sum_kernel,
        slots(small, joined, f32)
        + [((small, joined), f32), ((small, joined + 128), bf16), ((small, joined), bf16), ((small, joined + 128), bf16)]
        + [((64, 128), f32)],
        (place, *from_x, *from_y),
        [pltpu.VMEM((SIDE, SIDE, 8, joined), f32), pltpu.VMEM((eighth, joined), f32)],
        scalars=1,
        vmem=16 * 2**20,
    )
    first = exchange(parts[:4], stride_y)
    second = exchange(parts[4:], stride_x)
    *parts, kept = call(
        second_sum_kernel,
        [((16, joined), f32), ((16, joined + 256), bf16), ((16, joined), bf16), ((16, joined + 256), bf16)]
        + [((64, 128), f32)],
        (place, *first, *second, kept),
        [pltpu.VMEM((SIDE, 2, 8, joined), f32)],
        scalars=1,
        vmem=16 * 2**20,
    )
    last = exchange(parts, stride_z)
    grad_in_proj, grad_out_proj, grad_input = call(
        last_sum_kernel,
        [((8, inner + channels), f32), ((16, width), f32), ((rows, width), bf16)],
        (*last, kept, base),
        vmem=16 * 2**20,
    )
    return (layer_out, grad_input, grad_in_proj, grad_out_proj)


def solution(mesh):
    rows = P(("batch", "seq"), None)
    return jax.shard_map(
        shards,
        mesh=mesh,
        in_specs=(rows, rows) + (P(),) * 9,
        out_specs=(rows,) * 4,
        check_vma=False,
    )
```

```python
import functools

import jax
import jax.numpy as jnp
from jax import lax
from jax.experimental import pallas as pl
from jax.experimental.pallas import tpu as pltpu
from jax.sharding import PartitionSpec as P

epsilon = 1e-06
SIDE = 4
COUNT = SIDE**3
f32 = jnp.float32
bf16 = jnp.bfloat16
INTERPRET = False


def call(body, outs, args, scratch=(), scalars=0, unused=0, flops=10**9, vmem=58 * 2**20):
    after = len(args) - unused
    specs = [pl.BlockSpec(memory_space=pltpu.SMEM)] * scalars
    specs += [pl.BlockSpec(memory_space=pltpu.VMEM)] * (after - scalars)
    specs += [pl.BlockSpec(memory_space=pl.ANY)] * unused
    moved = sum(a.size * a.dtype.itemsize for a in args[:after])

    def used(*refs):
        body(*refs[:after], *refs[len(args) :])

    return pl.pallas_call(
        used,
        out_shape=[jax.ShapeDtypeStruct(shape, kind) for shape, kind in outs],
        in_specs=specs,
        out_specs=[pl.BlockSpec(memory_space=pltpu.VMEM)] * len(outs),
        scratch_shapes=list(scratch),
        compiler_params=pltpu.CompilerParams(vmem_limit_bytes=vmem),
        cost_estimate=pl.CostEstimate(flops=flops, bytes_accessed=moved, transcendentals=0),
        interpret=INTERPRET,
    )(*args)


def mm(left, right):
    return lax.dot_general(left, right, (((1,), (0,)), ((), ())), preferred_element_type=f32)


def mm_cols(left, right):
    return lax.dot_general(left, right, (((1,), (1,)), ((), ())), preferred_element_type=f32)


def mm_rows(left, right):
    return lax.dot_general(left, right, (((0,), (0,)), ((), ())), preferred_element_type=f32)


def iota(shape, dim):
    return lax.broadcasted_iota(jnp.int32, shape, dim)


def ones_where(mask):
    return jnp.where(mask, 1.0, 0.0).astype(bf16)


def anti(size):
    return ones_where(iota((size, size), 0) + iota((size, size), 1) == size - 1)


def pieces_of(value, count):
    found = []
    for _ in range(count):
        piece = value.astype(bf16)
        found.append(piece)
        value = value - piece.astype(f32)
    return found


def mirror_exact(block):
    turned = mm(block, anti(block.shape[1])).astype(bf16)
    return mm(anti(block.shape[0]), turned).astype(bf16)


def mirror_wide(block):
    high, low = pieces_of(block, 2)
    return mirror_exact(high).astype(f32) + mirror_exact(low).astype(f32)


def head_mask(heads, width):
    lanes = heads * width
    return ones_where(iota((heads, lanes), 0) == iota((heads, lanes), 1) // width)


def expand(value, mask):
    found = pieces_of(value, 3)
    return mm(jnp.concatenate(found, axis=1), jnp.concatenate([mask] * 3, axis=0))


def fold(value, mask, count=2):
    total = None
    for piece in pieces_of(value, count):
        part = mm_cols(piece, mask)
        total = part if total is None else total + part
    return total


def triangle(size, low):
    rows, cols = iota((size, size), 0), iota((size, size), 1)
    return rows >= cols if low else rows <= cols


def tri_sum(mask, value):
    total = None
    for piece in pieces_of(value, 3):
        part = mm(ones_where(mask), piece)
        total = part if total is None else total + part
    return total


def tri_sum_turned(mask, value):
    total = None
    for piece in pieces_of(value, 3):
        part = mm_rows(piece, ones_where(mask))
        total = part if total is None else total + part
    return total


def softplus(value):
    return jnp.maximum(value, 0.0) + jnp.log1p(jnp.exp(-jnp.abs(value)))


def sigmoid(value):
    return 1.0 / (1.0 + jnp.exp(-value))


def norm_rows(block, gain):
    wide = block.astype(f32)
    scale = lax.rsqrt(jnp.mean(wide * wide, axis=-1, keepdims=True) + epsilon)
    return (wide * scale * gain.reshape(1, -1)).astype(bf16)


def pre_kernel(
    seq, up, low, high, gain, in_proj, step_proj, conv_w, conv_b, step_bias, decay_log, out_proj,
    payload, both, normal, normal_halo, cot, gate, conv, d_gated, raw, step, cumul, cumul_t,
    ext,
):
    rows = seq.shape[0]
    inner = out_proj.shape[0]
    heads = step_bias.shape[0]
    state = (conv_w.shape[1] - inner) // 2
    taps = conv_w.shape[0]
    both[:rows, :] = seq[...]
    both[rows:, :] = mirror_exact(seq[...])
    cot[:rows, :] = up[...]
    cot[rows:, :] = mirror_exact(up[...])
    halo = jnp.concatenate([low[...], mirror_exact(high[...])], axis=0)
    normal[...] = norm_rows(both[...], gain[...])
    normal_halo[...] = norm_rows(halo, gain[...])
    gate[...] = mm(normal[...], in_proj[:, :inner]).astype(bf16)
    xbc = mm(normal[...], in_proj[:, inner:]).astype(bf16).astype(f32)
    xbc_halo = mm(normal_halo[...], in_proj[:, inner:]).astype(bf16).astype(f32)
    raw[...] = mm_cols(normal[...], step_proj[...])
    d_gated[...] = mm_cols(cot[...], out_proj[...]).astype(bf16)
    margin = low.shape[0]
    mask = head_mask(heads, inner // heads)
    ends = []
    for frame in range(2):
        at = slice(frame * rows, (frame + 1) * rows)
        ext[:8, :] = xbc_halo[(frame + 1) * margin - 8 : (frame + 1) * margin, :]
        ext[8:, :] = xbc[at, :]
        found = conv_b[...].reshape(1, -1)
        for tap in range(taps):
            start = 9 - taps + tap
            found = found + ext[start : start + rows, :] * conv_w[tap : tap + 1, :]
        conv[at, :] = found.astype(bf16)
        act = found * sigmoid(found)
        size = softplus(raw[at, :] + step_bias[...].reshape(1, -1))
        decay = -jnp.exp(decay_log[...].reshape(1, -1)) * size
        upto = tri_sum(triangle(rows, True), decay)
        step[at, :] = size
        cumul[at, :] = upto
        cumul_t[frame * heads : (frame + 1) * heads, :] = tri_sum_turned(triangle(rows, False), decay)
        end = upto[rows - 1 : rows, :]
        ends.append(end)
        spread = expand(jnp.concatenate([size * jnp.exp(end - upto), jnp.exp(upto)], axis=0), mask)
        driven = (act[:, :inner] * spread[:rows]).astype(bf16)
        local = mm_rows(driven, act[:, inner : inner + state].astype(bf16))
        wide = gate[at, :].astype(f32)
        d_mixed = d_gated[at, :].astype(f32) * (wide * sigmoid(wide))
        back = mm_rows((d_mixed * spread[rows:]).astype(bf16), act[:, inner + state :].astype(bf16))
        part = inner // SIDE
        for place, block in ((frame, local), (2 + frame, back)):
            block = block.astype(bf16).reshape(SIDE, part, state)
            payload[:, place * part : (place + 1) * part, :] = block
    packed = pack_totals(ends, heads, state)
    for to in range(SIDE):
        shifted = ones_where(iota((16, heads), 1) == iota((16, heads), 0) + to * (heads // SIDE))
        payload[to, inner:, :] = mm(shifted, packed).astype(bf16)


def pack_totals(ends, heads, state):
    chosen = iota((heads, heads), 0) == iota((heads, heads), 1)
    lanes = iota((heads, state), 1)
    packed = jnp.zeros((heads, state), f32)
    for frame in range(2):
        column = jnp.sum(jnp.where(chosen, ends[frame], 0.0), axis=1, keepdims=True)
        packed = pack_column(packed, column, lanes, frame)
    return packed.astype(bf16)


def pack_column(packed, column, lanes, frame):
    for nth, piece in enumerate(pieces_of(column, 3)):
        packed = jnp.where(lanes == 3 * frame + nth, piece.astype(f32), packed)
    return packed


def unpack_column(packed, frame):
    at = 3 * frame
    return (packed[:, at + 2 : at + 3] + packed[:, at + 1 : at + 2]) + packed[:, at : at + 1]


SCANS = ((0, False), (1, True), (0, True), (1, False))


def chain(got, totals, place, state, visit):
    frame, turned = SCANS[place]
    part = state.shape[0]
    size = part // SIDE
    order = range(SIDE - 1, -1, -1) if turned else range(SIDE)
    for at in order:
        visit(at, state)
        grown = jnp.exp(totals[at][frame])
        factors = [
            jnp.broadcast_to(grown[head : head + 1, :], (size, 1)) for head in range(part // size)
        ]
        state = jnp.concatenate(factors, axis=0) * state
        state = state + got[at, place * part : (place + 1) * part, :].astype(f32)
    return state


def tails_of(got, inner):
    found = []
    for at in range(SIDE):
        tail = got[at, inner:, :].astype(f32)
        found.append([unpack_column(tail, frame) for frame in range(2)])
    return found


def group_kernel(got, out):
    state = got.shape[2]
    inner = got.shape[1] - 16
    part = inner // SIDE
    totals = tails_of(got, inner)
    for place in range(4):
        block = chain(got, totals, place, jnp.zeros((part, state), f32), lambda at, value: None)
        out[:, 16 * place : 16 * place + 16, :] = block.reshape(16, 16, state).astype(bf16)
    lanes = iota((16, state), 1)
    packed = jnp.zeros((16, state), f32)
    for frame in range(2):
        column = jnp.maximum(totals[0][frame], -110.0)
        for at in range(1, SIDE):
            column = column + jnp.maximum(totals[at][frame], -110.0)
        packed = pack_column(packed, column, lanes, frame)
    chosen = ones_where(iota((16, 16), 1) == iota((16, 16), 0) // SIDE)
    packed = mm(chosen, packed.astype(bf16))
    out[:, 64:, :] = jnp.broadcast_to(packed.reshape(16, 1, state), (16, 8, state)).astype(bf16)


def spread_kernel(got, entering, out):
    state = got.shape[2]
    inner = got.shape[1] - 16
    part = inner // SIDE
    totals = tails_of(got, inner)
    for place in range(4):

        def visit(at, value, place=place):
            out[at, place * part : (place + 1) * part, :] = value.astype(bf16)

        block = entering[:, 16 * place : 16 * place + 16, :].astype(f32).reshape(part, state)
        chain(got, totals, place, block, visit)


def scan_kernel(got, out, wide, done):
    count, rows, state = got.shape
    wide[...] = got[...].astype(f32).reshape(count * rows, state)
    tails = wide[pl.ds(64, count, stride=rows), :]
    above = iota((count, count), 0)
    beside = iota((count, count), 1)
    after = ones_where(above > beside)
    weights = []
    for frame in range(2):
        column = jnp.maximum(unpack_column(tails, frame), -110.0)
        line = jnp.sum(jnp.where(above == beside, column, 0.0), axis=0, keepdims=True)
        between = None
        for piece in pieces_of(jnp.where(beside < above, line, 0.0), 3):
            part = mm(piece, after)
            between = part if between is None else between + part
        found = jnp.where(above > beside, jnp.exp(between), 0.0)
        weights.append(pieces_of(found, 2))
    for place, (frame, turned) in enumerate(SCANS):
        pair = weights[frame]
        block = jnp.concatenate(
            [wide[pl.ds(16 * place + row, count, stride=rows), :] for row in range(16)], axis=1
        ).astype(bf16)
        if turned:
            mixed = mm_rows(jnp.concatenate(pair, axis=1), block)
        else:
            mixed = mm(jnp.concatenate(pair, axis=0), block)
        mixed = mixed[:count] + mixed[count:]
        for row in range(16):
            done[pl.ds(16 * place + row, count, stride=64), :] = mixed[:, state * row : state * (row + 1)]
    out[...] = done[...].reshape(count, 64, state).astype(bf16)


def intra_kernel(
    conv, gate, d_gated, step, cumul, cumul_t, normal, normal_halo, skip_gain,
    silus, d_gates, pushed, mixed, d_inputs, lefts, held_back, d_convs, bc, d_bc, sums_out, normal_t, halo_t,
):
    for source, target in ((normal, normal_t), (normal_halo, halo_t)):
        count = source.shape[0]
        same = iota((count, count), 0) == iota((count, count), 1)
        target[...] = mm_rows(source[...], ones_where(same)).astype(bf16)
    rows = conv.shape[0] // 2
    inner = gate.shape[1]
    heads = step.shape[1]
    state = (conv.shape[1] - inner) // 2
    mask = head_mask(heads, inner // heads)
    lower = triangle(rows, True)
    first = iota((rows, 2 * inner // heads), 1) < inner // heads
    wide_pair = 2 * inner // heads
    skip = expand(jnp.broadcast_to(skip_gain[...].reshape(1, -1), (8, heads)), mask)[:1]
    for frame in range(2):
        at = slice(frame * rows, (frame + 1) * rows)
        found = conv[at, :].astype(f32)
        share = sigmoid(found)
        act = found * share
        d_convs[at, :] = (share * (1.0 + found * (1.0 - share))).astype(bf16)
        bc[at, :] = act[:, inner:].astype(bf16)
        bmat, cmat = bc[at, :state], bc[at, state:]
        upto = cumul[at, :]
        end = upto[rows - 1 : rows, :]
        spread = expand(jnp.concatenate([step[at, :], jnp.exp(upto), jnp.exp(end - upto)], axis=0), mask)
        sizes, grown, left = spread[:rows], spread[rows : 2 * rows], spread[2 * rows :]
        inputs = act[:, :inner]
        driven = inputs * sizes
        lefts[at, :] = (left * inputs).astype(bf16)
        held_back[at, :] = (left * driven).astype(bf16)
        wide = gate[at, :].astype(f32)
        opened = sigmoid(wide)
        silu = wide * opened
        silus[at, :] = silu.astype(bf16)
        d_out = d_gated[at, :].astype(f32)
        d_gates[at, :] = (d_out * (opened * (1.0 + wide * (1.0 - opened)))).astype(bf16)
        d_mixed = d_out * silu
        pushed[at, :] = (d_mixed * grown).astype(bf16)
        scores = mm_cols(cmat, bmat)
        line = cumul_t[frame * heads : (frame + 1) * heads, :]
        d_scores = jnp.zeros((rows, rows), f32)
        sums, by_size = [], []
        for pair in range(heads // 2):
            lanes = slice(pair * wide_pair, (pair + 1) * wide_pair)
            decays = []
            for head in (2 * pair, 2 * pair + 1):
                differ = upto[:, head : head + 1] - line[head : head + 1, :]
                decays.append(jnp.exp(jnp.where(lower, differ, -1e30)))
            weights = [(decay * scores).astype(bf16) for decay in decays]
            drive, d_mix = driven[:, lanes], d_mixed[:, lanes]
            drive_bf, d_mix_bf = drive.astype(bf16), d_mix.astype(bf16)
            drive_two = jnp.concatenate(
                [jnp.where(first, drive, 0.0), jnp.where(first, 0.0, drive)], axis=0
            ).astype(bf16)
            d_mix_two = jnp.concatenate(
                [jnp.where(first, d_mix, 0.0), jnp.where(first, 0.0, d_mix)], axis=0
            ).astype(bf16)
            mix = mm(jnp.concatenate(weights, axis=1), drive_two)
            d_weights = mm_cols(d_mix_two, drive_bf)
            d_drive = mm_rows(jnp.concatenate(weights, axis=0), d_mix_two)
            d_scores = d_scores + decays[0] * d_weights[:rows] + decays[1] * d_weights[rows:]
            mixed[at, lanes] = (mix + skip[:, lanes] * inputs[:, lanes]).astype(bf16)
            d_inputs[at, lanes] = (skip[:, lanes] * d_mix + d_drive * sizes[:, lanes]).astype(bf16)
            by_size.append(d_drive * inputs[:, lanes])
            sums.append(d_mix_bf.astype(f32) * mix - drive_bf.astype(f32) * d_drive)
        d_scores = d_scores.astype(bf16)
        d_bc[at, :state] = mm_rows(d_scores, cmat)
        d_bc[at, state:] = mm(d_scores, bmat)
        sums_out[at, :heads] = fold(jnp.concatenate(sums, axis=1), mask)
        sums_out[at, heads:] = fold(jnp.concatenate(by_size, axis=1), mask)


def post_kernel(
    place, got, silus, d_gates, pushed, mixed, d_inputs, lefts, held_back, d_convs, bc, d_bc, sums,
    raw, step, cumul, step_bias, decay_log, conv_w, cot, normal_t, halo_t,
    gated, d_gate, d_xbc, d_first, d_second, d_step, *refs,
):
    by_x, by_y, ext, d_conv_out, whole, parted = refs[:4], refs[4:8], refs[8], refs[9], refs[10], refs[11]
    rows = silus.shape[0] // 2
    inner = silus.shape[1]
    heads = step.shape[1]
    state = bc.shape[1] // 2
    mask = head_mask(heads, inner // heads)
    for frame in range(2):
        at = slice(frame * rows, (frame + 1) * rows)
        upto = cumul[at, :]
        size = step[at, :]
        end = upto[rows - 1 : rows, :]
        spread = expand(jnp.concatenate([jnp.exp(upto), size * jnp.exp(end - upto)], axis=0), mask)
        part = inner // SIDE
        carried = got[:, frame * part : (frame + 1) * part, :].reshape(inner, state)
        reach = got[:, (2 + frame) * part : (3 + frame) * part, :].reshape(inner, state)
        read = mm_cols(bc[at, state:], carried)
        full = mixed[at, :].astype(f32) + spread[:rows] * read
        gated[at, :] = (full * silus[at, :].astype(f32)).astype(bf16)
        d_gate[at, :] = (full * d_gates[at, :].astype(f32)).astype(bf16)
        d_cmat = d_bc[at, state:] + mm(pushed[at, :], carried)
        answer = mm_cols(bc[at, :state], reach)
        d_bmat = d_bc[at, :state] + mm(held_back[at, :], reach)
        products = carried.astype(f32) * reach.astype(f32)
        met = jnp.sum(products.reshape(heads, inner // heads, state), axis=1)
        met = jnp.sum(met, axis=1, keepdims=True)
        met = jnp.sum(jnp.where(iota((heads, heads), 0) == iota((heads, heads), 1), met, 0.0), axis=0, keepdims=True)
        folded = fold(
            jnp.concatenate([lefts[at, :].astype(f32) * answer, pushed[at, :].astype(f32) * read], axis=0), mask, 1
        )
        by_size, entered = folded[:rows], folded[rows:]
        held = by_size * size
        d_end = jnp.exp(end) * met + jnp.sum(held, axis=0, keepdims=True)
        d_decay = tri_sum(triangle(rows, False), sums[at, :heads] + entered - held) + d_end
        d_size = sums[at, heads:] + by_size - jnp.exp(decay_log[...].reshape(1, -1)) * d_decay
        d_step[at, :] = (d_size * sigmoid(raw[at, :] + step_bias[...].reshape(1, -1))).astype(bf16)
        d_act = jnp.concatenate([d_inputs[at, :].astype(f32) + spread[rows:] * answer, d_bmat, d_cmat], axis=1)
        margin = halo_t.shape[1] // 2
        ext[:margin, :] = jnp.zeros((margin, ext.shape[1]), f32)
        ext[margin : margin + rows, :] = d_act * d_convs[at, :].astype(f32)
        ext[margin + rows :, :] = jnp.zeros((8, ext.shape[1]), f32)
        taps = conv_w.shape[0]
        total = None
        for tap in range(taps):
            start = taps - 1 - tap
            part = ext[start : start + margin + rows, :] * conv_w[tap : tap + 1, :]
            total = part if total is None else total + part
        d_xbc[at, :] = total[margin:].astype(bf16)
        d_conv_out[frame * margin : (frame + 1) * margin, :] = total[:margin].astype(bf16)
        (d_first, d_second)[frame][...] = total[margin - 8 : margin]
    columns = cot.shape[1]
    half = d_xbc.shape[1] // 2
    out_term = mm_rows(gated[...], cot[...]).reshape(COUNT, 2, 8, columns)
    gate_term = mm(normal_t[...], d_gate[...]).reshape(COUNT // SIDE, SIDE, 8, inner)
    in_term = mm(normal_t[...], d_xbc[...]) + mm(halo_t[...], d_conv_out[...])
    whole[:, :columns] = out_term[:, 0].reshape(-1, columns).astype(bf16)
    whole[:, columns : 2 * columns] = out_term[:, 1].reshape(-1, columns).astype(bf16)
    whole[:, 2 * columns :] = in_term[:, :half].astype(bf16)
    parted[:, :, :, :inner] = gate_term
    parted[:, :, :, inner:] = in_term[:, half:].reshape(COUNT // SIDE, SIDE, 8, half)
    ring_out(lambda step: chunk_x(place, whole, step), by_x)
    ring_out(lambda step: chunk_y(place, parted, step), by_y)


def chunk_x(place, whole, step):
    chunk = whole.shape[0] // SIDE
    to = lax.rem(place[0] + step, SIDE)
    return whole[pl.ds(pl.multiple_of(to * chunk, chunk), chunk), :].astype(bf16)


def chunk_y(place, parted, step):
    block = parted[:, lax.rem(place[2] + step, SIDE)]
    return block.reshape(-1, block.shape[-1]).astype(bf16)


def ring_out(chunk_of, slots):
    keep, base, right, left = slots
    half = keep.shape[0] // 2
    keep[...] = chunk_of(0)
    ahead, opposite, behind = chunk_of(1), chunk_of(2), chunk_of(3)
    base[:half, :], base[half:, :] = ahead[:half], behind[half:]
    right[:half, :], right[half:, :] = opposite[:half], ahead[half:]
    left[:half, :], left[half:, :] = behind[:half], opposite[half:]


def relay_kernel(base_x, right_x, left_x, base_y, right_y, left_y, to_both, *outs):
    for base, right, left, on_right, on_left in (
        (base_x, right_x, left_x, outs[0], outs[1]),
        (base_y, right_y, left_y, outs[2], outs[3]),
    ):
        half = base.shape[0] // 2
        columns = base.shape[1]
        on_right[:, :columns] = (base[:half, :].astype(f32) + right[:half, :].astype(f32)).astype(bf16)
        on_left[:, :columns] = (base[half:, :].astype(f32) + left[half:, :].astype(f32)).astype(bf16)
    outs[2][:32, columns:] = to_both[:32, :]
    outs[3][:32, columns:] = to_both[32:, :]
    for target in outs[2:]:
        target[32:, columns:] = jnp.zeros((32, 128), bf16)


def ring_total(keep, right, left, on_right, on_left):
    half = keep.shape[0] // 2
    columns = keep.shape[1]
    first = keep[:half, :].astype(f32) + left[:half, :].astype(f32) + on_right[:, :columns].astype(f32)
    second = keep[half:, :].astype(f32) + right[half:, :].astype(f32) + on_left[:, :columns].astype(f32)
    return jnp.concatenate([first, second], axis=0)


def send_x(place, whole, slots):
    chunk = whole.shape[0] // SIDE
    for step in range(SIDE):
        to = lax.rem(place[0] + step, SIDE)
        block = whole[pl.ds(pl.multiple_of(to * chunk, chunk), chunk), :]
        slots[step][...] = block.astype(slots[step].dtype)


def send_y(place, parted, slots):
    for step in range(SIDE):
        block = parted[:, lax.rem(place[2] + step, SIDE)]
        slots[step][...] = block.reshape(slots[step].shape).astype(slots[step].dtype)


def norm_back(block, d_normal, gain):
    wide = block.astype(f32)
    scale = lax.rsqrt(jnp.mean(wide * wide, axis=-1, keepdims=True) + epsilon)
    d_scaled = d_normal * gain.reshape(1, -1)
    along = jnp.mean(d_scaled * wide, axis=-1, keepdims=True)
    return scale * d_scaled - wide * (scale * scale * scale * along)


def fold_rows(block):
    return jnp.concatenate([block[:, 128 * nth : 128 * (nth + 1)] for nth in range(4)], axis=0)


def unfold_rows(block):
    return jnp.concatenate([block[8 * nth : 8 * (nth + 1)] for nth in range(4)], axis=1)


def scalar_flag(condition):
    return jnp.where(condition, 1.0, 0.0)


def result_kernel(
    place, both, gain, gated, out_proj, d_gate, d_xbc, d_first, d_second, low, high, d_step, in_proj, step_proj,
    layer, base, to_both, d_whole,
):
    rows = both.shape[0] // 2
    inner = out_proj.shape[0]
    branch = mm(gated[...], out_proj[...])
    layer[...] = (branch[:rows] + mirror_wide(branch[rows:])).astype(bf16)
    d_whole[: 2 * rows, :] = d_xbc[...]
    edges = jnp.concatenate([d_first[...], d_second[...]], axis=0)
    d_whole[2 * rows :, :] = edges.astype(bf16)
    through = mm_cols(d_whole[...], in_proj[:, inner:])
    d_normal = mm_cols(d_gate[...], in_proj[:, :inner]) + through[: 2 * rows]
    d_normal = d_normal + mm(d_step[...], step_proj[...])
    d_wide = norm_back(both[...], d_normal, gain[...])
    base[...] = d_wide[:rows] + mirror_wide(d_wide[rows:])
    first = norm_back(low[8:, :], through[2 * rows : 2 * rows + 8], gain[...])
    second = norm_back(mirror_exact(high[...])[8:, :], through[2 * rows + 8 :], gain[...])
    at_start = (place[0] + place[1] + place[2]) == 0
    at_end = (place[0] + place[1] + place[2]) == 3 * (SIDE - 1)
    to_both[32:, :] = fold_rows(first * (1.0 - scalar_flag(at_start))).astype(bf16)
    to_both[:32, :] = fold_rows(mirror_wide(second) * (1.0 - scalar_flag(at_end))).astype(bf16)


def total_of(refs):
    total = refs[0][...].astype(f32)
    for ref in refs[1:]:
        total = total + ref[...].astype(f32)
    return total


def first_sum_kernel(place, *refs):
    from_x, from_y, by_y, by_x, kept = refs[:5], refs[5:10], refs[10:14], refs[14:18], refs[18]
    parted, whole = refs[19], refs[20]
    parted[...] = ring_total(*from_x).reshape(parted.shape)
    whole[...] = ring_total(*from_y)
    send_y(place, parted, by_y)
    columns = whole.shape[1]
    chunk = whole.shape[0] // SIDE
    for step in range(SIDE):
        to = lax.rem(place[0] + step, SIDE)
        block = whole[pl.ds(pl.multiple_of(to * chunk, chunk), chunk), :]
        by_x[step][:, :columns] = block.astype(by_x[step].dtype)
    high = from_y[3][:32, columns:].astype(f32)
    low = from_y[4][:32, columns:].astype(f32)
    on_high = scalar_flag((place[2] == 0) & (place[1] == SIDE - 1))
    on_low = scalar_flag((place[2] == SIDE - 1) & (place[1] == 0))
    by_x[1][:, columns:] = (high * on_high).astype(bf16)
    by_x[3][:, columns:] = (low * on_low).astype(bf16)
    kept[:32, :] = high * (1.0 - on_high)
    kept[32:, :] = low * (1.0 - on_low)


def second_sum_kernel(place, *refs):
    first, second, kept, by_z, kept_on, keep = refs[:4], refs[4:8], refs[8], refs[9:13], refs[13], refs[14]
    columns = first[0].shape[1]
    high = kept[:32, :] + second[1][:, columns:].astype(f32)
    low = kept[32:, :] + second[3][:, columns:].astype(f32)
    first = total_of(first).reshape(SIDE, 8, -1)
    total = second[0][...]
    for step in range(1, SIDE):
        total = total + second[step][:, :columns].astype(f32)
    second = total.reshape(SIDE, 8, -1)
    above = scalar_flag(place[2] == 0)
    below = scalar_flag(place[2] == SIDE - 1)
    keep[:, 0] = first
    keep[:, 1] = second
    for step in range(SIDE):
        block = keep[lax.rem(place[1] + step, SIDE)].reshape(16, columns)
        by_z[step][:, :columns] = block.astype(by_z[step].dtype)
    for step, edge, share in ((1, high, above), (3, low, below)):
        edge = edge * share
        by_z[step][:, columns:] = jnp.concatenate([edge[:16], edge[16:]], axis=1).astype(bf16)
    kept_on[:32, :] = high * (1.0 - above)
    kept_on[32:, :] = low * (1.0 - below)


def last_sum_kernel(own, up, across, down, kept, base, grad_in, grad_out, grad):
    joined = own.shape[1]
    total = own[...] + up[:, :joined].astype(f32) + across[...].astype(f32) + down[:, :joined].astype(f32)
    columns = grad_out.shape[1]
    grad_out[:8, :] = total[:8, :columns]
    grad_out[8:, :] = total[:8, columns : 2 * columns]
    grad_in[...] = jnp.concatenate([total[8:, : 2 * columns], total[:8, 2 * columns :], total[8:, 2 * columns :]], axis=1)
    edges = []
    for nth, recv in enumerate((up, down)):
        recv = recv[:, joined:].astype(f32)
        recv = jnp.concatenate([recv[:, :128], recv[:, 128:]], axis=0)
        edges.append(unfold_rows(kept[32 * nth : 32 * nth + 32, :] + recv))
    rows = base.shape[0]
    whole = jnp.concatenate([base[:8, :] + edges[0], base[8 : rows - 8, :], base[rows - 8 :, :] + edges[1]], axis=0)
    grad[...] = whole.astype(bf16)


def axis_pairs(stride, step):
    pairs = []
    for source in range(COUNT):
        digit = source // stride % SIDE
        pairs.append((source, source + ((digit + step) % SIDE - digit) * stride))
    return pairs


def exchange(parts, stride):
    return [parts[0]] + [lax.ppermute(parts[step], "seq", axis_pairs(stride, step)) for step in range(1, SIDE)]


def around(to_right, to_left, stride):
    return (
        lax.ppermute(to_right, "seq", axis_pairs(stride, 1)),
        lax.ppermute(to_left, "seq", axis_pairs(stride, SIDE - 1)),
    )


def transpose_over(parts, groups):
    return lax.all_to_all(parts, "seq", 0, 0, axis_index_groups=groups)


def slots(rows, columns, kind):
    return [((rows, columns), kind)] + [((rows, columns), bf16)] * (SIDE - 1)


def shards(
    sequence,
    upstream,
    norm_gain,
    in_proj,
    step_proj,
    conv_weight,
    conv_bias,
    step_bias,
    decay_log,
    skip_gain,
    out_proj,
):
    rows, width = sequence.shape
    inner = out_proj.shape[0]
    heads = step_bias.shape[0]
    state = inner // heads * 2
    channels = conv_weight.shape[1]
    both_rows = 2 * rows
    stride_x, stride_z, stride_y = SIDE * SIDE, SIDE, 1
    index = lax.axis_index("seq")
    place = jnp.stack([index // stride_x, index // stride_z % SIDE, index % SIDE]).astype(jnp.int32)
    beside = [[SIDE * base + digit for digit in range(SIDE)] for base in range(COUNT // SIDE)]
    across = [[base + SIDE * digit for digit in range(COUNT // SIDE)] for base in range(SIDE)]
    upward = [(i, i + 1) for i in range(COUNT - 1)]
    downward = [(i + 1, i) for i in range(COUNT - 1)]
    low = lax.ppermute(sequence[rows - 16 :], "seq", upward)
    high = lax.ppermute(sequence[:16], "seq", downward)
    step_turned = step_proj.T
    payload, both, normal, normal_halo, cot, gate, conv, d_gated, raw, step, cumul, cumul_t = call(
        pre_kernel,
        [
            ((SIDE, inner + 16, state), bf16),
            ((both_rows, width), bf16),
            ((both_rows, width), bf16),
            ((32, width), bf16),
            ((both_rows, width), bf16),
            ((both_rows, inner), bf16),
            ((both_rows, channels), bf16),
            ((both_rows, inner), bf16),
            ((both_rows, heads), f32),
            ((both_rows, heads), f32),
            ((both_rows, heads), f32),
            ((2 * heads, rows), f32),
        ],
        (
            sequence, upstream, low, high, norm_gain, in_proj, step_turned,
            conv_weight, conv_bias, step_bias, decay_log, out_proj,
        ),
        [pltpu.VMEM((rows + 8, channels), f32)],
    )
    got = transpose_over(payload, beside)
    (summary,) = call(group_kernel, [((COUNT // SIDE, 72, state), bf16)], (got,), vmem=16 * 2**20)
    summaries = transpose_over(summary, across)
    inner_values = call(
        intra_kernel,
        [((both_rows, inner), bf16)] * 7
        + [
            ((both_rows, channels), bf16),
            ((both_rows, 2 * state), bf16),
            ((both_rows, 2 * state), f32),
            ((both_rows, 2 * heads), f32),
            ((width, both_rows), bf16),
            ((width, 32), bf16),
        ],
        (conv, gate, d_gated, step, cumul, cumul_t, normal, normal_halo, skip_gain),
        flops=8 * 10**9,
    )
    normal_t, halo_t = inner_values[-2:]
    groups = COUNT // SIDE
    (scanned,) = call(
        scan_kernel,
        [((groups, 64, state), bf16)],
        (summaries,),
        [pltpu.VMEM((groups * 72, state), f32), pltpu.VMEM((groups * 64, state), f32)],
        vmem=16 * 2**20,
    )
    entering = transpose_over(scanned, across)
    (spread,) = call(spread_kernel, [((SIDE, inner, state), bf16)], (got, entering), vmem=16 * 2**20)
    states = transpose_over(spread, beside)
    eighth = 8 * COUNT // SIDE
    joined = inner + channels // 2
    gated, d_gate, d_xbc, d_first, d_second, d_step, *parts = call(
        post_kernel,
        [
            ((both_rows, inner), bf16),
            ((both_rows, inner), bf16),
            ((both_rows, channels), bf16),
            ((8, channels), f32),
            ((8, channels), f32),
            ((both_rows, heads), bf16),
        ]
        + slots(eighth, joined, bf16) * 2,
        (
            place, states, *inner_values[:-2], raw, step, cumul,
            step_bias, decay_log, conv_weight, cot, normal_t, halo_t,
        ),
        [
            pltpu.VMEM((rows + 24, channels), f32),
            pltpu.VMEM((32, channels), bf16),
            pltpu.VMEM((8 * COUNT, joined), bf16),
            pltpu.VMEM((COUNT // SIDE, SIDE, 8, joined), f32),
        ],
        scalars=1,
    )
    layer_out, base, to_both = call(
        result_kernel,
        [((rows, width), bf16), ((rows, width), f32), ((64, 128), bf16)],
        (
            place, both, norm_gain, gated, out_proj, d_gate, d_xbc, d_first, d_second, low, high, d_step,
            in_proj, step_turned,
        ),
        [pltpu.VMEM((both_rows + 16, channels), bf16)],
        scalars=1,
        flops=8 * 10**9,
    )
    keep_x, base_x, right_x, left_x, keep_y, base_y, right_y, left_y = parts
    right_x, left_x = around(right_x, left_x, stride_x)
    right_y, left_y = around(right_y, left_y, stride_y)
    relayed = call(
        relay_kernel,
        [((eighth // 2, joined), bf16)] * 2 + [((eighth // 2, joined + 128), bf16)] * 2,
        (base_x, right_x, left_x, base_y, right_y, left_y, to_both),
        vmem=16 * 2**20,
    )
    from_x = [keep_x, right_x, left_x, *around(relayed[0], relayed[1], stride_x)]
    from_y = [keep_y, right_y, left_y, *around(relayed[2], relayed[3], stride_y)]
    small = eighth // SIDE
    *parts, kept = call(
        first_sum_kernel,
        slots(small, joined, f32)
        + [((small, joined), f32), ((small, joined + 128), bf16), ((small, joined), bf16), ((small, joined + 128), bf16)]
        + [((64, 128), f32)],
        (place, *from_x, *from_y),
        [pltpu.VMEM((SIDE, SIDE, 8, joined), f32), pltpu.VMEM((eighth, joined), f32)],
        scalars=1,
        vmem=16 * 2**20,
    )
    first = exchange(parts[:4], stride_y)
    second = exchange(parts[4:], stride_x)
    *parts, kept = call(
        second_sum_kernel,
        [((16, joined), f32), ((16, joined + 256), bf16), ((16, joined), bf16), ((16, joined + 256), bf16)]
        + [((64, 128), f32)],
        (place, *first, *second, kept),
        [pltpu.VMEM((SIDE, 2, 8, joined), f32)],
        scalars=1,
        vmem=16 * 2**20,
    )
    last = exchange(parts, stride_z)
    grad_in_proj, grad_out_proj, grad_input = call(
        last_sum_kernel,
        [((8, inner + channels), f32), ((16, width), f32), ((rows, width), bf16)],
        (*last, kept, base),
        vmem=16 * 2**20,
    )
    return (layer_out, grad_input, grad_in_proj, grad_out_proj)


def solution(mesh):
    rows = P(("batch", "seq"), None)
    return jax.shard_map(
        shards,
        mesh=mesh,
        in_specs=(rows, rows) + (P(),) * 9,
        out_specs=(rows,) * 4,
        check_vma=False,
    )
```

```python
import functools

import jax
import jax.numpy as jnp
from jax import lax
from jax.experimental import pallas as pl
from jax.experimental.pallas import tpu as pltpu
from jax.sharding import PartitionSpec as P

epsilon = 1e-06
SIDE = 4
COUNT = SIDE**3
f32 = jnp.float32
bf16 = jnp.bfloat16
INTERPRET = False


def call(body, outs, args, scratch=(), scalars=0, unused=0, flops=10**9, vmem=58 * 2**20):
    after = len(args) - unused
    specs = [pl.BlockSpec(memory_space=pltpu.SMEM)] * scalars
    specs += [pl.BlockSpec(memory_space=pltpu.VMEM)] * (after - scalars)
    specs += [pl.BlockSpec(memory_space=pl.ANY)] * unused
    moved = sum(a.size * a.dtype.itemsize for a in args[:after])

    def used(*refs):
        body(*refs[:after], *refs[len(args) :])

    return pl.pallas_call(
        used,
        out_shape=[jax.ShapeDtypeStruct(shape, kind) for shape, kind in outs],
        in_specs=specs,
        out_specs=[pl.BlockSpec(memory_space=pltpu.VMEM)] * len(outs),
        scratch_shapes=list(scratch),
        compiler_params=pltpu.CompilerParams(vmem_limit_bytes=vmem),
        cost_estimate=pl.CostEstimate(flops=flops, bytes_accessed=moved, transcendentals=0),
        interpret=INTERPRET,
    )(*args)


def mm(left, right):
    return lax.dot_general(left, right, (((1,), (0,)), ((), ())), preferred_element_type=f32)


def mm_cols(left, right):
    return lax.dot_general(left, right, (((1,), (1,)), ((), ())), preferred_element_type=f32)


def mm_rows(left, right):
    return lax.dot_general(left, right, (((0,), (0,)), ((), ())), preferred_element_type=f32)


def iota(shape, dim):
    return lax.broadcasted_iota(jnp.int32, shape, dim)


def ones_where(mask):
    return jnp.where(mask, 1.0, 0.0).astype(bf16)


def anti(size):
    return ones_where(iota((size, size), 0) + iota((size, size), 1) == size - 1)


def pieces_of(value, count):
    found = []
    for _ in range(count):
        piece = value.astype(bf16)
        found.append(piece)
        value = value - piece.astype(f32)
    return found


def mirror_exact(block):
    turned = mm(block, anti(block.shape[1])).astype(bf16)
    return mm(anti(block.shape[0]), turned).astype(bf16)


def mirror_wide(block):
    high, low = pieces_of(block, 2)
    return mirror_exact(high).astype(f32) + mirror_exact(low).astype(f32)


def head_mask(heads, width):
    lanes = heads * width
    return ones_where(iota((heads, lanes), 0) == iota((heads, lanes), 1) // width)


def expand(value, mask):
    found = pieces_of(value, 3)
    return mm(jnp.concatenate(found, axis=1), jnp.concatenate([mask] * 3, axis=0))


def fold(value, mask, count=2):
    total = None
    for piece in pieces_of(value, count):
        part = mm_cols(piece, mask)
        total = part if total is None else total + part
    return total


def triangle(size, low):
    rows, cols = iota((size, size), 0), iota((size, size), 1)
    return rows >= cols if low else rows <= cols


def tri_sum(mask, value):
    width = value.shape[1]
    total = mm(ones_where(mask), jnp.concatenate(pieces_of(value, 3), axis=1))
    return total[:, :width] + total[:, width : 2 * width] + total[:, 2 * width :]


def tri_sum_turned(mask, value):
    width = value.shape[1]
    total = mm_rows(jnp.concatenate(pieces_of(value, 3), axis=1), ones_where(mask))
    return total[:width] + total[width : 2 * width] + total[2 * width :]


def softplus(value):
    return jnp.maximum(value, 0.0) + jnp.log1p(jnp.exp(-jnp.abs(value)))


def sigmoid(value):
    return 1.0 / (1.0 + jnp.exp(-value))


def norm_rows(block, gain):
    wide = block.astype(f32)
    scale = lax.rsqrt(jnp.mean(wide * wide, axis=-1, keepdims=True) + epsilon)
    return (wide * scale * gain.reshape(1, -1)).astype(bf16)


def pre_kernel(
    seq, up, low, high, gain, in_proj, step_proj, conv_w, conv_b, step_bias, decay_log, out_proj,
    payload, both, normal, normal_halo, cot, gate, conv, d_gated, raw, step, cumul,
    ext,
):
    rows = seq.shape[0]
    inner = out_proj.shape[0]
    heads = step_bias.shape[0]
    state = (conv_w.shape[1] - inner) // 2
    taps = conv_w.shape[0]
    turned = mm(jnp.concatenate([seq[...], up[...], high[...]], axis=0), anti(seq.shape[1])).astype(bf16)
    flip = anti(rows)
    both[:rows, :] = seq[...]
    both[rows:, :] = mm(flip, turned[:rows]).astype(bf16)
    cot[:rows, :] = up[...]
    cot[rows:, :] = mm(flip, turned[rows : 2 * rows]).astype(bf16)
    halo = jnp.concatenate([low[...], mm(anti(high.shape[0]), turned[2 * rows :]).astype(bf16)], axis=0)
    normal[...] = norm_rows(both[...], gain[...])
    normal_halo[...] = norm_rows(halo, gain[...])
    gate[...] = mm(normal[...], in_proj[:, :inner]).astype(bf16)
    xbc = mm(normal[...], in_proj[:, inner:]).astype(bf16).astype(f32)
    xbc_halo = mm(normal_halo[...], in_proj[:, inner:]).astype(bf16).astype(f32)
    raw[...] = mm_cols(normal[...], step_proj[...])
    d_gated[...] = mm_cols(cot[...], out_proj[...]).astype(bf16)
    margin = low.shape[0]
    mask = head_mask(heads, inner // heads)
    ends = []
    for frame in range(2):
        at = slice(frame * rows, (frame + 1) * rows)
        ext[:8, :] = xbc_halo[(frame + 1) * margin - 8 : (frame + 1) * margin, :]
        ext[8:, :] = xbc[at, :]
        found = conv_b[...].reshape(1, -1)
        for tap in range(taps):
            start = 9 - taps + tap
            found = found + ext[start : start + rows, :] * conv_w[tap : tap + 1, :]
        conv[at, :] = found.astype(bf16)
        act = found * sigmoid(found)
        size = softplus(raw[at, :] + step_bias[...].reshape(1, -1))
        decay = -jnp.exp(decay_log[...].reshape(1, -1)) * size
        upto = tri_sum(triangle(rows, True), decay)
        step[at, :] = size
        cumul[at, :] = upto
        end = upto[rows - 1 : rows, :]
        ends.append(end)
        spread = expand(jnp.concatenate([size * jnp.exp(end - upto), jnp.exp(upto)], axis=0), mask)
        driven = (act[:, :inner] * spread[:rows]).astype(bf16)
        local = mm_rows(driven, act[:, inner : inner + state].astype(bf16))
        wide = gate[at, :].astype(f32)
        d_mixed = d_gated[at, :].astype(f32) * (wide * sigmoid(wide))
        back = mm_rows((d_mixed * spread[rows:]).astype(bf16), act[:, inner + state :].astype(bf16))
        part = inner // SIDE
        for place, block in ((frame, local), (2 + frame, back)):
            block = block.astype(bf16).reshape(SIDE, part, state)
            payload[:, place * part : (place + 1) * part, :] = block
    packed = pack_totals(ends, heads, state)
    for to in range(SIDE):
        shifted = ones_where(iota((16, heads), 1) == iota((16, heads), 0) + to * (heads // SIDE))
        payload[to, inner:, :] = mm(shifted, packed).astype(bf16)


def pack_totals(ends, heads, state):
    chosen = iota((heads, heads), 0) == iota((heads, heads), 1)
    lanes = iota((heads, state), 1)
    packed = jnp.zeros((heads, state), f32)
    for frame in range(2):
        column = jnp.sum(jnp.where(chosen, ends[frame], 0.0), axis=1, keepdims=True)
        packed = pack_column(packed, column, lanes, frame)
    return packed.astype(bf16)


def pack_column(packed, column, lanes, frame):
    for nth, piece in enumerate(pieces_of(column, 3)):
        packed = jnp.where(lanes == 3 * frame + nth, piece.astype(f32), packed)
    return packed


def unpack_column(packed, frame):
    at = 3 * frame
    return (packed[:, at + 2 : at + 3] + packed[:, at + 1 : at + 2]) + packed[:, at : at + 1]


SCANS = ((0, False), (1, True), (0, True), (1, False))


def chain(got, totals, place, state, visit):
    frame, turned = SCANS[place]
    part = state.shape[0]
    size = part // SIDE
    order = range(SIDE - 1, -1, -1) if turned else range(SIDE)
    for at in order:
        visit(at, state)
        grown = jnp.exp(totals[at][frame])
        factors = [
            jnp.broadcast_to(grown[head : head + 1, :], (size, 1)) for head in range(part // size)
        ]
        state = jnp.concatenate(factors, axis=0) * state
        state = state + got[at, place * part : (place + 1) * part, :].astype(f32)
    return state


def tails_of(got, inner):
    found = []
    for at in range(SIDE):
        tail = got[at, inner:, :].astype(f32)
        found.append([unpack_column(tail, frame) for frame in range(2)])
    return found


def group_kernel(got, out):
    state = got.shape[2]
    inner = got.shape[1] - 16
    part = inner // SIDE
    totals = tails_of(got, inner)
    for place in range(4):
        block = chain(got, totals, place, jnp.zeros((part, state), f32), lambda at, value: None)
        out[:, 16 * place : 16 * place + 16, :] = block.reshape(16, 16, state).astype(bf16)
    lanes = iota((16, state), 1)
    packed = jnp.zeros((16, state), f32)
    for frame in range(2):
        column = jnp.maximum(totals[0][frame], -110.0)
        for at in range(1, SIDE):
            column = column + jnp.maximum(totals[at][frame], -110.0)
        packed = pack_column(packed, column, lanes, frame)
    chosen = ones_where(iota((16, 16), 1) == iota((16, 16), 0) // SIDE)
    packed = mm(chosen, packed.astype(bf16))
    out[:, 64:, :] = jnp.broadcast_to(packed.reshape(16, 1, state), (16, 8, state)).astype(bf16)


def spread_kernel(got, entering, out):
    state = got.shape[2]
    inner = got.shape[1] - 16
    part = inner // SIDE
    totals = tails_of(got, inner)
    for place in range(4):

        def visit(at, value, place=place):
            out[at, place * part : (place + 1) * part, :] = value.astype(bf16)

        block = entering[:, 16 * place : 16 * place + 16, :].astype(f32).reshape(part, state)
        chain(got, totals, place, block, visit)


def scan_kernel(got, out, wide, done):
    count, rows, state = got.shape
    wide[...] = got[...].astype(f32).reshape(count * rows, state)
    tails = wide[pl.ds(64, count, stride=rows), :]
    above = iota((count, count), 0)
    beside = iota((count, count), 1)
    after = ones_where(above > beside)
    weights = []
    for frame in range(2):
        column = jnp.maximum(unpack_column(tails, frame), -110.0)
        line = jnp.sum(jnp.where(above == beside, column, 0.0), axis=0, keepdims=True)
        between = None
        for piece in pieces_of(jnp.where(beside < above, line, 0.0), 3):
            part = mm(piece, after)
            between = part if between is None else between + part
        found = jnp.where(above > beside, jnp.exp(between), 0.0)
        weights.append(pieces_of(found, 2))
    for place, (frame, turned) in enumerate(SCANS):
        pair = weights[frame]
        block = jnp.concatenate(
            [wide[pl.ds(16 * place + row, count, stride=rows), :] for row in range(16)], axis=1
        ).astype(bf16)
        if turned:
            mixed = mm_rows(jnp.concatenate(pair, axis=1), block)
        else:
            mixed = mm(jnp.concatenate(pair, axis=0), block)
        mixed = mixed[:count] + mixed[count:]
        for row in range(16):
            done[pl.ds(16 * place + row, count, stride=64), :] = mixed[:, state * row : state * (row + 1)]
    out[...] = done[...].reshape(count, 64, state).astype(bf16)


def intra_kernel(
    conv, gate, d_gated, step, cumul, decay_log, normal, normal_halo, skip_gain,
    silus, d_gates, pushed, mixed, d_inputs, lefts, held_back, d_convs, bc, d_bc, sums_out, normal_t, halo_t,
):
    for source, target in ((normal, normal_t), (normal_halo, halo_t)):
        count = source.shape[0]
        same = iota((count, count), 0) == iota((count, count), 1)
        target[...] = mm_rows(source[...], ones_where(same)).astype(bf16)
    rows = conv.shape[0] // 2
    inner = gate.shape[1]
    heads = step.shape[1]
    state = (conv.shape[1] - inner) // 2
    mask = head_mask(heads, inner // heads)
    lower = triangle(rows, True)
    first = iota((rows, 2 * inner // heads), 1) < inner // heads
    wide_pair = 2 * inner // heads
    skip = expand(jnp.broadcast_to(skip_gain[...].reshape(1, -1), (8, heads)), mask)[:1]
    for frame in range(2):
        at = slice(frame * rows, (frame + 1) * rows)
        found = conv[at, :].astype(f32)
        share = sigmoid(found)
        act = found * share
        d_convs[at, :] = (share * (1.0 + found * (1.0 - share))).astype(bf16)
        bc[at, :] = act[:, inner:].astype(bf16)
        bmat, cmat = bc[at, :state], bc[at, state:]
        upto = cumul[at, :]
        end = upto[rows - 1 : rows, :]
        spread = expand(jnp.concatenate([step[at, :], jnp.exp(upto), jnp.exp(end - upto)], axis=0), mask)
        sizes, grown, left = spread[:rows], spread[rows : 2 * rows], spread[2 * rows :]
        inputs = act[:, :inner]
        driven = inputs * sizes
        lefts[at, :] = (left * inputs).astype(bf16)
        held_back[at, :] = (left * driven).astype(bf16)
        wide = gate[at, :].astype(f32)
        opened = sigmoid(wide)
        silu = wide * opened
        silus[at, :] = silu.astype(bf16)
        d_out = d_gated[at, :].astype(f32)
        d_gates[at, :] = (d_out * (opened * (1.0 + wide * (1.0 - opened)))).astype(bf16)
        d_mixed = d_out * silu
        pushed[at, :] = (d_mixed * grown).astype(bf16)
        scores = mm_cols(cmat, bmat)
        line = tri_sum_turned(triangle(rows, False), -jnp.exp(decay_log[...].reshape(1, -1)) * step[at, :])
        d_scores = jnp.zeros((rows, rows), f32)
        sums, by_size = [], []
        for pair in range(heads // 2):
            lanes = slice(pair * wide_pair, (pair + 1) * wide_pair)
            decays = []
            for head in (2 * pair, 2 * pair + 1):
                differ = upto[:, head : head + 1] - line[head : head + 1, :]
                decays.append(jnp.exp(jnp.where(lower, differ, -1e30)))
            weights = [(decay * scores).astype(bf16) for decay in decays]
            drive, d_mix = driven[:, lanes], d_mixed[:, lanes]
            drive_bf, d_mix_bf = drive.astype(bf16), d_mix.astype(bf16)
            drive_two = jnp.concatenate(
                [jnp.where(first, drive, 0.0), jnp.where(first, 0.0, drive)], axis=0
            ).astype(bf16)
            d_mix_two = jnp.concatenate(
                [jnp.where(first, d_mix, 0.0), jnp.where(first, 0.0, d_mix)], axis=0
            ).astype(bf16)
            mix = mm(jnp.concatenate(weights, axis=1), drive_two)
            d_weights = mm_cols(d_mix_two, drive_bf)
            d_drive = mm_rows(jnp.concatenate(weights, axis=0), d_mix_two)
            d_scores = d_scores + decays[0] * d_weights[:rows] + decays[1] * d_weights[rows:]
            mixed[at, lanes] = (mix + skip[:, lanes] * inputs[:, lanes]).astype(bf16)
            d_inputs[at, lanes] = (skip[:, lanes] * d_mix + d_drive * sizes[:, lanes]).astype(bf16)
            by_size.append(d_drive * inputs[:, lanes])
            sums.append(d_mix_bf.astype(f32) * mix - drive_bf.astype(f32) * d_drive)
        d_scores = d_scores.astype(bf16)
        d_bc[at, :state] = mm_rows(d_scores, cmat)
        d_bc[at, state:] = mm(d_scores, bmat)
        sums_out[at, :heads] = fold(jnp.concatenate(sums, axis=1), mask)
        sums_out[at, heads:] = fold(jnp.concatenate(by_size, axis=1), mask)


def post_kernel(
    place, got, silus, d_gates, pushed, mixed, d_inputs, lefts, held_back, d_convs, bc, d_bc, sums,
    raw, step, cumul, step_bias, decay_log, conv_w, cot, normal_t, halo_t,
    gated, d_gate, d_xbc, d_first, d_second, d_step, *refs,
):
    by_x, by_y, ext, d_conv_out, whole, parted = refs[:4], refs[4:8], refs[8], refs[9], refs[10], refs[11]
    rows = silus.shape[0] // 2
    inner = silus.shape[1]
    heads = step.shape[1]
    state = bc.shape[1] // 2
    mask = head_mask(heads, inner // heads)
    for frame in range(2):
        at = slice(frame * rows, (frame + 1) * rows)
        upto = cumul[at, :]
        size = step[at, :]
        end = upto[rows - 1 : rows, :]
        spread = expand(jnp.concatenate([jnp.exp(upto), size * jnp.exp(end - upto)], axis=0), mask)
        part = inner // SIDE
        carried = got[:, frame * part : (frame + 1) * part, :].reshape(inner, state)
        reach = got[:, (2 + frame) * part : (3 + frame) * part, :].reshape(inner, state)
        read = mm_cols(bc[at, state:], carried)
        full = mixed[at, :].astype(f32) + spread[:rows] * read
        gated[at, :] = (full * silus[at, :].astype(f32)).astype(bf16)
        d_gate[at, :] = (full * d_gates[at, :].astype(f32)).astype(bf16)
        d_cmat = d_bc[at, state:] + mm(pushed[at, :], carried)
        answer = mm_cols(bc[at, :state], reach)
        d_bmat = d_bc[at, :state] + mm(held_back[at, :], reach)
        products = carried.astype(f32) * reach.astype(f32)
        met = jnp.sum(products.reshape(heads, inner // heads, state), axis=1)
        met = jnp.sum(met, axis=1, keepdims=True)
        met = jnp.sum(jnp.where(iota((heads, heads), 0) == iota((heads, heads), 1), met, 0.0), axis=0, keepdims=True)
        folded = fold(
            jnp.concatenate([lefts[at, :].astype(f32) * answer, pushed[at, :].astype(f32) * read], axis=0), mask, 1
        )
        by_size, entered = folded[:rows], folded[rows:]
        held = by_size * size
        d_end = jnp.exp(end) * met + jnp.sum(held, axis=0, keepdims=True)
        d_decay = tri_sum(triangle(rows, False), sums[at, :heads] + entered - held) + d_end
        d_size = sums[at, heads:] + by_size - jnp.exp(decay_log[...].reshape(1, -1)) * d_decay
        d_step[at, :] = (d_size * sigmoid(raw[at, :] + step_bias[...].reshape(1, -1))).astype(bf16)
        d_act = jnp.concatenate([d_inputs[at, :].astype(f32) + spread[rows:] * answer, d_bmat, d_cmat], axis=1)
        margin = halo_t.shape[1] // 2
        ext[:margin, :] = jnp.zeros((margin, ext.shape[1]), f32)
        ext[margin : margin + rows, :] = d_act * d_convs[at, :].astype(f32)
        ext[margin + rows :, :] = jnp.zeros((8, ext.shape[1]), f32)
        taps = conv_w.shape[0]
        total = None
        for tap in range(taps):
            start = taps - 1 - tap
            part = ext[start : start + margin + rows, :] * conv_w[tap : tap + 1, :]
            total = part if total is None else total + part
        d_xbc[at, :] = total[margin:].astype(bf16)
        d_conv_out[frame * margin : (frame + 1) * margin, :] = total[:margin].astype(bf16)
        (d_first, d_second)[frame][...] = total[margin - 8 : margin]
    columns = cot.shape[1]
    half = d_xbc.shape[1] // 2
    out_term = mm_rows(gated[...], cot[...]).reshape(COUNT, 2, 8, columns)
    gate_term = mm(normal_t[...], d_gate[...]).reshape(COUNT // SIDE, SIDE, 8, inner)
    in_term = mm(normal_t[...], d_xbc[...]) + mm(halo_t[...], d_conv_out[...])
    whole[:, :columns] = out_term[:, 0].reshape(-1, columns).astype(bf16)
    whole[:, columns : 2 * columns] = out_term[:, 1].reshape(-1, columns).astype(bf16)
    whole[:, 2 * columns :] = in_term[:, :half].astype(bf16)
    parted[:, :, :, :inner] = gate_term
    parted[:, :, :, inner:] = in_term[:, half:].reshape(COUNT // SIDE, SIDE, 8, half)
    ring_out(lambda step: chunk_x(place, whole, step), by_x)
    ring_out(lambda step: chunk_y(place, parted, step), by_y)


def chunk_x(place, whole, step):
    chunk = whole.shape[0] // SIDE
    to = lax.rem(place[0] + step, SIDE)
    return whole[pl.ds(pl.multiple_of(to * chunk, chunk), chunk), :].astype(bf16)


def chunk_y(place, parted, step):
    block = parted[:, lax.rem(place[2] + step, SIDE)]
    return block.reshape(-1, block.shape[-1]).astype(bf16)


def ring_out(chunk_of, slots):
    keep, base, right, left = slots
    half = keep.shape[0] // 2
    keep[...] = chunk_of(0)
    ahead, opposite, behind = chunk_of(1), chunk_of(2), chunk_of(3)
    base[:half, :], base[half:, :] = ahead[:half], behind[half:]
    right[:half, :], right[half:, :] = opposite[:half], ahead[half:]
    left[:half, :], left[half:, :] = behind[:half], opposite[half:]


def relay_kernel(base_x, right_x, left_x, base_y, right_y, left_y, to_both, *outs):
    for base, right, left, on_right, on_left in (
        (base_x, right_x, left_x, outs[0], outs[1]),
        (base_y, right_y, left_y, outs[2], outs[3]),
    ):
        half = base.shape[0] // 2
        columns = base.shape[1]
        on_right[:, :columns] = (base[:half, :].astype(f32) + right[:half, :].astype(f32)).astype(bf16)
        on_left[:, :columns] = (base[half:, :].astype(f32) + left[half:, :].astype(f32)).astype(bf16)
    outs[2][:32, columns:] = to_both[:32, :]
    outs[3][:32, columns:] = to_both[32:, :]
    for target in outs[2:]:
        target[32:, columns:] = jnp.zeros((32, 128), bf16)


def ring_total(keep, right, left, on_right, on_left):
    half = keep.shape[0] // 2
    columns = keep.shape[1]
    first = keep[:half, :].astype(f32) + left[:half, :].astype(f32) + on_right[:, :columns].astype(f32)
    second = keep[half:, :].astype(f32) + right[half:, :].astype(f32) + on_left[:, :columns].astype(f32)
    return jnp.concatenate([first, second], axis=0)


def send_x(place, whole, slots):
    chunk = whole.shape[0] // SIDE
    for step in range(SIDE):
        to = lax.rem(place[0] + step, SIDE)
        block = whole[pl.ds(pl.multiple_of(to * chunk, chunk), chunk), :]
        slots[step][...] = block.astype(slots[step].dtype)


def send_y(place, parted, slots):
    for step in range(SIDE):
        block = parted[:, lax.rem(place[2] + step, SIDE)]
        slots[step][...] = block.reshape(slots[step].shape).astype(slots[step].dtype)


def norm_back(block, d_normal, gain):
    wide = block.astype(f32)
    scale = lax.rsqrt(jnp.mean(wide * wide, axis=-1, keepdims=True) + epsilon)
    d_scaled = d_normal * gain.reshape(1, -1)
    along = jnp.mean(d_scaled * wide, axis=-1, keepdims=True)
    return scale * d_scaled - wide * (scale * scale * scale * along)


def fold_rows(block):
    return jnp.concatenate([block[:, 128 * nth : 128 * (nth + 1)] for nth in range(4)], axis=0)


def unfold_rows(block):
    return jnp.concatenate([block[8 * nth : 8 * (nth + 1)] for nth in range(4)], axis=1)


def scalar_flag(condition):
    return jnp.where(condition, 1.0, 0.0)


def result_kernel(
    place, both, gain, gated, out_proj, d_gate, d_xbc, d_first, d_second, low, high, d_step, in_proj, step_proj,
    layer, base, to_both, d_whole,
):
    rows = both.shape[0] // 2
    inner = out_proj.shape[0]
    branch = mm(gated[...], out_proj[...])
    layer[...] = (branch[:rows] + mirror_wide(branch[rows:])).astype(bf16)
    d_whole[: 2 * rows, :] = d_xbc[...]
    edges = jnp.concatenate([d_first[...], d_second[...]], axis=0)
    d_whole[2 * rows :, :] = edges.astype(bf16)
    through = mm_cols(d_whole[...], in_proj[:, inner:])
    d_normal = mm_cols(d_gate[...], in_proj[:, :inner]) + through[: 2 * rows]
    d_normal = d_normal + mm(d_step[...], step_proj[...])
    d_wide = norm_back(both[...], d_normal, gain[...])
    base[...] = d_wide[:rows] + mirror_wide(d_wide[rows:])
    first = norm_back(low[8:, :], through[2 * rows : 2 * rows + 8], gain[...])
    second = norm_back(mirror_exact(high[...])[8:, :], through[2 * rows + 8 :], gain[...])
    at_start = (place[0] + place[1] + place[2]) == 0
    at_end = (place[0] + place[1] + place[2]) == 3 * (SIDE - 1)
    to_both[32:, :] = fold_rows(first * (1.0 - scalar_flag(at_start))).astype(bf16)
    to_both[:32, :] = fold_rows(mirror_wide(second) * (1.0 - scalar_flag(at_end))).astype(bf16)


def total_of(refs):
    total = refs[0][...].astype(f32)
    for ref in refs[1:]:
        total = total + ref[...].astype(f32)
    return total


def first_sum_kernel(place, *refs):
    from_x, from_y, by_y, by_x, kept = refs[:5], refs[5:10], refs[10:14], refs[14:18], refs[18]
    parted, whole = refs[19], refs[20]
    parted[...] = ring_total(*from_x).reshape(parted.shape)
    whole[...] = ring_total(*from_y)
    send_y(place, parted, by_y)
    columns = whole.shape[1]
    chunk = whole.shape[0] // SIDE
    for step in range(SIDE):
        to = lax.rem(place[0] + step, SIDE)
        block = whole[pl.ds(pl.multiple_of(to * chunk, chunk), chunk), :]
        by_x[step][:, :columns] = block.astype(by_x[step].dtype)
    high = from_y[3][:32, columns:].astype(f32)
    low = from_y[4][:32, columns:].astype(f32)
    on_high = scalar_flag((place[2] == 0) & (place[1] == SIDE - 1))
    on_low = scalar_flag((place[2] == SIDE - 1) & (place[1] == 0))
    by_x[1][:, columns:] = (high * on_high).astype(bf16)
    by_x[3][:, columns:] = (low * on_low).astype(bf16)
    kept[:32, :] = high * (1.0 - on_high)
    kept[32:, :] = low * (1.0 - on_low)


def second_sum_kernel(place, *refs):
    first, second, kept, by_z, kept_on, keep = refs[:4], refs[4:8], refs[8], refs[9:13], refs[13], refs[14]
    columns = first[0].shape[1]
    high = kept[:32, :] + second[1][:, columns:].astype(f32)
    low = kept[32:, :] + second[3][:, columns:].astype(f32)
    first = total_of(first).reshape(SIDE, 8, -1)
    total = second[0][...]
    for step in range(1, SIDE):
        total = total + second[step][:, :columns].astype(f32)
    second = total.reshape(SIDE, 8, -1)
    above = scalar_flag(place[2] == 0)
    below = scalar_flag(place[2] == SIDE - 1)
    keep[:, 0] = first
    keep[:, 1] = second
    for step in range(SIDE):
        block = keep[lax.rem(place[1] + step, SIDE)].reshape(16, columns)
        by_z[step][:, :columns] = block.astype(by_z[step].dtype)
    for step, edge, share in ((1, high, above), (3, low, below)):
        edge = edge * share
        by_z[step][:, columns:] = jnp.concatenate([edge[:16], edge[16:]], axis=1).astype(bf16)
    kept_on[:32, :] = high * (1.0 - above)
    kept_on[32:, :] = low * (1.0 - below)


def last_sum_kernel(own, up, across, down, kept, base, grad_in, grad_out, grad):
    joined = own.shape[1]
    total = own[...] + up[:, :joined].astype(f32) + across[...].astype(f32) + down[:, :joined].astype(f32)
    columns = grad_out.shape[1]
    grad_out[:8, :] = total[:8, :columns]
    grad_out[8:, :] = total[:8, columns : 2 * columns]
    grad_in[...] = jnp.concatenate([total[8:, : 2 * columns], total[:8, 2 * columns :], total[8:, 2 * columns :]], axis=1)
    edges = []
    for nth, recv in enumerate((up, down)):
        recv = recv[:, joined:].astype(f32)
        recv = jnp.concatenate([recv[:, :128], recv[:, 128:]], axis=0)
        edges.append(unfold_rows(kept[32 * nth : 32 * nth + 32, :] + recv))
    rows = base.shape[0]
    whole = jnp.concatenate([base[:8, :] + edges[0], base[8 : rows - 8, :], base[rows - 8 :, :] + edges[1]], axis=0)
    grad[...] = whole.astype(bf16)


def axis_pairs(stride, step):
    pairs = []
    for source in range(COUNT):
        digit = source // stride % SIDE
        pairs.append((source, source + ((digit + step) % SIDE - digit) * stride))
    return pairs


def exchange(parts, stride):
    return [parts[0]] + [lax.ppermute(parts[step], "seq", axis_pairs(stride, step)) for step in range(1, SIDE)]


def around(to_right, to_left, stride):
    return (
        lax.ppermute(to_right, "seq", axis_pairs(stride, 1)),
        lax.ppermute(to_left, "seq", axis_pairs(stride, SIDE - 1)),
    )


def transpose_over(parts, groups):
    return lax.all_to_all(parts, "seq", 0, 0, axis_index_groups=groups)


def slots(rows, columns, kind):
    return [((rows, columns), kind)] + [((rows, columns), bf16)] * (SIDE - 1)


def shards(
    sequence,
    upstream,
    norm_gain,
    in_proj,
    step_proj,
    conv_weight,
    conv_bias,
    step_bias,
    decay_log,
    skip_gain,
    out_proj,
):
    rows, width = sequence.shape
    inner = out_proj.shape[0]
    heads = step_bias.shape[0]
    state = inner // heads * 2
    channels = conv_weight.shape[1]
    both_rows = 2 * rows
    stride_x, stride_z, stride_y = SIDE * SIDE, SIDE, 1
    index = lax.axis_index("seq")
    place = jnp.stack([index // stride_x, index // stride_z % SIDE, index % SIDE]).astype(jnp.int32)
    beside = [[SIDE * base + digit for digit in range(SIDE)] for base in range(COUNT // SIDE)]
    across = [[base + SIDE * digit for digit in range(COUNT // SIDE)] for base in range(SIDE)]
    upward = [(i, i + 1) for i in range(COUNT - 1)]
    downward = [(i + 1, i) for i in range(COUNT - 1)]
    low = lax.ppermute(sequence[rows - 16 :], "seq", upward)
    high = lax.ppermute(sequence[:16], "seq", downward)
    step_turned = step_proj.T
    payload, both, normal, normal_halo, cot, gate, conv, d_gated, raw, step, cumul = call(
        pre_kernel,
        [
            ((SIDE, inner + 16, state), bf16),
            ((both_rows, width), bf16),
            ((both_rows, width), bf16),
            ((32, width), bf16),
            ((both_rows, width), bf16),
            ((both_rows, inner), bf16),
            ((both_rows, channels), bf16),
            ((both_rows, inner), bf16),
            ((both_rows, heads), f32),
            ((both_rows, heads), f32),
            ((both_rows, heads), f32),
        ],
        (
            sequence, upstream, low, high, norm_gain, in_proj, step_turned,
            conv_weight, conv_bias, step_bias, decay_log, out_proj,
        ),
        [pltpu.VMEM((rows + 8, channels), f32)],
    )
    got = transpose_over(payload, beside)
    (summary,) = call(group_kernel, [((COUNT // SIDE, 72, state), bf16)], (got,), vmem=16 * 2**20)
    summaries = transpose_over(summary, across)
    inner_values = call(
        intra_kernel,
        [((both_rows, inner), bf16)] * 7
        + [
            ((both_rows, channels), bf16),
            ((both_rows, 2 * state), bf16),
            ((both_rows, 2 * state), f32),
            ((both_rows, 2 * heads), f32),
            ((width, both_rows), bf16),
            ((width, 32), bf16),
        ],
        (conv, gate, d_gated, step, cumul, decay_log, normal, normal_halo, skip_gain),
        flops=8 * 10**9,
    )
    normal_t, halo_t = inner_values[-2:]
    groups = COUNT // SIDE
    (scanned,) = call(
        scan_kernel,
        [((groups, 64, state), bf16)],
        (summaries,),
        [pltpu.VMEM((groups * 72, state), f32), pltpu.VMEM((groups * 64, state), f32)],
        vmem=16 * 2**20,
    )
    entering = transpose_over(scanned, across)
    (spread,) = call(spread_kernel, [((SIDE, inner, state), bf16)], (got, entering), vmem=16 * 2**20)
    states = transpose_over(spread, beside)
    eighth = 8 * COUNT // SIDE
    joined = inner + channels // 2
    gated, d_gate, d_xbc, d_first, d_second, d_step, *parts = call(
        post_kernel,
        [
            ((both_rows, inner), bf16),
            ((both_rows, inner), bf16),
            ((both_rows, channels), bf16),
            ((8, channels), f32),
            ((8, channels), f32),
            ((both_rows, heads), bf16),
        ]
        + slots(eighth, joined, bf16) * 2,
        (
            place, states, *inner_values[:-2], raw, step, cumul,
            step_bias, decay_log, conv_weight, cot, normal_t, halo_t,
        ),
        [
            pltpu.VMEM((rows + 24, channels), f32),
            pltpu.VMEM((32, channels), bf16),
            pltpu.VMEM((8 * COUNT, joined), bf16),
            pltpu.VMEM((COUNT // SIDE, SIDE, 8, joined), f32),
        ],
        scalars=1,
    )
    layer_out, base, to_both = call(
        result_kernel,
        [((rows, width), bf16), ((rows, width), f32), ((64, 128), bf16)],
        (
            place, both, norm_gain, gated, out_proj, d_gate, d_xbc, d_first, d_second, low, high, d_step,
            in_proj, step_turned,
        ),
        [pltpu.VMEM((both_rows + 16, channels), bf16)],
        scalars=1,
        flops=8 * 10**9,
    )
    keep_x, base_x, right_x, left_x, keep_y, base_y, right_y, left_y = parts
    right_x, left_x = around(right_x, left_x, stride_x)
    right_y, left_y = around(right_y, left_y, stride_y)
    relayed = call(
        relay_kernel,
        [((eighth // 2, joined), bf16)] * 2 + [((eighth // 2, joined + 128), bf16)] * 2,
        (base_x, right_x, left_x, base_y, right_y, left_y, to_both),
        vmem=16 * 2**20,
    )
    from_x = [keep_x, right_x, left_x, *around(relayed[0], relayed[1], stride_x)]
    from_y = [keep_y, right_y, left_y, *around(relayed[2], relayed[3], stride_y)]
    small = eighth // SIDE
    *parts, kept = call(
        first_sum_kernel,
        slots(small, joined, f32)
        + [((small, joined), f32), ((small, joined + 128), bf16), ((small, joined), bf16), ((small, joined + 128), bf16)]
        + [((64, 128), f32)],
        (place, *from_x, *from_y),
        [pltpu.VMEM((SIDE, SIDE, 8, joined), f32), pltpu.VMEM((eighth, joined), f32)],
        scalars=1,
        vmem=16 * 2**20,
    )
    first = exchange(parts[:4], stride_y)
    second = exchange(parts[4:], stride_x)
    *parts, kept = call(
        second_sum_kernel,
        [((16, joined), f32), ((16, joined + 256), bf16), ((16, joined), bf16), ((16, joined + 256), bf16)]
        + [((64, 128), f32)],
        (place, *first, *second, kept),
        [pltpu.VMEM((SIDE, 2, 8, joined), f32)],
        scalars=1,
        vmem=16 * 2**20,
    )
    last = exchange(parts, stride_z)
    grad_in_proj, grad_out_proj, grad_input = call(
        last_sum_kernel,
        [((8, inner + channels), f32), ((16, width), f32), ((rows, width), bf16)],
        (*last, kept, base),
        vmem=16 * 2**20,
    )
    return (layer_out, grad_input, grad_in_proj, grad_out_proj)


def solution(mesh):
    rows = P(("batch", "seq"), None)
    return jax.shard_map(
        shards,
        mesh=mesh,
        in_specs=(rows, rows) + (P(),) * 9,
        out_specs=(rows,) * 4,
        check_vma=False,
    )
```

```python
import functools

import jax
import jax.numpy as jnp
from jax import lax
from jax.experimental import pallas as pl
from jax.experimental.pallas import tpu as pltpu
from jax.sharding import PartitionSpec as P

epsilon = 1e-06
SIDE = 4
COUNT = SIDE**3
f32 = jnp.float32
bf16 = jnp.bfloat16
INTERPRET = False


def call(body, outs, args, scratch=(), scalars=0, unused=0, flops=10**9, vmem=58 * 2**20):
    after = len(args) - unused
    specs = [pl.BlockSpec(memory_space=pltpu.SMEM)] * scalars
    specs += [pl.BlockSpec(memory_space=pltpu.VMEM)] * (after - scalars)
    specs += [pl.BlockSpec(memory_space=pl.ANY)] * unused
    moved = sum(a.size * a.dtype.itemsize for a in args[:after])

    def used(*refs):
        body(*refs[:after], *refs[len(args) :])

    return pl.pallas_call(
        used,
        out_shape=[jax.ShapeDtypeStruct(shape, kind) for shape, kind in outs],
        in_specs=specs,
        out_specs=[pl.BlockSpec(memory_space=pltpu.VMEM)] * len(outs),
        scratch_shapes=list(scratch),
        compiler_params=pltpu.CompilerParams(vmem_limit_bytes=vmem),
        cost_estimate=pl.CostEstimate(flops=flops, bytes_accessed=moved, transcendentals=0),
        interpret=INTERPRET,
    )(*args)


def mm(left, right):
    return lax.dot_general(left, right, (((1,), (0,)), ((), ())), preferred_element_type=f32)


def mm_cols(left, right):
    return lax.dot_general(left, right, (((1,), (1,)), ((), ())), preferred_element_type=f32)


def mm_rows(left, right):
    return lax.dot_general(left, right, (((0,), (0,)), ((), ())), preferred_element_type=f32)


def iota(shape, dim):
    return lax.broadcasted_iota(jnp.int32, shape, dim)


def ones_where(mask):
    return jnp.where(mask, 1.0, 0.0).astype(bf16)


def anti(size):
    return ones_where(iota((size, size), 0) + iota((size, size), 1) == size - 1)


def pieces_of(value, count):
    found = []
    for _ in range(count):
        piece = value.astype(bf16)
        found.append(piece)
        value = value - piece.astype(f32)
    return found


def mirror_exact(block):
    turned = mm(block, anti(block.shape[1])).astype(bf16)
    return mm(anti(block.shape[0]), turned).astype(bf16)


def mirror_wide(block):
    high, low = pieces_of(block, 2)
    return mirror_exact(high).astype(f32) + mirror_exact(low).astype(f32)


def head_mask(heads, width):
    lanes = heads * width
    return ones_where(iota((heads, lanes), 0) == iota((heads, lanes), 1) // width)


def expand(value, mask):
    found = pieces_of(value, 3)
    return mm(jnp.concatenate(found, axis=1), jnp.concatenate([mask] * 3, axis=0))


def fold(value, mask, count=2):
    total = None
    for piece in pieces_of(value, count):
        part = mm_cols(piece, mask)
        total = part if total is None else total + part
    return total


def triangle(size, low):
    rows, cols = iota((size, size), 0), iota((size, size), 1)
    return rows >= cols if low else rows <= cols


def tri_sum(mask, value):
    total = None
    for piece in pieces_of(value, 3):
        part = mm(ones_where(mask), piece)
        total = part if total is None else total + part
    return total


def tri_sum_turned(mask, value):
    total = None
    for piece in pieces_of(value, 3):
        part = mm_rows(piece, ones_where(mask))
        total = part if total is None else total + part
    return total


def softplus(value):
    return jnp.maximum(value, 0.0) + jnp.log1p(jnp.exp(-jnp.abs(value)))


def sigmoid(value):
    return 1.0 / (1.0 + jnp.exp(-value))


def norm_rows(block, gain):
    wide = block.astype(f32)
    scale = lax.rsqrt(jnp.mean(wide * wide, axis=-1, keepdims=True) + epsilon)
    return (wide * scale * gain.reshape(1, -1)).astype(bf16)


def pre_kernel(
    seq, up, low, high, gain, in_proj, step_proj, conv_w, conv_b, step_bias, decay_log, out_proj,
    payload, both, normal, normal_halo, cot, gate, conv, d_gated, raw, step, cumul, cumul_t,
    ext,
):
    rows = seq.shape[0]
    inner = out_proj.shape[0]
    heads = step_bias.shape[0]
    state = (conv_w.shape[1] - inner) // 2
    taps = conv_w.shape[0]
    both[:rows, :] = seq[...]
    both[rows:, :] = mirror_exact(seq[...])
    cot[:rows, :] = up[...]
    cot[rows:, :] = mirror_exact(up[...])
    halo = jnp.concatenate([low[...], mirror_exact(high[...])], axis=0)
    normal[...] = norm_rows(both[...], gain[...])
    normal_halo[...] = norm_rows(halo, gain[...])
    gate[...] = mm(normal[...], in_proj[:, :inner]).astype(bf16)
    xbc = mm(normal[...], in_proj[:, inner:]).astype(bf16).astype(f32)
    xbc_halo = mm(normal_halo[...], in_proj[:, inner:]).astype(bf16).astype(f32)
    raw[...] = mm_cols(normal[...], step_proj[...])
    d_gated[...] = mm_cols(cot[...], out_proj[...]).astype(bf16)
    margin = low.shape[0]
    mask = head_mask(heads, inner // heads)
    ends = []
    for frame in range(2):
        at = slice(frame * rows, (frame + 1) * rows)
        ext[:8, :] = xbc_halo[(frame + 1) * margin - 8 : (frame + 1) * margin, :]
        ext[8:, :] = xbc[at, :]
        found = conv_b[...].reshape(1, -1)
        for tap in range(taps):
            start = 9 - taps + tap
            found = found + ext[start : start + rows, :] * conv_w[tap : tap + 1, :]
        conv[at, :] = found.astype(bf16)
        act = found * sigmoid(found)
        size = softplus(raw[at, :] + step_bias[...].reshape(1, -1))
        decay = -jnp.exp(decay_log[...].reshape(1, -1)) * size
        upto = tri_sum(triangle(rows, True), decay)
        step[at, :] = size
        cumul[at, :] = upto
        cumul_t[frame * heads : (frame + 1) * heads, :] = tri_sum_turned(triangle(rows, False), decay)
        end = upto[rows - 1 : rows, :]
        ends.append(end)
        spread = expand(jnp.concatenate([size * jnp.exp(end - upto), jnp.exp(upto)], axis=0), mask)
        driven = (act[:, :inner] * spread[:rows]).astype(bf16)
        local = mm_rows(driven, act[:, inner : inner + state].astype(bf16))
        wide = gate[at, :].astype(f32)
        d_mixed = d_gated[at, :].astype(f32) * (wide * sigmoid(wide))
        back = mm_rows((d_mixed * spread[rows:]).astype(bf16), act[:, inner + state :].astype(bf16))
        part = inner // SIDE
        for place, block in ((frame, local), (2 + frame, back)):
            block = block.astype(bf16).reshape(SIDE, part, state)
            payload[:, place * part : (place + 1) * part, :] = block
    packed = pack_totals(ends, heads, state)
    for to in range(SIDE):
        shifted = ones_where(iota((16, heads), 1) == iota((16, heads), 0) + to * (heads // SIDE))
        payload[to, inner:, :] = mm(shifted, packed).astype(bf16)


def pack_totals(ends, heads, state):
    chosen = iota((heads, heads), 0) == iota((heads, heads), 1)
    lanes = iota((heads, state), 1)
    packed = jnp.zeros((heads, state), f32)
    for frame in range(2):
        column = jnp.sum(jnp.where(chosen, ends[frame], 0.0), axis=1, keepdims=True)
        packed = pack_column(packed, column, lanes, frame)
    return packed.astype(bf16)


def pack_column(packed, column, lanes, frame):
    for nth, piece in enumerate(pieces_of(column, 3)):
        packed = jnp.where(lanes == 3 * frame + nth, piece.astype(f32), packed)
    return packed


def unpack_column(packed, frame):
    at = 3 * frame
    return (packed[:, at + 2 : at + 3] + packed[:, at + 1 : at + 2]) + packed[:, at : at + 1]


SCANS = ((0, False), (1, True), (0, True), (1, False))


def chain(got, totals, place, state, visit):
    frame, turned = SCANS[place]
    part = state.shape[0]
    size = part // SIDE
    order = range(SIDE - 1, -1, -1) if turned else range(SIDE)
    for at in order:
        visit(at, state)
        grown = jnp.exp(totals[at][frame])
        factors = [
            jnp.broadcast_to(grown[head : head + 1, :], (size, 1)) for head in range(part // size)
        ]
        state = jnp.concatenate(factors, axis=0) * state
        state = state + got[at, place * part : (place + 1) * part, :].astype(f32)
    return state


def tails_of(got, inner):
    found = []
    for at in range(SIDE):
        tail = got[at, inner:, :].astype(f32)
        found.append([unpack_column(tail, frame) for frame in range(2)])
    return found


def group_kernel(got, out):
    state = got.shape[2]
    inner = got.shape[1] - 16
    part = inner // SIDE
    totals = tails_of(got, inner)
    for place in range(4):
        block = chain(got, totals, place, jnp.zeros((part, state), f32), lambda at, value: None)
        out[:, 16 * place : 16 * place + 16, :] = block.reshape(16, 16, state).astype(bf16)
    lanes = iota((16, state), 1)
    packed = jnp.zeros((16, state), f32)
    for frame in range(2):
        column = jnp.maximum(totals[0][frame], -110.0)
        for at in range(1, SIDE):
            column = column + jnp.maximum(totals[at][frame], -110.0)
        packed = pack_column(packed, column, lanes, frame)
    chosen = ones_where(iota((16, 16), 1) == iota((16, 16), 0) // SIDE)
    packed = mm(chosen, packed.astype(bf16))
    out[:, 64:, :] = jnp.broadcast_to(packed.reshape(16, 1, state), (16, 8, state)).astype(bf16)


def spread_kernel(got, entering, out):
    state = got.shape[2]
    inner = got.shape[1] - 16
    part = inner // SIDE
    totals = tails_of(got, inner)
    for place in range(4):

        def visit(at, value, place=place):
            out[at, place * part : (place + 1) * part, :] = value.astype(bf16)

        block = entering[:, 16 * place : 16 * place + 16, :].astype(f32).reshape(part, state)
        chain(got, totals, place, block, visit)


def scan_kernel(got, out, wide, done):
    count, rows, state = got.shape
    wide[...] = got[...].astype(f32).reshape(count * rows, state)
    tails = wide[pl.ds(64, count, stride=rows), :]
    above = iota((count, count), 0)
    beside = iota((count, count), 1)
    after = ones_where(above > beside)
    weights = []
    for frame in range(2):
        column = jnp.maximum(unpack_column(tails, frame), -110.0)
        line = jnp.sum(jnp.where(above == beside, column, 0.0), axis=0, keepdims=True)
        between = None
        for piece in pieces_of(jnp.where(beside < above, line, 0.0), 3):
            part = mm(piece, after)
            between = part if between is None else between + part
        found = jnp.where(above > beside, jnp.exp(between), 0.0)
        weights.append(pieces_of(found, 2))
    for place, (frame, turned) in enumerate(SCANS):
        pair = weights[frame]
        block = jnp.concatenate(
            [wide[pl.ds(16 * place + row, count, stride=rows), :] for row in range(16)], axis=1
        ).astype(bf16)
        if turned:
            mixed = mm_rows(jnp.concatenate(pair, axis=1), block)
        else:
            mixed = mm(jnp.concatenate(pair, axis=0), block)
        mixed = mixed[:count] + mixed[count:]
        for row in range(16):
            done[pl.ds(16 * place + row, count, stride=64), :] = mixed[:, state * row : state * (row + 1)]
    out[...] = done[...].reshape(count, 64, state).astype(bf16)


def intra_kernel(
    conv, gate, d_gated, step, cumul, cumul_t, normal, normal_halo, skip_gain,
    silus, d_gates, pushed, mixed, d_inputs, lefts, held_back, d_convs, bc, d_bc, sums_out, normal_t, halo_t,
):
    for source, target in ((normal, normal_t), (normal_halo, halo_t)):
        count = source.shape[0]
        same = iota((count, count), 0) == iota((count, count), 1)
        target[...] = mm_rows(source[...], ones_where(same)).astype(bf16)
    rows = conv.shape[0] // 2
    inner = gate.shape[1]
    heads = step.shape[1]
    state = (conv.shape[1] - inner) // 2
    mask = head_mask(heads, inner // heads)
    lower = triangle(rows, True)
    first = iota((rows, 2 * inner // heads), 1) < inner // heads
    wide_pair = 2 * inner // heads
    skip = expand(jnp.broadcast_to(skip_gain[...].reshape(1, -1), (8, heads)), mask)[:1]
    for frame in range(2):
        at = slice(frame * rows, (frame + 1) * rows)
        found = conv[at, :].astype(f32)
        share = sigmoid(found)
        act = found * share
        d_convs[at, :] = (share * (1.0 + found * (1.0 - share))).astype(bf16)
        bc[at, :] = act[:, inner:].astype(bf16)
        bmat, cmat = bc[at, :state], bc[at, state:]
        upto = cumul[at, :]
        end = upto[rows - 1 : rows, :]
        spread = expand(jnp.concatenate([step[at, :], jnp.exp(upto), jnp.exp(end - upto)], axis=0), mask)
        sizes, grown, left = spread[:rows], spread[rows : 2 * rows], spread[2 * rows :]
        inputs = act[:, :inner]
        driven = inputs * sizes
        lefts[at, :] = (left * inputs).astype(bf16)
        held_back[at, :] = (left * driven).astype(bf16)
        wide = gate[at, :].astype(f32)
        opened = sigmoid(wide)
        silu = wide * opened
        silus[at, :] = silu.astype(bf16)
        d_out = d_gated[at, :].astype(f32)
        d_gates[at, :] = (d_out * (opened * (1.0 + wide * (1.0 - opened)))).astype(bf16)
        d_mixed = d_out * silu
        pushed[at, :] = (d_mixed * grown).astype(bf16)
        scores = mm_cols(cmat, bmat)
        line = cumul_t[frame * heads : (frame + 1) * heads, :]
        d_scores = jnp.zeros((rows, rows), f32)
        sums, by_size = [], []
        for pair in range(heads // 2):
            lanes = slice(pair * wide_pair, (pair + 1) * wide_pair)
            decays = []
            for head in (2 * pair, 2 * pair + 1):
                differ = upto[:, head : head + 1] - line[head : head + 1, :]
                decays.append(jnp.exp(jnp.where(lower, differ, -1e30)))
            weights = [(decay * scores).astype(bf16) for decay in decays]
            drive, d_mix = driven[:, lanes], d_mixed[:, lanes]
            drive_bf, d_mix_bf = drive.astype(bf16), d_mix.astype(bf16)
            drive_two = jnp.concatenate(
                [jnp.where(first, drive, 0.0), jnp.where(first, 0.0, drive)], axis=0
            ).astype(bf16)
            d_mix_two = jnp.concatenate(
                [jnp.where(first, d_mix, 0.0), jnp.where(first, 0.0, d_mix)], axis=0
            ).astype(bf16)
            mix = mm(jnp.concatenate(weights, axis=1), drive_two)
            d_weights = mm_cols(d_mix_two, drive_bf)
            d_drive = mm_rows(jnp.concatenate(weights, axis=0), d_mix_two)
            d_scores = d_scores + decays[0] * d_weights[:rows] + decays[1] * d_weights[rows:]
            mixed[at, lanes] = (mix + skip[:, lanes] * inputs[:, lanes]).astype(bf16)
            d_inputs[at, lanes] = (skip[:, lanes] * d_mix + d_drive * sizes[:, lanes]).astype(bf16)
            by_size.append(d_drive * inputs[:, lanes])
            sums.append(d_mix_bf.astype(f32) * mix - drive_bf.astype(f32) * d_drive)
        d_scores = d_scores.astype(bf16)
        d_bc[at, :state] = mm_rows(d_scores, cmat)
        d_bc[at, state:] = mm(d_scores, bmat)
        sums_out[at, :heads] = fold(jnp.concatenate(sums, axis=1), mask)
        sums_out[at, heads:] = fold(jnp.concatenate(by_size, axis=1), mask)


def post_kernel(
    place, got, silus, d_gates, pushed, mixed, d_inputs, lefts, held_back, d_convs, bc, d_bc, sums,
    raw, step, cumul, step_bias, decay_log, conv_w, cot, normal_t, halo_t,
    gated, d_gate, d_xbc, d_first, d_second, d_step, *refs,
):
    by_x, by_y, ext, d_conv_out, whole, parted = refs[:4], refs[4:8], refs[8], refs[9], refs[10], refs[11]
    rows = silus.shape[0] // 2
    inner = silus.shape[1]
    heads = step.shape[1]
    state = bc.shape[1] // 2
    mask = head_mask(heads, inner // heads)
    for frame in range(2):
        at = slice(frame * rows, (frame + 1) * rows)
        upto = cumul[at, :]
        size = step[at, :]
        end = upto[rows - 1 : rows, :]
        spread = expand(jnp.concatenate([jnp.exp(upto), size * jnp.exp(end - upto)], axis=0), mask)
        part = inner // SIDE
        carried = got[:, frame * part : (frame + 1) * part, :].reshape(inner, state)
        reach = got[:, (2 + frame) * part : (3 + frame) * part, :].reshape(inner, state)
        read = mm_cols(bc[at, state:], carried)
        full = mixed[at, :].astype(f32) + spread[:rows] * read
        gated[at, :] = (full * silus[at, :].astype(f32)).astype(bf16)
        d_gate[at, :] = (full * d_gates[at, :].astype(f32)).astype(bf16)
        d_cmat = d_bc[at, state:] + mm(pushed[at, :], carried)
        answer = mm_cols(bc[at, :state], reach)
        d_bmat = d_bc[at, :state] + mm(held_back[at, :], reach)
        products = carried.astype(f32) * reach.astype(f32)
        met = jnp.sum(products.reshape(heads, inner // heads, state), axis=1)
        met = jnp.sum(met, axis=1, keepdims=True)
        met = jnp.sum(jnp.where(iota((heads, heads), 0) == iota((heads, heads), 1), met, 0.0), axis=0, keepdims=True)
        folded = fold(
            jnp.concatenate([lefts[at, :].astype(f32) * answer, pushed[at, :].astype(f32) * read], axis=0), mask, 1
        )
        by_size, entered = folded[:rows], folded[rows:]
        held = by_size * size
        d_end = jnp.exp(end) * met + jnp.sum(held, axis=0, keepdims=True)
        d_decay = tri_sum(triangle(rows, False), sums[at, :heads] + entered - held) + d_end
        d_size = sums[at, heads:] + by_size - jnp.exp(decay_log[...].reshape(1, -1)) * d_decay
        d_step[at, :] = (d_size * sigmoid(raw[at, :] + step_bias[...].reshape(1, -1))).astype(bf16)
        d_act = jnp.concatenate([d_inputs[at, :].astype(f32) + spread[rows:] * answer, d_bmat, d_cmat], axis=1)
        margin = halo_t.shape[1] // 2
        ext[:margin, :] = jnp.zeros((margin, ext.shape[1]), f32)
        ext[margin : margin + rows, :] = d_act * d_convs[at, :].astype(f32)
        ext[margin + rows :, :] = jnp.zeros((8, ext.shape[1]), f32)
        taps = conv_w.shape[0]
        total = None
        for tap in range(taps):
            start = taps - 1 - tap
            part = ext[start : start + margin + rows, :] * conv_w[tap : tap + 1, :]
            total = part if total is None else total + part
        d_xbc[at, :] = total[margin:].astype(bf16)
        d_conv_out[frame * margin : (frame + 1) * margin, :] = total[:margin].astype(bf16)
        (d_first, d_second)[frame][...] = total[margin - 8 : margin]
    columns = cot.shape[1]
    half = d_xbc.shape[1] // 2
    out_term = mm_rows(gated[...], cot[...]).reshape(COUNT, 2, 8, columns)
    gate_term = mm(normal_t[...], d_gate[...]).reshape(COUNT // SIDE, SIDE, 8, inner)
    in_term = mm(normal_t[...], d_xbc[...]) + mm(halo_t[...], d_conv_out[...])
    whole[:, :columns] = out_term[:, 0].reshape(-1, columns).astype(bf16)
    whole[:, columns : 2 * columns] = out_term[:, 1].reshape(-1, columns).astype(bf16)
    whole[:, 2 * columns :] = in_term[:, :half].astype(bf16)
    parted[:, :, :, :inner] = gate_term
    parted[:, :, :, inner:] = in_term[:, half:].reshape(COUNT // SIDE, SIDE, 8, half)
    ring_out(lambda step: chunk_x(place, whole, step), by_x)
    ring_out(lambda step: chunk_y(place, parted, step), by_y)


def chunk_x(place, whole, step):
    chunk = whole.shape[0] // SIDE
    to = lax.rem(place[0] + step, SIDE)
    return whole[pl.ds(pl.multiple_of(to * chunk, chunk), chunk), :].astype(bf16)


def chunk_y(place, parted, step):
    block = parted[:, lax.rem(place[2] + step, SIDE)]
    return block.reshape(-1, block.shape[-1]).astype(bf16)


def ring_out(chunk_of, slots):
    keep, base, right, left = slots
    half = keep.shape[0] // 2
    keep[...] = chunk_of(0)
    ahead, opposite, behind = chunk_of(1), chunk_of(2), chunk_of(3)
    base[:half, :], base[half:, :] = ahead[:half], behind[half:]
    right[:half, :], right[half:, :] = opposite[:half], ahead[half:]
    left[:half, :], left[half:, :] = behind[:half], opposite[half:]


def relay_kernel(base_x, right_x, left_x, base_y, right_y, left_y, to_both, *outs):
    for base, right, left, on_right, on_left in (
        (base_x, right_x, left_x, outs[0], outs[1]),
        (base_y, right_y, left_y, outs[2], outs[3]),
    ):
        half = base.shape[0] // 2
        columns = base.shape[1]
        on_right[:, :columns] = (base[:half, :].astype(f32) + right[:half, :].astype(f32)).astype(bf16)
        on_left[:, :columns] = (base[half:, :].astype(f32) + left[half:, :].astype(f32)).astype(bf16)
    outs[2][:32, columns:] = to_both[:32, :]
    outs[3][:32, columns:] = to_both[32:, :]
    for target in outs[2:]:
        target[32:, columns:] = jnp.zeros((32, 128), bf16)


def ring_total(keep, right, left, on_right, on_left):
    half = keep.shape[0] // 2
    columns = keep.shape[1]
    first = keep[:half, :].astype(f32) + left[:half, :].astype(f32) + on_right[:, :columns].astype(f32)
    second = keep[half:, :].astype(f32) + right[half:, :].astype(f32) + on_left[:, :columns].astype(f32)
    return jnp.concatenate([first, second], axis=0)


def send_x(place, whole, slots):
    chunk = whole.shape[0] // SIDE
    for step in range(SIDE):
        to = lax.rem(place[0] + step, SIDE)
        block = whole[pl.ds(pl.multiple_of(to * chunk, chunk), chunk), :]
        slots[step][...] = block.astype(slots[step].dtype)


def send_y(place, parted, slots):
    for step in range(SIDE):
        block = parted[:, lax.rem(place[2] + step, SIDE)]
        slots[step][...] = block.reshape(slots[step].shape).astype(slots[step].dtype)


def norm_back(block, d_normal, gain):
    wide = block.astype(f32)
    scale = lax.rsqrt(jnp.mean(wide * wide, axis=-1, keepdims=True) + epsilon)
    d_scaled = d_normal * gain.reshape(1, -1)
    along = jnp.mean(d_scaled * wide, axis=-1, keepdims=True)
    return scale * d_scaled - wide * (scale * scale * scale * along)


def fold_rows(block):
    return jnp.concatenate([block[:, 128 * nth : 128 * (nth + 1)] for nth in range(4)], axis=0)


def unfold_rows(block):
    return jnp.concatenate([block[8 * nth : 8 * (nth + 1)] for nth in range(4)], axis=1)


def scalar_flag(condition):
    return jnp.where(condition, 1.0, 0.0)


def result_kernel(
    place, both, gain, gated, out_proj, d_gate, d_xbc, d_first, d_second, low, high, d_step, in_proj, step_proj,
    layer, base, to_both, d_whole,
):
    rows = both.shape[0] // 2
    inner = out_proj.shape[0]
    branch = mm(gated[...], out_proj[...])
    layer[...] = (branch[:rows] + mirror_wide(branch[rows:])).astype(bf16)
    d_whole[: 2 * rows, :] = d_xbc[...]
    edges = jnp.concatenate([d_first[...], d_second[...]], axis=0)
    d_whole[2 * rows :, :] = edges.astype(bf16)
    through = mm_cols(d_whole[...], in_proj[:, inner:])
    d_normal = mm_cols(d_gate[...], in_proj[:, :inner]) + through[: 2 * rows]
    d_normal = d_normal + mm(d_step[...], step_proj[...])
    d_wide = norm_back(both[...], d_normal, gain[...])
    base[...] = d_wide[:rows] + mirror_wide(d_wide[rows:])
    first = norm_back(low[8:, :], through[2 * rows : 2 * rows + 8], gain[...])
    second = norm_back(mirror_exact(high[...])[8:, :], through[2 * rows + 8 :], gain[...])
    at_start = (place[0] + place[1] + place[2]) == 0
    at_end = (place[0] + place[1] + place[2]) == 3 * (SIDE - 1)
    to_both[32:, :] = fold_rows(first * (1.0 - scalar_flag(at_start))).astype(bf16)
    to_both[:32, :] = fold_rows(mirror_wide(second) * (1.0 - scalar_flag(at_end))).astype(bf16)


def total_of(refs):
    total = refs[0][...].astype(f32)
    for ref in refs[1:]:
        total = total + ref[...].astype(f32)
    return total


def first_sum_kernel(place, *refs):
    from_x, from_y, by_y, by_x, kept = refs[:5], refs[5:10], refs[10:14], refs[14], refs[15]
    parted, whole = refs[16], refs[17]
    parted[...] = ring_total(*from_x).reshape(parted.shape)
    whole[...] = ring_total(*from_y)
    send_y(place, parted, by_y)
    columns = whole.shape[1]
    high = from_y[3][:32, columns:].astype(f32)
    low = from_y[4][:32, columns:].astype(f32)
    on_high = scalar_flag((place[2] == 0) & (place[1] == SIDE - 1))
    on_low = scalar_flag((place[2] == SIDE - 1) & (place[1] == 0))
    by_x[:, :, :columns] = whole[...].astype(bf16).reshape(SIDE, -1, columns)
    for to in range(SIDE):
        up = on_high * scalar_flag(lax.rem(place[0] + 1, SIDE) == to)
        down = on_low * scalar_flag(lax.rem(place[0] + SIDE - 1, SIDE) == to)
        by_x[to, :, columns:] = (high * up + low * down).astype(bf16)
    kept[:32, :] = high * (1.0 - on_high)
    kept[32:, :] = low * (1.0 - on_low)


def second_sum_kernel(place, *refs):
    first, second, kept, by_z, kept_on, keep = refs[:4], refs[4], refs[5], refs[6:10], refs[10], refs[11]
    columns = first[0].shape[1]
    high, low = kept[:32, :], kept[32:, :]
    total = None
    for source in range(SIDE):
        block = second[source].astype(f32)
        edge = block[:, columns:]
        high = high + edge * scalar_flag(lax.rem(place[0] + SIDE - 1, SIDE) == source)
        low = low + edge * scalar_flag(lax.rem(place[0] + 1, SIDE) == source)
        total = block[:, :columns] if total is None else total + block[:, :columns]
    first = total_of(first).reshape(SIDE, 8, -1)
    second = total.reshape(SIDE, 8, -1)
    above = scalar_flag(place[2] == 0)
    below = scalar_flag(place[2] == SIDE - 1)
    keep[:, 0] = first
    keep[:, 1] = second
    for step in range(SIDE):
        block = keep[lax.rem(place[1] + step, SIDE)].reshape(16, columns)
        by_z[step][:, :columns] = block.astype(by_z[step].dtype)
    for step, edge, share in ((1, high, above), (3, low, below)):
        edge = edge * share
        by_z[step][:, columns:] = jnp.concatenate([edge[:16], edge[16:]], axis=1).astype(bf16)
    kept_on[:32, :] = high * (1.0 - above)
    kept_on[32:, :] = low * (1.0 - below)


def last_sum_kernel(own, up, across, down, kept, base, grad_in, grad_out, grad):
    joined = own.shape[1]
    total = own[...] + up[:, :joined].astype(f32) + across[...].astype(f32) + down[:, :joined].astype(f32)
    columns = grad_out.shape[1]
    grad_out[:8, :] = total[:8, :columns]
    grad_out[8:, :] = total[:8, columns : 2 * columns]
    grad_in[...] = jnp.concatenate([total[8:, : 2 * columns], total[:8, 2 * columns :], total[8:, 2 * columns :]], axis=1)
    edges = []
    for nth, recv in enumerate((up, down)):
        recv = recv[:, joined:].astype(f32)
        recv = jnp.concatenate([recv[:, :128], recv[:, 128:]], axis=0)
        edges.append(unfold_rows(kept[32 * nth : 32 * nth + 32, :] + recv))
    rows = base.shape[0]
    whole = jnp.concatenate([base[:8, :] + edges[0], base[8 : rows - 8, :], base[rows - 8 :, :] + edges[1]], axis=0)
    grad[...] = whole.astype(bf16)


def axis_pairs(stride, step):
    pairs = []
    for source in range(COUNT):
        digit = source // stride % SIDE
        pairs.append((source, source + ((digit + step) % SIDE - digit) * stride))
    return pairs


def exchange(parts, stride):
    return [parts[0]] + [lax.ppermute(parts[step], "seq", axis_pairs(stride, step)) for step in range(1, SIDE)]


def around(to_right, to_left, stride):
    return (
        lax.ppermute(to_right, "seq", axis_pairs(stride, 1)),
        lax.ppermute(to_left, "seq", axis_pairs(stride, SIDE - 1)),
    )


def transpose_over(parts, groups):
    return lax.all_to_all(parts, "seq", 0, 0, axis_index_groups=groups)


def slots(rows, columns, kind):
    return [((rows, columns), kind)] + [((rows, columns), bf16)] * (SIDE - 1)


def shards(
    sequence,
    upstream,
    norm_gain,
    in_proj,
    step_proj,
    conv_weight,
    conv_bias,
    step_bias,
    decay_log,
    skip_gain,
    out_proj,
):
    rows, width = sequence.shape
    inner = out_proj.shape[0]
    heads = step_bias.shape[0]
    state = inner // heads * 2
    channels = conv_weight.shape[1]
    both_rows = 2 * rows
    stride_x, stride_z, stride_y = SIDE * SIDE, SIDE, 1
    index = lax.axis_index("seq")
    place = jnp.stack([index // stride_x, index // stride_z % SIDE, index % SIDE]).astype(jnp.int32)
    lined = [[base + stride_x * digit for digit in range(SIDE)] for base in range(stride_x)]
    beside = [[SIDE * base + digit for digit in range(SIDE)] for base in range(COUNT // SIDE)]
    across = [[base + SIDE * digit for digit in range(COUNT // SIDE)] for base in range(SIDE)]
    upward = [(i, i + 1) for i in range(COUNT - 1)]
    downward = [(i + 1, i) for i in range(COUNT - 1)]
    low = lax.ppermute(sequence[rows - 16 :], "seq", upward)
    high = lax.ppermute(sequence[:16], "seq", downward)
    step_turned = step_proj.T
    payload, both, normal, normal_halo, cot, gate, conv, d_gated, raw, step, cumul, cumul_t = call(
        pre_kernel,
        [
            ((SIDE, inner + 16, state), bf16),
            ((both_rows, width), bf16),
            ((both_rows, width), bf16),
            ((32, width), bf16),
            ((both_rows, width), bf16),
            ((both_rows, inner), bf16),
            ((both_rows, channels), bf16),
            ((both_rows, inner), bf16),
            ((both_rows, heads), f32),
            ((both_rows, heads), f32),
            ((both_rows, heads), f32),
            ((2 * heads, rows), f32),
        ],
        (
            sequence, upstream, low, high, norm_gain, in_proj, step_turned,
            conv_weight, conv_bias, step_bias, decay_log, out_proj,
        ),
        [pltpu.VMEM((rows + 8, channels), f32)],
    )
    got = transpose_over(payload, beside)
    (summary,) = call(group_kernel, [((COUNT // SIDE, 72, state), bf16)], (got,), vmem=16 * 2**20)
    summaries = transpose_over(summary, across)
    inner_values = call(
        intra_kernel,
        [((both_rows, inner), bf16)] * 7
        + [
            ((both_rows, channels), bf16),
            ((both_rows, 2 * state), bf16),
            ((both_rows, 2 * state), f32),
            ((both_rows, 2 * heads), f32),
            ((width, both_rows), bf16),
            ((width, 32), bf16),
        ],
        (conv, gate, d_gated, step, cumul, cumul_t, normal, normal_halo, skip_gain),
        flops=8 * 10**9,
    )
    normal_t, halo_t = inner_values[-2:]
    groups = COUNT // SIDE
    (scanned,) = call(
        scan_kernel,
        [((groups, 64, state), bf16)],
        (summaries,),
        [pltpu.VMEM((groups * 72, state), f32), pltpu.VMEM((groups * 64, state), f32)],
        vmem=16 * 2**20,
    )
    entering = transpose_over(scanned, across)
    (spread,) = call(spread_kernel, [((SIDE, inner, state), bf16)], (got, entering), vmem=16 * 2**20)
    states = transpose_over(spread, beside)
    eighth = 8 * COUNT // SIDE
    joined = inner + channels // 2
    gated, d_gate, d_xbc, d_first, d_second, d_step, *parts = call(
        post_kernel,
        [
            ((both_rows, inner), bf16),
            ((both_rows, inner), bf16),
            ((both_rows, channels), bf16),
            ((8, channels), f32),
            ((8, channels), f32),
            ((both_rows, heads), bf16),
        ]
        + slots(eighth, joined, bf16) * 2,
        (
            place, states, *inner_values[:-2], raw, step, cumul,
            step_bias, decay_log, conv_weight, cot, normal_t, halo_t,
        ),
        [
            pltpu.VMEM((rows + 24, channels), f32),
            pltpu.VMEM((32, channels), bf16),
            pltpu.VMEM((8 * COUNT, joined), bf16),
            pltpu.VMEM((COUNT // SIDE, SIDE, 8, joined), f32),
        ],
        scalars=1,
    )
    layer_out, base, to_both = call(
        result_kernel,
        [((rows, width), bf16), ((rows, width), f32), ((64, 128), bf16)],
        (
            place, both, norm_gain, gated, out_proj, d_gate, d_xbc, d_first, d_second, low, high, d_step,
            in_proj, step_turned,
        ),
        [pltpu.VMEM((both_rows + 16, channels), bf16)],
        scalars=1,
        flops=8 * 10**9,
    )
    keep_x, base_x, right_x, left_x, keep_y, base_y, right_y, left_y = parts
    right_x, left_x = around(right_x, left_x, stride_x)
    right_y, left_y = around(right_y, left_y, stride_y)
    relayed = call(
        relay_kernel,
        [((eighth // 2, joined), bf16)] * 2 + [((eighth // 2, joined + 128), bf16)] * 2,
        (base_x, right_x, left_x, base_y, right_y, left_y, to_both),
        vmem=16 * 2**20,
    )
    from_x = [keep_x, right_x, left_x, *around(relayed[0], relayed[1], stride_x)]
    from_y = [keep_y, right_y, left_y, *around(relayed[2], relayed[3], stride_y)]
    small = eighth // SIDE
    *parts, kept = call(
        first_sum_kernel,
        slots(small, joined, f32)
        + [((SIDE, small, joined + 128), bf16)]
        + [((64, 128), f32)],
        (place, *from_x, *from_y),
        [pltpu.VMEM((SIDE, SIDE, 8, joined), f32), pltpu.VMEM((eighth, joined), f32)],
        scalars=1,
        vmem=16 * 2**20,
    )
    first = exchange(parts[:4], stride_y)
    second = transpose_over(parts[4], lined)
    *parts, kept = call(
        second_sum_kernel,
        [((16, joined), f32), ((16, joined + 256), bf16), ((16, joined), bf16), ((16, joined + 256), bf16)]
        + [((64, 128), f32)],
        (place, *first, second, kept),
        [pltpu.VMEM((SIDE, 2, 8, joined), f32)],
        scalars=1,
        vmem=16 * 2**20,
    )
    last = exchange(parts, stride_z)
    grad_in_proj, grad_out_proj, grad_input = call(
        last_sum_kernel,
        [((8, inner + channels), f32), ((16, width), f32), ((rows, width), bf16)],
        (*last, kept, base),
        vmem=16 * 2**20,
    )
    return (layer_out, grad_input, grad_in_proj, grad_out_proj)


def solution(mesh):
    rows = P(("batch", "seq"), None)
    return jax.shard_map(
        shards,
        mesh=mesh,
        in_specs=(rows, rows) + (P(),) * 9,
        out_specs=(rows,) * 4,
        check_vma=False,
    )
```

```python
import functools

import jax
import jax.numpy as jnp
from jax import lax
from jax.experimental import pallas as pl
from jax.experimental.pallas import tpu as pltpu
from jax.sharding import PartitionSpec as P

epsilon = 1e-06
SIDE = 4
COUNT = SIDE**3
f32 = jnp.float32
bf16 = jnp.bfloat16
INTERPRET = False


def call(body, outs, args, scratch=(), scalars=0, unused=0, flops=10**9, vmem=58 * 2**20):
    after = len(args) - unused
    specs = [pl.BlockSpec(memory_space=pltpu.SMEM)] * scalars
    specs += [pl.BlockSpec(memory_space=pltpu.VMEM)] * (after - scalars)
    specs += [pl.BlockSpec(memory_space=pl.ANY)] * unused
    moved = sum(a.size * a.dtype.itemsize for a in args[:after])

    def used(*refs):
        body(*refs[:after], *refs[len(args) :])

    return pl.pallas_call(
        used,
        out_shape=[jax.ShapeDtypeStruct(shape, kind) for shape, kind in outs],
        in_specs=specs,
        out_specs=[pl.BlockSpec(memory_space=pltpu.VMEM)] * len(outs),
        scratch_shapes=list(scratch),
        compiler_params=pltpu.CompilerParams(vmem_limit_bytes=vmem),
        cost_estimate=pl.CostEstimate(flops=flops, bytes_accessed=moved, transcendentals=0),
        interpret=INTERPRET,
    )(*args)


def mm(left, right):
    return lax.dot_general(left, right, (((1,), (0,)), ((), ())), preferred_element_type=f32)


def mm_cols(left, right):
    return lax.dot_general(left, right, (((1,), (1,)), ((), ())), preferred_element_type=f32)


def mm_rows(left, right):
    return lax.dot_general(left, right, (((0,), (0,)), ((), ())), preferred_element_type=f32)


def iota(shape, dim):
    return lax.broadcasted_iota(jnp.int32, shape, dim)


def ones_where(mask):
    return jnp.where(mask, 1.0, 0.0).astype(bf16)


def anti(size):
    return ones_where(iota((size, size), 0) + iota((size, size), 1) == size - 1)


def pieces_of(value, count):
    found = []
    for _ in range(count):
        piece = value.astype(bf16)
        found.append(piece)
        value = value - piece.astype(f32)
    return found


def mirror_exact(block):
    turned = mm(block, anti(block.shape[1])).astype(bf16)
    return mm(anti(block.shape[0]), turned).astype(bf16)


def mirror_wide(block):
    high, low = pieces_of(block, 2)
    return mirror_exact(high).astype(f32) + mirror_exact(low).astype(f32)


def head_mask(heads, width):
    lanes = heads * width
    return ones_where(iota((heads, lanes), 0) == iota((heads, lanes), 1) // width)


def expand(value, mask):
    found = pieces_of(value, 3)
    return mm(jnp.concatenate(found, axis=1), jnp.concatenate([mask] * 3, axis=0))


def fold(value, mask, count=2):
    total = None
    for piece in pieces_of(value, count):
        part = mm_cols(piece, mask)
        total = part if total is None else total + part
    return total


def triangle(size, low):
    rows, cols = iota((size, size), 0), iota((size, size), 1)
    return rows >= cols if low else rows <= cols


def tri_sum(mask, value):
    total = None
    for piece in pieces_of(value, 3):
        part = mm(ones_where(mask), piece)
        total = part if total is None else total + part
    return total


def tri_sum_turned(mask, value):
    total = None
    for piece in pieces_of(value, 3):
        part = mm_rows(piece, ones_where(mask))
        total = part if total is None else total + part
    return total


def softplus(value):
    return jnp.maximum(value, 0.0) + jnp.log1p(jnp.exp(-jnp.abs(value)))


def sigmoid(value):
    return 1.0 / (1.0 + jnp.exp(-value))


def norm_rows(block, gain):
    wide = block.astype(f32)
    scale = lax.rsqrt(jnp.mean(wide * wide, axis=-1, keepdims=True) + epsilon)
    return (wide * scale * gain.reshape(1, -1)).astype(bf16)


def pre_kernel(
    seq, up, low, high, gain, in_proj, step_proj, conv_w, conv_b, step_bias, decay_log, out_proj,
    payload, both, normal, normal_halo, cot, gate, conv, d_gated, raw, step, cumul,
    ext,
):
    rows = seq.shape[0]
    inner = out_proj.shape[0]
    heads = step_bias.shape[0]
    state = (conv_w.shape[1] - inner) // 2
    taps = conv_w.shape[0]
    both[:rows, :] = seq[...]
    both[rows:, :] = mirror_exact(seq[...])
    cot[:rows, :] = up[...]
    cot[rows:, :] = mirror_exact(up[...])
    halo = jnp.concatenate([low[...], mirror_exact(high[...])], axis=0)
    normal[...] = norm_rows(both[...], gain[...])
    normal_halo[...] = norm_rows(halo, gain[...])
    gate[...] = mm(normal[...], in_proj[:, :inner]).astype(bf16)
    xbc = mm(normal[...], in_proj[:, inner:]).astype(bf16).astype(f32)
    xbc_halo = mm(normal_halo[...], in_proj[:, inner:]).astype(bf16).astype(f32)
    raw[...] = mm_cols(normal[...], step_proj[...])
    d_gated[...] = mm_cols(cot[...], out_proj[...]).astype(bf16)
    margin = low.shape[0]
    mask = head_mask(heads, inner // heads)
    ends = []
    for frame in range(2):
        at = slice(frame * rows, (frame + 1) * rows)
        ext[:8, :] = xbc_halo[(frame + 1) * margin - 8 : (frame + 1) * margin, :]
        ext[8:, :] = xbc[at, :]
        found = conv_b[...].reshape(1, -1)
        for tap in range(taps):
            start = 9 - taps + tap
            found = found + ext[start : start + rows, :] * conv_w[tap : tap + 1, :]
        conv[at, :] = found.astype(bf16)
        act = found * sigmoid(found)
        size = softplus(raw[at, :] + step_bias[...].reshape(1, -1))
        decay = -jnp.exp(decay_log[...].reshape(1, -1)) * size
        upto = tri_sum(triangle(rows, True), decay)
        step[at, :] = size
        cumul[at, :] = upto
        end = upto[rows - 1 : rows, :]
        ends.append(end)
        spread = expand(jnp.concatenate([size * jnp.exp(end - upto), jnp.exp(upto)], axis=0), mask)
        driven = (act[:, :inner] * spread[:rows]).astype(bf16)
        local = mm_rows(driven, act[:, inner : inner + state].astype(bf16))
        wide = gate[at, :].astype(f32)
        d_mixed = d_gated[at, :].astype(f32) * (wide * sigmoid(wide))
        back = mm_rows((d_mixed * spread[rows:]).astype(bf16), act[:, inner + state :].astype(bf16))
        part = inner // SIDE
        for place, block in ((frame, local), (2 + frame, back)):
            block = block.astype(bf16).reshape(SIDE, part, state)
            payload[:, place * part : (place + 1) * part, :] = block
    packed = pack_totals(ends, heads, state)
    for to in range(SIDE):
        shifted = ones_where(iota((16, heads), 1) == iota((16, heads), 0) + to * (heads // SIDE))
        payload[to, inner:, :] = mm(shifted, packed).astype(bf16)


def pack_totals(ends, heads, state):
    chosen = iota((heads, heads), 0) == iota((heads, heads), 1)
    lanes = iota((heads, state), 1)
    packed = jnp.zeros((heads, state), f32)
    for frame in range(2):
        column = jnp.sum(jnp.where(chosen, ends[frame], 0.0), axis=1, keepdims=True)
        packed = pack_column(packed, column, lanes, frame)
    return packed.astype(bf16)


def pack_column(packed, column, lanes, frame):
    for nth, piece in enumerate(pieces_of(column, 3)):
        packed = jnp.where(lanes == 3 * frame + nth, piece.astype(f32), packed)
    return packed


def unpack_column(packed, frame):
    at = 3 * frame
    return (packed[:, at + 2 : at + 3] + packed[:, at + 1 : at + 2]) + packed[:, at : at + 1]


SCANS = ((0, False), (1, True), (0, True), (1, False))


def chain(got, totals, place, state, visit):
    frame, turned = SCANS[place]
    part = state.shape[0]
    size = part // SIDE
    order = range(SIDE - 1, -1, -1) if turned else range(SIDE)
    for at in order:
        visit(at, state)
        grown = jnp.exp(totals[at][frame])
        factors = [
            jnp.broadcast_to(grown[head : head + 1, :], (size, 1)) for head in range(part // size)
        ]
        state = jnp.concatenate(factors, axis=0) * state
        state = state + got[at, place * part : (place + 1) * part, :].astype(f32)
    return state


def tails_of(got, inner):
    found = []
    for at in range(SIDE):
        tail = got[at, inner:, :].astype(f32)
        found.append([unpack_column(tail, frame) for frame in range(2)])
    return found


def group_kernel(got, out):
    state = got.shape[2]
    inner = got.shape[1] - 16
    part = inner // SIDE
    totals = tails_of(got, inner)
    blocks = []
    for place in range(4):
        block = chain(got, totals, place, jnp.zeros((part, state), f32), lambda at, value: None)
        blocks.append(block.reshape(16, 16, state))
    lanes = iota((16, state), 1)
    packed = jnp.zeros((16, state), f32)
    for frame in range(2):
        column = jnp.maximum(totals[0][frame], -110.0)
        for at in range(1, SIDE):
            column = column + jnp.maximum(totals[at][frame], -110.0)
        packed = pack_column(packed, column, lanes, frame)
    chosen = ones_where(iota((16, 16), 1) == iota((16, 16), 0) // SIDE)
    packed = mm(chosen, packed.astype(bf16))
    blocks.append(jnp.broadcast_to(packed.reshape(16, 1, state), (16, 8, state)))
    out[...] = jnp.concatenate(blocks, axis=1).astype(bf16)


def spread_kernel(got, entering, out):
    state = got.shape[2]
    inner = got.shape[1] - 16
    part = inner // SIDE
    totals = tails_of(got, inner)
    for place in range(4):

        def visit(at, value, place=place):
            out[at, place * part : (place + 1) * part, :] = value.astype(bf16)

        block = entering[:, 16 * place : 16 * place + 16, :].astype(f32).reshape(part, state)
        chain(got, totals, place, block, visit)


def scan_kernel(got, out, wide, done):
    count, rows, state = got.shape
    wide[...] = got[...].astype(f32).reshape(count * rows, state)
    tails = wide[pl.ds(64, count, stride=rows), :]
    above = iota((count, count), 0)
    beside = iota((count, count), 1)
    after = ones_where(above > beside)
    weights = []
    for frame in range(2):
        column = jnp.maximum(unpack_column(tails, frame), -110.0)
        line = jnp.sum(jnp.where(above == beside, column, 0.0), axis=0, keepdims=True)
        between = None
        for piece in pieces_of(jnp.where(beside < above, line, 0.0), 3):
            part = mm(piece, after)
            between = part if between is None else between + part
        found = jnp.where(above > beside, jnp.exp(between), 0.0)
        weights.append(pieces_of(found, 2))
    for place, (frame, turned) in enumerate(SCANS):
        pair = weights[frame]
        block = jnp.concatenate(
            [wide[pl.ds(16 * place + row, count, stride=rows), :] for row in range(16)], axis=1
        ).astype(bf16)
        if turned:
            mixed = mm_rows(jnp.concatenate(pair, axis=1), block)
        else:
            mixed = mm(jnp.concatenate(pair, axis=0), block)
        mixed = mixed[:count] + mixed[count:]
        for row in range(16):
            done[pl.ds(16 * place + row, count, stride=64), :] = mixed[:, state * row : state * (row + 1)]
    out[...] = done[...].reshape(count, 64, state).astype(bf16)


def intra_kernel(
    conv, gate, d_gated, step, cumul, decay_log, normal, normal_halo, skip_gain,
    silus, d_gates, pushed, mixed, d_inputs, lefts, held_back, d_convs, bc, d_bc, sums_out, normal_t, halo_t,
):
    for source, target in ((normal, normal_t), (normal_halo, halo_t)):
        count = source.shape[0]
        same = iota((count, count), 0) == iota((count, count), 1)
        target[...] = mm_rows(source[...], ones_where(same)).astype(bf16)
    rows = conv.shape[0] // 2
    inner = gate.shape[1]
    heads = step.shape[1]
    state = (conv.shape[1] - inner) // 2
    mask = head_mask(heads, inner // heads)
    lower = triangle(rows, True)
    first = iota((rows, 2 * inner // heads), 1) < inner // heads
    wide_pair = 2 * inner // heads
    skip = expand(jnp.broadcast_to(skip_gain[...].reshape(1, -1), (8, heads)), mask)[:1]
    for frame in range(2):
        at = slice(frame * rows, (frame + 1) * rows)
        found = conv[at, :].astype(f32)
        share = sigmoid(found)
        act = found * share
        d_convs[at, :] = (share * (1.0 + found * (1.0 - share))).astype(bf16)
        bc[at, :] = act[:, inner:].astype(bf16)
        bmat, cmat = bc[at, :state], bc[at, state:]
        upto = cumul[at, :]
        end = upto[rows - 1 : rows, :]
        spread = expand(jnp.concatenate([step[at, :], jnp.exp(upto), jnp.exp(end - upto)], axis=0), mask)
        sizes, grown, left = spread[:rows], spread[rows : 2 * rows], spread[2 * rows :]
        inputs = act[:, :inner]
        driven = inputs * sizes
        lefts[at, :] = (left * inputs).astype(bf16)
        held_back[at, :] = (left * driven).astype(bf16)
        wide = gate[at, :].astype(f32)
        opened = sigmoid(wide)
        silu = wide * opened
        silus[at, :] = silu.astype(bf16)
        d_out = d_gated[at, :].astype(f32)
        d_gates[at, :] = (d_out * (opened * (1.0 + wide * (1.0 - opened)))).astype(bf16)
        d_mixed = d_out * silu
        pushed[at, :] = (d_mixed * grown).astype(bf16)
        scores = mm_cols(cmat, bmat)
        line = tri_sum_turned(triangle(rows, False), -jnp.exp(decay_log[...].reshape(1, -1)) * step[at, :])
        d_scores = jnp.zeros((rows, rows), f32)
        sums, by_size = [], []
        for pair in range(heads // 2):
            lanes = slice(pair * wide_pair, (pair + 1) * wide_pair)
            decays = []
            for head in (2 * pair, 2 * pair + 1):
                differ = upto[:, head : head + 1] - line[head : head + 1, :]
                decays.append(jnp.exp(jnp.where(lower, differ, -1e30)))
            weights = [(decay * scores).astype(bf16) for decay in decays]
            drive, d_mix = driven[:, lanes], d_mixed[:, lanes]
            drive_bf, d_mix_bf = drive.astype(bf16), d_mix.astype(bf16)
            drive_two = jnp.concatenate(
                [jnp.where(first, drive, 0.0), jnp.where(first, 0.0, drive)], axis=0
            ).astype(bf16)
            d_mix_two = jnp.concatenate(
                [jnp.where(first, d_mix, 0.0), jnp.where(first, 0.0, d_mix)], axis=0
            ).astype(bf16)
            mix = mm(jnp.concatenate(weights, axis=1), drive_two)
            d_weights = mm_cols(d_mix_two, drive_bf)
            d_drive = mm_rows(jnp.concatenate(weights, axis=0), d_mix_two)
            d_scores = d_scores + decays[0] * d_weights[:rows] + decays[1] * d_weights[rows:]
            mixed[at, lanes] = (mix + skip[:, lanes] * inputs[:, lanes]).astype(bf16)
            d_inputs[at, lanes] = (skip[:, lanes] * d_mix + d_drive * sizes[:, lanes]).astype(bf16)
            by_size.append(d_drive * inputs[:, lanes])
            sums.append(d_mix_bf.astype(f32) * mix - drive_bf.astype(f32) * d_drive)
        d_scores = d_scores.astype(bf16)
        d_bc[at, :state] = mm_rows(d_scores, cmat)
        d_bc[at, state:] = mm(d_scores, bmat)
        sums_out[at, :heads] = fold(jnp.concatenate(sums, axis=1), mask)
        sums_out[at, heads:] = fold(jnp.concatenate(by_size, axis=1), mask)


def post_kernel(
    place, got, silus, d_gates, pushed, mixed, d_inputs, lefts, held_back, d_convs, bc, d_bc, sums,
    raw, step, cumul, step_bias, decay_log, conv_w, cot, normal_t, halo_t,
    gated, d_gate, d_xbc, d_first, d_second, d_step, *refs,
):
    by_x, by_y, ext, d_conv_out, whole, parted = refs[:4], refs[4:8], refs[8], refs[9], refs[10], refs[11]
    rows = silus.shape[0] // 2
    inner = silus.shape[1]
    heads = step.shape[1]
    state = bc.shape[1] // 2
    mask = head_mask(heads, inner // heads)
    for frame in range(2):
        at = slice(frame * rows, (frame + 1) * rows)
        upto = cumul[at, :]
        size = step[at, :]
        end = upto[rows - 1 : rows, :]
        spread = expand(jnp.concatenate([jnp.exp(upto), size * jnp.exp(end - upto)], axis=0), mask)
        part = inner // SIDE
        carried = got[:, frame * part : (frame + 1) * part, :].reshape(inner, state)
        reach = got[:, (2 + frame) * part : (3 + frame) * part, :].reshape(inner, state)
        read = mm_cols(bc[at, state:], carried)
        full = mixed[at, :].astype(f32) + spread[:rows] * read
        gated[at, :] = (full * silus[at, :].astype(f32)).astype(bf16)
        d_gate[at, :] = (full * d_gates[at, :].astype(f32)).astype(bf16)
        d_cmat = d_bc[at, state:] + mm(pushed[at, :], carried)
        answer = mm_cols(bc[at, :state], reach)
        d_bmat = d_bc[at, :state] + mm(held_back[at, :], reach)
        products = carried.astype(f32) * reach.astype(f32)
        met = jnp.sum(products.reshape(heads, inner // heads, state), axis=1)
        met = jnp.sum(met, axis=1, keepdims=True)
        met = jnp.sum(jnp.where(iota((heads, heads), 0) == iota((heads, heads), 1), met, 0.0), axis=0, keepdims=True)
        folded = fold(
            jnp.concatenate([lefts[at, :].astype(f32) * answer, pushed[at, :].astype(f32) * read], axis=0), mask, 1
        )
        by_size, entered = folded[:rows], folded[rows:]
        held = by_size * size
        d_end = jnp.exp(end) * met + jnp.sum(held, axis=0, keepdims=True)
        d_decay = tri_sum(triangle(rows, False), sums[at, :heads] + entered - held) + d_end
        d_size = sums[at, heads:] + by_size - jnp.exp(decay_log[...].reshape(1, -1)) * d_decay
        d_step[at, :] = (d_size * sigmoid(raw[at, :] + step_bias[...].reshape(1, -1))).astype(bf16)
        d_act = jnp.concatenate([d_inputs[at, :].astype(f32) + spread[rows:] * answer, d_bmat, d_cmat], axis=1)
        margin = halo_t.shape[1] // 2
        ext[:margin, :] = jnp.zeros((margin, ext.shape[1]), f32)
        ext[margin : margin + rows, :] = d_act * d_convs[at, :].astype(f32)
        ext[margin + rows :, :] = jnp.zeros((8, ext.shape[1]), f32)
        taps = conv_w.shape[0]
        total = None
        for tap in range(taps):
            start = taps - 1 - tap
            part = ext[start : start + margin + rows, :] * conv_w[tap : tap + 1, :]
            total = part if total is None else total + part
        d_xbc[at, :] = total[margin:].astype(bf16)
        d_conv_out[frame * margin : (frame + 1) * margin, :] = total[:margin].astype(bf16)
        (d_first, d_second)[frame][...] = total[margin - 8 : margin]
    columns = cot.shape[1]
    half = d_xbc.shape[1] // 2
    out_term = mm_rows(gated[...], cot[...]).reshape(COUNT, 2, 8, columns)
    gate_term = mm(normal_t[...], d_gate[...]).reshape(COUNT // SIDE, SIDE, 8, inner)
    in_term = mm(normal_t[...], d_xbc[...]) + mm(halo_t[...], d_conv_out[...])
    whole[:, :columns] = out_term[:, 0].reshape(-1, columns).astype(bf16)
    whole[:, columns : 2 * columns] = out_term[:, 1].reshape(-1, columns).astype(bf16)
    whole[:, 2 * columns :] = in_term[:, :half].astype(bf16)
    parted[:, :, :, :inner] = gate_term
    parted[:, :, :, inner:] = in_term[:, half:].reshape(COUNT // SIDE, SIDE, 8, half)
    ring_out(lambda step: chunk_x(place, whole, step), by_x)
    ring_out(lambda step: chunk_y(place, parted, step), by_y)


def chunk_x(place, whole, step):
    chunk = whole.shape[0] // SIDE
    to = lax.rem(place[0] + step, SIDE)
    return whole[pl.ds(pl.multiple_of(to * chunk, chunk), chunk), :].astype(bf16)


def chunk_y(place, parted, step):
    block = parted[:, lax.rem(place[2] + step, SIDE)]
    return block.reshape(-1, block.shape[-1]).astype(bf16)


def ring_out(chunk_of, slots):
    keep, base, right, left = slots
    half = keep.shape[0] // 2
    keep[...] = chunk_of(0)
    ahead, opposite, behind = chunk_of(1), chunk_of(2), chunk_of(3)
    base[:half, :], base[half:, :] = ahead[:half], behind[half:]
    right[:half, :], right[half:, :] = opposite[:half], ahead[half:]
    left[:half, :], left[half:, :] = behind[:half], opposite[half:]


def relay_kernel(base_x, right_x, left_x, base_y, right_y, left_y, to_both, *outs):
    for base, right, left, on_right, on_left in (
        (base_x, right_x, left_x, outs[0], outs[1]),
        (base_y, right_y, left_y, outs[2], outs[3]),
    ):
        half = base.shape[0] // 2
        columns = base.shape[1]
        on_right[:, :columns] = (base[:half, :].astype(f32) + right[:half, :].astype(f32)).astype(bf16)
        on_left[:, :columns] = (base[half:, :].astype(f32) + left[half:, :].astype(f32)).astype(bf16)
    outs[2][:32, columns:] = to_both[:32, :]
    outs[3][:32, columns:] = to_both[32:, :]
    for target in outs[2:]:
        target[32:, columns:] = jnp.zeros((32, 128), bf16)


def ring_total(keep, right, left, on_right, on_left):
    half = keep.shape[0] // 2
    columns = keep.shape[1]
    first = keep[:half, :].astype(f32) + left[:half, :].astype(f32) + on_right[:, :columns].astype(f32)
    second = keep[half:, :].astype(f32) + right[half:, :].astype(f32) + on_left[:, :columns].astype(f32)
    return jnp.concatenate([first, second], axis=0)


def send_x(place, whole, slots):
    chunk = whole.shape[0] // SIDE
    for step in range(SIDE):
        to = lax.rem(place[0] + step, SIDE)
        block = whole[pl.ds(pl.multiple_of(to * chunk, chunk), chunk), :]
        slots[step][...] = block.astype(slots[step].dtype)


def send_y(place, parted, slots):
    for step in range(SIDE):
        block = parted[:, lax.rem(place[2] + step, SIDE)]
        slots[step][...] = block.reshape(slots[step].shape).astype(slots[step].dtype)


def norm_back(block, d_normal, gain):
    wide = block.astype(f32)
    scale = lax.rsqrt(jnp.mean(wide * wide, axis=-1, keepdims=True) + epsilon)
    d_scaled = d_normal * gain.reshape(1, -1)
    along = jnp.mean(d_scaled * wide, axis=-1, keepdims=True)
    return scale * d_scaled - wide * (scale * scale * scale * along)


def fold_rows(block):
    return jnp.concatenate([block[:, 128 * nth : 128 * (nth + 1)] for nth in range(4)], axis=0)


def unfold_rows(block):
    return jnp.concatenate([block[8 * nth : 8 * (nth + 1)] for nth in range(4)], axis=1)


def scalar_flag(condition):
    return jnp.where(condition, 1.0, 0.0)


def result_kernel(
    place, both, gain, gated, out_proj, d_gate, d_xbc, d_first, d_second, low, high, d_step, in_proj, step_proj,
    layer, base, to_both, d_whole,
):
    rows = both.shape[0] // 2
    inner = out_proj.shape[0]
    branch = mm(gated[...], out_proj[...])
    layer[...] = (branch[:rows] + mirror_wide(branch[rows:])).astype(bf16)
    d_whole[: 2 * rows, :] = d_xbc[...]
    edges = jnp.concatenate([d_first[...], d_second[...]], axis=0)
    d_whole[2 * rows :, :] = edges.astype(bf16)
    through = mm_cols(d_whole[...], in_proj[:, inner:])
    d_normal = mm_cols(d_gate[...], in_proj[:, :inner]) + through[: 2 * rows]
    d_normal = d_normal + mm(d_step[...], step_proj[...])
    d_wide = norm_back(both[...], d_normal, gain[...])
    base[...] = d_wide[:rows] + mirror_wide(d_wide[rows:])
    first = norm_back(low[...].astype(f32)[8:], through[2 * rows : 2 * rows + 8], gain[...])
    second = norm_back(mirror_exact(high[...]).astype(f32)[8:], through[2 * rows + 8 :], gain[...])
    at_start = (place[0] + place[1] + place[2]) == 0
    at_end = (place[0] + place[1] + place[2]) == 3 * (SIDE - 1)
    to_both[32:, :] = fold_rows(first * (1.0 - scalar_flag(at_start))).astype(bf16)
    to_both[:32, :] = fold_rows(mirror_wide(second) * (1.0 - scalar_flag(at_end))).astype(bf16)


def total_of(refs):
    total = refs[0][...].astype(f32)
    for ref in refs[1:]:
        total = total + ref[...].astype(f32)
    return total


def first_sum_kernel(place, *refs):
    from_x, from_y, by_y, by_x, kept = refs[:5], refs[5:10], refs[10:14], refs[14:18], refs[18]
    parted, whole = refs[19], refs[20]
    parted[...] = ring_total(*from_x).reshape(parted.shape)
    whole[...] = ring_total(*from_y)
    send_y(place, parted, by_y)
    columns = whole.shape[1]
    chunk = whole.shape[0] // SIDE
    for step in range(SIDE):
        to = lax.rem(place[0] + step, SIDE)
        block = whole[pl.ds(pl.multiple_of(to * chunk, chunk), chunk), :]
        by_x[step][:, :columns] = block.astype(by_x[step].dtype)
    high = from_y[3][:32, columns:].astype(f32)
    low = from_y[4][:32, columns:].astype(f32)
    on_high = scalar_flag((place[2] == 0) & (place[1] == SIDE - 1))
    on_low = scalar_flag((place[2] == SIDE - 1) & (place[1] == 0))
    by_x[1][:, columns:] = (high * on_high).astype(bf16)
    by_x[3][:, columns:] = (low * on_low).astype(bf16)
    kept[:32, :] = high * (1.0 - on_high)
    kept[32:, :] = low * (1.0 - on_low)


def second_sum_kernel(place, *refs):
    first, second, kept, by_z, kept_on, keep = refs[:4], refs[4:8], refs[8], refs[9:13], refs[13], refs[14]
    columns = first[0].shape[1]
    high = kept[:32, :] + second[1][:, columns:].astype(f32)
    low = kept[32:, :] + second[3][:, columns:].astype(f32)
    first = total_of(first).reshape(SIDE, 8, -1)
    total = second[0][...]
    for step in range(1, SIDE):
        total = total + second[step][:, :columns].astype(f32)
    second = total.reshape(SIDE, 8, -1)
    above = scalar_flag(place[2] == 0)
    below = scalar_flag(place[2] == SIDE - 1)
    keep[:, 0] = first
    keep[:, 1] = second
    for step in range(SIDE):
        block = keep[lax.rem(place[1] + step, SIDE)].reshape(16, columns)
        by_z[step][:, :columns] = block.astype(by_z[step].dtype)
    for step, edge, share in ((1, high, above), (3, low, below)):
        edge = edge * share
        by_z[step][:, columns:] = jnp.concatenate([edge[:16], edge[16:]], axis=1).astype(bf16)
    kept_on[:32, :] = high * (1.0 - above)
    kept_on[32:, :] = low * (1.0 - below)


def last_sum_kernel(own, up, across, down, kept, base, grad_in, grad_out, grad):
    joined = own.shape[1]
    total = own[...] + up[:, :joined].astype(f32) + across[...].astype(f32) + down[:, :joined].astype(f32)
    columns = grad_out.shape[1]
    grad_out[:8, :] = total[:8, :columns]
    grad_out[8:, :] = total[:8, columns : 2 * columns]
    grad_in[...] = jnp.concatenate([total[8:, : 2 * columns], total[:8, 2 * columns :], total[8:, 2 * columns :]], axis=1)
    edges = []
    for nth, recv in enumerate((up, down)):
        recv = recv[:, joined:].astype(f32)
        recv = jnp.concatenate([recv[:, :128], recv[:, 128:]], axis=0)
        edges.append(unfold_rows(kept[32 * nth : 32 * nth + 32, :] + recv))
    rows = base.shape[0]
    whole = jnp.concatenate([base[:8, :] + edges[0], base[8 : rows - 8, :], base[rows - 8 :, :] + edges[1]], axis=0)
    grad[...] = whole.astype(bf16)


def axis_pairs(stride, step):
    pairs = []
    for source in range(COUNT):
        digit = source // stride % SIDE
        pairs.append((source, source + ((digit + step) % SIDE - digit) * stride))
    return pairs


def exchange(parts, stride):
    return [parts[0]] + [lax.ppermute(parts[step], "seq", axis_pairs(stride, step)) for step in range(1, SIDE)]


def around(to_right, to_left, stride):
    return (
        lax.ppermute(to_right, "seq", axis_pairs(stride, 1)),
        lax.ppermute(to_left, "seq", axis_pairs(stride, SIDE - 1)),
    )


def transpose_over(parts, groups):
    return lax.all_to_all(parts, "seq", 0, 0, axis_index_groups=groups)


def slots(rows, columns, kind):
    return [((rows, columns), kind)] + [((rows, columns), bf16)] * (SIDE - 1)


def shards(
    sequence,
    upstream,
    norm_gain,
    in_proj,
    step_proj,
    conv_weight,
    conv_bias,
    step_bias,
    decay_log,
    skip_gain,
    out_proj,
):
    rows, width = sequence.shape
    inner = out_proj.shape[0]
    heads = step_bias.shape[0]
    state = inner // heads * 2
    channels = conv_weight.shape[1]
    both_rows = 2 * rows
    stride_x, stride_z, stride_y = SIDE * SIDE, SIDE, 1
    index = lax.axis_index("seq")
    place = jnp.stack([index // stride_x, index // stride_z % SIDE, index % SIDE]).astype(jnp.int32)
    beside = [[SIDE * base + digit for digit in range(SIDE)] for base in range(COUNT // SIDE)]
    across = [[base + SIDE * digit for digit in range(COUNT // SIDE)] for base in range(SIDE)]
    upward = [(i, i + 1) for i in range(COUNT - 1)]
    downward = [(i + 1, i) for i in range(COUNT - 1)]
    low = lax.ppermute(sequence[rows - 16 :], "seq", upward)
    high = lax.ppermute(sequence[:16], "seq", downward)
    step_turned = step_proj.T
    payload, both, normal, normal_halo, cot, gate, conv, d_gated, raw, step, cumul = call(
        pre_kernel,
        [
            ((SIDE, inner + 16, state), bf16),
            ((both_rows, width), bf16),
            ((both_rows, width), bf16),
            ((32, width), bf16),
            ((both_rows, width), bf16),
            ((both_rows, inner), bf16),
            ((both_rows, channels), bf16),
            ((both_rows, inner), bf16),
            ((both_rows, heads), f32),
            ((both_rows, heads), f32),
            ((both_rows, heads), f32),
        ],
        (
            sequence, upstream, low, high, norm_gain, in_proj, step_turned,
            conv_weight, conv_bias, step_bias, decay_log, out_proj,
        ),
        [pltpu.VMEM((rows + 8, channels), f32)],
    )
    got = transpose_over(payload, beside)
    (summary,) = call(group_kernel, [((COUNT // SIDE, 72, state), bf16)], (got,), vmem=16 * 2**20)
    summaries = transpose_over(summary, across)
    inner_values = call(
        intra_kernel,
        [((both_rows, inner), bf16)] * 7
        + [
            ((both_rows, channels), bf16),
            ((both_rows, 2 * state), bf16),
            ((both_rows, 2 * state), f32),
            ((both_rows, 2 * heads), f32),
            ((width, both_rows), bf16),
            ((width, 32), bf16),
        ],
        (conv, gate, d_gated, step, cumul, decay_log, normal, normal_halo, skip_gain),
        flops=8 * 10**9,
    )
    normal_t, halo_t = inner_values[-2:]
    groups = COUNT // SIDE
    (scanned,) = call(
        scan_kernel,
        [((groups, 64, state), bf16)],
        (summaries,),
        [pltpu.VMEM((groups * 72, state), f32), pltpu.VMEM((groups * 64, state), f32)],
        vmem=16 * 2**20,
    )
    entering = transpose_over(scanned, across)
    (spread,) = call(spread_kernel, [((SIDE, inner, state), bf16)], (got, entering), vmem=16 * 2**20)
    states = transpose_over(spread, beside)
    eighth = 8 * COUNT // SIDE
    joined = inner + channels // 2
    gated, d_gate, d_xbc, d_first, d_second, d_step, *parts = call(
        post_kernel,
        [
            ((both_rows, inner), bf16),
            ((both_rows, inner), bf16),
            ((both_rows, channels), bf16),
            ((8, channels), f32),
            ((8, channels), f32),
            ((both_rows, heads), bf16),
        ]
        + slots(eighth, joined, bf16) * 2,
        (
            place, states, *inner_values[:-2], raw, step, cumul,
            step_bias, decay_log, conv_weight, cot, normal_t, halo_t,
        ),
        [
            pltpu.VMEM((rows + 24, channels), f32),
            pltpu.VMEM((32, channels), bf16),
            pltpu.VMEM((8 * COUNT, joined), bf16),
            pltpu.VMEM((COUNT // SIDE, SIDE, 8, joined), f32),
        ],
        scalars=1,
    )
    layer_out, base, to_both = call(
        result_kernel,
        [((rows, width), bf16), ((rows, width), f32), ((64, 128), bf16)],
        (
            place, both, norm_gain, gated, out_proj, d_gate, d_xbc, d_first, d_second, low, high, d_step,
            in_proj, step_turned,
        ),
        [pltpu.VMEM((both_rows + 16, channels), bf16)],
        scalars=1,
        flops=8 * 10**9,
    )
    keep_x, base_x, right_x, left_x, keep_y, base_y, right_y, left_y = parts
    right_x, left_x = around(right_x, left_x, stride_x)
    right_y, left_y = around(right_y, left_y, stride_y)
    relayed = call(
        relay_kernel,
        [((eighth // 2, joined), bf16)] * 2 + [((eighth // 2, joined + 128), bf16)] * 2,
        (base_x, right_x, left_x, base_y, right_y, left_y, to_both),
        vmem=16 * 2**20,
    )
    from_x = [keep_x, right_x, left_x, *around(relayed[0], relayed[1], stride_x)]
    from_y = [keep_y, right_y, left_y, *around(relayed[2], relayed[3], stride_y)]
    small = eighth // SIDE
    *parts, kept = call(
        first_sum_kernel,
        slots(small, joined, f32)
        + [((small, joined), f32), ((small, joined + 128), bf16), ((small, joined), bf16), ((small, joined + 128), bf16)]
        + [((64, 128), f32)],
        (place, *from_x, *from_y),
        [pltpu.VMEM((SIDE, SIDE, 8, joined), f32), pltpu.VMEM((eighth, joined), f32)],
        scalars=1,
        vmem=16 * 2**20,
    )
    first = exchange(parts[:4], stride_y)
    second = exchange(parts[4:], stride_x)
    *parts, kept = call(
        second_sum_kernel,
        [((16, joined), f32), ((16, joined + 256), bf16), ((16, joined), bf16), ((16, joined + 256), bf16)]
        + [((64, 128), f32)],
        (place, *first, *second, kept),
        [pltpu.VMEM((SIDE, 2, 8, joined), f32)],
        scalars=1,
        vmem=16 * 2**20,
    )
    last = exchange(parts, stride_z)
    grad_in_proj, grad_out_proj, grad_input = call(
        last_sum_kernel,
        [((8, inner + channels), f32), ((16, width), f32), ((rows, width), bf16)],
        (*last, kept, base),
        vmem=16 * 2**20,
    )
    return (layer_out, grad_input, grad_in_proj, grad_out_proj)


def solution(mesh):
    rows = P(("batch", "seq"), None)
    return jax.shard_map(
        shards,
        mesh=mesh,
        in_specs=(rows, rows) + (P(),) * 9,
        out_specs=(rows,) * 4,
        check_vma=False,
    )
```

```python
import functools

import jax
import jax.numpy as jnp
from jax import lax
from jax.experimental import pallas as pl
from jax.experimental.pallas import tpu as pltpu
from jax.sharding import PartitionSpec as P

epsilon = 1e-06
SIDE = 4
COUNT = SIDE**3
f32 = jnp.float32
bf16 = jnp.bfloat16
INTERPRET = False


def call(body, outs, args, scratch=(), scalars=0, unused=0, flops=10**9, vmem=58 * 2**20):
    after = len(args) - unused
    specs = [pl.BlockSpec(memory_space=pltpu.SMEM)] * scalars
    specs += [pl.BlockSpec(memory_space=pltpu.VMEM)] * (after - scalars)
    specs += [pl.BlockSpec(memory_space=pl.ANY)] * unused
    moved = sum(a.size * a.dtype.itemsize for a in args[:after])

    def used(*refs):
        body(*refs[:after], *refs[len(args) :])

    return pl.pallas_call(
        used,
        out_shape=[jax.ShapeDtypeStruct(shape, kind) for shape, kind in outs],
        in_specs=specs,
        out_specs=[pl.BlockSpec(memory_space=pltpu.VMEM)] * len(outs),
        scratch_shapes=list(scratch),
        compiler_params=pltpu.CompilerParams(vmem_limit_bytes=vmem),
        cost_estimate=pl.CostEstimate(flops=flops, bytes_accessed=moved, transcendentals=0),
        interpret=INTERPRET,
    )(*args)


def mm(left, right):
    return lax.dot_general(left, right, (((1,), (0,)), ((), ())), preferred_element_type=f32)


def mm_cols(left, right):
    return lax.dot_general(left, right, (((1,), (1,)), ((), ())), preferred_element_type=f32)


def mm_rows(left, right):
    return lax.dot_general(left, right, (((0,), (0,)), ((), ())), preferred_element_type=f32)


def iota(shape, dim):
    return lax.broadcasted_iota(jnp.int32, shape, dim)


def ones_where(mask):
    return jnp.where(mask, 1.0, 0.0).astype(bf16)


def anti(size):
    return ones_where(iota((size, size), 0) + iota((size, size), 1) == size - 1)


def pieces_of(value, count):
    found = []
    for _ in range(count):
        piece = value.astype(bf16)
        found.append(piece)
        value = value - piece.astype(f32)
    return found


def mirror_exact(block):
    turned = mm(block, anti(block.shape[1])).astype(bf16)
    return mm(anti(block.shape[0]), turned).astype(bf16)


def mirror_wide(block):
    high, low = pieces_of(block, 2)
    return mirror_exact(high).astype(f32) + mirror_exact(low).astype(f32)


def head_mask(heads, width):
    lanes = heads * width
    return ones_where(iota((heads, lanes), 0) == iota((heads, lanes), 1) // width)


def expand(value, mask):
    found = pieces_of(value, 3)
    return mm(jnp.concatenate(found, axis=1), jnp.concatenate([mask] * 3, axis=0))


def fold(value, mask, count=2):
    total = None
    for piece in pieces_of(value, count):
        part = mm_cols(piece, mask)
        total = part if total is None else total + part
    return total


def triangle(size, low):
    rows, cols = iota((size, size), 0), iota((size, size), 1)
    return rows >= cols if low else rows <= cols


def tri_sum(mask, value):
    total = None
    for piece in pieces_of(value, 3):
        part = mm(ones_where(mask), piece)
        total = part if total is None else total + part
    return total


def tri_sum_turned(mask, value):
    total = None
    for piece in pieces_of(value, 3):
        part = mm_rows(piece, ones_where(mask))
        total = part if total is None else total + part
    return total


def softplus(value):
    return jnp.maximum(value, 0.0) + jnp.log1p(jnp.exp(-jnp.abs(value)))


def sigmoid(value):
    return 1.0 / (1.0 + jnp.exp(-value))


def norm_rows(block, gain):
    wide = block.astype(f32)
    scale = lax.rsqrt(jnp.mean(wide * wide, axis=-1, keepdims=True) + epsilon)
    return (wide * scale * gain.reshape(1, -1)).astype(bf16)


def pre_kernel(
    seq, up, low, high, gain, in_proj, step_proj, conv_w, conv_b, step_bias, decay_log, out_proj,
    payload, both, normal, normal_halo, cot, gate, conv, d_gated, raw, step, cumul, cumul_t,
    ext,
):
    rows = seq.shape[0]
    inner = out_proj.shape[0]
    heads = step_bias.shape[0]
    state = (conv_w.shape[1] - inner) // 2
    taps = conv_w.shape[0]
    both[:rows, :] = seq[...]
    both[rows:, :] = mirror_exact(seq[...])
    cot[:rows, :] = up[...]
    cot[rows:, :] = mirror_exact(up[...])
    halo = jnp.concatenate([low[...], mirror_exact(high[...])], axis=0)
    normal[...] = norm_rows(both[...], gain[...])
    normal_halo[...] = norm_rows(halo, gain[...])
    gate[...] = mm(normal[...], in_proj[:, :inner]).astype(bf16)
    xbc = mm(normal[...], in_proj[:, inner:]).astype(bf16).astype(f32)
    xbc_halo = mm(normal_halo[...], in_proj[:, inner:]).astype(bf16).astype(f32)
    raw[...] = mm_cols(normal[...], step_proj[...])
    d_gated[...] = mm_cols(cot[...], out_proj[...]).astype(bf16)
    margin = low.shape[0]
    mask = head_mask(heads, inner // heads)
    ends = []
    for frame in range(2):
        at = slice(frame * rows, (frame + 1) * rows)
        ext[:8, :] = xbc_halo[(frame + 1) * margin - 8 : (frame + 1) * margin, :]
        ext[8:, :] = xbc[at, :]
        found = conv_b[...].reshape(1, -1)
        for tap in range(taps):
            start = 9 - taps + tap
            found = found + ext[start : start + rows, :] * conv_w[tap : tap + 1, :]
        conv[at, :] = found.astype(bf16)
        act = found * sigmoid(found)
        size = softplus(raw[at, :] + step_bias[...].reshape(1, -1))
        decay = -jnp.exp(decay_log[...].reshape(1, -1)) * size
        upto = tri_sum(triangle(rows, True), decay)
        step[at, :] = size
        cumul[at, :] = upto
        cumul_t[frame * heads : (frame + 1) * heads, :] = tri_sum_turned(triangle(rows, False), decay)
        end = upto[rows - 1 : rows, :]
        ends.append(end)
        spread = expand(jnp.concatenate([size * jnp.exp(end - upto), jnp.exp(upto)], axis=0), mask)
        driven = (act[:, :inner] * spread[:rows]).astype(bf16)
        local = mm_rows(driven, act[:, inner : inner + state].astype(bf16))
        wide = gate[at, :].astype(f32)
        d_mixed = d_gated[at, :].astype(f32) * (wide * sigmoid(wide))
        back = mm_rows((d_mixed * spread[rows:]).astype(bf16), act[:, inner + state :].astype(bf16))
        part = inner // SIDE
        for place, block in ((frame, local), (2 + frame, back)):
            block = block.astype(bf16).reshape(SIDE, part, state)
            payload[:, place * part : (place + 1) * part, :] = block
    packed = pack_totals(ends, heads, state)
    for to in range(SIDE):
        shifted = ones_where(iota((16, heads), 1) == iota((16, heads), 0) + to * (heads // SIDE))
        payload[to, inner:, :] = mm(shifted, packed).astype(bf16)


def pack_totals(ends, heads, state):
    chosen = iota((heads, heads), 0) == iota((heads, heads), 1)
    lanes = iota((heads, state), 1)
    packed = jnp.zeros((heads, state), f32)
    for frame in range(2):
        column = jnp.sum(jnp.where(chosen, ends[frame], 0.0), axis=1, keepdims=True)
        packed = pack_column(packed, column, lanes, frame)
    return packed.astype(bf16)


def pack_column(packed, column, lanes, frame):
    for nth, piece in enumerate(pieces_of(column, 3)):
        packed = jnp.where(lanes == 3 * frame + nth, piece.astype(f32), packed)
    return packed


def unpack_column(packed, frame):
    at = 3 * frame
    return (packed[:, at + 2 : at + 3] + packed[:, at + 1 : at + 2]) + packed[:, at : at + 1]


SCANS = ((0, False), (1, True), (0, True), (1, False))


def chain(got, totals, place, state, visit):
    frame, turned = SCANS[place]
    part = state.shape[0]
    size = part // SIDE
    order = range(SIDE - 1, -1, -1) if turned else range(SIDE)
    for at in order:
        visit(at, state)
        grown = jnp.exp(totals[at][frame])
        factors = [
            jnp.broadcast_to(grown[head : head + 1, :], (size, 1)) for head in range(part // size)
        ]
        state = jnp.concatenate(factors, axis=0) * state
        state = state + got[at, place * part : (place + 1) * part, :].astype(f32)
    return state


def tails_of(got, inner):
    found = []
    for at in range(SIDE):
        tail = got[at, inner:, :].astype(f32)
        found.append([unpack_column(tail, frame) for frame in range(2)])
    return found


def group_kernel(got, out):
    state = got.shape[2]
    inner = got.shape[1] - 16
    part = inner // SIDE
    totals = tails_of(got, inner)
    blocks = []
    for place in range(4):
        block = chain(got, totals, place, jnp.zeros((part, state), f32), lambda at, value: None)
        blocks.append(block.reshape(16, 16, state))
    lanes = iota((16, state), 1)
    packed = jnp.zeros((16, state), f32)
    for frame in range(2):
        column = jnp.maximum(totals[0][frame], -110.0)
        for at in range(1, SIDE):
            column = column + jnp.maximum(totals[at][frame], -110.0)
        packed = pack_column(packed, column, lanes, frame)
    chosen = ones_where(iota((16, 16), 1) == iota((16, 16), 0) // SIDE)
    packed = mm(chosen, packed.astype(bf16))
    blocks.append(jnp.broadcast_to(packed.reshape(16, 1, state), (16, 8, state)))
    out[...] = jnp.concatenate(blocks, axis=1).astype(bf16)


def spread_kernel(got, entering, out):
    state = got.shape[2]
    inner = got.shape[1] - 16
    part = inner // SIDE
    totals = tails_of(got, inner)
    for place in range(4):

        def visit(at, value, place=place):
            out[at, place * part : (place + 1) * part, :] = value.astype(bf16)

        block = entering[:, 16 * place : 16 * place + 16, :].astype(f32).reshape(part, state)
        chain(got, totals, place, block, visit)


def scan_kernel(got, out, wide, done):
    count, rows, state = got.shape
    wide[...] = got[...].astype(f32).reshape(count * rows, state)
    tails = wide[pl.ds(64, count, stride=rows), :]
    above = iota((count, count), 0)
    beside = iota((count, count), 1)
    after = ones_where(above > beside)
    weights = []
    for frame in range(2):
        column = jnp.maximum(unpack_column(tails, frame), -110.0)
        line = jnp.sum(jnp.where(above == beside, column, 0.0), axis=0, keepdims=True)
        between = None
        for piece in pieces_of(jnp.where(beside < above, line, 0.0), 3):
            part = mm(piece, after)
            between = part if between is None else between + part
        found = jnp.where(above > beside, jnp.exp(between), 0.0)
        weights.append(pieces_of(found, 2))
    for place, (frame, turned) in enumerate(SCANS):
        pair = weights[frame]
        block = jnp.concatenate(
            [wide[pl.ds(16 * place + row, count, stride=rows), :] for row in range(16)], axis=1
        ).astype(bf16)
        if turned:
            mixed = mm_rows(jnp.concatenate(pair, axis=1), block)
        else:
            mixed = mm(jnp.concatenate(pair, axis=0), block)
        mixed = mixed[:count] + mixed[count:]
        for row in range(16):
            done[pl.ds(16 * place + row, count, stride=64), :] = mixed[:, state * row : state * (row + 1)]
    out[...] = done[...].reshape(count, 64, state).astype(bf16)


def intra_kernel(
    conv, gate, d_gated, step, cumul, cumul_t, normal, normal_halo, skip_gain,
    silus, d_gates, pushed, mixed, d_inputs, lefts, held_back, d_convs, bc, d_bc, sums_out, normal_t, halo_t,
):
    for source, target in ((normal, normal_t), (normal_halo, halo_t)):
        count = source.shape[0]
        same = iota((count, count), 0) == iota((count, count), 1)
        target[...] = mm_rows(source[...], ones_where(same)).astype(bf16)
    rows = conv.shape[0] // 2
    inner = gate.shape[1]
    heads = step.shape[1]
    state = (conv.shape[1] - inner) // 2
    mask = head_mask(heads, inner // heads)
    lower = triangle(rows, True)
    first = iota((rows, 2 * inner // heads), 1) < inner // heads
    wide_pair = 2 * inner // heads
    skip = expand(jnp.broadcast_to(skip_gain[...].reshape(1, -1), (8, heads)), mask)[:1]
    for frame in range(2):
        at = slice(frame * rows, (frame + 1) * rows)
        found = conv[at, :].astype(f32)
        share = sigmoid(found)
        act = found * share
        d_convs[at, :] = (share * (1.0 + found * (1.0 - share))).astype(bf16)
        bc[at, :] = act[:, inner:].astype(bf16)
        bmat, cmat = bc[at, :state], bc[at, state:]
        upto = cumul[at, :]
        end = upto[rows - 1 : rows, :]
        spread = expand(jnp.concatenate([step[at, :], jnp.exp(upto), jnp.exp(end - upto)], axis=0), mask)
        sizes, grown, left = spread[:rows], spread[rows : 2 * rows], spread[2 * rows :]
        inputs = act[:, :inner]
        driven = inputs * sizes
        lefts[at, :] = (left * inputs).astype(bf16)
        held_back[at, :] = (left * driven).astype(bf16)
        wide = gate[at, :].astype(f32)
        opened = sigmoid(wide)
        silu = wide * opened
        silus[at, :] = silu.astype(bf16)
        d_out = d_gated[at, :].astype(f32)
        d_gates[at, :] = (d_out * (opened * (1.0 + wide * (1.0 - opened)))).astype(bf16)
        d_mixed = d_out * silu
        pushed[at, :] = (d_mixed * grown).astype(bf16)
        scores = mm_cols(cmat, bmat)
        line = cumul_t[frame * heads : (frame + 1) * heads, :]
        d_scores = jnp.zeros((rows, rows), f32)
        sums, by_size = [], []
        for pair in range(heads // 2):
            lanes = slice(pair * wide_pair, (pair + 1) * wide_pair)
            decays = []
            for head in (2 * pair, 2 * pair + 1):
                differ = upto[:, head : head + 1] - line[head : head + 1, :]
                decays.append(jnp.exp(jnp.where(lower, differ, -1e30)))
            weights = [(decay * scores).astype(bf16) for decay in decays]
            drive, d_mix = driven[:, lanes], d_mixed[:, lanes]
            drive_bf, d_mix_bf = drive.astype(bf16), d_mix.astype(bf16)
            drive_two = jnp.concatenate(
                [jnp.where(first, drive, 0.0), jnp.where(first, 0.0, drive)], axis=0
            ).astype(bf16)
            d_mix_two = jnp.concatenate(
                [jnp.where(first, d_mix, 0.0), jnp.where(first, 0.0, d_mix)], axis=0
            ).astype(bf16)
            mix = mm(jnp.concatenate(weights, axis=1), drive_two)
            d_weights = mm_cols(d_mix_two, drive_bf)
            d_drive = mm_rows(jnp.concatenate(weights, axis=0), d_mix_two)
            d_scores = d_scores + decays[0] * d_weights[:rows] + decays[1] * d_weights[rows:]
            mixed[at, lanes] = (mix + skip[:, lanes] * inputs[:, lanes]).astype(bf16)
            d_inputs[at, lanes] = (skip[:, lanes] * d_mix + d_drive * sizes[:, lanes]).astype(bf16)
            by_size.append(d_drive * inputs[:, lanes])
            sums.append(d_mix_bf.astype(f32) * mix - drive_bf.astype(f32) * d_drive)
        d_scores = d_scores.astype(bf16)
        d_bc[at, :state] = mm_rows(d_scores, cmat)
        d_bc[at, state:] = mm(d_scores, bmat)
        sums_out[at, :heads] = fold(jnp.concatenate(sums, axis=1), mask)
        sums_out[at, heads:] = fold(jnp.concatenate(by_size, axis=1), mask)


def post_kernel(
    place, got, silus, d_gates, pushed, mixed, d_inputs, lefts, held_back, d_convs, bc, d_bc, sums,
    raw, step, cumul, step_bias, decay_log, conv_w, cot, normal_t, halo_t,
    gated, d_gate, d_xbc, d_first, d_second, d_step, *refs,
):
    by_x, by_y, ext, d_conv_out, whole, parted = refs[:4], refs[4:8], refs[8], refs[9], refs[10], refs[11]
    rows = silus.shape[0] // 2
    inner = silus.shape[1]
    heads = step.shape[1]
    state = bc.shape[1] // 2
    mask = head_mask(heads, inner // heads)
    for frame in range(2):
        at = slice(frame * rows, (frame + 1) * rows)
        upto = cumul[at, :]
        size = step[at, :]
        end = upto[rows - 1 : rows, :]
        spread = expand(jnp.concatenate([jnp.exp(upto), size * jnp.exp(end - upto)], axis=0), mask)
        part = inner // SIDE
        carried = got[:, frame * part : (frame + 1) * part, :].reshape(inner, state)
        reach = got[:, (2 + frame) * part : (3 + frame) * part, :].reshape(inner, state)
        read = mm_cols(bc[at, state:], carried)
        full = mixed[at, :].astype(f32) + spread[:rows] * read
        gated[at, :] = (full * silus[at, :].astype(f32)).astype(bf16)
        d_gate[at, :] = (full * d_gates[at, :].astype(f32)).astype(bf16)
        d_cmat = d_bc[at, state:] + mm(pushed[at, :], carried)
        answer = mm_cols(bc[at, :state], reach)
        d_bmat = d_bc[at, :state] + mm(held_back[at, :], reach)
        products = carried.astype(f32) * reach.astype(f32)
        met = jnp.sum(products.reshape(heads, inner // heads, state), axis=1)
        met = jnp.sum(met, axis=1, keepdims=True)
        met = jnp.sum(jnp.where(iota((heads, heads), 0) == iota((heads, heads), 1), met, 0.0), axis=0, keepdims=True)
        folded = fold(
            jnp.concatenate([lefts[at, :].astype(f32) * answer, pushed[at, :].astype(f32) * read], axis=0), mask, 1
        )
        by_size, entered = folded[:rows], folded[rows:]
        held = by_size * size
        d_end = jnp.exp(end) * met + jnp.sum(held, axis=0, keepdims=True)
        d_decay = tri_sum(triangle(rows, False), sums[at, :heads] + entered - held) + d_end
        d_size = sums[at, heads:] + by_size - jnp.exp(decay_log[...].reshape(1, -1)) * d_decay
        d_step[at, :] = (d_size * sigmoid(raw[at, :] + step_bias[...].reshape(1, -1))).astype(bf16)
        d_act = jnp.concatenate([d_inputs[at, :].astype(f32) + spread[rows:] * answer, d_bmat, d_cmat], axis=1)
        margin = halo_t.shape[1] // 2
        ext[:margin, :] = jnp.zeros((margin, ext.shape[1]), f32)
        ext[margin : margin + rows, :] = d_act * d_convs[at, :].astype(f32)
        ext[margin + rows :, :] = jnp.zeros((8, ext.shape[1]), f32)
        taps = conv_w.shape[0]
        total = None
        for tap in range(taps):
            start = taps - 1 - tap
            part = ext[start : start + margin + rows, :] * conv_w[tap : tap + 1, :]
            total = part if total is None else total + part
        d_xbc[at, :] = total[margin:].astype(bf16)
        d_conv_out[frame * margin : (frame + 1) * margin, :] = total[:margin].astype(bf16)
        (d_first, d_second)[frame][...] = total[margin - 8 : margin]
    columns = cot.shape[1]
    half = d_xbc.shape[1] // 2
    out_term = mm_rows(gated[...], cot[...]).reshape(COUNT, 2, 8, columns)
    gate_term = mm(normal_t[...], d_gate[...]).reshape(COUNT // SIDE, SIDE, 8, inner)
    in_term = mm(normal_t[...], d_xbc[...]) + mm(halo_t[...], d_conv_out[...])
    whole[:, :columns] = out_term[:, 0].reshape(-1, columns).astype(bf16)
    whole[:, columns : 2 * columns] = out_term[:, 1].reshape(-1, columns).astype(bf16)
    whole[:, 2 * columns :] = in_term[:, :half].astype(bf16)
    parted[:, :, :, :inner] = gate_term
    parted[:, :, :, inner:] = in_term[:, half:].reshape(COUNT // SIDE, SIDE, 8, half)
    ring_out(lambda step: chunk_x(place, whole, step), by_x)
    ring_out(lambda step: chunk_y(place, parted, step), by_y)


def chunk_x(place, whole, step):
    chunk = whole.shape[0] // SIDE
    to = lax.rem(place[0] + step, SIDE)
    return whole[pl.ds(pl.multiple_of(to * chunk, chunk), chunk), :].astype(bf16)


def chunk_y(place, parted, step):
    block = parted[:, lax.rem(place[2] + step, SIDE)]
    return block.reshape(-1, block.shape[-1]).astype(bf16)


def ring_out(chunk_of, slots):
    keep, base, right, left = slots
    half = keep.shape[0] // 2
    keep[...] = chunk_of(0)
    ahead, opposite, behind = chunk_of(1), chunk_of(2), chunk_of(3)
    base[:half, :], base[half:, :] = ahead[:half], behind[half:]
    right[:half, :], right[half:, :] = opposite[:half], ahead[half:]
    left[:half, :], left[half:, :] = behind[:half], opposite[half:]


def relay_kernel(base_x, right_x, left_x, base_y, right_y, left_y, to_both, *outs):
    for base, right, left, on_right, on_left in (
        (base_x, right_x, left_x, outs[0], outs[1]),
        (base_y, right_y, left_y, outs[2], outs[3]),
    ):
        half = base.shape[0] // 2
        columns = base.shape[1]
        on_right[:, :columns] = (base[:half, :].astype(f32) + right[:half, :].astype(f32)).astype(bf16)
        on_left[:, :columns] = (base[half:, :].astype(f32) + left[half:, :].astype(f32)).astype(bf16)
    outs[2][:32, columns:] = to_both[:32, :]
    outs[3][:32, columns:] = to_both[32:, :]
    for target in outs[2:]:
        target[32:, columns:] = jnp.zeros((32, 128), bf16)


def ring_total(keep, right, left, on_right, on_left):
    half = keep.shape[0] // 2
    columns = keep.shape[1]
    first = keep[:half, :].astype(f32) + left[:half, :].astype(f32) + on_right[:, :columns].astype(f32)
    second = keep[half:, :].astype(f32) + right[half:, :].astype(f32) + on_left[:, :columns].astype(f32)
    return jnp.concatenate([first, second], axis=0)


def send_x(place, whole, slots):
    chunk = whole.shape[0] // SIDE
    for step in range(SIDE):
        to = lax.rem(place[0] + step, SIDE)
        block = whole[pl.ds(pl.multiple_of(to * chunk, chunk), chunk), :]
        slots[step][...] = block.astype(slots[step].dtype)


def send_y(place, parted, slots):
    for step in range(SIDE):
        block = parted[:, lax.rem(place[2] + step, SIDE)]
        slots[step][...] = block.reshape(slots[step].shape).astype(slots[step].dtype)


def norm_back(block, d_normal, gain):
    wide = block.astype(f32)
    scale = lax.rsqrt(jnp.mean(wide * wide, axis=-1, keepdims=True) + epsilon)
    d_scaled = d_normal * gain.reshape(1, -1)
    along = jnp.mean(d_scaled * wide, axis=-1, keepdims=True)
    return scale * d_scaled - wide * (scale * scale * scale * along)


def fold_rows(block):
    return jnp.concatenate([block[:, 128 * nth : 128 * (nth + 1)] for nth in range(4)], axis=0)


def unfold_rows(block):
    return jnp.concatenate([block[8 * nth : 8 * (nth + 1)] for nth in range(4)], axis=1)


def scalar_flag(condition):
    return jnp.where(condition, 1.0, 0.0)


def result_kernel(
    place, both, gain, gated, out_proj, d_gate, d_xbc, d_first, d_second, low, high, d_step, in_proj, step_proj,
    layer, base, to_both, d_whole,
):
    rows = both.shape[0] // 2
    inner = out_proj.shape[0]
    branch = mm(gated[...], out_proj[...])
    layer[...] = (branch[:rows] + mirror_wide(branch[rows:])).astype(bf16)
    d_whole[: 2 * rows, :] = d_xbc[...]
    edges = jnp.concatenate([d_first[...], d_second[...]], axis=0)
    d_whole[2 * rows :, :] = edges.astype(bf16)
    through = mm_cols(d_whole[...], in_proj[:, inner:])
    d_normal = mm_cols(d_gate[...], in_proj[:, :inner]) + through[: 2 * rows]
    d_normal = d_normal + mm(d_step[...], step_proj[...])
    d_wide = norm_back(both[...], d_normal, gain[...])
    base[...] = d_wide[:rows] + mirror_wide(d_wide[rows:])
    first = norm_back(low[...].astype(f32)[8:], through[2 * rows : 2 * rows + 8], gain[...])
    second = norm_back(mirror_exact(high[...]).astype(f32)[8:], through[2 * rows + 8 :], gain[...])
    at_start = (place[0] + place[1] + place[2]) == 0
    at_end = (place[0] + place[1] + place[2]) == 3 * (SIDE - 1)
    to_both[32:, :] = fold_rows(first * (1.0 - scalar_flag(at_start))).astype(bf16)
    to_both[:32, :] = fold_rows(mirror_wide(second) * (1.0 - scalar_flag(at_end))).astype(bf16)


def total_of(refs):
    total = refs[0][...].astype(f32)
    for ref in refs[1:]:
        total = total + ref[...].astype(f32)
    return total


def first_sum_kernel(place, *refs):
    from_x, from_y, by_y, by_x, kept = refs[:5], refs[5:10], refs[10:14], refs[14:18], refs[18]
    parted, whole = refs[19], refs[20]
    parted[...] = ring_total(*from_x).reshape(parted.shape)
    whole[...] = ring_total(*from_y)
    send_y(place, parted, by_y)
    columns = whole.shape[1]
    chunk = whole.shape[0] // SIDE
    for step in range(SIDE):
        to = lax.rem(place[0] + step, SIDE)
        block = whole[pl.ds(pl.multiple_of(to * chunk, chunk), chunk), :]
        by_x[step][:, :columns] = block.astype(by_x[step].dtype)
    high = from_y[3][:32, columns:].astype(f32)
    low = from_y[4][:32, columns:].astype(f32)
    on_high = scalar_flag((place[2] == 0) & (place[1] == SIDE - 1))
    on_low = scalar_flag((place[2] == SIDE - 1) & (place[1] == 0))
    by_x[1][:, columns:] = (high * on_high).astype(bf16)
    by_x[3][:, columns:] = (low * on_low).astype(bf16)
    kept[:32, :] = high * (1.0 - on_high)
    kept[32:, :] = low * (1.0 - on_low)


def second_sum_kernel(place, *refs):
    first, second, kept, by_z, kept_on, keep = refs[:4], refs[4:8], refs[8], refs[9:13], refs[13], refs[14]
    columns = first[0].shape[1]
    high = kept[:32, :] + second[1][:, columns:].astype(f32)
    low = kept[32:, :] + second[3][:, columns:].astype(f32)
    first = total_of(first).reshape(SIDE, 8, -1)
    total = second[0][...]
    for step in range(1, SIDE):
        total = total + second[step][:, :columns].astype(f32)
    second = total.reshape(SIDE, 8, -1)
    above = scalar_flag(place[2] == 0)
    below = scalar_flag(place[2] == SIDE - 1)
    keep[:, 0] = first
    keep[:, 1] = second
    for step in range(SIDE):
        block = keep[lax.rem(place[1] + step, SIDE)].reshape(16, columns)
        by_z[step][:, :columns] = block.astype(by_z[step].dtype)
    for step, edge, share in ((1, high, above), (3, low, below)):
        edge = edge * share
        by_z[step][:, columns:] = jnp.concatenate([edge[:16], edge[16:]], axis=1).astype(bf16)
    kept_on[:32, :] = high * (1.0 - above)
    kept_on[32:, :] = low * (1.0 - below)


def last_sum_kernel(own, up, across, down, kept, base, grad_in, grad_out, grad):
    joined = own.shape[1]
    total = own[...] + up[:, :joined].astype(f32) + across[...].astype(f32) + down[:, :joined].astype(f32)
    columns = grad_out.shape[1]
    grad_out[:8, :] = total[:8, :columns]
    grad_out[8:, :] = total[:8, columns : 2 * columns]
    grad_in[...] = jnp.concatenate([total[8:, : 2 * columns], total[:8, 2 * columns :], total[8:, 2 * columns :]], axis=1)
    edges = []
    for nth, recv in enumerate((up, down)):
        recv = recv[:, joined:].astype(f32)
        recv = jnp.concatenate([recv[:, :128], recv[:, 128:]], axis=0)
        edges.append(unfold_rows(kept[32 * nth : 32 * nth + 32, :] + recv))
    rows = base.shape[0]
    whole = jnp.concatenate([base[:8, :] + edges[0], base[8 : rows - 8, :], base[rows - 8 :, :] + edges[1]], axis=0)
    grad[...] = whole.astype(bf16)


def axis_pairs(stride, step):
    pairs = []
    for source in range(COUNT):
        digit = source // stride % SIDE
        pairs.append((source, source + ((digit + step) % SIDE - digit) * stride))
    return pairs


def exchange(parts, stride):
    return [parts[0]] + [lax.ppermute(parts[step], "seq", axis_pairs(stride, step)) for step in range(1, SIDE)]


def around(to_right, to_left, stride):
    return (
        lax.ppermute(to_right, "seq", axis_pairs(stride, 1)),
        lax.ppermute(to_left, "seq", axis_pairs(stride, SIDE - 1)),
    )


def transpose_over(parts, groups):
    return lax.all_to_all(parts, "seq", 0, 0, axis_index_groups=groups)


def slots(rows, columns, kind):
    return [((rows, columns), kind)] + [((rows, columns), bf16)] * (SIDE - 1)


def shards(
    sequence,
    upstream,
    norm_gain,
    in_proj,
    step_proj,
    conv_weight,
    conv_bias,
    step_bias,
    decay_log,
    skip_gain,
    out_proj,
):
    rows, width = sequence.shape
    inner = out_proj.shape[0]
    heads = step_bias.shape[0]
    state = inner // heads * 2
    channels = conv_weight.shape[1]
    both_rows = 2 * rows
    stride_x, stride_z, stride_y = SIDE * SIDE, SIDE, 1
    index = lax.axis_index("seq")
    place = jnp.stack([index // stride_x, index // stride_z % SIDE, index % SIDE]).astype(jnp.int32)
    beside = [[SIDE * base + digit for digit in range(SIDE)] for base in range(COUNT // SIDE)]
    across = [[base + SIDE * digit for digit in range(COUNT // SIDE)] for base in range(SIDE)]
    upward = [(i, i + 1) for i in range(COUNT - 1)]
    downward = [(i + 1, i) for i in range(COUNT - 1)]
    low = lax.ppermute(sequence[rows - 16 :], "seq", upward)
    high = lax.ppermute(sequence[:16], "seq", downward)
    step_turned = step_proj.T
    payload, both, normal, normal_halo, cot, gate, conv, d_gated, raw, step, cumul, cumul_t = call(
        pre_kernel,
        [
            ((SIDE, inner + 16, state), bf16),
            ((both_rows, width), bf16),
            ((both_rows, width), bf16),
            ((32, width), bf16),
            ((both_rows, width), bf16),
            ((both_rows, inner), bf16),
            ((both_rows, channels), bf16),
            ((both_rows, inner), bf16),
            ((both_rows, heads), f32),
            ((both_rows, heads), f32),
            ((both_rows, heads), f32),
            ((2 * heads, rows), f32),
        ],
        (
            sequence, upstream, low, high, norm_gain, in_proj, step_turned,
            conv_weight, conv_bias, step_bias, decay_log, out_proj,
        ),
        [pltpu.VMEM((rows + 8, channels), f32)],
    )
    got = transpose_over(payload, beside)
    (summary,) = call(group_kernel, [((COUNT // SIDE, 72, state), bf16)], (got,), vmem=16 * 2**20)
    summaries = transpose_over(summary, across)
    inner_values = call(
        intra_kernel,
        [((both_rows, inner), bf16)] * 7
        + [
            ((both_rows, channels), bf16),
            ((both_rows, 2 * state), bf16),
            ((both_rows, 2 * state), f32),
            ((both_rows, 2 * heads), f32),
            ((width, both_rows), bf16),
            ((width, 32), bf16),
        ],
        (conv, gate, d_gated, step, cumul, cumul_t, normal, normal_halo, skip_gain),
        flops=8 * 10**9,
    )
    normal_t, halo_t = inner_values[-2:]
    groups = COUNT // SIDE
    (scanned,) = call(
        scan_kernel,
        [((groups, 64, state), bf16)],
        (summaries,),
        [pltpu.VMEM((groups * 72, state), f32), pltpu.VMEM((groups * 64, state), f32)],
        vmem=16 * 2**20,
    )
    entering = transpose_over(scanned, across)
    (spread,) = call(spread_kernel, [((SIDE, inner, state), bf16)], (got, entering), vmem=16 * 2**20)
    states = transpose_over(spread, beside)
    eighth = 8 * COUNT // SIDE
    joined = inner + channels // 2
    gated, d_gate, d_xbc, d_first, d_second, d_step, *parts = call(
        post_kernel,
        [
            ((both_rows, inner), bf16),
            ((both_rows, inner), bf16),
            ((both_rows, channels), bf16),
            ((8, channels), f32),
            ((8, channels), f32),
            ((both_rows, heads), bf16),
        ]
        + slots(eighth, joined, bf16) * 2,
        (
            place, states, *inner_values[:-2], raw, step, cumul,
            step_bias, decay_log, conv_weight, cot, normal_t, halo_t,
        ),
        [
            pltpu.VMEM((rows + 24, channels), f32),
            pltpu.VMEM((32, channels), bf16),
            pltpu.VMEM((8 * COUNT, joined), bf16),
            pltpu.VMEM((COUNT // SIDE, SIDE, 8, joined), f32),
        ],
        scalars=1,
    )
    layer_out, base, to_both = call(
        result_kernel,
        [((rows, width), bf16), ((rows, width), f32), ((64, 128), bf16)],
        (
            place, both, norm_gain, gated, out_proj, d_gate, d_xbc, d_first, d_second, low, high, d_step,
            in_proj, step_turned,
        ),
        [pltpu.VMEM((both_rows + 16, channels), bf16)],
        scalars=1,
        flops=8 * 10**9,
    )
    keep_x, base_x, right_x, left_x, keep_y, base_y, right_y, left_y = parts
    right_x, left_x = around(right_x, left_x, stride_x)
    right_y, left_y = around(right_y, left_y, stride_y)
    relayed = call(
        relay_kernel,
        [((eighth // 2, joined), bf16)] * 2 + [((eighth // 2, joined + 128), bf16)] * 2,
        (base_x, right_x, left_x, base_y, right_y, left_y, to_both),
        vmem=16 * 2**20,
    )
    from_x = [keep_x, right_x, left_x, *around(relayed[0], relayed[1], stride_x)]
    from_y = [keep_y, right_y, left_y, *around(relayed[2], relayed[3], stride_y)]
    small = eighth // SIDE
    *parts, kept = call(
        first_sum_kernel,
        slots(small, joined, f32)
        + [((small, joined), f32), ((small, joined + 128), bf16), ((small, joined), bf16), ((small, joined + 128), bf16)]
        + [((64, 128), f32)],
        (place, *from_x, *from_y),
        [pltpu.VMEM((SIDE, SIDE, 8, joined), f32), pltpu.VMEM((eighth, joined), f32)],
        scalars=1,
        vmem=16 * 2**20,
    )
    first = exchange(parts[:4], stride_y)
    second = exchange(parts[4:], stride_x)
    *parts, kept = call(
        second_sum_kernel,
        [((16, joined), f32), ((16, joined + 256), bf16), ((16, joined), bf16), ((16, joined + 256), bf16)]
        + [((64, 128), f32)],
        (place, *first, *second, kept),
        [pltpu.VMEM((SIDE, 2, 8, joined), f32)],
        scalars=1,
        vmem=16 * 2**20,
    )
    last = exchange(parts, stride_z)
    grad_in_proj, grad_out_proj, grad_input = call(
        last_sum_kernel,
        [((8, inner + channels), f32), ((16, width), f32), ((rows, width), bf16)],
        (*last, kept, base),
        vmem=16 * 2**20,
    )
    return (layer_out, grad_input, grad_in_proj, grad_out_proj)


def solution(mesh):
    rows = P(("batch", "seq"), None)
    return jax.shard_map(
        shards,
        mesh=mesh,
        in_specs=(rows, rows) + (P(),) * 9,
        out_specs=(rows,) * 4,
        check_vma=False,
    )
```
